32 devices in a mesh: seq: 1, res: 32 (over z, y, x, core).
Axes of the slice: x: 2, y: 2, z: 4, core: 2. Of those that a mesh axis runs over, the one named last changes fastest.
Arguments:
- extra_activations: bfloat16 [32, 65536], P('seq', 'res'), may hold values from -6 to 6
- twofold_representation: bfloat16 [1024, 1024, 128], P('res', 'seq'), may hold values from -6 to 6
- present_indicator: int32 [32, 1024], P('seq', 'res'), may hold values 0 or 1
- amino_presence: int32 [1024], P('res'), may hold values 0 or 1
- twofold_offset_matrix: bfloat16 [128, 8], replicated, may hold values from -1.5859375 to 1.5859375
- horizontal_matrix: bfloat16 [64, 256], replicated, may hold values from -8 to 8, as said below
- horizontal_exit_matrix: bfloat16 [64, 64], replicated, may hold values from -1.5 to 1.5
- vertical_matrix: bfloat16 [64, 144], replicated, may hold values from -8 to 8, as said below
- vertical_exit_matrix: bfloat16 [64, 64], replicated, may hold values from -0.75 to 0.75
Outputs:
- msa_out: bfloat16 [32, 65536], P('seq', 'res')
The draws below stay inside these ranges and needn't reach their ends.
Inputs may be any that keep to these rules, and one draw needn't show every extreme that they name: `horizontal_matrix`: a projection matrix. `vertical_matrix`: a projection matrix.
All inputs are finite; a program needn't handle non-finite values. No bound on the sum of `present_indicator` or of `amino_presence` on one device may be relied on, other than what follows from the above.
Results may differ from the reference program's by a relative error of at most 0.02.
The reference program's roundings to bfloat16 on the way count: a program that leaves them out, or rounds other values in their place, can miss the bound.
Values may be sent and summed in bfloat16 or wider, within the bound.
No kernel may reach another device: no remote copies, remote signals or barrier semaphores. Data moves between devices by JAX's collectives and lax.ppermute only.
A program may use at most 64 MiB of HBM per device.

```python
import jax
import jax.numpy as jnp
from jax import lax

EXTRA_FEATURES = 64
CZ = 128
ATTN_HEAD_SUM = 8
PER_HEAD_FEATURE = 8
HOMOLOG_SUM = 32
AMINO_ACID_SUM = 1024


def draw_extra_activations(key, part):
    key = jax.random.fold_in(key, 37)
    random_first = jax.random.fold_in(key, 0)
    random_draws = jax.random.normal(random_first, (HOMOLOG_SUM, AMINO_ACID_SUM, EXTRA_FEATURES), jnp.float32)
    answer_tuple = random_draws
    answer_tuple = jnp.clip(answer_tuple, -6.0, 6.0)
    return answer_tuple.reshape(HOMOLOG_SUM, AMINO_ACID_SUM * EXTRA_FEATURES).astype(jnp.bfloat16)


def draw_horizontal_matrix(key, part):
    key = jax.random.fold_in(key, 11)
    random_first, random_second = jax.random.split(key)
    hidden_size = ATTN_HEAD_SUM * PER_HEAD_FEATURE
    broadcast_factor = jax.random.normal(random_first, (EXTRA_FEATURES, hidden_size), jnp.float32) * EXTRA_FEATURES ** (-0.5)
    remainder_list = jax.random.normal(random_second, (EXTRA_FEATURES, 3 * hidden_size), jnp.float32) * EXTRA_FEATURES ** (-0.5)
    queries = broadcast_factor
    keyed = remainder_list[:, :hidden_size]
    answer_tuple = jnp.concatenate([queries, keyed, remainder_list[:, hidden_size:]], axis=1)
    return answer_tuple.astype(jnp.bfloat16)


def draw_vertical_matrix(key, part):
    key = jax.random.fold_in(key, 23)
    random_second = jax.random.fold_in(key, 1)
    random_third = jax.random.fold_in(key, 2)
    hidden_size = ATTN_HEAD_SUM * PER_HEAD_FEATURE
    remainder_list = jax.random.normal(random_second, (EXTRA_FEATURES, 2 * hidden_size), jnp.float32) * EXTRA_FEATURES ** (-0.5)
    trailing_part = jax.random.normal(random_third, (EXTRA_FEATURES, 2 * PER_HEAD_FEATURE), jnp.float32) * EXTRA_FEATURES ** (-0.5)
    queries = remainder_list[:, :hidden_size]
    keyed = trailing_part[:, :PER_HEAD_FEATURE]
    answer_tuple = jnp.concatenate([queries, remainder_list[:, hidden_size:], keyed, trailing_part[:, PER_HEAD_FEATURE:]], axis=1)
    return answer_tuple.astype(jnp.bfloat16)


def touch_ends(result, rng, low, top_value):
    longest = result.shape.index(max(result.shape))
    spots = []
    for shift in (0, 1):
        where = [jax.random.randint(jax.random.fold_in(rng, axis), (), 0, length) for axis, length in enumerate(result.shape)]
        where[longest] = (where[longest] + shift) % result.shape[longest]
        spots.append(tuple(where))
    return result.at[spots[0]].set(low).at[spots[1]].set(top_value)


def shard_levels(stream_key, extent, shards, smallest, top_value):
    level, own = 1.0, jax.random.fold_in(stream_key, 6)
    for position, blocks in shards:
        draws = jnp.exp(jax.random.uniform(jax.random.fold_in(own, position), (blocks,), jnp.float32, smallest / len(shards), top_value / len(shards)))
        level = level * jnp.repeat(draws, extent[position] // blocks).reshape([-1 if axis == position else 1 for axis in range(len(extent))])
    return level


def noise(stream_key, shape, width, limit, cuts=(), kind=jnp.bfloat16):
    entries = jax.random.normal(stream_key, shape, jnp.float32) * width
    if len(cuts) > 0:
        entries = shard_levels(stream_key, shape, cuts, -0.22, 0.18) * entries
    return jnp.clip(entries, min=-limit, max=limit).astype(kind)


def setup_inputs(seed: int = 0) -> dict:
    keys = jax.random.split(jax.random.key(seed), 10)
    extra_activations = draw_extra_activations(jax.random.fold_in(keys[9], 71), 0)
    twofold_representation = noise(keys[1], (AMINO_ACID_SUM, AMINO_ACID_SUM, CZ), 1.0, 6.0, ((0, 32),))
    present_indicator = touch_ends((jax.random.randint(keys[2], (HOMOLOG_SUM, AMINO_ACID_SUM), 0, 20) < 17).astype(jnp.int32), jax.random.fold_in(keys[2], 1), 0, 1)
    amino_presence = touch_ends((jax.random.randint(keys[3], (AMINO_ACID_SUM,), 0, 10) < 9).astype(jnp.int32), jax.random.fold_in(keys[3], 1), 0, 1)
    twofold_offset_matrix = noise(keys[4], (CZ, ATTN_HEAD_SUM), (3 * CZ ** -0.5), 1.5859375)
    horizontal_matrix = draw_horizontal_matrix(jax.random.fold_in(keys[9], 71), 0)
    horizontal_exit_matrix = noise(keys[6], (ATTN_HEAD_SUM * PER_HEAD_FEATURE, EXTRA_FEATURES), (2 * (ATTN_HEAD_SUM * PER_HEAD_FEATURE) ** -0.5), 1.5)
    vertical_matrix = draw_vertical_matrix(jax.random.fold_in(keys[9], 71), 0)
    vertical_exit_matrix = noise(keys[8], (ATTN_HEAD_SUM * PER_HEAD_FEATURE, EXTRA_FEATURES), (ATTN_HEAD_SUM * PER_HEAD_FEATURE) ** -0.5, 0.75)
    return dict(extra_activations=extra_activations, twofold_representation=twofold_representation, present_indicator=present_indicator, amino_presence=amino_presence, twofold_offset_matrix=twofold_offset_matrix, horizontal_matrix=horizontal_matrix, horizontal_exit_matrix=horizontal_exit_matrix, vertical_matrix=vertical_matrix, vertical_exit_matrix=vertical_exit_matrix)


def layer_normalize(values_in):
    centre = values_in - lax.optimization_barrier(jnp.mean(values_in, axis=-1, keepdims=True))
    spread = lax.optimization_barrier(jnp.mean(centre * centre, axis=-1, keepdims=True))
    return centre * lax.rsqrt(spread + 1e-05)

def column_delta(homolog_line, kept_entries, vertical_matrix, vertical_exit_matrix, head_number, head_channel_width):
    sequence_count, column_count, feature_size = homolog_line.shape
    hidden_size = head_number * head_channel_width
    column_normalized = layer_normalize(homolog_line.astype(jnp.float32)).astype(jnp.bfloat16)
    mapped_linear = jnp.dot(column_normalized.reshape(-1, feature_size), vertical_matrix, preferred_element_type=jnp.float32)
    mapped_linear = mapped_linear.reshape(sequence_count, column_count, -1)
    column_query = mapped_linear[..., :hidden_size]
    column_gate = mapped_linear[..., hidden_size:2 * hidden_size]
    column_key = mapped_linear[..., 2 * hidden_size:2 * hidden_size + head_channel_width]
    column_value = mapped_linear[..., 2 * hidden_size + head_channel_width:]
    query_total = lax.optimization_barrier(jnp.sum(kept_entries[..., None] * column_query, axis=0))
    kept_count = lax.optimization_barrier(jnp.sum(kept_entries, axis=0))
    mean_query = query_total / jnp.maximum(kept_count, 1.0)[:, None] * head_channel_width ** (-0.5)
    logits = jnp.einsum('ihc,sic->sih', mean_query.reshape(column_count, head_number, head_channel_width), column_key)
    logits = logits + 1000000000.0 * (kept_entries - 1.0)[..., None]
    exped = jnp.exp(logits - lax.optimization_barrier(jnp.max(logits, axis=0, keepdims=True)))
    attended_output = jnp.einsum('sih,sic->ihc', exped, column_value) / lax.optimization_barrier(jnp.sum(exped, axis=0))[..., None]
    gated = jax.nn.sigmoid(column_gate).reshape(sequence_count, column_count, head_number, head_channel_width) * attended_output[None]
    gated = gated.reshape(sequence_count * column_count, hidden_size).astype(jnp.bfloat16)
    horizontal_update = jnp.dot(gated, vertical_exit_matrix, preferred_element_type=jnp.float32).reshape(sequence_count, column_count, feature_size)
    return (homolog_line.astype(jnp.float32) + horizontal_update).astype(jnp.bfloat16)

def reference(extra_activations, twofold_representation, present_indicator, amino_presence, twofold_offset_matrix, horizontal_matrix, horizontal_exit_matrix, vertical_matrix, vertical_exit_matrix):
    hidden_size = ATTN_HEAD_SUM * PER_HEAD_FEATURE
    horizontal_items = extra_activations.reshape(HOMOLOG_SUM, AMINO_ACID_SUM, EXTRA_FEATURES)
    kept_entries = (present_indicator * amino_presence[None, :]).astype(jnp.float32)
    standardised = layer_normalize(horizontal_items.astype(jnp.float32)).astype(jnp.bfloat16)
    mapped_linear = jnp.dot(standardised.reshape(-1, EXTRA_FEATURES), horizontal_matrix, preferred_element_type=jnp.float32)
    mapped_linear = mapped_linear.reshape(HOMOLOG_SUM, AMINO_ACID_SUM, 4 * hidden_size)
    queries = (mapped_linear[..., :hidden_size] * PER_HEAD_FEATURE ** (-0.5)).astype(jnp.bfloat16)
    keys_all = mapped_linear[..., hidden_size:2 * hidden_size].astype(jnp.bfloat16)
    values_all = mapped_linear[..., 2 * hidden_size:3 * hidden_size].astype(jnp.bfloat16)
    gating = mapped_linear[..., 3 * hidden_size:]
    pair_normed = layer_normalize(twofold_representation.astype(jnp.float32)).astype(jnp.bfloat16)
    pair_bias = jnp.dot(pair_normed.reshape(-1, CZ), twofold_offset_matrix, preferred_element_type=jnp.float32)
    pair_bias = pair_bias.reshape(AMINO_ACID_SUM, AMINO_ACID_SUM, ATTN_HEAD_SUM).astype(jnp.bfloat16)
    bias_heads = jnp.transpose(pair_bias.astype(jnp.float32), (2, 0, 1))

    def one_row(inputs):
        row_query, row_key, row_value, row_kept = inputs
        query_heads = row_query.astype(jnp.float32).reshape(AMINO_ACID_SUM, ATTN_HEAD_SUM, PER_HEAD_FEATURE)
        key_heads = row_key.astype(jnp.float32).reshape(AMINO_ACID_SUM, ATTN_HEAD_SUM, PER_HEAD_FEATURE)
        value_heads = row_value.astype(jnp.float32).reshape(AMINO_ACID_SUM, ATTN_HEAD_SUM, PER_HEAD_FEATURE)
        logits = jnp.einsum('ihc,jhc->hij', query_heads, key_heads) + bias_heads
        logits = logits + 1000000000.0 * (row_kept - 1.0)[None, None, :]
        exped = jnp.exp(logits - lax.optimization_barrier(jnp.max(logits, axis=-1, keepdims=True)))
        weights = exped.astype(jnp.bfloat16).astype(jnp.float32)
        summed = jnp.einsum('hij,jhc->ihc', weights, value_heads)
        summed = summed / jnp.transpose(lax.optimization_barrier(jnp.sum(exped, axis=-1)), (1, 0))[..., None]
        return summed.reshape(AMINO_ACID_SUM, hidden_size)
    attended_output = lax.map(one_row, (queries, keys_all, values_all, kept_entries))
    row_gated = (jax.nn.sigmoid(gating) * attended_output).astype(jnp.bfloat16)
    horizontal_update = jnp.dot(row_gated.reshape(-1, hidden_size), horizontal_exit_matrix, preferred_element_type=jnp.float32)
    homolog_line = (horizontal_items.astype(jnp.float32) + horizontal_update.reshape(HOMOLOG_SUM, AMINO_ACID_SUM, EXTRA_FEATURES)).astype(jnp.bfloat16)
    ultimate_update = column_delta(homolog_line, kept_entries, vertical_matrix, vertical_exit_matrix, ATTN_HEAD_SUM, PER_HEAD_FEATURE)
    return ultimate_update.reshape(HOMOLOG_SUM, AMINO_ACID_SUM * EXTRA_FEATURES)
```

```python
import functools
import math

import jax
import jax.numpy as jnp
from jax import lax
from jax.experimental import pallas as pl
from jax.experimental.pallas import tpu as pltpu
from jax.sharding import PartitionSpec as P

F32 = jnp.float32
BF16 = jnp.bfloat16
LOG2E = math.log2(math.e)
EPS = 1e-05
VMEM_LIMIT = 56 * 1024 * 1024

NT = (((1,), (1,)), ((), ()))


def mm(a, b):
    return jnp.dot(a, b, preferred_element_type=F32)


def mm_nt(a, b):
    return lax.dot_general(a, b, NT, preferred_element_type=F32)


def iota(shape, axis):
    return lax.broadcasted_iota(jnp.int32, shape, axis)


def one_hot(condition):
    return jnp.where(condition, 1.0, 0.0).astype(BF16)


def block_matrix(size, block, on_diagonal, elsewhere):
    row, col = iota((size, size), 0), iota((size, size), 1)
    inside = jnp.where(row == col, on_diagonal, elsewhere)
    return jnp.where(row // block == col // block, inside, 0.0).astype(BF16)


def halves(value):
    high = value.astype(BF16)
    return high, (value - high.astype(F32)).astype(BF16)


def mm_split(value, matrix):
    high, low = halves(value)
    return mm(high, matrix) + mm(low, matrix)


def paired_norm(x, width):
    lanes = x.shape[1]
    centre = mm(x, block_matrix(lanes, width, 1.0 - 1.0 / width, -1.0 / width))
    spread = mm_split(centre * centre, block_matrix(lanes, width, 1.0 / width, 1.0 / width))
    return (centre * lax.rsqrt(spread + EPS)).astype(BF16)


def row_shuffle(rows, inner, outer):
    total = rows.shape[0]
    row, col = iota((total, total), 0), iota((total, total), 1)
    return mm(one_hot(col == (row % inner) * outer + row // inner), rows).astype(BF16)


def prep_kernel(groups, m_ref, present_ref, amino_ref, *outs):
    chunk_refs, line_ref = outs[:groups], outs[groups]
    lines, width = m_ref.shape
    pairs = width // 128
    stacked = jnp.concatenate([m_ref[:, t * 128 : (t + 1) * 128] for t in range(pairs)], axis=0)
    normed = paired_norm(stacked, 64)
    both = row_shuffle(jnp.concatenate([normed, stacked], axis=1), pairs, lines)
    line_ref[...] = both[:, 128:]
    kept = (present_ref[...] * amino_ref[...]).astype(F32).astype(BF16)
    size = lines // groups
    residues = 2 * pairs
    for g in range(groups):
        chunk_refs[g][: size * pairs, :] = both[g * size * pairs : (g + 1) * size * pairs, :128]
        row, col = iota((128, lines), 0), iota((128, lines), 1)
        spread = mm(one_hot((row % size == col - g * size) & (row < 2 * size)), kept).astype(BF16)
        row, col = iota((pairs, residues), 0), iota((pairs, residues), 1)
        even = mm_nt(one_hot(col == 2 * row), spread)
        odd = mm_nt(one_hot(col == 2 * row + 1), spread)
        chunk_refs[g][size * pairs :, :] = jnp.where(
            iota((pairs, 128), 1) < size, even, odd
        ).astype(BF16)


def bias_kernel(x_ref, w_ref, out_ref, acc_ref):
    step = pl.program_id(0)
    heads = w_ref.shape[0]
    per_step, keys, channels = x_ref.shape
    centring = block_matrix(channels, channels, 1.0 - 1.0 / channels, -1.0 / channels)
    mean_row = jnp.full((heads, channels), 1.0 / channels, BF16)
    for n in range(per_step):
        centre = mm(x_ref[n], centring).astype(BF16)
        projected = mm_nt(w_ref[...], centre)
        spread = mm_nt(mean_row, centre * centre)
        start = pl.multiple_of((step * per_step + n) * heads, heads)
        acc_ref[pl.ds(start, heads), :] = projected * lax.rsqrt(spread + EPS)

    @pl.when(step == pl.num_programs(0) - 1)
    def _():
        out_ref[...] = acc_ref[...].astype(BF16)


def order_kernel(residues, index_of, me_ref, bias_ref, out_ref):
    keys = bias_ref.shape[1]
    lane = iota((1, keys), 1)
    half = keys // 2
    parity, rest = lane // half, lane % half
    place, pair = rest // (residues // 2), rest % (residues // 2)
    target = (index_of(place) ^ me_ref[0]) * residues + 2 * pair + parity
    piece = 256
    total = jnp.zeros(bias_ref.shape, F32)
    for start in range(0, keys, piece):
        chosen = one_hot(iota((piece, keys), 0) + start == target)
        total = total + mm(bias_ref[:, start : start + piece], chosen)
    out_ref[...] = total * LOG2E


def attend_kernel(heads, pieces, size, pairs, own_ref, wq_ref, wk_ref, wv_ref, bias_ref, *refs):
    piece_refs, out_ref, mask_ref, query_ref = refs[: len(pieces)], refs[-3], refs[-2], refs[-1]
    depth = 128 // (2 * heads)
    rows = pairs * 2 * heads
    order = sorted(
        (place, n, k) for n, places in enumerate(pieces) for k, place in enumerate(places)
    )
    keys = len(order) * pairs
    present = jnp.concatenate(
        [piece_refs[n][k, size * pairs :, :] for _, n, k in order], axis=0
    )
    identity = one_hot(iota((2 * size, 128), 0) == iota((2 * size, 128), 1))
    mask_ref[...] = (1e9 * LOG2E) * (mm_nt(identity, present) - 1.0)
    query = mm(own_ref[: size * pairs, :], wq_ref[...]) * (depth**-0.5)
    query_ref[...] = query.astype(BF16).astype(F32)
    lane, row = iota((2 * heads, 128), 1), iota((2 * heads, 128), 0)
    own_head = jnp.where(lane // depth == row, 1.0, 0.0)[None]
    low_lanes = iota((rows, 128), 1) < 64

    def one_line(s, carry):
        q = query_ref[pl.ds(pl.multiple_of(s * pairs, pairs), pairs), :]
        spread = (q[:, None, :] * own_head).reshape(rows, 128).astype(BF16)
        folded = (mm(spread, wk_ref[...]) * LOG2E).astype(BF16)
        start = pl.multiple_of(s * pairs, pairs)
        keyed = jnp.concatenate(
            [piece_refs[n][k, pl.ds(start, pairs), :] for _, n, k in order], axis=0
        )
        logits = [
            mm_nt(folded[:, 128 * p : 128 * (p + 1)], keyed)
            + bias_ref[:, p * keys : (p + 1) * keys]
            + mask_ref[pl.ds(p * size + s, 1), :]
            for p in range(2)
        ]
        peak = jnp.max(jnp.maximum(logits[0], logits[1]), axis=-1, keepdims=True)
        exped = [jnp.exp2(part - peak) for part in logits]
        total = jnp.sum(exped[0] + exped[1], axis=-1, keepdims=True)
        summed = [mm(part.astype(BF16), keyed) for part in exped]
        mean = (jnp.where(low_lanes, summed[0], summed[1]) / total).astype(BF16)
        valued = mm(mean, wv_ref[...]).reshape(pairs, 2 * heads, 128)
        out_ref[pl.ds(start, pairs), :] = jnp.sum(valued * own_head, axis=1)
        return carry

    lax.fori_loop(0, size, one_line, 0)


def final_kernel(
    lines, with_column, normed_refs, line_ref, attended_refs, present_ref, amino_ref, weights, out_ref
):
    wg, wo, wc, wout = weights
    total = line_ref.shape[0]
    pairs = total // lines
    normed = jnp.concatenate([r[: total // len(normed_refs), :] for r in normed_refs], axis=0)
    attended = jnp.concatenate([r[...] for r in attended_refs], axis=0)
    gated = (jax.nn.sigmoid(mm(normed, wg[...])) * attended).astype(BF16)
    row = (line_ref[...].astype(F32) + mm(gated, wo[...])).astype(BF16)
    if not with_column:
        out_ref[...] = row
        return
    kept_small = (present_ref[...] * amino_ref[...]).astype(F32).astype(BF16)
    spread = mm(one_hot(iota((total, lines), 0) // pairs == iota((total, lines), 1)), kept_small)
    own = iota((total, 2 * pairs), 1) // 2 == iota((total, 2 * pairs), 0) % pairs
    sides = one_hot(iota((2 * pairs, 128), 0) % 2 == iota((2 * pairs, 128), 1) // 64)
    kept = mm(jnp.where(own, spread, 0.0).astype(BF16), sides)

    projected = mm(paired_norm(row, 64), wc[...])
    query, gate, key, value = [projected[:, 128 * n : 128 * (n + 1)] for n in range(4)]

    def grid(a):
        return a.reshape(lines, pairs, 128)

    count = jnp.maximum(jnp.sum(grid(kept), axis=0), 1.0)
    mean_query = jnp.sum(grid(kept * query), axis=0) / count * (8**-0.5)
    same_head = block_matrix(128, 8, 1.0, 1.0)
    product = (mean_query[None] * grid(key)).reshape(total, 128)
    logits = grid(mm_split(product, same_head) + 1e9 * (kept - 1.0))
    exped = jnp.exp(logits - jnp.max(logits, axis=0, keepdims=True))
    mixed = jnp.sum(exped * grid(value), axis=0) / jnp.sum(exped, axis=0)
    gated = (jax.nn.sigmoid(grid(gate)) * mixed[None]).reshape(total, 128).astype(BF16)
    result = (row.astype(F32) + mm(gated, wout[...])).astype(BF16)
    shuffled = row_shuffle(result, lines, pairs)
    for t in range(pairs):
        out_ref[:, t * 128 : (t + 1) * 128] = shuffled[t * lines : (t + 1) * lines, :]


def call(kernel, out_shape, *args, **options):
    flops = options.pop("flops", 0)
    limit = pltpu.CompilerParams(vmem_limit_bytes=VMEM_LIMIT)
    moved = sum(a.size * a.dtype.itemsize for a in args)
    cost = pl.CostEstimate(flops=flops, bytes_accessed=moved, transcendentals=0)
    return pl.pallas_call(
        kernel, out_shape=out_shape, compiler_params=limit, cost_estimate=cost, **options
    )(*args)


def shape(*dims, dtype=BF16):
    return jax.ShapeDtypeStruct(dims, dtype)


def twice(matrix):
    return jnp.kron(jnp.eye(2, dtype=matrix.dtype), matrix)


def exchange(x, flip, devices):
    return lax.ppermute(x, "res", [(d, d ^ flip) for d in range(devices)])


def layer_normalize(values_in):
    centre = values_in - jnp.mean(values_in, axis=-1, keepdims=True)
    spread = jnp.mean(centre * centre, axis=-1, keepdims=True)
    return centre * lax.rsqrt(spread + EPS)


def column_complete(line, kept, vertical_matrix, vertical_exit_matrix, heads, depth):
    lines, columns, features = line.shape
    hidden = heads * depth
    normed = layer_normalize(line.astype(F32)).astype(BF16)
    projected = mm(normed.reshape(-1, features), vertical_matrix).reshape(lines, columns, -1)
    query, gate = projected[..., :hidden], projected[..., hidden : 2 * hidden]
    key = projected[..., 2 * hidden : 2 * hidden + depth]
    value = projected[..., 2 * hidden + depth :]
    count = jnp.maximum(jnp.sum(kept, axis=0), 1.0)[:, None]
    mean_query = jnp.sum(kept[..., None] * query, axis=0) / count * depth**-0.5
    logits = jnp.einsum("ihc,sic->sih", mean_query.reshape(columns, heads, depth), key)
    logits = logits + 1e9 * (kept - 1.0)[..., None]
    exped = jnp.exp(logits - jnp.max(logits, axis=0, keepdims=True))
    mixed = jnp.einsum("sih,sic->ihc", exped, value) / jnp.sum(exped, axis=0)[..., None]
    gate = jax.nn.sigmoid(gate).reshape(lines, columns, heads, depth)
    gated = (gate * mixed[None]).reshape(-1, hidden).astype(BF16)
    update = mm(gated, vertical_exit_matrix).reshape(lines, columns, features)
    return (line.astype(F32) + update).astype(BF16)


def on_device(
    seq_size,
    res_size,
    extra_activations,
    pair,
    present,
    amino,
    offset_matrix,
    horizontal_matrix,
    horizontal_exit_matrix,
    vertical_matrix,
    vertical_exit_matrix,
):
    lines, residues = present.shape
    pairs = residues // 2
    hidden = horizontal_exit_matrix.shape[0]
    heads = offset_matrix.shape[1]
    depth = hidden // heads
    groups = 4
    size = lines // groups
    chunk_rows = size * pairs + pairs
    keys = res_size * residues
    rows = residues * heads
    amino_row = amino.reshape(1, residues)

    prepared = call(
        functools.partial(prep_kernel, groups),
        [shape(chunk_rows, 128)] * groups + [shape(lines * pairs, 128)],
        extra_activations,
        present,
        amino_row,
    )
    chunks, line = prepared[:groups], prepared[groups]

    gathered = []
    core, near, far, high = 1, 2, 4, 8
    for g, chunk in enumerate(chunks):
        first, second = (near, far) if g % 2 == 0 else (far, near)
        column = jnp.stack([chunk] + [exchange(chunk, high * k, res_size) for k in range(1, 4)])
        plane = jnp.concatenate([column, exchange(column, first, res_size)])
        other = exchange(plane, second, res_size)
        whole = jnp.concatenate([plane, other])
        mirrored = exchange(whole, core, res_size)
        gathered.append((whole, mirrored))

    per_step = 4
    bias = call(
        bias_kernel,
        shape(rows, pair.shape[1]),
        pair,
        offset_matrix.T,
        grid=(residues // per_step,),
        in_specs=[
            pl.BlockSpec((per_step,) + pair.shape[1:], lambda n: (n, 0, 0)),
            pl.BlockSpec((heads, pair.shape[2]), lambda n: (0, 0)),
        ],
        out_specs=pl.BlockSpec((rows, pair.shape[1]), lambda n: (0, 0)),
        scratch_shapes=[pltpu.VMEM((rows, pair.shape[1]), F32)],
        flops=4 * pair.size * 128,
    )
    if seq_size > 1:
        bias = lax.all_gather(bias, "seq", axis=1, tiled=True)

    def index_of(place):
        return (place % 4) * 8 + (place // 8 % 2) * 4 + (place // 4 % 2) * 2 + place // 16

    me = lax.axis_index("res").astype(jnp.int32).reshape(1)
    vmem = pl.BlockSpec(memory_space=pltpu.VMEM)
    bias = call(
        functools.partial(order_kernel, residues, index_of),
        shape(rows, keys, dtype=F32),
        me,
        bias,
        in_specs=[pl.BlockSpec(memory_space=pltpu.SMEM), vmem],
        flops=2 * rows * keys * keys,
    )

    w_query, w_key, w_value, w_gate = [
        horizontal_matrix[:, n * hidden : (n + 1) * hidden] for n in range(4)
    ]
    folded = jnp.concatenate([w_key.T, w_key.T], axis=0)
    empty = jnp.zeros_like(folded)
    wk = jnp.concatenate([folded, empty, empty, folded], axis=1)
    wv = jnp.tile(w_value, (2, 2))
    wq = twice(w_query)

    attended = []
    for g, (whole, mirrored) in enumerate(gathered):
        half = whole.shape[0]
        if g % 2 == 0:
            places = list(range(half))
        else:
            places = [(n // 4 % 2) * 8 + (n // 8) * 4 + n % 4 for n in range(half)]
        pieces = (tuple(places), tuple(p + half for p in places))
        attended.append(
            call(
                functools.partial(attend_kernel, heads, pieces, size, pairs),
                shape(size * pairs, 128, dtype=F32),
                chunks[g],
                wq,
                wk,
                wv,
                bias,
                whole,
                mirrored,
                scratch_shapes=[
                    pltpu.VMEM((2 * size, keys // 2), F32),
                    pltpu.VMEM((size * pairs, 128), F32),
                ],
                flops=size * rows * keys * 2 * 256 * 2,
            )
        )

    w_column = [
        vertical_matrix[:, :hidden],
        vertical_matrix[:, hidden : 2 * hidden],
        jnp.tile(vertical_matrix[:, 2 * hidden : 2 * hidden + depth], (1, heads)),
        jnp.tile(vertical_matrix[:, 2 * hidden + depth :], (1, heads)),
    ]
    weights = (
        twice(w_gate),
        twice(horizontal_exit_matrix),
        jnp.concatenate([twice(w) for w in w_column], axis=1),
        twice(vertical_exit_matrix),
    )
    with_column = seq_size == 1

    def finish(*refs):
        final_kernel(
            lines,
            with_column,
            refs[:groups],
            refs[groups],
            refs[groups + 1 : 2 * groups + 1],
            refs[2 * groups + 1],
            refs[2 * groups + 2],
            refs[2 * groups + 3 : 2 * groups + 7],
            refs[-1],
        )

    out_shape = shape(*extra_activations.shape) if with_column else shape(lines * pairs, 128)
    result = call(finish, out_shape, *chunks, line, *attended, present, amino_row, *weights)
    if with_column:
        return result
    row = result.reshape(lines, residues, hidden)
    kept = (present * amino_row).astype(BF16)
    moved = lax.all_to_all(row, "seq", split_axis=1, concat_axis=0, tiled=True)
    moved_kept = lax.all_to_all(kept, "seq", split_axis=1, concat_axis=0, tiled=True)
    updated = column_complete(
        moved, moved_kept.astype(F32), vertical_matrix, vertical_exit_matrix, heads, depth
    )
    back = lax.all_to_all(updated, "seq", split_axis=0, concat_axis=1, tiled=True)
    return back.reshape(extra_activations.shape)


def solution(mesh):
    in_specs = (
        P("seq", "res"),
        P("res", "seq", None),
        P("seq", "res"),
        P("res"),
        P(),
        P(),
        P(),
        P(),
        P(),
    )
    sizes = mesh.shape
    return jax.shard_map(
        functools.partial(on_device, sizes["seq"], sizes["res"]),
        mesh=mesh,
        in_specs=in_specs,
        out_specs=P("seq", "res"),
        check_vma=False,
    )
```

```python
import functools
import math

import jax
import jax.numpy as jnp
from jax import lax
from jax.experimental import pallas as pl
from jax.experimental.pallas import tpu as pltpu
from jax.sharding import PartitionSpec as P

F32 = jnp.float32
BF16 = jnp.bfloat16
LOG2E = math.log2(math.e)
EPS = 1e-05
VMEM_LIMIT = 56 * 1024 * 1024

NT = (((1,), (1,)), ((), ()))


def mm(a, b):
    return jnp.dot(a, b, preferred_element_type=F32)


def mm_nt(a, b):
    return lax.dot_general(a, b, NT, preferred_element_type=F32)


def iota(shape, axis):
    return lax.broadcasted_iota(jnp.int32, shape, axis)


def one_hot(condition):
    return jnp.where(condition, 1.0, 0.0).astype(BF16)


def block_matrix(size, block, on_diagonal, elsewhere):
    row, col = iota((size, size), 0), iota((size, size), 1)
    inside = jnp.where(row == col, on_diagonal, elsewhere)
    return jnp.where(row // block == col // block, inside, 0.0).astype(BF16)


def halves(value):
    high = value.astype(BF16)
    return high, (value - high.astype(F32)).astype(BF16)


def mm_split(value, matrix):
    high, low = halves(value)
    return mm(high, matrix) + mm(low, matrix)


def paired_norm(x, width):
    lanes = x.shape[1]
    centre = mm(x, block_matrix(lanes, width, 1.0 - 1.0 / width, -1.0 / width))
    spread = mm_split(centre * centre, block_matrix(lanes, width, 1.0 / width, 1.0 / width))
    return (centre * lax.rsqrt(spread + EPS)).astype(BF16)


def row_shuffle(rows, inner, outer):
    total = rows.shape[0]
    row, col = iota((total, total), 0), iota((total, total), 1)
    return mm(one_hot(col == (row % inner) * outer + row // inner), rows).astype(BF16)


def prep_kernel(groups, me_ref, m_ref, present_ref, amino_ref, *refs):
    keep_refs, send_ref, normed_ref, line_ref, spread_ref = refs[:groups], *refs[groups:]
    lines, width = m_ref.shape
    pairs = width // 128
    stacked = jnp.concatenate([m_ref[:, t * 128 : (t + 1) * 128] for t in range(pairs)], axis=0)
    normed = paired_norm(stacked, 64)
    both = row_shuffle(jnp.concatenate([normed, stacked], axis=1), pairs, lines)
    normed_ref[...] = both[:, :128]
    line_ref[...] = both[:, 128:]
    kept = (present_ref[...] * amino_ref[...]).astype(F32).astype(BF16)
    size = lines // (2 * groups)
    residues = 2 * pairs
    for n in range(2 * groups):
        row, col = iota((128, lines), 0), iota((128, lines), 1)
        spread = mm(one_hot((row % size == col - n * size) & (row < 2 * size)), kept).astype(BF16)
        row, col = iota((pairs, residues), 0), iota((pairs, residues), 1)
        even = mm_nt(one_hot(col == 2 * row), spread)
        odd = mm_nt(one_hot(col == 2 * row + 1), spread)
        spread_ref[n] = jnp.where(iota((pairs, 128), 1) < size, even, odd).astype(BF16)
    core = me_ref[0] % 2
    rows = size * pairs
    for g in range(groups):
        mine, theirs = core * groups + g, (1 - core) * groups + g
        start = g * (rows + pairs)
        keep_refs[g][:rows, :] = normed_ref[pl.ds(pl.multiple_of(mine * rows, rows), rows), :]
        keep_refs[g][rows:, :] = spread_ref[mine]
        send_ref[start : start + rows, :] = normed_ref[
            pl.ds(pl.multiple_of(theirs * rows, rows), rows), :
        ]
        send_ref[start + rows : start + rows + pairs, :] = spread_ref[theirs]


def bias_kernel(x_ref, w_ref, out_ref, acc_ref):
    step = pl.program_id(0)
    heads = w_ref.shape[0]
    per_step, keys, channels = x_ref.shape
    centring = block_matrix(2 * channels, channels, 1.0 - 1.0 / channels, -1.0 / channels)
    averaging = block_matrix(2 * channels, channels, 1.0 / channels, 1.0 / channels)
    for n in range(0, per_step, 2):
        centre = mm(jnp.concatenate([x_ref[n], x_ref[n + 1]], axis=1), centring)
        spread = mm_split(centre * centre, averaging)
        normed = (centre * lax.rsqrt(spread + EPS)).astype(BF16)
        for k in range(2):
            start = pl.multiple_of((step * per_step + n + k) * heads, heads)
            part = normed[:, k * channels : (k + 1) * channels]
            acc_ref[pl.ds(start, heads), :] = mm_nt(w_ref[...], part)

    @pl.when(step == pl.num_programs(0) - 1)
    def _():
        out_ref[...] = acc_ref[...].astype(BF16)


def order_kernel(residues, device_of, me_ref, own_ref, peer_ref, out_ref):
    rows, keys = own_ref.shape
    lane = iota((1, keys), 1)
    half = keys // 2
    parity, rest = lane // half, lane % half
    place, pair = rest // (residues // 2), rest % (residues // 2)
    target = device_of(place, me_ref[0] % 2) * residues + 2 * pair + parity
    piece = 256
    total = jnp.zeros((2 * rows, keys), F32)
    for start in range(0, keys, piece):
        chosen = one_hot(iota((piece, keys), 0) + start == target)
        both = jnp.concatenate(
            [own_ref[:, start : start + piece], peer_ref[:, start : start + piece]], axis=0
        )
        total = total + mm(both, chosen)
    out_ref[...] = total * LOG2E


def attend_kernel(
    heads, size, pairs, own_ref, peer_ref, wq_ref, wk_ref, wv_ref, wg_ref, bias_ref, keyed_ref,
    mine_ref, theirs_ref, mask_ref, query_ref, attended_ref,
):
    depth = 128 // (2 * heads)
    rows = pairs * 2 * heads
    chips = keyed_ref.shape[0]
    lead = size * pairs
    stride = lead + pairs
    places = [(chip, half * stride) for chip in range(chips) for half in range(2)]
    keys = len(places) * pairs
    present = jnp.concatenate(
        [keyed_ref[n, at + lead : at + stride, :] for n, at in places], axis=0
    )
    identity = one_hot(iota((2 * size, 128), 0) == iota((2 * size, 128), 1))
    mask_ref[...] = (1e9 * LOG2E) * (mm_nt(identity, present) - 1.0)
    for n, ref in enumerate((own_ref, peer_ref)):
        query = mm(ref[:lead, :], wq_ref[...]) * (depth**-0.5)
        query_ref[n] = query.astype(BF16).astype(F32)
    lane, row = iota((2 * heads, 128), 1), iota((2 * heads, 128), 0)
    own_head = jnp.where(lane // depth == row, 1.0, 0.0)[None]
    low_lanes = iota((keys, 128), 1) < 64
    ones = jnp.ones((keys, 128), BF16)

    def one_line(s, carry):
        start = pl.multiple_of(s * pairs, pairs)
        keyed = jnp.concatenate(
            [keyed_ref[n, pl.ds(at + start, pairs), :] for n, at in places], axis=0
        )
        zero = jnp.zeros_like(keyed)
        valued = [
            jnp.concatenate([jnp.where(low_lanes, keyed, zero), ones], axis=1),
            jnp.concatenate([jnp.where(low_lanes, zero, keyed), ones], axis=1),
        ]
        masks = [mask_ref[pl.ds(p * size + s, 1), :] for p in range(2)]

        def logits_of(n):
            q = query_ref[n, pl.ds(start, pairs), :]
            spread = (q[:, None, :] * own_head).reshape(rows, 128).astype(BF16)
            folded = (mm(spread, wk_ref[...]) * LOG2E).astype(BF16)
            return [
                mm_nt(folded[:, 128 * p : 128 * (p + 1)], keyed)
                + bias_ref[n * rows : (n + 1) * rows, p * keys : (p + 1) * keys]
                + masks[p]
                for p in range(2)
            ]

        def finish(n, logits):
            peak = jnp.max(jnp.maximum(logits[0], logits[1]), axis=-1, keepdims=True)
            exped = [jnp.exp2(part - peak).astype(BF16) for part in logits]
            summed = mm(exped[0], valued[0]) + mm(exped[1], valued[1])
            mean = (summed[:, :128] / summed[:, 128:]).astype(BF16)
            mixed = mm(mean, wv_ref[...]).reshape(pairs, 2 * heads, 128)
            attended_ref[n, pl.ds(start, pairs), :] = jnp.sum(mixed * own_head, axis=1)

        first = logits_of(0)
        second = logits_of(1)
        finish(0, first)
        finish(1, second)
        return carry

    lax.fori_loop(0, size, one_line, 0, unroll=2)
    for n, (ref, out_ref) in enumerate(((own_ref, mine_ref), (peer_ref, theirs_ref))):
        gate = jax.nn.sigmoid(mm(ref[:lead, :], wg_ref[...]))
        out_ref[...] = (gate * attended_ref[n]).astype(BF16)


def final_kernel(
    lines, groups, with_column, me_ref, line_ref, present_ref, amino_ref, wo, wc, wout, *refs
):
    mine_refs, theirs_refs = refs[:groups], refs[groups : 2 * groups]
    out_ref, gated_ref = refs[-2:]
    total = line_ref.shape[0]
    pairs = total // lines
    core = me_ref[0] % 2
    share = total // (2 * groups)
    for g in range(groups):
        for owner, ref in ((core, mine_refs[g]), (1 - core, theirs_refs[g])):
            at = pl.multiple_of((owner * groups + g) * share, share)
            gated_ref[pl.ds(at, share), :] = ref[...]
    row = (line_ref[...].astype(F32) + mm(gated_ref[...], wo[...])).astype(BF16)
    if not with_column:
        out_ref[...] = row
        return
    kept_small = (present_ref[...] * amino_ref[...]).astype(F32).astype(BF16)
    spread = mm(one_hot(iota((total, lines), 0) // pairs == iota((total, lines), 1)), kept_small)
    own = iota((total, 2 * pairs), 1) // 2 == iota((total, 2 * pairs), 0) % pairs
    sides = one_hot(iota((2 * pairs, 128), 0) % 2 == iota((2 * pairs, 128), 1) // 64)
    kept = mm(jnp.where(own, spread, 0.0).astype(BF16), sides)

    projected = mm(paired_norm(row, 64), wc[...])
    query, gate, key, value = [projected[:, 128 * n : 128 * (n + 1)] for n in range(4)]

    def grid(a):
        return a.reshape(lines, pairs, 128)

    count = jnp.maximum(jnp.sum(grid(kept), axis=0), 1.0)
    mean_query = jnp.sum(grid(kept * query), axis=0) / count * (8**-0.5)
    same_head = block_matrix(128, 8, 1.0, 1.0)
    product = (mean_query[None] * grid(key)).reshape(total, 128)
    logits = grid(mm_split(product, same_head) + 1e9 * (kept - 1.0))
    exped = jnp.exp(logits - jnp.max(logits, axis=0, keepdims=True))
    mixed = jnp.sum(exped * grid(value), axis=0) / jnp.sum(exped, axis=0)
    gated = (jax.nn.sigmoid(grid(gate)) * mixed[None]).reshape(total, 128).astype(BF16)
    result = (row.astype(F32) + mm(gated, wout[...])).astype(BF16)
    shuffled = row_shuffle(result, lines, pairs)
    for t in range(pairs):
        out_ref[:, t * 128 : (t + 1) * 128] = shuffled[t * lines : (t + 1) * lines, :]


def call(kernel, out_shape, *args, **options):
    flops = options.pop("flops", 0)
    limit = pltpu.CompilerParams(vmem_limit_bytes=VMEM_LIMIT)
    moved = sum(a.size * a.dtype.itemsize for a in args)
    cost = pl.CostEstimate(flops=flops, bytes_accessed=moved, transcendentals=0)
    return pl.pallas_call(
        kernel, out_shape=out_shape, compiler_params=limit, cost_estimate=cost, **options
    )(*args)


def shape(*dims, dtype=BF16):
    return jax.ShapeDtypeStruct(dims, dtype)


def twice(matrix):
    return jnp.kron(jnp.eye(2, dtype=matrix.dtype), matrix)


def exchange(x, flip, devices):
    return lax.ppermute(x, "res", [(d, d ^ flip) for d in range(devices)])


def ring_path(chips):
    if chips != 16:
        return list(range(chips))
    columns = [0, 1, 3, 2]
    path = []
    for n, column in enumerate(columns):
        heights = range(4) if n % 2 == 0 else range(3, -1, -1)
        path += [4 * z + column for z in heights]
    return path


def layer_normalize(values_in):
    centre = values_in - jnp.mean(values_in, axis=-1, keepdims=True)
    spread = jnp.mean(centre * centre, axis=-1, keepdims=True)
    return centre * lax.rsqrt(spread + EPS)


def column_complete(line, kept, vertical_matrix, vertical_exit_matrix, heads, depth):
    lines, columns, features = line.shape
    hidden = heads * depth
    normed = layer_normalize(line.astype(F32)).astype(BF16)
    projected = mm(normed.reshape(-1, features), vertical_matrix).reshape(lines, columns, -1)
    query, gate = projected[..., :hidden], projected[..., hidden : 2 * hidden]
    key = projected[..., 2 * hidden : 2 * hidden + depth]
    value = projected[..., 2 * hidden + depth :]
    count = jnp.maximum(jnp.sum(kept, axis=0), 1.0)[:, None]
    mean_query = jnp.sum(kept[..., None] * query, axis=0) / count * depth**-0.5
    logits = jnp.einsum("ihc,sic->sih", mean_query.reshape(columns, heads, depth), key)
    logits = logits + 1e9 * (kept - 1.0)[..., None]
    exped = jnp.exp(logits - jnp.max(logits, axis=0, keepdims=True))
    mixed = jnp.einsum("sih,sic->ihc", exped, value) / jnp.sum(exped, axis=0)[..., None]
    gate = jax.nn.sigmoid(gate).reshape(lines, columns, heads, depth)
    gated = (gate * mixed[None]).reshape(-1, hidden).astype(BF16)
    update = mm(gated, vertical_exit_matrix).reshape(lines, columns, features)
    return (line.astype(F32) + update).astype(BF16)


def on_device(
    seq_size,
    res_size,
    extra_activations,
    pair,
    present,
    amino,
    offset_matrix,
    horizontal_matrix,
    horizontal_exit_matrix,
    vertical_matrix,
    vertical_exit_matrix,
):
    lines, residues = present.shape
    pairs = residues // 2
    hidden = horizontal_exit_matrix.shape[0]
    heads = offset_matrix.shape[1]
    depth = hidden // heads
    groups = 2
    size = lines // (2 * groups)
    lead = size * pairs
    keys = res_size * residues
    rows = residues * heads
    chips = res_size // 2
    amino_row = amino.reshape(1, residues)
    me = lax.axis_index("res").astype(jnp.int32).reshape(1)
    smem = pl.BlockSpec(memory_space=pltpu.SMEM)
    vmem = pl.BlockSpec(memory_space=pltpu.VMEM)

    prepared = call(
        functools.partial(prep_kernel, groups),
        [shape(lead + pairs, 128)] * groups
        + [shape(groups * (lead + pairs), 128)]
        + [shape(lines * pairs, 128)] * 2,
        me,
        extra_activations,
        present,
        amino_row,
        in_specs=[smem, vmem, vmem, vmem],
        scratch_shapes=[pltpu.VMEM((2 * groups, pairs, 128), BF16)],
    )
    keeps, send, line = prepared[:groups], prepared[groups], prepared[groups + 2]

    received = exchange(send, 1, res_size).reshape(groups, lead + pairs, 128)
    path = ring_path(chips)
    rings = [[2 * c for c in path], [2 * c + 1 for c in reversed(path)]]
    gathered = [
        lax.all_gather(
            jnp.concatenate([keeps[g], received[g]], axis=0),
            "res",
            axis_index_groups=rings,
        )
        for g in range(groups)
    ]

    per_step = 4
    bias = call(
        bias_kernel,
        shape(rows, pair.shape[1]),
        pair,
        offset_matrix.T,
        grid=(residues // per_step,),
        in_specs=[
            pl.BlockSpec((per_step,) + pair.shape[1:], lambda n: (n, 0, 0)),
            pl.BlockSpec((heads, pair.shape[2]), lambda n: (0, 0)),
        ],
        out_specs=pl.BlockSpec((rows, pair.shape[1]), lambda n: (0, 0)),
        scratch_shapes=[pltpu.VMEM((rows, pair.shape[1]), F32)],
        flops=4 * pair.size * 128,
    )
    if seq_size > 1:
        bias = lax.all_gather(bias, "seq", axis=1, tiled=True)

    def device_of(place, core):
        at = place // 2
        at = jnp.where(core == 0, at, chips - 1 - at)
        chip = jnp.zeros_like(at)
        for n, c in enumerate(path):
            chip = jnp.where(at == n, c, chip)
        return 2 * chip + (place % 2 + core) % 2

    bias = call(
        functools.partial(order_kernel, residues, device_of),
        shape(2 * rows, keys, dtype=F32),
        me,
        bias,
        exchange(bias, 1, res_size),
        in_specs=[smem, vmem, vmem],
        flops=4 * rows * keys * keys,
    )

    w_query, w_key, w_value, w_gate = [
        horizontal_matrix[:, n * hidden : (n + 1) * hidden] for n in range(4)
    ]
    folded = jnp.concatenate([w_key.T, w_key.T], axis=0)
    empty = jnp.zeros_like(folded)
    wk = jnp.concatenate([folded, empty, empty, folded], axis=1)
    wv = jnp.tile(w_value, (2, 2))
    wq, wg = twice(w_query), twice(w_gate)

    attended = [
        call(
            functools.partial(attend_kernel, heads, size, pairs),
            [shape(lead, 128)] * 2,
            keeps[g],
            received[g],
            wq,
            wk,
            wv,
            wg,
            bias,
            gathered[g],
            scratch_shapes=[
                pltpu.VMEM((2 * size, keys // 2), F32),
                pltpu.VMEM((2, lead, 128), F32),
                pltpu.VMEM((2, lead, 128), F32),
            ],
            flops=2 * size * rows * keys * 2 * 256 * 2,
        )
        for g in range(groups)
    ]
    returned = [exchange(theirs, 1, res_size) for _, theirs in attended]

    w_column = [
        vertical_matrix[:, :hidden],
        vertical_matrix[:, hidden : 2 * hidden],
        jnp.tile(vertical_matrix[:, 2 * hidden : 2 * hidden + depth], (1, heads)),
        jnp.tile(vertical_matrix[:, 2 * hidden + depth :], (1, heads)),
    ]
    with_column = seq_size == 1
    final_args = [
        me,
        line,
        present,
        amino_row,
        twice(horizontal_exit_matrix),
        jnp.concatenate([twice(w) for w in w_column], axis=1),
        twice(vertical_exit_matrix),
    ]
    final_args += [mine for mine, _ in attended] + returned
    result = call(
        functools.partial(final_kernel, lines, groups, with_column),
        shape(*extra_activations.shape) if with_column else shape(lines * pairs, 128),
        *final_args,
        in_specs=[smem] + [vmem] * (len(final_args) - 1),
        scratch_shapes=[pltpu.VMEM((lines * pairs, 128), BF16)],
    )
    if with_column:
        return result
    row = result.reshape(lines, residues, hidden)
    kept = (present * amino_row).astype(BF16)
    moved = lax.all_to_all(row, "seq", split_axis=1, concat_axis=0, tiled=True)
    moved_kept = lax.all_to_all(kept, "seq", split_axis=1, concat_axis=0, tiled=True)
    updated = column_complete(
        moved, moved_kept.astype(F32), vertical_matrix, vertical_exit_matrix, heads, depth
    )
    back = lax.all_to_all(updated, "seq", split_axis=0, concat_axis=1, tiled=True)
    return back.reshape(extra_activations.shape)


def solution(mesh):
    in_specs = (
        P("seq", "res"),
        P("res", "seq", None),
        P("seq", "res"),
        P("res"),
        P(),
        P(),
        P(),
        P(),
        P(),
    )
    sizes = mesh.shape
    return jax.shard_map(
        functools.partial(on_device, sizes["seq"], sizes["res"]),
        mesh=mesh,
        in_specs=in_specs,
        out_specs=P("seq", "res"),
        check_vma=False,
    )
```

```python
import functools
import math

import jax
import jax.numpy as jnp
from jax import lax
from jax.experimental import pallas as pl
from jax.experimental.pallas import tpu as pltpu
from jax.sharding import PartitionSpec as P

F32 = jnp.float32
BF16 = jnp.bfloat16
LOG2E = math.log2(math.e)
EPS = 1e-05
VMEM_LIMIT = 56 * 1024 * 1024

NT = (((1,), (1,)), ((), ()))


def mm(a, b):
    return jnp.dot(a, b, preferred_element_type=F32)


def mm_nt(a, b):
    return lax.dot_general(a, b, NT, preferred_element_type=F32)


def iota(shape, axis):
    return lax.broadcasted_iota(jnp.int32, shape, axis)


def one_hot(condition):
    return jnp.where(condition, 1.0, 0.0).astype(BF16)


def block_matrix(size, block, on_diagonal, elsewhere):
    row, col = iota((size, size), 0), iota((size, size), 1)
    inside = jnp.where(row == col, on_diagonal, elsewhere)
    return jnp.where(row // block == col // block, inside, 0.0).astype(BF16)


def halves(value):
    high = value.astype(BF16)
    return high, (value - high.astype(F32)).astype(BF16)


def mm_split(value, matrix):
    high, low = halves(value)
    return mm(high, matrix) + mm(low, matrix)


def paired_norm(x, width):
    lanes = x.shape[1]
    centre = mm(x, block_matrix(lanes, width, 1.0 - 1.0 / width, -1.0 / width))
    spread = mm_split(centre * centre, block_matrix(lanes, width, 1.0 / width, 1.0 / width))
    return (centre * lax.rsqrt(spread + EPS)).astype(BF16)


def row_shuffle(rows, inner, outer):
    total = rows.shape[0]
    row, col = iota((total, total), 0), iota((total, total), 1)
    return mm(one_hot(col == (row % inner) * outer + row // inner), rows).astype(BF16)


def prep_kernel(groups, me_ref, m_ref, present_ref, amino_ref, *refs):
    keep_ref, send_ref, line_ref, normed_ref, spread_ref = refs
    lines, width = m_ref.shape
    pairs = width // 128
    stacked = jnp.concatenate([m_ref[:, t * 128 : (t + 1) * 128] for t in range(pairs)], axis=0)
    normed = paired_norm(stacked, 64)
    both = row_shuffle(jnp.concatenate([normed, stacked], axis=1), pairs, lines)
    normed_ref[...] = both[:, :128]
    line_ref[...] = both[:, 128:]
    kept = (present_ref[...] * amino_ref[...]).astype(F32).astype(BF16)
    size = lines // (2 * groups)
    residues = 2 * pairs
    row, col = iota((pairs, residues), 0), iota((pairs, residues), 1)
    evens, odds = one_hot(col == 2 * row), one_hot(col == 2 * row + 1)
    row, col = iota((128, lines), 0) - 64, iota((128, lines), 1)
    for n in range(2 * groups):
        chosen = (row >= 0) & (row < 2 * size) & (row % size == col - n * size)
        spread = mm(one_hot(chosen), kept).astype(BF16)
        first = iota((pairs, 128), 1) < 64 + size
        spread_ref[n] = jnp.where(first, mm_nt(evens, spread), mm_nt(odds, spread)).astype(BF16)
    core = me_ref[0] % 2
    rows = size * pairs
    for ref, half in ((keep_ref, core), (send_ref, 1 - core)):
        for g in range(groups):
            index, start = half * groups + g, g * (rows + pairs)
            ref[start : start + rows, :] = normed_ref[
                pl.ds(pl.multiple_of(index * rows, rows), rows), :
            ]
            ref[start + rows : start + rows + pairs, :] = spread_ref[index]


def bias_kernel(x_ref, w_ref, out_ref, acc_ref):
    step = pl.program_id(0)
    heads = w_ref.shape[1]
    per_step, keys, channels = x_ref.shape
    per_tile = 128 // heads
    steps = per_tile // per_step
    centring = block_matrix(2 * channels, channels, 1.0 - 1.0 / channels, -1.0 / channels)
    averaging = block_matrix(2 * channels, channels, 1.0 / channels, 1.0 / channels)
    lane = iota((channels, 128), 1)
    wide = mm(w_ref[...], one_hot(iota((heads, 128), 1) % heads == iota((heads, 128), 0)))
    placed = []
    for n in range(per_step):
        mine = lane // heads == (step % steps) * per_step + n
        placed.append(jnp.where(mine, wide, 0.0).astype(BF16))
    placed = jnp.concatenate(placed, axis=0)
    tile = step // steps

    @pl.when(step % steps == 0)
    def _():
        acc_ref[tile] = jnp.zeros(acc_ref.shape[1:], F32)

    piece = 128
    for r in range(0, keys, piece):
        normed = []
        for n in range(0, per_step, 2):
            x = jnp.concatenate([x_ref[n, r : r + piece], x_ref[n + 1, r : r + piece]], axis=1)
            centre = mm(x, centring)
            spread = mm_split(centre * centre, averaging)
            normed.append((centre * lax.rsqrt(spread + EPS)).astype(BF16))
        acc_ref[tile, r : r + piece, :] += mm(jnp.concatenate(normed, axis=1), placed)

    @pl.when(step == pl.num_programs(0) - 1)
    def _():
        for n in range(acc_ref.shape[0]):
            out_ref[n * 128 : (n + 1) * 128, :] = acc_ref[n].T.astype(BF16)


def order_kernel(
    groups, size, pairs, heads, pieces, me_ref, own_ref, peer_ref, keep_ref, received_ref, w_ref,
    bias_ref, lhs_ref,
):
    rows, keys = own_ref.shape
    residues = 2 * pairs
    lane = iota((1, keys), 1)
    each = keys // pieces
    which, rest = lane // each, lane % each
    parity, rest = rest // (each // 2), rest % (each // 2)
    place, pair = rest // pairs, rest % pairs
    device = me_ref[0] ^ ((place % 2) + 2 * which + 2 * pieces * (place // 2))
    target = device * residues + 2 * pair + parity
    total = jnp.zeros((2 * rows, keys), F32)
    for start in range(0, keys, 256):
        chosen = one_hot(iota((256, keys), 0) + start == target)
        both = jnp.concatenate(
            [own_ref[:, start : start + 256], peer_ref[:, start : start + 256]], axis=0
        )
        total = total + mm(both, chosen)
    bias_ref[...] = total * LOG2E

    hidden = w_ref.shape[0]
    depth = hidden // heads
    row, col = iota((128, hidden), 0), iota((128, hidden), 1)
    twice_rows = one_hot(row % hidden == col)
    row, col = iota((4 * hidden, 128), 0), iota((4 * hidden, 128), 1)
    wq = mm(mm(twice_rows, w_ref[...]).astype(BF16), one_hot(row == col % hidden))
    row, col = iota((128, 128), 0), iota((128, 128), 1)
    wq = jnp.where(row // hidden == col // hidden, wq, 0.0).astype(BF16)
    row, col = iota((128, 4 * hidden), 0), iota((128, 4 * hidden), 1)
    wk = mm_nt(one_hot(col == hidden + row % hidden), w_ref[...]).astype(BF16)
    row, col = iota((hidden, 128), 0), iota((hidden, 128), 1)
    wk = mm(wk, one_hot(row == col)).astype(BF16)
    lane, row = iota((2 * heads, 128), 1), iota((2 * heads, 128), 0)
    own_head = jnp.where(lane // depth == row, 1.0, 0.0)[None]
    lead = size * pairs
    lane = iota((rows, 128), 1) - hidden
    for g in range(groups):
        for n, ref in enumerate((keep_ref, received_ref)):
            start = g * (lead + pairs)
            query = mm(ref[start : start + lead, :], wq) * (depth**-0.5)
            query = query.astype(BF16).astype(F32)
            for s in range(size):
                q = query[s * pairs : (s + 1) * pairs]
                spread = (q[:, None, :] * own_head).reshape(rows, 128).astype(BF16)
                folded = mm(spread, wk) * LOG2E
                picked = (lane == s) | (lane == size + s)
                lhs_ref[g * size + s, n * rows : (n + 1) * rows, :] = jnp.where(
                    picked, 1.0, folded
                ).astype(BF16)


def masks_of(ref, size, pairs):
    lead = size * pairs
    present = jnp.concatenate(
        [ref[k, c, lead : lead + pairs, :] for k in range(ref.shape[0]) for c in range(2)], axis=0
    ).astype(F32)
    lane = iota(present.shape, 1) - 64
    hidden = (1e9 * LOG2E) * (present - 1.0)
    return [
        jnp.where((lane >= p * size) & (lane < (p + 1) * size), hidden, 0.0).astype(BF16)
        for p in range(2)
    ]


def keys_of(ref, masks, s, pairs):
    start = pl.multiple_of(s * pairs, pairs)
    even = jnp.concatenate(
        [ref[k, c, pl.ds(start, pairs), :] for k in range(ref.shape[0]) for c in range(2)], axis=0
    )
    odd = pltpu.roll(even.astype(F32), 64, 1).astype(BF16)
    low = iota(even.shape, 1) < 64
    one = jnp.ones_like(even)
    keyed = [jnp.where(low, x, m) for x, m in zip((even, odd), masks)]
    valued = [jnp.where(low, x, one) for x in (even, odd)]
    return jnp.concatenate(keyed, axis=0), jnp.concatenate(valued, axis=0)


def partial_sums(lhs, bias_ref, piece, keyed, valued):
    width = keyed.shape[0]
    logits = mm_nt(lhs, keyed) + bias_ref[:, piece * width : (piece + 1) * width]
    return mm(jnp.exp2(logits).astype(BF16), valued)


def start_kernel(groups, size, pairs, places, lhs_ref, bias_ref, *refs):
    out_ref = refs[-1]
    piece_refs = [refs[n * groups : (n + 1) * groups] for n in range(len(places))]
    masks = [[masks_of(ref, size, pairs) for ref in piece] for piece in piece_refs]

    def one_line(s, carry):
        for g in range(groups):
            line = g * size + s
            total = None
            for n, place in enumerate(places):
                keyed, valued = keys_of(piece_refs[n][g], masks[n][g], s, pairs)
                part = partial_sums(lhs_ref[line], bias_ref, place, keyed, valued)
                total = part if total is None else total + part
            out_ref[line] = total
        return carry

    lax.fori_loop(0, size, one_line, 0, unroll=2)


def finish_kernel(
    heads, groups, size, pairs, place, lhs_ref, bias_ref, sums_ref, w_ref, keep_ref, received_ref,
    *refs,
):
    piece_refs, far_refs = refs[:groups], refs[groups : 4 * groups]
    mine_ref, theirs_ref, attended_ref, range_ref, copy_ref = refs[4 * groups :]
    hidden = w_ref.shape[0]
    depth = hidden // heads
    lead = size * pairs
    row, col = iota((4 * hidden, 128), 0), iota((4 * hidden, 128), 1)
    pick_value = one_hot(row == 2 * hidden + col % hidden)
    pick_gate = one_hot(row == 3 * hidden + col % hidden)
    row, col = iota((128, hidden), 0), iota((128, hidden), 1)
    wv = mm(mm(one_hot(row == col), w_ref[...]).astype(BF16), pick_value).astype(BF16)
    wg = mm(mm(one_hot(row % hidden == col), w_ref[...]).astype(BF16), pick_gate)
    row, col = iota((128, 128), 0), iota((128, 128), 1)
    wg = jnp.where(row // hidden == col // hidden, wg, 0.0).astype(BF16)
    lane, row = iota((2 * heads, 128), 1), iota((2 * heads, 128), 0)
    own_head = jnp.where(lane // depth == row, 1.0, 0.0)[None]
    masks = [masks_of(ref, size, pairs) for ref in piece_refs]
    low = iota((lhs_ref.shape[1], 128), 1) < 64

    def settle(line, total):
        mean = jnp.where(low, total / pltpu.roll(total, 64, 1), 0.0).astype(BF16)
        mixed = mm(mean, wv).reshape(2 * pairs, 2 * heads, 128)
        summed = jnp.sum(mixed * own_head, axis=1)
        start = pl.multiple_of(line * pairs, pairs)
        for n in range(2):
            attended_ref[n, pl.ds(start, pairs), :] = summed[n * pairs : (n + 1) * pairs]

    range_ref[...] = jnp.ones(range_ref.shape, F32)

    def one_line(s, carry):
        for g in range(groups):
            line = g * size + s
            keyed, valued = keys_of(piece_refs[g], masks[g], s, pairs)
            total = sums_ref[line] + partial_sums(lhs_ref[line], bias_ref, place, keyed, valued)
            settle(line, total)
            weight = jnp.where(low, 1.0, total).reshape(-1, 8, 128)
            range_ref[0] = jnp.minimum(range_ref[0], jnp.min(weight, axis=0))
            range_ref[1] = jnp.maximum(range_ref[1], jnp.max(weight, axis=0))
        return carry

    lax.fori_loop(0, size, one_line, 0, unroll=2)
    fine = (range_ref[0] > 2.0**-80) & (range_ref[1] < 2.0**100)

    @pl.when(jnp.min(jnp.where(fine, 1.0, 0.0)) < 0.5)
    def _():
        for n, ref in enumerate(far_refs):
            pltpu.sync_copy(ref, copy_ref.at[n])
        for g in range(groups):
            ordered = [copy_ref.at[n * groups + g] for n in range(3)] + [piece_refs[g]]
            all_masks = [masks_of(ref, size, pairs) for ref in ordered]

            def exact_line(s, carry):
                line = g * size + s
                both = [keys_of(r, m, s, pairs) for r, m in zip(ordered, all_masks)]
                logits = []
                for n, (keyed, _) in enumerate(both):
                    width = keyed.shape[0]
                    bias = bias_ref[:, n * width : (n + 1) * width]
                    logits.append(mm_nt(lhs_ref[line], keyed) + bias)
                peak = functools.reduce(jnp.maximum, logits)
                peak = jnp.max(peak, axis=-1, keepdims=True)
                parts = [
                    mm(jnp.exp2(part - peak).astype(BF16), valued)
                    for part, (_, valued) in zip(logits, both)
                ]
                settle(line, sum(parts[1:], parts[0]))
                return carry

            lax.fori_loop(0, size, exact_line, 0)

    for n, (ref, out_ref) in enumerate(((keep_ref, mine_ref), (received_ref, theirs_ref))):
        for g in range(groups):
            start = g * (lead + pairs)
            gate = jax.nn.sigmoid(mm(ref[start : start + lead, :], wg))
            at = slice(g * lead, (g + 1) * lead)
            out_ref[at, :] = (gate * attended_ref[n, at, :]).astype(BF16)


def final_kernel(
    lines, with_column, me_ref, line_ref, present_ref, amino_ref, wo, wc, wout, mine_ref,
    theirs_ref, out_ref, gated_ref,
):
    total = line_ref.shape[0]
    pairs = total // lines
    core = me_ref[0] % 2
    share = total // 2
    for owner, ref in ((core, mine_ref), (1 - core, theirs_ref)):
        gated_ref[pl.ds(pl.multiple_of(owner * share, share), share), :] = ref[...]
    row = (line_ref[...].astype(F32) + mm(gated_ref[...], wo[...])).astype(BF16)
    if not with_column:
        out_ref[...] = row
        return
    kept_small = (present_ref[...] * amino_ref[...]).astype(F32).astype(BF16)
    spread = mm(one_hot(iota((total, lines), 0) // pairs == iota((total, lines), 1)), kept_small)
    own = iota((total, 2 * pairs), 1) // 2 == iota((total, 2 * pairs), 0) % pairs
    sides = one_hot(iota((2 * pairs, 128), 0) % 2 == iota((2 * pairs, 128), 1) // 64)
    kept = mm(jnp.where(own, spread, 0.0).astype(BF16), sides)

    projected = mm(paired_norm(row, 64), wc[...])
    query, gate, key, value = [projected[:, 128 * n : 128 * (n + 1)] for n in range(4)]

    def grid(a):
        return a.reshape(lines, pairs, 128)

    count = jnp.maximum(jnp.sum(grid(kept), axis=0), 1.0)
    mean_query = jnp.sum(grid(kept * query), axis=0) / count * (8**-0.5)
    same_head = block_matrix(128, 8, 1.0, 1.0)
    product = (mean_query[None] * grid(key)).reshape(total, 128)
    logits = grid(mm_split(product, same_head) + 1e9 * (kept - 1.0))
    exped = jnp.exp(logits - jnp.max(logits, axis=0, keepdims=True))
    mixed = jnp.sum(exped * grid(value), axis=0) / jnp.sum(exped, axis=0)
    gated = (jax.nn.sigmoid(grid(gate)) * mixed[None]).reshape(total, 128).astype(BF16)
    result = (row.astype(F32) + mm(gated, wout[...])).astype(BF16)
    shuffled = row_shuffle(result, lines, pairs)
    for t in range(pairs):
        out_ref[:, t * 128 : (t + 1) * 128] = shuffled[t * lines : (t + 1) * lines, :]


def call(kernel, out_shape, *args, **options):
    flops = options.pop("flops", 0)
    limit = pltpu.CompilerParams(vmem_limit_bytes=VMEM_LIMIT)
    moved = sum(a.size * a.dtype.itemsize for a in args)
    cost = pl.CostEstimate(flops=flops, bytes_accessed=moved, transcendentals=0)
    return pl.pallas_call(
        kernel, out_shape=out_shape, compiler_params=limit, cost_estimate=cost, **options
    )(*args)


def shape(*dims, dtype=BF16):
    return jax.ShapeDtypeStruct(dims, dtype)


def twice(matrix):
    return jnp.kron(jnp.eye(2, dtype=matrix.dtype), matrix)


def exchange(x, flip, devices):
    return lax.ppermute(x, "res", [(d, d ^ flip) for d in range(devices)])


def layer_normalize(values_in):
    centre = values_in - jnp.mean(values_in, axis=-1, keepdims=True)
    spread = jnp.mean(centre * centre, axis=-1, keepdims=True)
    return centre * lax.rsqrt(spread + EPS)


def column_complete(line, kept, vertical_matrix, vertical_exit_matrix, heads, depth):
    lines, columns, features = line.shape
    hidden = heads * depth
    normed = layer_normalize(line.astype(F32)).astype(BF16)
    projected = mm(normed.reshape(-1, features), vertical_matrix).reshape(lines, columns, -1)
    query, gate = projected[..., :hidden], projected[..., hidden : 2 * hidden]
    key = projected[..., 2 * hidden : 2 * hidden + depth]
    value = projected[..., 2 * hidden + depth :]
    count = jnp.maximum(jnp.sum(kept, axis=0), 1.0)[:, None]
    mean_query = jnp.sum(kept[..., None] * query, axis=0) / count * depth**-0.5
    logits = jnp.einsum("ihc,sic->sih", mean_query.reshape(columns, heads, depth), key)
    logits = logits + 1e9 * (kept - 1.0)[..., None]
    exped = jnp.exp(logits - jnp.max(logits, axis=0, keepdims=True))
    mixed = jnp.einsum("sih,sic->ihc", exped, value) / jnp.sum(exped, axis=0)[..., None]
    gate = jax.nn.sigmoid(gate).reshape(lines, columns, heads, depth)
    gated = (gate * mixed[None]).reshape(-1, hidden).astype(BF16)
    update = mm(gated, vertical_exit_matrix).reshape(lines, columns, features)
    return (line.astype(F32) + update).astype(BF16)


def on_device(
    seq_size,
    res_size,
    extra_activations,
    pair,
    present,
    amino,
    offset_matrix,
    horizontal_matrix,
    horizontal_exit_matrix,
    vertical_matrix,
    vertical_exit_matrix,
):
    lines, residues = present.shape
    pairs = residues // 2
    hidden = horizontal_exit_matrix.shape[0]
    heads = offset_matrix.shape[1]
    depth = hidden // heads
    groups = 2
    size = lines // (2 * groups)
    lead = size * pairs
    keys = res_size * residues
    rows = residues * heads
    core_bit, near, far, high = 1, 2, 4, 8
    amino_row = amino.reshape(1, residues)
    me = lax.axis_index("res").astype(jnp.int32).reshape(1)
    smem = pl.BlockSpec(memory_space=pltpu.SMEM)
    vmem = pl.BlockSpec(memory_space=pltpu.VMEM)

    rest = lead + pairs
    keep, send, line = call(
        functools.partial(prep_kernel, groups),
        [shape(groups * rest, 128)] * 2 + [shape(lines * pairs, 128)],
        me,
        extra_activations,
        present,
        amino_row,
        in_specs=[smem, vmem, vmem, vmem],
        scratch_shapes=[
            pltpu.VMEM((lines * pairs, 128), BF16),
            pltpu.VMEM((2 * groups, pairs, 128), BF16),
        ],
    )

    received = exchange(send, core_bit, res_size)
    chunk = jnp.concatenate([keep, received], axis=0)
    levels = [chunk] + [exchange(chunk, high * k, res_size) for k in range(1, res_size // high)]
    column = jnp.stack(levels).reshape(len(levels), 2, groups, rest, 128)
    own = [column[:, :, g] for g in range(groups)]
    beside = [exchange(part, near, res_size) for part in own]
    across = [exchange(part, far, res_size) for part in own]
    corner = [
        exchange(beside[g], far, res_size) if g % 2 == 0 else exchange(across[g], near, res_size)
        for g in range(groups)
    ]

    per_step = 4
    bias = call(
        bias_kernel,
        shape(rows, pair.shape[1]),
        pair,
        offset_matrix,
        grid=(residues // per_step,),
        in_specs=[
            pl.BlockSpec((per_step,) + pair.shape[1:], lambda n: (n, 0, 0)),
            pl.BlockSpec(offset_matrix.shape, lambda n: (0, 0)),
        ],
        out_specs=pl.BlockSpec((rows, pair.shape[1]), lambda n: (0, 0)),
        scratch_shapes=[pltpu.VMEM((rows // 128, pair.shape[1], 128), F32)],
        flops=4 * pair.size * 128,
    )
    if seq_size > 1:
        bias = lax.all_gather(bias, "seq", axis=1, tiled=True)
    pieces = 4
    bias, lhs = call(
        functools.partial(order_kernel, groups, size, pairs, heads, pieces),
        [shape(2 * rows, keys, dtype=F32), shape(groups * size, 2 * rows, 128)],
        me,
        bias,
        exchange(bias, core_bit, res_size),
        keep,
        received,
        horizontal_matrix,
        in_specs=[smem] + [vmem] * 5,
        flops=4 * rows * keys * keys,
    )
    sums = call(
        functools.partial(start_kernel, groups, size, pairs, (0, 1, 2)),
        shape(groups * size, 2 * rows, 128, dtype=F32),
        lhs,
        bias,
        *own,
        *beside,
        *across,
        flops=groups * size * rows * keys * 2 * 256 * 2,
    )
    anywhere = pl.BlockSpec(memory_space=pl.ANY)
    mine, theirs = call(
        functools.partial(finish_kernel, heads, groups, size, pairs, 3),
        [shape(groups * lead, 128)] * 2,
        lhs,
        bias,
        sums,
        horizontal_matrix,
        keep,
        received,
        *corner,
        *own,
        *beside,
        *across,
        in_specs=[vmem] * (6 + groups) + [anywhere] * (3 * groups),
        scratch_shapes=[
            pltpu.VMEM((2, groups * lead, 128), F32),
            pltpu.VMEM((2, 8, 128), F32),
            pltpu.VMEM((3 * groups,) + own[0].shape, BF16),
        ],
        flops=groups * size * rows * keys * 2 * 256,
    )
    returned = exchange(theirs, core_bit, res_size)

    w_column = [
        vertical_matrix[:, :hidden],
        vertical_matrix[:, hidden : 2 * hidden],
        jnp.tile(vertical_matrix[:, 2 * hidden : 2 * hidden + depth], (1, heads)),
        jnp.tile(vertical_matrix[:, 2 * hidden + depth :], (1, heads)),
    ]
    with_column = seq_size == 1
    final_args = [
        me,
        line,
        present,
        amino_row,
        twice(horizontal_exit_matrix),
        jnp.concatenate([twice(w) for w in w_column], axis=1),
        twice(vertical_exit_matrix),
    ]
    final_args += [mine, returned]
    result = call(
        functools.partial(final_kernel, lines, with_column),
        shape(*extra_activations.shape) if with_column else shape(lines * pairs, 128),
        *final_args,
        in_specs=[smem] + [vmem] * (len(final_args) - 1),
        scratch_shapes=[pltpu.VMEM((lines * pairs, 128), BF16)],
    )
    if with_column:
        return result
    row = result.reshape(lines, residues, hidden)
    kept = (present * amino_row).astype(BF16)
    moved = lax.all_to_all(row, "seq", split_axis=1, concat_axis=0, tiled=True)
    moved_kept = lax.all_to_all(kept, "seq", split_axis=1, concat_axis=0, tiled=True)
    updated = column_complete(
        moved, moved_kept.astype(F32), vertical_matrix, vertical_exit_matrix, heads, depth
    )
    back = lax.all_to_all(updated, "seq", split_axis=0, concat_axis=1, tiled=True)
    return back.reshape(extra_activations.shape)


def solution(mesh):
    in_specs = (
        P("seq", "res"),
        P("res", "seq", None),
        P("seq", "res"),
        P("res"),
        P(),
        P(),
        P(),
        P(),
        P(),
    )
    sizes = mesh.shape
    return jax.shard_map(
        functools.partial(on_device, sizes["seq"], sizes["res"]),
        mesh=mesh,
        in_specs=in_specs,
        out_specs=P("seq", "res"),
        check_vma=False,
    )
```

```python
import functools
import math

import jax
import jax.numpy as jnp
from jax import lax
from jax.experimental import pallas as pl
from jax.experimental.pallas import tpu as pltpu
from jax.sharding import PartitionSpec as P

F32 = jnp.float32
BF16 = jnp.bfloat16
LOG2E = math.log2(math.e)
EPS = 1e-05

NT = (((1,), (1,)), ((), ()))


def mm(a, b):
    return jnp.dot(a, b, preferred_element_type=F32)


def mm_nt(a, b):
    return lax.dot_general(a, b, NT, preferred_element_type=F32)


def iota(shape, axis):
    return lax.broadcasted_iota(jnp.int32, shape, axis)


def one_hot(condition):
    return jnp.where(condition, 1.0, 0.0).astype(BF16)


def block_matrix(size, block, on_diagonal, elsewhere):
    row, col = iota((size, 1), 0), iota((1, size), 1)
    inside = jnp.where(row == col, on_diagonal, elsewhere)
    return jnp.where(row // block == col // block, inside, 0.0).astype(BF16)


def halves(value):
    high = value.astype(BF16)
    return high, (value - high.astype(F32)).astype(BF16)


def mm_split(value, matrix):
    high, low = halves(value)
    return mm(high, matrix) + mm(low, matrix)


def paired_norm(x, width):
    lanes = x.shape[1]
    centre = mm(x, block_matrix(lanes, width, 1.0 - 1.0 / width, -1.0 / width))
    spread = mm_split(centre * centre, block_matrix(lanes, width, 1.0 / width, 1.0 / width))
    return (centre * lax.rsqrt(spread + EPS)).astype(BF16)


def row_shuffle(rows, inner, outer):
    total = rows.shape[0]
    row, col = iota((total, 1), 0), iota((1, total), 1)
    return mm(one_hot(col == (row % inner) * outer + row // inner), rows).astype(BF16)


def prep_kernel(groups, me_ref, m_ref, present_ref, amino_ref, *refs):
    keep_ref, send_ref, line_ref, normed_ref, spread_ref = refs
    lines, width = m_ref.shape
    pairs = width // 128
    stacked = jnp.concatenate([m_ref[:, t * 128 : (t + 1) * 128] for t in range(pairs)], axis=0)
    normed = paired_norm(stacked, 64)
    both = row_shuffle(jnp.concatenate([normed, stacked], axis=1), pairs, lines)
    normed_ref[...] = both[:, :128]
    line_ref[...] = both[:, 128:]
    kept = (present_ref[...] * amino_ref[...]).astype(F32).astype(BF16)
    size = lines // (2 * groups)
    residues = 2 * pairs
    row, col = iota((pairs, residues), 0), iota((pairs, residues), 1)
    evens, odds = one_hot(col == 2 * row), one_hot(col == 2 * row + 1)
    row, col = iota((128, lines), 0) - 64, iota((128, lines), 1)
    for n in range(2 * groups):
        chosen = (row >= 0) & (row < 2 * size) & (row % size == col - n * size)
        spread = mm(one_hot(chosen), kept).astype(BF16)
        first = iota((pairs, 128), 1) < 64 + size
        spread_ref[n] = jnp.where(first, mm_nt(evens, spread), mm_nt(odds, spread)).astype(BF16)
    core = me_ref[0] % 2
    rows = size * pairs
    for ref, half in ((keep_ref, core), (send_ref, 1 - core)):
        for g in range(groups):
            index, start = half * groups + g, g * (rows + pairs)
            ref[start : start + rows, :] = normed_ref[
                pl.ds(pl.multiple_of(index * rows, rows), rows), :
            ]
            ref[start + rows : start + rows + pairs, :] = spread_ref[index]


def bias_kernel(x_ref, w_ref, after_ref, out_ref, acc_ref):
    step = pl.program_id(0)
    heads = w_ref.shape[1]
    per_step, keys, channels = x_ref.shape
    per_tile = 128 // heads
    steps = per_tile // per_step
    centring = block_matrix(2 * channels, channels, 1.0 - 1.0 / channels, -1.0 / channels)
    averaging = block_matrix(2 * channels, channels, 1.0 / channels, 1.0 / channels)
    lane = iota((channels, 128), 1)
    wide = mm(w_ref[...], one_hot(iota((heads, 128), 1) % heads == iota((heads, 128), 0)))
    placed = []
    for n in range(per_step):
        mine = lane // heads == (step % steps) * per_step + n
        placed.append(jnp.where(mine, wide, 0.0).astype(BF16))
    placed = jnp.concatenate(placed, axis=0)
    tile = step // steps

    @pl.when(step % steps == 0)
    def _():
        acc_ref[tile] = jnp.zeros(acc_ref.shape[1:], F32)

    averaging = jnp.concatenate([averaging, averaging], axis=0)
    piece = 512
    for r in range(0, keys, piece):
        normed = []
        for n in range(0, per_step, 2):
            x = jnp.concatenate([x_ref[n, r : r + piece], x_ref[n + 1, r : r + piece]], axis=1)
            centre = mm(x, centring)
            spread = mm(jnp.concatenate(halves(centre * centre), axis=1), averaging)
            normed.append((centre * lax.rsqrt(spread + EPS)).astype(BF16))
        acc_ref[tile, r : r + piece, :] += mm(jnp.concatenate(normed, axis=1), placed)

    @pl.when(step == pl.num_programs(0) - 1)
    def _():
        for n in range(acc_ref.shape[0]):
            out_ref[n * 128 : (n + 1) * 128, :] = acc_ref[n].T.astype(BF16)


def order_kernel(
    groups, size, pairs, heads, pieces, me_ref, own_ref, peer_ref, keep_ref, received_ref, w_ref,
    bias_ref, lhs_ref,
):
    rows, keys = own_ref.shape
    residues = 2 * pairs
    lane = iota((1, keys), 1)
    each = keys // pieces
    which, rest = lane // each, lane % each
    parity, rest = rest // (each // 2), rest % (each // 2)
    place, pair = rest // pairs, rest % pairs
    device = me_ref[0] ^ ((place % 2) + 2 * which + 2 * pieces * (place // 2))
    target = device * residues + 2 * pair + parity
    total = jnp.zeros((2 * rows, keys), F32)
    for start in range(0, keys, 256):
        chosen = one_hot(iota((256, keys), 0) + start == target)
        both = jnp.concatenate(
            [own_ref[:, start : start + 256], peer_ref[:, start : start + 256]], axis=0
        )
        total = total + mm(both, chosen)
    bias_ref[...] = total * LOG2E

    hidden = w_ref.shape[0]
    depth = hidden // heads
    row, col = iota((128, hidden), 0), iota((128, hidden), 1)
    twice_rows = one_hot(row % hidden == col)
    row, col = iota((4 * hidden, 128), 0), iota((4 * hidden, 128), 1)
    wq = mm(mm(twice_rows, w_ref[...]).astype(BF16), one_hot(row == col % hidden))
    row, col = iota((128, 128), 0), iota((128, 128), 1)
    wq = jnp.where(row // hidden == col // hidden, wq, 0.0).astype(BF16)
    row, col = iota((128, 4 * hidden), 0), iota((128, 4 * hidden), 1)
    wk = mm_nt(one_hot(col == hidden + row % hidden), w_ref[...]).astype(BF16)
    row, col = iota((hidden, 128), 0), iota((hidden, 128), 1)
    wk = mm(wk, one_hot(row == col)).astype(BF16)
    lane, row = iota((2 * heads, 128), 1), iota((2 * heads, 128), 0)
    own_head = jnp.where(lane // depth == row, 1.0, 0.0)[None]
    lead = size * pairs
    lane = iota((rows, 128), 1) - hidden
    for g in range(groups):
        for n, ref in enumerate((keep_ref, received_ref)):
            start = g * (lead + pairs)
            query = mm(ref[start : start + lead, :], wq) * (depth**-0.5)
            query = query.astype(BF16).astype(F32)
            for s in range(size):
                q = query[s * pairs : (s + 1) * pairs]
                spread = (q[:, None, :] * own_head).reshape(rows, 128).astype(BF16)
                folded = mm(spread, wk) * LOG2E
                picked = (lane == s) | (lane == size + s)
                lhs_ref[g * size + s, n * rows : (n + 1) * rows, :] = jnp.where(
                    picked, 1.0, folded
                ).astype(BF16)


def masks_of(ref, size, pairs):
    lead = size * pairs
    present = jnp.concatenate(
        [ref[k, c, lead : lead + pairs, :] for k in range(ref.shape[0]) for c in range(2)], axis=0
    ).astype(F32)
    lane = iota(present.shape, 1) - 64
    hidden = (1e9 * LOG2E) * (present - 1.0)
    return [
        jnp.where((lane >= p * size) & (lane < (p + 1) * size), hidden, 0.0).astype(BF16)
        for p in range(2)
    ]


def keys_of(ref, masks, s, pairs):
    start = pl.multiple_of(s * pairs, pairs)
    even = jnp.concatenate(
        [ref[k, c, pl.ds(start, pairs), :] for k in range(ref.shape[0]) for c in range(2)], axis=0
    )
    odd = pltpu.roll(even.astype(F32), 64, 1).astype(BF16)
    low = iota(even.shape, 1) < 64
    one = jnp.ones_like(even)
    keyed = [jnp.where(low, x, m) for x, m in zip((even, odd), masks)]
    valued = [jnp.where(low, x, one) for x in (even, odd)]
    return jnp.concatenate(keyed, axis=0), jnp.concatenate(valued, axis=0)


def partial_sums(lhs, bias_ref, piece, keyed, valued):
    width = keyed.shape[0]
    logits = mm_nt(lhs, keyed) + bias_ref[:, piece * width : (piece + 1) * width]
    return mm(jnp.exp2(logits).astype(BF16), valued)


def start_kernel(groups, size, pairs, places, lhs_ref, bias_ref, *refs):
    out_ref = refs[-1]
    piece_refs = [refs[n * groups : (n + 1) * groups] for n in range(len(places))]
    masks = [[masks_of(ref, size, pairs) for ref in piece] for piece in piece_refs]

    def one_line(s, carry):
        for g in range(groups):
            line = g * size + s
            total = None
            for n, place in enumerate(places):
                keyed, valued = keys_of(piece_refs[n][g], masks[n][g], s, pairs)
                part = partial_sums(lhs_ref[line], bias_ref, place, keyed, valued)
                total = part if total is None else total + part
            out_ref[line] = total
        return carry

    lax.fori_loop(0, size, one_line, 0, unroll=2)


def finish_kernel(
    heads, groups, size, pairs, place, lhs_ref, bias_ref, sums_ref, w_ref, keep_ref, received_ref,
    *refs,
):
    piece_refs, far_refs = refs[:groups], refs[groups : 4 * groups]
    mine_ref, theirs_ref, attended_ref, range_ref, copy_ref = refs[4 * groups :]
    hidden = w_ref.shape[0]
    depth = hidden // heads
    lead = size * pairs
    row, col = iota((4 * hidden, 128), 0), iota((4 * hidden, 128), 1)
    pick_value = one_hot(row == 2 * hidden + col % hidden)
    pick_gate = one_hot(row == 3 * hidden + col % hidden)
    row, col = iota((128, hidden), 0), iota((128, hidden), 1)
    wv = mm(mm(one_hot(row == col), w_ref[...]).astype(BF16), pick_value).astype(BF16)
    wg = mm(mm(one_hot(row % hidden == col), w_ref[...]).astype(BF16), pick_gate)
    row, col = iota((128, 128), 0), iota((128, 128), 1)
    wg = jnp.where(row // hidden == col // hidden, wg, 0.0).astype(BF16)
    lane, row = iota((2 * heads, 128), 1), iota((2 * heads, 128), 0)
    own_head = jnp.where(lane // depth == row, 1.0, 0.0)[None]
    masks = [masks_of(ref, size, pairs) for ref in piece_refs]
    low = iota((lhs_ref.shape[1], 128), 1) < 64
    row, col = iota((128, 1), 0), iota((1, 128), 1)
    averaged = jnp.where(row + 0 * col < hidden, 0.0, 1.0 / (128 - hidden)).astype(BF16)
    wv = jnp.concatenate([wv, averaged], axis=1)
    wv = jnp.concatenate([wv, wv], axis=0)
    own_head = jnp.concatenate([own_head, own_head], axis=2)

    def settle(line, total):
        mixed = mm(jnp.concatenate(halves(total), axis=1), wv)
        summed = jnp.sum(mixed.reshape(2 * pairs, 2 * heads, 256) * own_head, axis=1)
        summed = summed[:, :128] / summed[:, 128:]
        start = pl.multiple_of(line * pairs, pairs)
        for n in range(2):
            attended_ref[n, pl.ds(start, pairs), :] = summed[n * pairs : (n + 1) * pairs]

    range_ref[...] = jnp.ones(range_ref.shape, F32)

    def one_line(s, carry):
        for g in range(groups):
            line = g * size + s
            keyed, valued = keys_of(piece_refs[g], masks[g], s, pairs)
            total = sums_ref[line] + partial_sums(lhs_ref[line], bias_ref, place, keyed, valued)
            settle(line, total)
            weight = jnp.where(low, 1.0, total).reshape(-1, 8, 128)
            range_ref[0] = jnp.minimum(range_ref[0], jnp.min(weight, axis=0))
            range_ref[1] = jnp.maximum(range_ref[1], jnp.max(weight, axis=0))
        return carry

    lax.fori_loop(0, size, one_line, 0, unroll=2)
    fine = (range_ref[0] > 2.0**-80) & (range_ref[1] < 2.0**100)

    @pl.when(jnp.min(jnp.where(fine, 1.0, 0.0)) < 0.5)
    def _():
        for n, ref in enumerate(far_refs):
            pltpu.sync_copy(ref, copy_ref.at[n])
        for g in range(groups):
            ordered = [copy_ref.at[n * groups + g] for n in range(3)] + [piece_refs[g]]
            all_masks = [masks_of(ref, size, pairs) for ref in ordered]

            def exact_line(s, carry):
                line = g * size + s
                both = [keys_of(r, m, s, pairs) for r, m in zip(ordered, all_masks)]
                logits = []
                for n, (keyed, _) in enumerate(both):
                    width = keyed.shape[0]
                    bias = bias_ref[:, n * width : (n + 1) * width]
                    logits.append(mm_nt(lhs_ref[line], keyed) + bias)
                peak = functools.reduce(jnp.maximum, logits)
                peak = jnp.max(peak, axis=-1, keepdims=True)
                parts = [
                    mm(jnp.exp2(part - peak).astype(BF16), valued)
                    for part, (_, valued) in zip(logits, both)
                ]
                settle(line, sum(parts[1:], parts[0]))
                return carry

            lax.fori_loop(0, size, exact_line, 0)

    for n, (ref, out_ref) in enumerate(((keep_ref, mine_ref), (received_ref, theirs_ref))):
        for g in range(groups):
            start = g * (lead + pairs)
            gate = jax.nn.sigmoid(mm(ref[start : start + lead, :], wg))
            at = slice(g * lead, (g + 1) * lead)
            out_ref[at, :] = (gate * attended_ref[n, at, :]).astype(BF16)


def final_kernel(
    lines, heads, with_column, me_ref, line_ref, present_ref, amino_ref, wo_ref, wc_ref, wout_ref,
    mine_ref, theirs_ref, out_ref, gated_ref,
):
    total = line_ref.shape[0]
    pairs = total // lines
    core = me_ref[0] % 2
    share = total // 2
    for owner, ref in ((core, mine_ref), (1 - core, theirs_ref)):
        gated_ref[pl.ds(pl.multiple_of(owner * share, share), share), :] = ref[...]
    hidden = wo_ref.shape[0]
    depth = hidden // heads
    rows_twice = one_hot(iota((128, 1), 0) % hidden == iota((1, hidden), 1))
    same_residue = iota((128, 1), 0) // hidden == iota((1, 128), 1) // hidden

    def twice(matrix, picked):
        wide = mm(mm(rows_twice, matrix).astype(BF16), picked)
        return jnp.where(same_residue, wide, 0.0).astype(BF16)

    def columns(width, chosen):
        return one_hot(iota((width, 1), 0) == chosen)

    lane = iota((1, 128), 1)
    wo = twice(wo_ref[...], columns(hidden, lane % hidden))
    row = (line_ref[...].astype(F32) + mm(gated_ref[...], wo)).astype(BF16)
    if not with_column:
        out_ref[...] = row
        return
    kept_small = (present_ref[...] * amino_ref[...]).astype(F32).astype(BF16)
    spread = mm(one_hot(iota((total, lines), 0) // pairs == iota((total, lines), 1)), kept_small)
    own = iota((total, 2 * pairs), 1) // 2 == iota((total, 2 * pairs), 0) % pairs
    sides = one_hot(iota((2 * pairs, 128), 0) % 2 == iota((2 * pairs, 128), 1) // 64)
    kept = mm(jnp.where(own, spread, 0.0).astype(BF16), sides)

    choices = [
        lane % hidden,
        hidden + lane % hidden,
        2 * hidden + lane % depth,
        2 * hidden + depth + lane % depth,
    ]
    wc = [twice(wc_ref[...], columns(wc_ref.shape[1], chosen)) for chosen in choices]
    projected = mm(paired_norm(row, 64), jnp.concatenate(wc, axis=1))
    query, gate, key, value = [projected[:, 128 * n : 128 * (n + 1)] for n in range(4)]

    def grid(a):
        return a.reshape(lines, pairs, 128)

    count = jnp.maximum(jnp.sum(grid(kept), axis=0), 1.0)
    mean_query = jnp.sum(grid(kept * query), axis=0) / count * (depth**-0.5)
    same_head = block_matrix(128, depth, 1.0, 1.0)
    product = (mean_query[None] * grid(key)).reshape(total, 128)
    logits = grid(mm_split(product, same_head) + 1e9 * (kept - 1.0))
    exped = jnp.exp(logits - jnp.max(logits, axis=0, keepdims=True))
    mixed = jnp.sum(exped * grid(value), axis=0) / jnp.sum(exped, axis=0)
    gated = (jax.nn.sigmoid(grid(gate)) * mixed[None]).reshape(total, 128).astype(BF16)
    wout = twice(wout_ref[...], columns(hidden, lane % hidden))
    result = (row.astype(F32) + mm(gated, wout)).astype(BF16)
    shuffled = row_shuffle(result, lines, pairs)
    for t in range(pairs):
        out_ref[:, t * 128 : (t + 1) * 128] = shuffled[t * lines : (t + 1) * lines, :]


def call(kernel, out_shape, *args, **options):
    flops = options.pop("flops", 0)
    limit = pltpu.CompilerParams(vmem_limit_bytes=options.pop("mib", 8) * 1024 * 1024)
    moved = sum(a.size * a.dtype.itemsize for a in args)
    cost = pl.CostEstimate(flops=flops, bytes_accessed=moved, transcendentals=0)
    return pl.pallas_call(
        kernel, out_shape=out_shape, compiler_params=limit, cost_estimate=cost, **options
    )(*args)


def shape(*dims, dtype=BF16):
    return jax.ShapeDtypeStruct(dims, dtype)


def exchange(x, flip, devices):
    return lax.ppermute(x, "res", [(d, d ^ flip) for d in range(devices)])


def layer_normalize(values_in):
    centre = values_in - jnp.mean(values_in, axis=-1, keepdims=True)
    spread = jnp.mean(centre * centre, axis=-1, keepdims=True)
    return centre * lax.rsqrt(spread + EPS)


def column_complete(line, kept, vertical_matrix, vertical_exit_matrix, heads, depth):
    lines, columns, features = line.shape
    hidden = heads * depth
    normed = layer_normalize(line.astype(F32)).astype(BF16)
    projected = mm(normed.reshape(-1, features), vertical_matrix).reshape(lines, columns, -1)
    query, gate = projected[..., :hidden], projected[..., hidden : 2 * hidden]
    key = projected[..., 2 * hidden : 2 * hidden + depth]
    value = projected[..., 2 * hidden + depth :]
    count = jnp.maximum(jnp.sum(kept, axis=0), 1.0)[:, None]
    mean_query = jnp.sum(kept[..., None] * query, axis=0) / count * depth**-0.5
    logits = jnp.einsum("ihc,sic->sih", mean_query.reshape(columns, heads, depth), key)
    logits = logits + 1e9 * (kept - 1.0)[..., None]
    exped = jnp.exp(logits - jnp.max(logits, axis=0, keepdims=True))
    mixed = jnp.einsum("sih,sic->ihc", exped, value) / jnp.sum(exped, axis=0)[..., None]
    gate = jax.nn.sigmoid(gate).reshape(lines, columns, heads, depth)
    gated = (gate * mixed[None]).reshape(-1, hidden).astype(BF16)
    update = mm(gated, vertical_exit_matrix).reshape(lines, columns, features)
    return (line.astype(F32) + update).astype(BF16)


def on_device(
    seq_size,
    res_size,
    extra_activations,
    pair,
    present,
    amino,
    offset_matrix,
    horizontal_matrix,
    horizontal_exit_matrix,
    vertical_matrix,
    vertical_exit_matrix,
):
    lines, residues = present.shape
    pairs = residues // 2
    hidden = horizontal_exit_matrix.shape[0]
    heads = offset_matrix.shape[1]
    depth = hidden // heads
    groups = 2
    size = lines // (2 * groups)
    lead = size * pairs
    keys = res_size * residues
    rows = residues * heads
    core_bit, near, far, high = 1, 2, 4, 8
    amino_row = amino.reshape(1, residues)
    me = lax.axis_index("res").astype(jnp.int32).reshape(1)
    smem = pl.BlockSpec(memory_space=pltpu.SMEM)
    vmem = pl.BlockSpec(memory_space=pltpu.VMEM)

    rest = lead + pairs
    keep, send, line = call(
        functools.partial(prep_kernel, groups),
        [shape(groups * rest, 128)] * 2 + [shape(lines * pairs, 128)],
        me,
        extra_activations,
        present,
        amino_row,
        in_specs=[smem, vmem, vmem, vmem],
        scratch_shapes=[
            pltpu.VMEM((lines * pairs, 128), BF16),
            pltpu.VMEM((2 * groups, pairs, 128), BF16),
        ],
    )

    received = exchange(send, core_bit, res_size)
    chunk = jnp.concatenate([keep, received], axis=0)
    levels = [chunk] + [exchange(chunk, high * k, res_size) for k in range(1, res_size // high)]
    column = jnp.stack(levels).reshape(len(levels), 2, groups, rest, 128)
    own = [column[:, :, g] for g in range(groups)]
    beside = [exchange(part, near, res_size) for part in own]
    across = [exchange(part, far, res_size) for part in own]
    corner = [
        exchange(beside[g], far, res_size) if g % 2 == 0 else exchange(across[g], near, res_size)
        for g in range(groups)
    ]

    per_step = 4
    bias = call(
        bias_kernel,
        shape(rows, pair.shape[1]),
        pair,
        offset_matrix,
        chunk,
        grid=(residues // per_step,),
        in_specs=[
            pl.BlockSpec((per_step,) + pair.shape[1:], lambda n: (n, 0, 0)),
            pl.BlockSpec(offset_matrix.shape, lambda n: (0, 0)),
            pl.BlockSpec(memory_space=pl.ANY),
        ],
        out_specs=pl.BlockSpec((rows, pair.shape[1]), lambda n: (0, 0)),
        scratch_shapes=[pltpu.VMEM((rows // 128, pair.shape[1], 128), F32)],
        flops=16 * pair.size * 128,
        mib=16,
    )
    if seq_size > 1:
        bias = lax.all_gather(bias, "seq", axis=1, tiled=True)
    pieces = 4
    bias, lhs = call(
        functools.partial(order_kernel, groups, size, pairs, heads, pieces),
        [shape(2 * rows, keys, dtype=F32), shape(groups * size, 2 * rows, 128)],
        me,
        bias,
        exchange(bias, core_bit, res_size),
        keep,
        received,
        horizontal_matrix,
        in_specs=[smem] + [vmem] * 5,
        flops=4 * rows * keys * keys,
        mib=14,
    )
    sums = call(
        functools.partial(start_kernel, groups, size, pairs, (0, 1, 2)),
        shape(groups * size, 2 * rows, 128, dtype=F32),
        lhs,
        bias,
        *own,
        *beside,
        *across,
        flops=groups * size * rows * keys * 2 * 256 * 2,
        mib=18,
    )
    anywhere = pl.BlockSpec(memory_space=pl.ANY)
    mine, theirs = call(
        functools.partial(finish_kernel, heads, groups, size, pairs, 3),
        [shape(groups * lead, 128)] * 2,
        lhs,
        bias,
        sums,
        horizontal_matrix,
        keep,
        received,
        *corner,
        *own,
        *beside,
        *across,
        in_specs=[vmem] * (6 + groups) + [anywhere] * (3 * groups),
        scratch_shapes=[
            pltpu.VMEM((2, groups * lead, 128), F32),
            pltpu.VMEM((2, 8, 128), F32),
            pltpu.VMEM((3 * groups,) + own[0].shape, BF16),
        ],
        flops=groups * size * rows * keys * 2 * 256,
        mib=22,
    )
    returned = exchange(theirs, core_bit, res_size)

    with_column = seq_size == 1
    final_args = [
        me,
        line,
        present,
        amino_row,
        horizontal_exit_matrix,
        vertical_matrix,
        vertical_exit_matrix,
    ]
    final_args += [mine, returned]
    result = call(
        functools.partial(final_kernel, lines, heads, with_column),
        shape(*extra_activations.shape) if with_column else shape(lines * pairs, 128),
        *final_args,
        in_specs=[smem] + [vmem] * (len(final_args) - 1),
        scratch_shapes=[pltpu.VMEM((lines * pairs, 128), BF16)],
    )
    if with_column:
        return result
    row = result.reshape(lines, residues, hidden)
    kept = (present * amino_row).astype(BF16)
    moved = lax.all_to_all(row, "seq", split_axis=1, concat_axis=0, tiled=True)
    moved_kept = lax.all_to_all(kept, "seq", split_axis=1, concat_axis=0, tiled=True)
    updated = column_complete(
        moved, moved_kept.astype(F32), vertical_matrix, vertical_exit_matrix, heads, depth
    )
    back = lax.all_to_all(updated, "seq", split_axis=0, concat_axis=1, tiled=True)
    return back.reshape(extra_activations.shape)


def solution(mesh):
    in_specs = (
        P("seq", "res"),
        P("res", "seq", None),
        P("seq", "res"),
        P("res"),
        P(),
        P(),
        P(),
        P(),
        P(),
    )
    sizes = mesh.shape
    return jax.shard_map(
        functools.partial(on_device, sizes["seq"], sizes["res"]),
        mesh=mesh,
        in_specs=in_specs,
        out_specs=P("seq", "res"),
        check_vma=False,
    )
```

```python
import functools
import math

import jax
import jax.numpy as jnp
from jax import lax
from jax.experimental import pallas as pl
from jax.experimental.pallas import tpu as pltpu
from jax.sharding import PartitionSpec as P

F32 = jnp.float32
BF16 = jnp.bfloat16
LOG2E = math.log2(math.e)
EPS = 1e-05

NT = (((1,), (1,)), ((), ()))


def mm(a, b):
    return jnp.dot(a, b, preferred_element_type=F32)


def mm_nt(a, b):
    return lax.dot_general(a, b, NT, preferred_element_type=F32)


def iota(shape, axis):
    return lax.broadcasted_iota(jnp.int32, shape, axis)


def one_hot(condition):
    return jnp.where(condition, 1.0, 0.0).astype(BF16)


def block_matrix(size, block, on_diagonal, elsewhere):
    row, col = iota((size, 1), 0), iota((1, size), 1)
    inside = jnp.where(row == col, on_diagonal, elsewhere)
    return jnp.where(row // block == col // block, inside, 0.0).astype(BF16)


def halves(value):
    high = value.astype(BF16)
    return high, (value - high.astype(F32)).astype(BF16)


def mm_split(value, matrix):
    high, low = halves(value)
    return mm(high, matrix) + mm(low, matrix)


def paired_norm(x, width):
    lanes = x.shape[1]
    centre = mm(x, block_matrix(lanes, width, 1.0 - 1.0 / width, -1.0 / width))
    spread = mm_split(centre * centre, block_matrix(lanes, width, 1.0 / width, 1.0 / width))
    return (centre * lax.rsqrt(spread + EPS)).astype(BF16)


def row_shuffle(rows, inner, outer):
    total = rows.shape[0]
    row, col = iota((total, 1), 0), iota((1, total), 1)
    return mm(one_hot(col == (row % inner) * outer + row // inner), rows).astype(BF16)


def prep_kernel(groups, me_ref, m_ref, kept_ref, *refs):
    keep_ref, send_ref, line_ref, normed_ref, spread_ref = refs
    lines, width = m_ref.shape
    pairs = width // 128
    stacked = jnp.concatenate([m_ref[:, t * 128 : (t + 1) * 128] for t in range(pairs)], axis=0)
    normed = paired_norm(stacked, 64)
    both = row_shuffle(jnp.concatenate([normed, stacked], axis=1), pairs, lines)
    normed_ref[...] = both[:, :128]
    line_ref[...] = both[:, 128:]
    kept = kept_ref[...]
    size = lines // (2 * groups)
    residues = 2 * pairs
    row, col = iota((pairs, residues), 0), iota((pairs, residues), 1)
    evens, odds = one_hot(col == 2 * row), one_hot(col == 2 * row + 1)
    row, col = iota((128, lines), 0) - 64, iota((128, lines), 1)
    for n in range(2 * groups):
        chosen = (row >= 0) & (row < 2 * size) & (row % size == col - n * size)
        spread = mm(one_hot(chosen), kept).astype(BF16)
        first = iota((pairs, 128), 1) < 64 + size
        spread_ref[n] = jnp.where(first, mm_nt(evens, spread), mm_nt(odds, spread)).astype(BF16)
    core = me_ref[0] % 2
    rows = size * pairs
    for ref, half in ((keep_ref, core), (send_ref, 1 - core)):
        for g in range(groups):
            index, start = half * groups + g, g * (rows + pairs)
            ref[start : start + rows, :] = normed_ref[
                pl.ds(pl.multiple_of(index * rows, rows), rows), :
            ]
            ref[start + rows : start + rows + pairs, :] = spread_ref[index]


def bias_kernel(x_ref, w_ref, after_ref, out_ref, acc_ref):
    step = pl.program_id(0)
    heads = w_ref.shape[0]
    per_step, keys, channels = x_ref.shape
    per_tile = 128 // heads
    steps = per_tile // per_step
    centring = block_matrix(2 * channels, channels, 1.0 - 1.0 / channels, -1.0 / channels)
    lane = iota((channels, 128), 1)
    spread = one_hot(iota((heads, 128), 1) % heads == iota((heads, 128), 0))
    wide = lax.dot_general(
        w_ref[...], spread, (((0,), (0,)), ((), ())), preferred_element_type=F32
    )
    placed = []
    for n in range(per_step):
        mine = lane // heads == (step % steps) * per_step + n
        placed.append(jnp.where(mine, wide, 0.0).astype(BF16))
    placed = jnp.concatenate(placed, axis=0)
    tile = step // steps

    @pl.when(step % steps == 0)
    def _():
        acc_ref[tile] = jnp.zeros(acc_ref.shape[1:], F32)

    piece = 512
    for r in range(0, keys, piece):
        normed = []
        for n in range(0, per_step, 2):
            x = jnp.concatenate([x_ref[n, r : r + piece], x_ref[n + 1, r : r + piece]], axis=1)
            centre = mm(x, centring)
            for part in (centre[:, :channels], centre[:, channels:]):
                spread = jnp.mean(part * part, axis=-1, keepdims=True)
                normed.append((part * lax.rsqrt(spread + EPS)).astype(BF16))
        acc_ref[tile, r : r + piece, :] += mm(jnp.concatenate(normed, axis=1), placed)

    @pl.when(step == pl.num_programs(0) - 1)
    def _():
        for n in range(acc_ref.shape[0]):
            out_ref[n * 128 : (n + 1) * 128, :] = acc_ref[n].T.astype(BF16)


def order_kernel(
    groups, size, pairs, heads, pieces, me_ref, own_ref, peer_ref, keep_ref, received_ref, w_ref,
    *refs,
):
    column_refs, (bias_ref, lhs_ref, sums_ref) = refs[:groups], refs[groups:]
    rows, keys = own_ref.shape
    residues = 2 * pairs
    lane = iota((1, keys), 1)
    each = keys // pieces
    which, rest = lane // each, lane % each
    parity, rest = rest // (each // 2), rest % (each // 2)
    place, pair = rest // pairs, rest % pairs
    device = me_ref[0] ^ ((place % 2) + 2 * which + 2 * pieces * (place // 2))
    target = device * residues + 2 * pair + parity
    total = jnp.zeros((2 * rows, keys), F32)
    for start in range(0, keys, 256):
        chosen = one_hot(iota((256, keys), 0) + start == target)
        both = jnp.concatenate(
            [own_ref[:, start : start + 256], peer_ref[:, start : start + 256]], axis=0
        )
        total = total + mm(both, chosen)
    bias_ref[...] = total * LOG2E

    hidden = w_ref.shape[0]
    depth = hidden // heads
    row, col = iota((128, hidden), 0), iota((128, hidden), 1)
    twice_rows = one_hot(row % hidden == col)
    row, col = iota((4 * hidden, 128), 0), iota((4 * hidden, 128), 1)
    wq = mm(mm(twice_rows, w_ref[...]).astype(BF16), one_hot(row == col % hidden))
    row, col = iota((128, 128), 0), iota((128, 128), 1)
    wq = jnp.where(row // hidden == col // hidden, wq, 0.0).astype(BF16)
    row, col = iota((128, 4 * hidden), 0), iota((128, 4 * hidden), 1)
    wk = mm_nt(one_hot(col == hidden + row % hidden), w_ref[...]).astype(BF16)
    row, col = iota((hidden, 128), 0), iota((hidden, 128), 1)
    wk = mm(wk, one_hot(row == col)).astype(BF16)
    lane, row = iota((2 * heads, 128), 1), iota((2 * heads, 128), 0)
    own_head = jnp.where(lane // depth == row, 1.0, 0.0)[None]
    lead = size * pairs
    lane = iota((rows, 128), 1) - hidden
    for g in range(groups):
        for n, ref in enumerate((keep_ref, received_ref)):
            start = g * (lead + pairs)
            query = mm(ref[start : start + lead, :], wq) * (depth**-0.5)
            query = query.astype(BF16).astype(F32)
            for s in range(size):
                q = query[s * pairs : (s + 1) * pairs]
                spread = (q[:, None, :] * own_head).reshape(rows, 128).astype(BF16)
                folded = mm(spread, wk) * LOG2E
                picked = (lane == s) | (lane == size + s)
                lhs_ref[g * size + s, n * rows : (n + 1) * rows, :] = jnp.where(
                    picked, 1.0, folded
                ).astype(BF16)
    add_pieces(groups, size, pairs, (0,), lhs_ref, bias_ref, None, column_refs, sums_ref)


def masks_of(ref, size, pairs):
    lead = size * pairs
    present = jnp.concatenate(
        [ref[k, c, lead : lead + pairs, :] for k in range(ref.shape[0]) for c in range(2)], axis=0
    ).astype(F32)
    lane = iota(present.shape, 1) - 64
    hidden = (1e9 * LOG2E) * (present - 1.0)
    return [
        jnp.where((lane >= p * size) & (lane < (p + 1) * size), hidden, 0.0).astype(BF16)
        for p in range(2)
    ]


def keys_of(ref, masks, s, pairs):
    start = pl.multiple_of(s * pairs, pairs)
    even = jnp.concatenate(
        [ref[k, c, pl.ds(start, pairs), :] for k in range(ref.shape[0]) for c in range(2)], axis=0
    )
    odd = pltpu.roll(even.astype(F32), 64, 1).astype(BF16)
    low = iota(even.shape, 1) < 64
    one = jnp.ones_like(even)
    keyed = [jnp.where(low, x, m) for x, m in zip((even, odd), masks)]
    valued = [jnp.where(low, x, one) for x in (even, odd)]
    return jnp.concatenate(keyed, axis=0), jnp.concatenate(valued, axis=0)


def partial_sums(lhs, bias_ref, piece, keyed, valued):
    width = keyed.shape[0]
    logits = mm_nt(lhs, keyed) + bias_ref[:, piece * width : (piece + 1) * width]
    return mm(jnp.exp2(logits).astype(BF16), valued)


def add_pieces(groups, size, pairs, places, lhs_ref, bias_ref, before_ref, piece_refs, out_ref):
    masks = [masks_of(ref, size, pairs) for ref in piece_refs]

    def one_line(s, carry):
        for g in range(groups):
            line = g * size + s
            total = None if before_ref is None else before_ref[line]
            for n, place in enumerate(places):
                at = n * groups + g
                keyed, valued = keys_of(piece_refs[at], masks[at], s, pairs)
                part = partial_sums(lhs_ref[line], bias_ref, place, keyed, valued)
                total = part if total is None else total + part
            out_ref[line] = total
        return carry

    lax.fori_loop(0, size, one_line, 0, unroll=2)


def start_kernel(groups, size, pairs, places, lhs_ref, bias_ref, before_ref, *refs):
    add_pieces(
        groups, size, pairs, places, lhs_ref, bias_ref, before_ref, refs[:-1], refs[-1]
    )


def finish_kernel(
    heads, groups, size, pairs, place, lhs_ref, bias_ref, sums_ref, w_ref, keep_ref, received_ref,
    *refs,
):
    piece_refs, far_refs = refs[:groups], refs[groups : 4 * groups]
    mine_ref, theirs_ref, attended_ref, range_ref, copy_ref = refs[4 * groups :]
    hidden = w_ref.shape[0]
    depth = hidden // heads
    lead = size * pairs
    row, col = iota((4 * hidden, 128), 0), iota((4 * hidden, 128), 1)
    pick_value = one_hot(row == 2 * hidden + col % hidden)
    pick_gate = one_hot(row == 3 * hidden + col % hidden)
    row, col = iota((128, hidden), 0), iota((128, hidden), 1)
    wv = mm(mm(one_hot(row == col), w_ref[...]).astype(BF16), pick_value).astype(BF16)
    wg = mm(mm(one_hot(row % hidden == col), w_ref[...]).astype(BF16), pick_gate)
    row, col = iota((128, 128), 0), iota((128, 128), 1)
    wg = jnp.where(row // hidden == col // hidden, wg, 0.0).astype(BF16)
    lane, row = iota((2 * heads, 128), 1), iota((2 * heads, 128), 0)
    own_head = jnp.where(lane // depth == row, 1.0, 0.0)[None]
    masks = [masks_of(ref, size, pairs) for ref in piece_refs]
    low = iota((lhs_ref.shape[1], 128), 1) < 64
    row, col = iota((128, 1), 0), iota((1, 128), 1)
    averaged = jnp.where(row + 0 * col < hidden, 0.0, 1.0 / (128 - hidden)).astype(BF16)
    wv = jnp.concatenate([wv, averaged], axis=1)
    wv = jnp.concatenate([wv, wv], axis=0)
    own_head = jnp.concatenate([own_head, own_head], axis=2)

    def settle(line, total):
        mixed = mm(jnp.concatenate(halves(total), axis=1), wv)
        summed = jnp.sum(mixed.reshape(2 * pairs, 2 * heads, 256) * own_head, axis=1)
        summed = summed[:, :128] / summed[:, 128:]
        start = pl.multiple_of(line * pairs, pairs)
        for n in range(2):
            attended_ref[n, pl.ds(start, pairs), :] = summed[n * pairs : (n + 1) * pairs]

    range_ref[...] = jnp.ones(range_ref.shape, F32)

    def one_line(s, carry):
        for g in range(groups):
            line = g * size + s
            keyed, valued = keys_of(piece_refs[g], masks[g], s, pairs)
            total = sums_ref[line] + partial_sums(lhs_ref[line], bias_ref, place, keyed, valued)
            settle(line, total)
            weight = jnp.where(low, 1.0, total).reshape(-1, 8, 128)
            range_ref[0] = jnp.minimum(range_ref[0], jnp.min(weight, axis=0))
            range_ref[1] = jnp.maximum(range_ref[1], jnp.max(weight, axis=0))
        return carry

    lax.fori_loop(0, size, one_line, 0, unroll=2)
    fine = (range_ref[0] > 2.0**-80) & (range_ref[1] < 2.0**100)

    @pl.when(jnp.min(jnp.where(fine, 1.0, 0.0)) < 0.5)
    def _():
        for n, ref in enumerate(far_refs):
            pltpu.sync_copy(ref, copy_ref.at[n])
        for g in range(groups):
            ordered = [copy_ref.at[n * groups + g] for n in range(3)] + [piece_refs[g]]
            all_masks = [masks_of(ref, size, pairs) for ref in ordered]

            def exact_line(s, carry):
                line = g * size + s
                both = [keys_of(r, m, s, pairs) for r, m in zip(ordered, all_masks)]
                logits = []
                for n, (keyed, _) in enumerate(both):
                    width = keyed.shape[0]
                    bias = bias_ref[:, n * width : (n + 1) * width]
                    logits.append(mm_nt(lhs_ref[line], keyed) + bias)
                peak = functools.reduce(jnp.maximum, logits)
                peak = jnp.max(peak, axis=-1, keepdims=True)
                parts = [
                    mm(jnp.exp2(part - peak).astype(BF16), valued)
                    for part, (_, valued) in zip(logits, both)
                ]
                settle(line, sum(parts[1:], parts[0]))
                return carry

            lax.fori_loop(0, size, exact_line, 0)

    for n, (ref, out_ref) in enumerate(((keep_ref, mine_ref), (received_ref, theirs_ref))):
        for g in range(groups):
            start = g * (lead + pairs)
            gate = jax.nn.sigmoid(mm(ref[start : start + lead, :], wg))
            at = slice(g * lead, (g + 1) * lead)
            out_ref[at, :] = (gate * attended_ref[n, at, :]).astype(BF16)


def final_kernel(
    lines, heads, with_column, me_ref, line_ref, kept_ref, wo_ref, wc_ref, wout_ref,
    mine_ref, theirs_ref, out_ref, gated_ref,
):
    total = line_ref.shape[0]
    pairs = total // lines
    core = me_ref[0] % 2
    share = total // 2
    for owner, ref in ((core, mine_ref), (1 - core, theirs_ref)):
        gated_ref[pl.ds(pl.multiple_of(owner * share, share), share), :] = ref[...]
    hidden = wo_ref.shape[0]
    depth = hidden // heads
    rows_twice = one_hot(iota((128, 1), 0) % hidden == iota((1, hidden), 1))
    same_residue = iota((128, 1), 0) // hidden == iota((1, 128), 1) // hidden

    def twice(matrix, picked):
        wide = mm(mm(rows_twice, matrix).astype(BF16), picked)
        return jnp.where(same_residue, wide, 0.0).astype(BF16)

    def columns(width, chosen):
        return one_hot(iota((width, 1), 0) == chosen)

    lane = iota((1, 128), 1)
    wo = twice(wo_ref[...], columns(hidden, lane % hidden))
    row = (line_ref[...].astype(F32) + mm(gated_ref[...], wo)).astype(BF16)
    if not with_column:
        out_ref[...] = row
        return
    spread = mm(one_hot(iota((total, lines), 0) // pairs == iota((total, lines), 1)), kept_ref[...])
    own = iota((total, 2 * pairs), 1) // 2 == iota((total, 2 * pairs), 0) % pairs
    sides = one_hot(iota((2 * pairs, 128), 0) % 2 == iota((2 * pairs, 128), 1) // 64)
    kept = mm(jnp.where(own, spread, 0.0).astype(BF16), sides)

    choices = [
        lane % hidden,
        hidden + lane % hidden,
        2 * hidden + lane % depth,
        2 * hidden + depth + lane % depth,
    ]
    wc = [twice(wc_ref[...], columns(wc_ref.shape[1], chosen)) for chosen in choices]
    projected = mm(paired_norm(row, 64), jnp.concatenate(wc, axis=1))
    query, gate, key, value = [projected[:, 128 * n : 128 * (n + 1)] for n in range(4)]

    def grid(a):
        return a.reshape(lines, pairs, 128)

    count = jnp.maximum(jnp.sum(grid(kept), axis=0), 1.0)
    mean_query = jnp.sum(grid(kept * query), axis=0) / count * (depth**-0.5)
    same_head = block_matrix(128, depth, 1.0, 1.0)
    product = (mean_query[None] * grid(key)).reshape(total, 128)
    logits = grid(mm_split(product, same_head) + 1e9 * (kept - 1.0))
    exped = jnp.exp(logits - jnp.max(logits, axis=0, keepdims=True))
    mixed = jnp.sum(exped * grid(value), axis=0) / jnp.sum(exped, axis=0)
    gated = (jax.nn.sigmoid(grid(gate)) * mixed[None]).reshape(total, 128).astype(BF16)
    wout = twice(wout_ref[...], columns(hidden, lane % hidden))
    result = (row.astype(F32) + mm(gated, wout)).astype(BF16)
    shuffled = row_shuffle(result, lines, pairs)
    for t in range(pairs):
        out_ref[:, t * 128 : (t + 1) * 128] = shuffled[t * lines : (t + 1) * lines, :]


def call(kernel, out_shape, *args, **options):
    flops = options.pop("flops", 0)
    limit = pltpu.CompilerParams(vmem_limit_bytes=options.pop("mib", 8) * 1024 * 1024)
    moved = sum(a.size * a.dtype.itemsize for a in args)
    cost = pl.CostEstimate(flops=flops, bytes_accessed=moved, transcendentals=0)
    return pl.pallas_call(
        kernel, out_shape=out_shape, compiler_params=limit, cost_estimate=cost, **options
    )(*args)


def shape(*dims, dtype=BF16):
    return jax.ShapeDtypeStruct(dims, dtype)


def exchange(x, flip, devices):
    return lax.ppermute(x, "res", [(d, d ^ flip) for d in range(devices)])


def layer_normalize(values_in):
    centre = values_in - jnp.mean(values_in, axis=-1, keepdims=True)
    spread = jnp.mean(centre * centre, axis=-1, keepdims=True)
    return centre * lax.rsqrt(spread + EPS)


def column_complete(line, kept, vertical_matrix, vertical_exit_matrix, heads, depth):
    lines, columns, features = line.shape
    hidden = heads * depth
    normed = layer_normalize(line.astype(F32)).astype(BF16)
    projected = mm(normed.reshape(-1, features), vertical_matrix).reshape(lines, columns, -1)
    query, gate = projected[..., :hidden], projected[..., hidden : 2 * hidden]
    key = projected[..., 2 * hidden : 2 * hidden + depth]
    value = projected[..., 2 * hidden + depth :]
    count = jnp.maximum(jnp.sum(kept, axis=0), 1.0)[:, None]
    mean_query = jnp.sum(kept[..., None] * query, axis=0) / count * depth**-0.5
    logits = jnp.einsum("ihc,sic->sih", mean_query.reshape(columns, heads, depth), key)
    logits = logits + 1e9 * (kept - 1.0)[..., None]
    exped = jnp.exp(logits - jnp.max(logits, axis=0, keepdims=True))
    mixed = jnp.einsum("sih,sic->ihc", exped, value) / jnp.sum(exped, axis=0)[..., None]
    gate = jax.nn.sigmoid(gate).reshape(lines, columns, heads, depth)
    gated = (gate * mixed[None]).reshape(-1, hidden).astype(BF16)
    update = mm(gated, vertical_exit_matrix).reshape(lines, columns, features)
    return (line.astype(F32) + update).astype(BF16)


def on_device(
    seq_size,
    res_size,
    extra_activations,
    pair,
    present,
    amino,
    offset_matrix,
    horizontal_matrix,
    horizontal_exit_matrix,
    vertical_matrix,
    vertical_exit_matrix,
):
    lines, residues = present.shape
    pairs = residues // 2
    hidden = horizontal_exit_matrix.shape[0]
    heads = offset_matrix.shape[1]
    depth = hidden // heads
    groups = 2
    size = lines // (2 * groups)
    lead = size * pairs
    keys = res_size * residues
    rows = residues * heads
    core_bit, near, far, high = 1, 2, 4, 8
    kept = (present * amino[None, :]).astype(BF16)
    me = lax.axis_index("res").astype(jnp.int32).reshape(1)
    smem = pl.BlockSpec(memory_space=pltpu.SMEM)
    vmem = pl.BlockSpec(memory_space=pltpu.VMEM)

    rest = lead + pairs
    keep, send, line = call(
        functools.partial(prep_kernel, groups),
        [shape(groups * rest, 128)] * 2 + [shape(lines * pairs, 128)],
        me,
        extra_activations,
        kept,
        in_specs=[smem, vmem, vmem],
        scratch_shapes=[
            pltpu.VMEM((lines * pairs, 128), BF16),
            pltpu.VMEM((2 * groups, pairs, 128), BF16),
        ],
    )

    received = exchange(send, core_bit, res_size)
    chunk = jnp.concatenate([keep, received], axis=0)
    levels = [chunk] + [exchange(chunk, high * k, res_size) for k in range(1, res_size // high)]
    column = jnp.stack(levels).reshape(len(levels), 2, groups, rest, 128)
    own = [column[:, :, g] for g in range(groups)]
    beside = [exchange(part, near, res_size) for part in own]
    across = [exchange(part, far, res_size) for part in own]
    per_step = 4
    bias = call(
        bias_kernel,
        shape(rows, pair.shape[1]),
        pair,
        offset_matrix.T,
        chunk,
        grid=(residues // per_step,),
        in_specs=[
            pl.BlockSpec((per_step,) + pair.shape[1:], lambda n: (n, 0, 0)),
            pl.BlockSpec(offset_matrix.shape[::-1], lambda n: (0, 0)),
            pl.BlockSpec(memory_space=pl.ANY),
        ],
        out_specs=pl.BlockSpec((rows, pair.shape[1]), lambda n: (0, 0)),
        scratch_shapes=[pltpu.VMEM((rows // 128, pair.shape[1], 128), F32)],
        flops=16 * pair.size * 128,
        mib=57,
    )
    if seq_size > 1:
        bias = lax.all_gather(bias, "seq", axis=1, tiled=True)
    pieces = 4
    bias, lhs, sums = call(
        functools.partial(order_kernel, groups, size, pairs, heads, pieces),
        [
            shape(2 * rows, keys, dtype=F32),
            shape(groups * size, 2 * rows, 128),
            shape(groups * size, 2 * rows, 128, dtype=F32),
        ],
        me,
        bias,
        exchange(bias, core_bit, res_size),
        keep,
        received,
        horizontal_matrix,
        *own,
        in_specs=[smem] + [vmem] * (5 + groups),
        flops=8 * rows * keys * keys,
        mib=18,
    )
    beside[0], across[1], bias = lax.optimization_barrier((beside[0], across[1], bias))
    corner = [
        exchange(beside[g], far, res_size) if g % 2 == 0 else exchange(across[g], near, res_size)
        for g in range(groups)
    ]
    sums = call(
        functools.partial(start_kernel, groups, size, pairs, (1, 2)),
        shape(groups * size, 2 * rows, 128, dtype=F32),
        lhs,
        bias,
        sums,
        *beside,
        *across,
        flops=groups * size * rows * keys * 2 * 256 * 4,
        mib=22,
    )
    anywhere = pl.BlockSpec(memory_space=pl.ANY)
    mine, theirs = call(
        functools.partial(finish_kernel, heads, groups, size, pairs, 3),
        [shape(groups * lead, 128)] * 2,
        lhs,
        bias,
        sums,
        horizontal_matrix,
        keep,
        received,
        *corner,
        *own,
        *beside,
        *across,
        in_specs=[vmem] * (6 + groups) + [anywhere] * (3 * groups),
        scratch_shapes=[
            pltpu.VMEM((2, groups * lead, 128), F32),
            pltpu.VMEM((2, 8, 128), F32),
            pltpu.VMEM((3 * groups,) + own[0].shape, BF16),
        ],
        flops=groups * size * rows * keys * 2 * 256,
        mib=22,
    )
    returned = exchange(theirs, core_bit, res_size)

    with_column = seq_size == 1
    final_args = [
        me,
        line,
        kept,
        horizontal_exit_matrix,
        vertical_matrix,
        vertical_exit_matrix,
    ]
    final_args += [mine, returned]
    result = call(
        functools.partial(final_kernel, lines, heads, with_column),
        shape(*extra_activations.shape) if with_column else shape(lines * pairs, 128),
        *final_args,
        in_specs=[smem] + [vmem] * (len(final_args) - 1),
        scratch_shapes=[pltpu.VMEM((lines * pairs, 128), BF16)],
    )
    if with_column:
        return result
    row = result.reshape(lines, residues, hidden)
    moved = lax.all_to_all(row, "seq", split_axis=1, concat_axis=0, tiled=True)
    moved_kept = lax.all_to_all(kept, "seq", split_axis=1, concat_axis=0, tiled=True)
    updated = column_complete(
        moved, moved_kept.astype(F32), vertical_matrix, vertical_exit_matrix, heads, depth
    )
    back = lax.all_to_all(updated, "seq", split_axis=0, concat_axis=1, tiled=True)
    return back.reshape(extra_activations.shape)


def solution(mesh):
    in_specs = (
        P("seq", "res"),
        P("res", "seq", None),
        P("seq", "res"),
        P("res"),
        P(),
        P(),
        P(),
        P(),
        P(),
    )
    sizes = mesh.shape
    return jax.shard_map(
        functools.partial(on_device, sizes["seq"], sizes["res"]),
        mesh=mesh,
        in_specs=in_specs,
        out_specs=P("seq", "res"),
        check_vma=False,
    )
```

```python
import functools
import math

import jax
import jax.numpy as jnp
from jax import lax
from jax.experimental import pallas as pl
from jax.experimental.pallas import tpu as pltpu
from jax.sharding import PartitionSpec as P

F32 = jnp.float32
BF16 = jnp.bfloat16
LOG2E = math.log2(math.e)
EPS = 1e-05

NT = (((1,), (1,)), ((), ()))


def mm(a, b):
    return jnp.dot(a, b, preferred_element_type=F32)


def mm_nt(a, b):
    return lax.dot_general(a, b, NT, preferred_element_type=F32)


def iota(shape, axis):
    return lax.broadcasted_iota(jnp.int32, shape, axis)


def one_hot(condition):
    return jnp.where(condition, 1.0, 0.0).astype(BF16)


def block_matrix(size, block, on_diagonal, elsewhere):
    row, col = iota((size, 1), 0), iota((1, size), 1)
    inside = jnp.where(row == col, on_diagonal, elsewhere)
    return jnp.where(row // block == col // block, inside, 0.0).astype(BF16)


def halves(value):
    high = value.astype(BF16)
    return high, (value - high.astype(F32)).astype(BF16)


def mm_split(value, matrix):
    high, low = halves(value)
    return mm(high, matrix) + mm(low, matrix)


def paired_norm(x, width):
    lanes = x.shape[1]
    centre = mm(x, block_matrix(lanes, width, 1.0 - 1.0 / width, -1.0 / width))
    spread = mm_split(centre * centre, block_matrix(lanes, width, 1.0 / width, 1.0 / width))
    return (centre * lax.rsqrt(spread + EPS)).astype(BF16)


def row_shuffle(rows, inner, outer):
    total = rows.shape[0]
    row, col = iota((total, 1), 0), iota((1, total), 1)
    return mm(one_hot(col == (row % inner) * outer + row // inner), rows).astype(BF16)


def prep_kernel(groups, me_ref, m_ref, kept_ref, *refs):
    keep_ref, send_ref, line_ref, normed_ref, spread_ref = refs
    lines, width = m_ref.shape
    pairs = width // 128
    stacked = jnp.concatenate([m_ref[:, t * 128 : (t + 1) * 128] for t in range(pairs)], axis=0)
    normed = paired_norm(stacked, 64)
    both = row_shuffle(jnp.concatenate([normed, stacked], axis=1), pairs, lines)
    normed_ref[...] = both[:, :128]
    line_ref[...] = both[:, 128:]
    kept = kept_ref[...]
    size = lines // (2 * groups)
    residues = 2 * pairs
    row, col = iota((pairs, residues), 0), iota((pairs, residues), 1)
    evens, odds = one_hot(col == 2 * row), one_hot(col == 2 * row + 1)
    row, col = iota((128, lines), 0) - 64, iota((128, lines), 1)
    core = me_ref[0] % 2
    for n in range(2 * groups):
        start = jnp.where(n // groups == core, 0, 2 * size)
        chosen = (row >= start) & (row < start + 2 * size) & (row % size == col - n * size)
        spread = mm(one_hot(chosen), kept).astype(BF16)
        first = iota((pairs, 128), 1) < 64 + size + start
        spread_ref[n] = jnp.where(first, mm_nt(evens, spread), mm_nt(odds, spread)).astype(BF16)
    rows = size * pairs
    for ref, half in ((keep_ref, core), (send_ref, 1 - core)):
        for g in range(groups):
            index = half * groups + g
            ref[g, :rows] = normed_ref[pl.ds(pl.multiple_of(index * rows, rows), rows), :]
            ref[g, rows:] = spread_ref[index]


def bias_kernel(whole, pieces, x_ref, w_ref, after_ref, me_ref, *refs):
    outs, (acc_ref, centring_ref, wide_ref) = refs[:-3], refs[-3:]
    step = pl.program_id(0)
    heads = w_ref.shape[0]
    per_step, keys, channels = x_ref.shape
    residues = per_step * pl.num_programs(0)
    pairs = residues // 2
    tiles = acc_ref.shape[0]
    width = tiles * 128

    @pl.when(step == 0)
    def _():
        centring_ref[...] = block_matrix(
            2 * channels, channels, 1.0 - 1.0 / channels, -1.0 / channels
        )
        spread = one_hot(iota((heads, 1), 0) == iota((1, width), 1) // residues)
        wide_ref[...] = lax.dot_general(
            w_ref[...], spread, (((0,), (0,)), ((), ())), preferred_element_type=F32
        )
        acc_ref[...] = jnp.zeros(acc_ref.shape, F32)

    lane = iota((1, width), 1) % residues
    placed = []
    for n in range(per_step):
        residue = step * per_step + n
        mine = lane == (residue % 2) * pairs + residue // 2
        placed.append(jnp.where(mine, wide_ref[...], 0.0).astype(BF16))
    placed = jnp.concatenate(placed, axis=0)
    centring = centring_ref[...]
    piece = min(512, keys)
    for r in range(0, keys, piece):
        normed = []
        for n in range(0, per_step, 2):
            x = jnp.concatenate([x_ref[n, r : r + piece], x_ref[n + 1, r : r + piece]], axis=1)
            centre = mm(x, centring)
            for part in (centre[:, :channels], centre[:, channels:]):
                spread = jnp.mean(part * part, axis=-1, keepdims=True)
                normed.append((part * lax.rsqrt(spread + EPS)).astype(BF16))
        added = mm(jnp.concatenate(normed, axis=1), placed)
        for n in range(tiles):
            acc_ref[n, r : r + piece, :] += added[:, n * 128 : (n + 1) * 128]

    @pl.when(step == pl.num_programs(0) - 1)
    def _():
        if not whole:
            for n in range(tiles):
                outs[0][n * 128 : (n + 1) * 128, :] = acc_ref[n].T.astype(BF16)
            return
        levels = keys // (2 * pieces * residues)
        for flip in range(2):
            user = me_ref[0] ^ flip
            starts = [
                (user ^ (c + 2 * q + 2 * pieces * k)) * residues + p
                for q in range(pieces)
                for p in range(2)
                for k in range(levels)
                for c in range(2)
            ]
            for n in range(tiles):
                for at in range(0, keys, 128):
                    rows = [
                        acc_ref[n, pl.ds(start, pairs, stride=2), :]
                        for start in starts[at // pairs : (at + 128) // pairs]
                    ]
                    turned = jnp.concatenate(rows, axis=0).T.astype(BF16)
                    if flip == 0:
                        turned = turned.astype(F32) * LOG2E
                    outs[flip][n * 128 : (n + 1) * 128, at : at + 128] = turned


def order_kernel(residues, pieces, me_ref, bias_ref, own_ref, send_ref):
    rows, keys = bias_ref.shape
    pairs = residues // 2
    lane = iota((1, keys), 1)
    each = keys // pieces
    which, rest = lane // each, lane % each
    parity, rest = rest // (each // 2), rest % (each // 2)
    place, pair = rest // pairs, rest % pairs
    for flip, out_ref in enumerate((own_ref, send_ref)):
        device = me_ref[0] ^ flip ^ ((place % 2) + 2 * which + 2 * pieces * (place // 2))
        target = device * residues + 2 * pair + parity
        total = jnp.zeros((rows, keys), F32)
        for start in range(0, keys, 256):
            chosen = one_hot(iota((256, keys), 0) + start == target)
            total = total + mm(bias_ref[:, start : start + 256], chosen)
        out_ref[...] = total * LOG2E if flip == 0 else total.astype(BF16)


def query_kernel(
    groups, size, pairs, heads, own_ref, peer_ref, keep_ref, received_ref, w_ref, *refs
):
    column_refs, (bias_ref, lhs_ref, sums_ref) = refs[:groups], refs[groups:]
    rows = own_ref.shape[0]
    bias_ref[:rows, :] = own_ref[...]
    bias_ref[rows:, :] = peer_ref[...].astype(F32) * LOG2E

    hidden = w_ref.shape[0]
    depth = hidden // heads
    twice_rows = one_hot(iota((128, 1), 0) % hidden == iota((1, hidden), 1))
    wq = mm(
        mm(twice_rows, w_ref[...]).astype(BF16),
        one_hot(iota((4 * hidden, 1), 0) == iota((1, 128), 1) % hidden),
    )
    same_residue = iota((128, 1), 0) // hidden == iota((1, 128), 1) // hidden
    wq = jnp.where(same_residue, wq, 0.0).astype(BF16)
    picked = one_hot(iota((1, 4 * hidden), 1) == hidden + iota((128, 1), 0) % hidden)
    wk = mm_nt(picked, w_ref[...]).astype(BF16)
    wk = mm(wk, one_hot(iota((hidden, 1), 0) == iota((1, 128), 1))).astype(BF16)
    lead = size * pairs
    lane = iota((1, 128), 1)
    spare = lane - hidden
    for g in range(groups):
        for n, ref in enumerate((keep_ref, received_ref)):
            query = (mm(ref[g, :lead], wq) * (depth**-0.5)).astype(BF16).astype(F32)
            for s in range(size):
                q = query[s * pairs : (s + 1) * pairs]
                spread = [
                    jnp.where(lane // depth == p * heads + h, q, 0.0).astype(BF16)
                    for h in range(heads)
                    for p in range(2)
                ]
                folded = mm(jnp.concatenate(spread, axis=0), wk) * LOG2E
                picks = (spare >= 0) & (spare < 4 * size) & (spare % size == s)
                lhs_ref[g * size + s, n * rows : (n + 1) * rows, :] = jnp.where(
                    picks, 1.0, folded
                ).astype(BF16)
    add_pieces(groups, size, pairs, (0,) * groups, lhs_ref, bias_ref, None, column_refs, sums_ref)


def masks_of(ref, size, pairs):
    start = 2 * size * pairs
    lane = iota((1, 128), 1) - 64
    masks = []
    for p in range(2):
        blocks = []
        for k in range(ref.shape[0]):
            hidden = (1e9 * LOG2E) * (ref[k, start : start + pairs, :].astype(F32) - 1.0)
            for c in range(2):
                first = (2 * c + p) * size
                mine = (lane >= first) & (lane < first + size)
                blocks.append(jnp.where(mine, hidden, 0.0).astype(BF16))
        masks.append(jnp.concatenate(blocks, axis=0))
    return masks


def keys_of(ref, masks, s, size, pairs):
    start = pl.multiple_of(s * pairs, pairs)
    even = jnp.concatenate(
        [
            ref[k, pl.ds(c * size * pairs + start, pairs), :]
            for k in range(ref.shape[0])
            for c in range(2)
        ],
        axis=0,
    )
    odd = pltpu.roll(even.astype(F32), 64, 1).astype(BF16)
    low = iota(even.shape, 1) < 64
    one = jnp.ones_like(even)
    keyed = [jnp.where(low, x, m) for x, m in zip((even, odd), masks)]
    valued = [jnp.where(low, x, one) for x in (even, odd)]
    return jnp.concatenate(keyed, axis=0), jnp.concatenate(valued, axis=0)


def partial_sums(lhs, bias_ref, piece, keyed, valued):
    width = keyed.shape[0]
    logits = mm_nt(lhs, keyed) + bias_ref[:, piece * width : (piece + 1) * width]
    return mm(jnp.exp2(logits).astype(BF16), valued)


def add_pieces(groups, size, pairs, places, lhs_ref, bias_ref, before_ref, piece_refs, out_ref):
    masks = [masks_of(ref, size, pairs) for ref in piece_refs]

    def one_line(s, carry):
        for g in range(groups):
            line = g * size + s
            keyed, valued = keys_of(piece_refs[g], masks[g], s, size, pairs)
            total = partial_sums(lhs_ref[line], bias_ref, places[g], keyed, valued)
            out_ref[line] = total if before_ref is None else before_ref[line] + total
        return carry

    lax.fori_loop(0, size, one_line, 0, unroll=2)


def add_kernel(groups, size, pairs, places, lhs_ref, bias_ref, before_ref, *refs):
    add_pieces(
        groups, size, pairs, places, lhs_ref, bias_ref, before_ref, refs[:-1], refs[-1]
    )


def finish_kernel(
    heads, groups, size, pairs, place, lhs_ref, bias_ref, sums_ref, w_ref, keep_ref, received_ref,
    *refs,
):
    piece_refs, far_refs = refs[:groups], refs[groups : 4 * groups]
    mine_ref, theirs_ref, high_ref, low_ref, range_ref, copy_ref = refs[4 * groups :]
    hidden = w_ref.shape[0]
    depth = hidden // heads
    lead = size * pairs
    blocks = 2 * heads
    row, col = iota((128, 1), 0), iota((1, 256), 1)
    picked = one_hot(iota((4 * hidden, 1), 0) == 2 * hidden + col % hidden)
    picked = jnp.where(col < 128, picked, jnp.zeros_like(picked))
    wv = mm(mm(one_hot(row == iota((1, hidden), 1)), w_ref[...]).astype(BF16), picked)
    counted = (row >= hidden) & (col >= 128)
    wv = jnp.where(counted, 1.0 / (128 - hidden), wv)
    owner = col % 128 // depth
    wv = jnp.concatenate(
        [
            jnp.where(owner == p * heads + h, wv, 0.0).astype(BF16)
            for h in range(heads)
            for p in range(2)
        ],
        axis=0,
    )
    lane = iota((1, 128), 1)
    wg = mm(
        mm(one_hot(row % hidden == iota((1, hidden), 1)), w_ref[...]).astype(BF16),
        one_hot(iota((4 * hidden, 1), 0) == 3 * hidden + lane % hidden),
    )
    wg = jnp.where(row // hidden == lane // hidden, wg, 0.0).astype(BF16)
    masks = [masks_of(ref, size, pairs) for ref in piece_refs]
    low = iota((lhs_ref.shape[1], 128), 1) < 64

    def settle(line, total):
        start = pl.multiple_of(line * pairs, pairs)
        for ref, part in zip((high_ref, low_ref), halves(total)):
            for n in range(2):
                for b in range(blocks):
                    at = (n * blocks + b) * pairs
                    ref[n, pl.ds(start, pairs), b * 128 : (b + 1) * 128] = part[at : at + pairs]

    range_ref[...] = jnp.ones(range_ref.shape, F32)

    def one_line(s, carry):
        for g in range(groups):
            line = g * size + s
            keyed, valued = keys_of(piece_refs[g], masks[g], s, size, pairs)
            total = sums_ref[line] + partial_sums(lhs_ref[line], bias_ref, place, keyed, valued)
            settle(line, total)
            weight = jnp.where(low, 1.0, total).reshape(-1, 8, 128)
            range_ref[0] = jnp.minimum(range_ref[0], jnp.min(weight, axis=0))
            range_ref[1] = jnp.maximum(range_ref[1], jnp.max(weight, axis=0))
        return carry

    lax.fori_loop(0, size, one_line, 0, unroll=2)
    fine = (range_ref[0] > 2.0**-80) & (range_ref[1] < 2.0**100)

    @pl.when(jnp.min(jnp.where(fine, 1.0, 0.0)) < 0.5)
    def _():
        for n, ref in enumerate(far_refs):
            pltpu.sync_copy(ref, copy_ref.at[n])
        for g in range(groups):
            ordered = [copy_ref.at[n * groups + g] for n in range(3)] + [piece_refs[g]]
            all_masks = [masks_of(ref, size, pairs) for ref in ordered]

            def exact_line(s, carry):
                line = g * size + s
                both = [keys_of(r, m, s, size, pairs) for r, m in zip(ordered, all_masks)]
                logits = []
                for n, (keyed, _) in enumerate(both):
                    width = keyed.shape[0]
                    bias = bias_ref[:, n * width : (n + 1) * width]
                    logits.append(mm_nt(lhs_ref[line], keyed) + bias)
                peak = functools.reduce(jnp.maximum, logits)
                peak = jnp.max(peak, axis=-1, keepdims=True)
                parts = [
                    mm(jnp.exp2(part - peak).astype(BF16), valued)
                    for part, (_, valued) in zip(logits, both)
                ]
                settle(line, sum(parts[1:], parts[0]))
                return carry

            lax.fori_loop(0, size, exact_line, 0)

    for n, (ref, out_ref) in enumerate(((keep_ref, mine_ref), (received_ref, theirs_ref))):
        mixed = mm(high_ref[n], wv) + mm(low_ref[n], wv)
        mixed = mixed[:, :128] / mixed[:, 128:]
        for g in range(groups):
            gate = jax.nn.sigmoid(mm(ref[g, :lead], wg))
            at = slice(g * lead, (g + 1) * lead)
            out_ref[at, :] = (gate * mixed[at]).astype(BF16)


def final_kernel(
    lines, heads, with_column, me_ref, line_ref, kept_ref, wo_ref, wc_ref, wout_ref,
    mine_ref, theirs_ref, out_ref, gated_ref,
):
    total = line_ref.shape[0]
    pairs = total // lines
    core = me_ref[0] % 2
    share = total // 2
    for owner, ref in ((core, mine_ref), (1 - core, theirs_ref)):
        gated_ref[pl.ds(pl.multiple_of(owner * share, share), share), :] = ref[...]
    hidden = wo_ref.shape[0]
    depth = hidden // heads
    rows_twice = one_hot(iota((128, 1), 0) % hidden == iota((1, hidden), 1))
    same_residue = iota((128, 1), 0) // hidden == iota((1, 128), 1) // hidden

    def twice(matrix, picked):
        wide = mm(mm(rows_twice, matrix).astype(BF16), picked)
        return jnp.where(same_residue, wide, 0.0).astype(BF16)

    def columns(width, chosen):
        return one_hot(iota((width, 1), 0) == chosen)

    lane = iota((1, 128), 1)
    wo = twice(wo_ref[...], columns(hidden, lane % hidden))
    row = (line_ref[...].astype(F32) + mm(gated_ref[...], wo)).astype(BF16)
    if not with_column:
        out_ref[...] = row
        return
    spread = mm(one_hot(iota((total, lines), 0) // pairs == iota((total, lines), 1)), kept_ref[...])
    own = iota((total, 2 * pairs), 1) // 2 == iota((total, 2 * pairs), 0) % pairs
    sides = one_hot(iota((2 * pairs, 128), 0) % 2 == iota((2 * pairs, 128), 1) // 64)
    kept = mm(jnp.where(own, spread, 0.0).astype(BF16), sides)

    choices = [
        lane % hidden,
        hidden + lane % hidden,
        2 * hidden + lane % depth,
        2 * hidden + depth + lane % depth,
    ]
    wc = [twice(wc_ref[...], columns(wc_ref.shape[1], chosen)) for chosen in choices]
    projected = mm(paired_norm(row, 64), jnp.concatenate(wc, axis=1))
    query, gate, key, value = [projected[:, 128 * n : 128 * (n + 1)] for n in range(4)]

    def grid(a):
        return a.reshape(lines, pairs, 128)

    count = jnp.maximum(jnp.sum(grid(kept), axis=0), 1.0)
    mean_query = jnp.sum(grid(kept * query), axis=0) / count * (depth**-0.5)
    same_head = block_matrix(128, depth, 1.0, 1.0)
    product = (mean_query[None] * grid(key)).reshape(total, 128)
    logits = grid(mm_split(product, same_head) + 1e9 * (kept - 1.0))
    exped = jnp.exp(logits - jnp.max(logits, axis=0, keepdims=True))
    mixed = jnp.sum(exped * grid(value), axis=0) / jnp.sum(exped, axis=0)
    gated = (jax.nn.sigmoid(grid(gate)) * mixed[None]).reshape(total, 128).astype(BF16)
    wout = twice(wout_ref[...], columns(hidden, lane % hidden))
    result = (row.astype(F32) + mm(gated, wout)).astype(BF16)
    shuffled = row_shuffle(result, lines, pairs)
    for t in range(pairs):
        out_ref[:, t * 128 : (t + 1) * 128] = shuffled[t * lines : (t + 1) * lines, :]


def call(kernel, out_shape, *args, **options):
    flops = options.pop("flops", 0)
    limit = pltpu.CompilerParams(vmem_limit_bytes=options.pop("mib", 8) * 1024 * 1024)
    moved = sum(a.size * a.dtype.itemsize for a in args)
    cost = pl.CostEstimate(flops=flops, bytes_accessed=moved, transcendentals=0)
    return pl.pallas_call(
        kernel, out_shape=out_shape, compiler_params=limit, cost_estimate=cost, **options
    )(*args)


def shape(*dims, dtype=BF16):
    return jax.ShapeDtypeStruct(dims, dtype)


def exchange(x, flip, devices):
    return lax.ppermute(x, "res", [(d, d ^ flip) for d in range(devices)])


def layer_normalize(values_in):
    centre = values_in - jnp.mean(values_in, axis=-1, keepdims=True)
    spread = jnp.mean(centre * centre, axis=-1, keepdims=True)
    return centre * lax.rsqrt(spread + EPS)


def column_complete(line, kept, vertical_matrix, vertical_exit_matrix, heads, depth):
    lines, columns, features = line.shape
    hidden = heads * depth
    normed = layer_normalize(line.astype(F32)).astype(BF16)
    projected = mm(normed.reshape(-1, features), vertical_matrix).reshape(lines, columns, -1)
    query, gate = projected[..., :hidden], projected[..., hidden : 2 * hidden]
    key = projected[..., 2 * hidden : 2 * hidden + depth]
    value = projected[..., 2 * hidden + depth :]
    count = jnp.maximum(jnp.sum(kept, axis=0), 1.0)[:, None]
    mean_query = jnp.sum(kept[..., None] * query, axis=0) / count * depth**-0.5
    logits = jnp.einsum("ihc,sic->sih", mean_query.reshape(columns, heads, depth), key)
    logits = logits + 1e9 * (kept - 1.0)[..., None]
    exped = jnp.exp(logits - jnp.max(logits, axis=0, keepdims=True))
    mixed = jnp.einsum("sih,sic->ihc", exped, value) / jnp.sum(exped, axis=0)[..., None]
    gate = jax.nn.sigmoid(gate).reshape(lines, columns, heads, depth)
    gated = (gate * mixed[None]).reshape(-1, hidden).astype(BF16)
    update = mm(gated, vertical_exit_matrix).reshape(lines, columns, features)
    return (line.astype(F32) + update).astype(BF16)


def on_device(
    seq_size,
    res_size,
    extra_activations,
    pair,
    present,
    amino,
    offset_matrix,
    horizontal_matrix,
    horizontal_exit_matrix,
    vertical_matrix,
    vertical_exit_matrix,
):
    lines, residues = present.shape
    pairs = residues // 2
    hidden = horizontal_exit_matrix.shape[0]
    heads = offset_matrix.shape[1]
    depth = hidden // heads
    groups = 2
    size = lines // (2 * groups)
    lead = size * pairs
    keys = res_size * residues
    rows = residues * heads
    core_bit, near, far, high = 1, 2, 4, 8
    kept = (present * amino[None, :]).astype(BF16)
    me = lax.axis_index("res").astype(jnp.int32).reshape(1)
    smem = pl.BlockSpec(memory_space=pltpu.SMEM)
    vmem = pl.BlockSpec(memory_space=pltpu.VMEM)

    rest = lead + pairs
    keep, send, line = call(
        functools.partial(prep_kernel, groups),
        [shape(groups, rest, 128)] * 2 + [shape(lines * pairs, 128)],
        me,
        extra_activations,
        kept,
        in_specs=[smem, vmem, vmem],
        scratch_shapes=[
            pltpu.VMEM((lines * pairs, 128), BF16),
            pltpu.VMEM((2 * groups, pairs, 128), BF16),
        ],
    )

    received = exchange(send, core_bit, res_size)
    chunk = jnp.concatenate(
        [keep[:, :lead], received[:, :lead], keep[:, lead:] + received[:, lead:]], axis=1
    )
    levels = [chunk] + [exchange(chunk, high * k, res_size) for k in range(1, res_size // high)]
    own = [jnp.stack([level[g] for level in levels]) for g in range(groups)]
    beside = [exchange(part, near, res_size) for part in own]
    across = [exchange(part, far, res_size) for part in own]

    per_step = 8
    pieces = 4
    whole = seq_size == 1
    bias_rows = [shape(rows, keys, dtype=F32), shape(rows, keys)]
    bias = call(
        functools.partial(bias_kernel, whole, pieces),
        bias_rows if whole else [shape(rows, pair.shape[1])],
        pair,
        offset_matrix.T,
        chunk,
        me,
        grid=(residues // per_step,),
        in_specs=[
            pl.BlockSpec((per_step,) + pair.shape[1:], lambda n: (n, 0, 0)),
            pl.BlockSpec(offset_matrix.shape[::-1], lambda n: (0, 0)),
            pl.BlockSpec(memory_space=pl.ANY),
            smem,
        ],
        out_specs=[pl.BlockSpec((rows, pair.shape[1]), lambda n: (0, 0))] * (1 + whole),
        scratch_shapes=[
            pltpu.VMEM((rows // 128, pair.shape[1], 128), F32),
            pltpu.VMEM((2 * pair.shape[2], 2 * pair.shape[2]), BF16),
            pltpu.VMEM((pair.shape[2], rows), F32),
        ],
        flops=16 * pair.size * 128,
        mib=57,
    )
    if not whole:
        bias = call(
            functools.partial(order_kernel, residues, pieces),
            bias_rows,
            me,
            lax.all_gather(bias[0], "seq", axis=1, tiled=True),
            in_specs=[smem, vmem],
            mib=14,
        )
    bias, lhs, sums = call(
        functools.partial(query_kernel, groups, size, pairs, heads),
        [
            shape(2 * rows, keys, dtype=F32),
            shape(groups * size, 2 * rows, 128),
            shape(groups * size, 2 * rows, 128, dtype=F32),
        ],
        bias[0],
        exchange(bias[1], core_bit, res_size),
        keep,
        received,
        horizontal_matrix,
        *own,
        in_specs=[vmem] * (5 + groups),
        flops=8 * rows * keys * keys,
        mib=18,
    )

    def add(sums, places, parts):
        return call(
            functools.partial(add_kernel, groups, size, pairs, places),
            shape(*sums.shape, dtype=F32),
            lhs,
            bias,
            sums,
            *parts,
            flops=groups * size * rows * keys * 2 * 256 * 2,
            mib=20,
        )

    beside[0], across[1], sums = lax.optimization_barrier((beside[0], across[1], sums))
    corner = [
        exchange(beside[g], far, res_size) if g % 2 == 0 else exchange(across[g], near, res_size)
        for g in range(groups)
    ]
    sums = add(sums, (1, 2), (beside[0], across[1]))
    beside[1], across[0], sums = lax.optimization_barrier((beside[1], across[0], sums))
    sums = add(sums, (2, 1), (across[0], beside[1]))
    corner[0], corner[1], sums = lax.optimization_barrier((corner[0], corner[1], sums))
    anywhere = pl.BlockSpec(memory_space=pl.ANY)
    mine, theirs = call(
        functools.partial(finish_kernel, heads, groups, size, pairs, 3),
        [shape(groups * lead, 128)] * 2,
        lhs,
        bias,
        sums,
        horizontal_matrix,
        keep,
        received,
        *corner,
        *own,
        *beside,
        *across,
        in_specs=[vmem] * (6 + groups) + [anywhere] * (3 * groups),
        scratch_shapes=[
            pltpu.VMEM((2, groups * lead, 128 * 2 * heads), BF16),
            pltpu.VMEM((2, groups * lead, 128 * 2 * heads), BF16),
            pltpu.VMEM((2, 8, 128), F32),
            pltpu.VMEM((3 * groups,) + own[0].shape, BF16),
        ],
        flops=groups * size * rows * keys * 2 * 256,
        mib=24,
    )
    returned = exchange(theirs, core_bit, res_size)

    with_column = seq_size == 1
    final_args = [
        me,
        line,
        kept,
        horizontal_exit_matrix,
        vertical_matrix,
        vertical_exit_matrix,
    ]
    final_args += [mine, returned]
    result = call(
        functools.partial(final_kernel, lines, heads, with_column),
        shape(*extra_activations.shape) if with_column else shape(lines * pairs, 128),
        *final_args,
        in_specs=[smem] + [vmem] * (len(final_args) - 1),
        scratch_shapes=[pltpu.VMEM((lines * pairs, 128), BF16)],
    )
    if with_column:
        return result
    row = result.reshape(lines, residues, hidden)
    moved = lax.all_to_all(row, "seq", split_axis=1, concat_axis=0, tiled=True)
    moved_kept = lax.all_to_all(kept, "seq", split_axis=1, concat_axis=0, tiled=True)
    updated = column_complete(
        moved, moved_kept.astype(F32), vertical_matrix, vertical_exit_matrix, heads, depth
    )
    back = lax.all_to_all(updated, "seq", split_axis=0, concat_axis=1, tiled=True)
    return back.reshape(extra_activations.shape)


def solution(mesh):
    in_specs = (
        P("seq", "res"),
        P("res", "seq", None),
        P("seq", "res"),
        P("res"),
        P(),
        P(),
        P(),
        P(),
        P(),
    )
    sizes = mesh.shape
    return jax.shard_map(
        functools.partial(on_device, sizes["seq"], sizes["res"]),
        mesh=mesh,
        in_specs=in_specs,
        out_specs=P("seq", "res"),
        check_vma=False,
    )
```

```python
import functools
import math

import jax
import jax.numpy as jnp
from jax import lax
from jax.experimental import pallas as pl
from jax.experimental.pallas import tpu as pltpu
from jax.sharding import PartitionSpec as P

F32 = jnp.float32
BF16 = jnp.bfloat16
LOG2E = math.log2(math.e)
EPS = 1e-05

NT = (((1,), (1,)), ((), ()))


def mm(a, b):
    return jnp.dot(a, b, preferred_element_type=F32)


def mm_nt(a, b):
    return lax.dot_general(a, b, NT, preferred_element_type=F32)


def iota(shape, axis):
    return lax.broadcasted_iota(jnp.int32, shape, axis)


def one_hot(condition):
    return jnp.where(condition, 1.0, 0.0).astype(BF16)


def block_matrix(size, block, on_diagonal, elsewhere):
    row, col = iota((size, 1), 0), iota((1, size), 1)
    inside = jnp.where(row == col, on_diagonal, elsewhere)
    return jnp.where(row // block == col // block, inside, 0.0).astype(BF16)


def halves(value):
    high = value.astype(BF16)
    return high, (value - high.astype(F32)).astype(BF16)


def mm_split(value, matrix):
    high, low = halves(value)
    return mm(high, matrix) + mm(low, matrix)


def paired_norm(x, width):
    lanes = x.shape[1]
    centre = mm(x, block_matrix(lanes, width, 1.0 - 1.0 / width, -1.0 / width))
    spread = mm_split(centre * centre, block_matrix(lanes, width, 1.0 / width, 1.0 / width))
    return (centre * lax.rsqrt(spread + EPS)).astype(BF16)


def row_shuffle(rows, inner, outer):
    total = rows.shape[0]
    row, col = iota((total, 1), 0), iota((1, total), 1)
    return mm(one_hot(col == (row % inner) * outer + row // inner), rows).astype(BF16)


def prep_kernel(groups, me_ref, m_ref, kept_ref, *refs):
    keep_ref, send_ref, line_ref, normed_ref, spread_ref = refs
    lines, width = m_ref.shape
    pairs = width // 128
    stacked = jnp.concatenate([m_ref[:, t * 128 : (t + 1) * 128] for t in range(pairs)], axis=0)
    normed = paired_norm(stacked, 64)
    both = row_shuffle(jnp.concatenate([normed, stacked], axis=1), pairs, lines)
    normed_ref[...] = both[:, :128]
    line_ref[...] = both[:, 128:]
    kept = kept_ref[...]
    size = lines // (2 * groups)
    residues = 2 * pairs
    row, col = iota((pairs, residues), 0), iota((pairs, residues), 1)
    evens, odds = one_hot(col == 2 * row), one_hot(col == 2 * row + 1)
    row, col = iota((128, lines), 0) - 64, iota((128, lines), 1)
    core = me_ref[0] % 2
    for n in range(2 * groups):
        start = jnp.where(n // groups == core, 0, 2 * size)
        chosen = (row >= start) & (row < start + 2 * size) & (row % size == col - n * size)
        spread = mm(one_hot(chosen), kept).astype(BF16)
        first = iota((pairs, 128), 1) < 64 + size + start
        spread_ref[n] = jnp.where(first, mm_nt(evens, spread), mm_nt(odds, spread)).astype(BF16)
    rows = size * pairs
    for ref, half in ((keep_ref, core), (send_ref, 1 - core)):
        for g in range(groups):
            index = half * groups + g
            ref[g, :rows] = normed_ref[pl.ds(pl.multiple_of(index * rows, rows), rows), :]
            ref[g, rows:] = spread_ref[index]


def bias_kernel(whole, pieces, x_ref, w_ref, after_ref, me_ref, *refs):
    outs, (acc_ref, centring_ref, averaging_ref, wide_ref) = refs[:-4], refs[-4:]
    step = pl.program_id(0)
    heads = w_ref.shape[0]
    per_step, keys, channels = x_ref.shape
    residues = per_step * pl.num_programs(0)
    pairs = residues // 2
    tiles = acc_ref.shape[0]
    width = tiles * 128

    @pl.when(step == 0)
    def _():
        centring_ref[...] = block_matrix(
            2 * channels, channels, 1.0 - 1.0 / channels, -1.0 / channels
        )
        averaging_ref[...] = block_matrix(
            2 * channels, channels, 1.0 / channels, 1.0 / channels
        )
        spread = one_hot(iota((heads, 1), 0) == iota((1, width), 1) // residues)
        wide_ref[...] = lax.dot_general(
            w_ref[...], spread, (((0,), (0,)), ((), ())), preferred_element_type=F32
        )
        acc_ref[...] = jnp.zeros(acc_ref.shape, F32)

    lane = iota((1, width), 1) % residues
    placed = []
    for n in range(per_step):
        residue = step * per_step + n
        mine = lane == (residue % 2) * pairs + residue // 2
        placed.append(jnp.where(mine, wide_ref[...], 0.0).astype(BF16))
    placed = jnp.concatenate(placed, axis=0)
    centring, averaging = centring_ref[...], averaging_ref[...]
    piece = min(512, keys)
    for r in range(0, keys, piece):
        normed = []
        for n in range(0, per_step, 2):
            x = jnp.concatenate([x_ref[n, r : r + piece], x_ref[n + 1, r : r + piece]], axis=1)
            centre = mm(x, centring)
            spread = mm((centre * centre).astype(BF16), averaging)
            normed.append((centre * lax.rsqrt(spread + EPS)).astype(BF16))
        added = mm(jnp.concatenate(normed, axis=1), placed)
        for n in range(tiles):
            acc_ref[n, r : r + piece, :] += added[:, n * 128 : (n + 1) * 128]

    @pl.when(step == pl.num_programs(0) - 1)
    def _():
        if not whole:
            for n in range(tiles):
                outs[0][n * 128 : (n + 1) * 128, :] = acc_ref[n].T.astype(BF16)
            return
        levels = keys // (2 * pieces * residues)
        for flip in range(2):
            user = me_ref[0] ^ flip
            starts = [
                ((user % (2 * pieces) ^ (c + 2 * q)) + 2 * pieces * k) * residues + p
                for q in range(pieces)
                for p in range(2)
                for k in range(levels)
                for c in range(2)
            ]
            for n in range(tiles):
                for at in range(0, keys, 128):
                    rows = [
                        acc_ref[n, pl.ds(start, pairs, stride=2), :]
                        for start in starts[at // pairs : (at + 128) // pairs]
                    ]
                    turned = jnp.concatenate(rows, axis=0).T.astype(BF16)
                    outs[flip][n * 128 : (n + 1) * 128, at : at + 128] = turned


def order_kernel(residues, pieces, me_ref, bias_ref, own_ref, send_ref):
    rows, keys = bias_ref.shape
    pairs = residues // 2
    lane = iota((1, keys), 1)
    each = keys // pieces
    which, rest = lane // each, lane % each
    parity, rest = rest // (each // 2), rest % (each // 2)
    place, pair = rest // pairs, rest % pairs
    for flip, out_ref in enumerate((own_ref, send_ref)):
        device = (me_ref[0] % (2 * pieces)) ^ flip ^ ((place % 2) + 2 * which)
        device = device + 2 * pieces * (place // 2)
        target = device * residues + 2 * pair + parity
        total = jnp.zeros((rows, keys), F32)
        for start in range(0, keys, 256):
            chosen = one_hot(iota((256, keys), 0) + start == target)
            total = total + mm(bias_ref[:, start : start + 256], chosen)
        out_ref[...] = total.astype(BF16)


def query_kernel(
    groups, size, pairs, heads, own_ref, peer_ref, keep_ref, received_ref, w_ref, *refs
):
    column_refs, (bias_ref, lhs_ref, sums_ref) = refs[:groups], refs[groups:]
    rows = own_ref.shape[0]
    bias_ref[:rows, :] = own_ref[...].astype(F32) * LOG2E
    bias_ref[rows:, :] = peer_ref[...].astype(F32) * LOG2E

    hidden = w_ref.shape[0]
    depth = hidden // heads
    twice_rows = one_hot(iota((128, 1), 0) % hidden == iota((1, hidden), 1))
    wq = mm(
        mm(twice_rows, w_ref[...]).astype(BF16),
        one_hot(iota((4 * hidden, 1), 0) == iota((1, 128), 1) % hidden),
    )
    same_residue = iota((128, 1), 0) // hidden == iota((1, 128), 1) // hidden
    wq = jnp.where(same_residue, wq, 0.0).astype(BF16)
    picked = one_hot(iota((1, 4 * hidden), 1) == hidden + iota((128, 1), 0) % hidden)
    wk = mm_nt(picked, w_ref[...]).astype(BF16)
    wk = mm(wk, one_hot(iota((hidden, 1), 0) == iota((1, 128), 1))).astype(BF16)
    lead = size * pairs
    lane = iota((1, 128), 1)
    spare = lane - hidden
    for g in range(groups):
        for n, ref in enumerate((keep_ref, received_ref)):
            query = (mm(ref[g, :lead], wq) * (depth**-0.5)).astype(BF16).astype(F32)
            for s in range(size):
                q = query[s * pairs : (s + 1) * pairs]
                spread = [
                    jnp.where(lane // depth == p * heads + h, q, 0.0).astype(BF16)
                    for h in range(heads)
                    for p in range(2)
                ]
                folded = mm(jnp.concatenate(spread, axis=0), wk) * LOG2E
                picks = (spare >= 0) & (spare < 4 * size) & (spare % size == s)
                lhs_ref[g * size + s, n * rows : (n + 1) * rows, :] = jnp.where(
                    picks, 1.0, folded
                ).astype(BF16)
    add_pieces(groups, size, pairs, (0,) * groups, lhs_ref, bias_ref, None, column_refs, sums_ref)


def masks_of(ref, size, pairs):
    start = 2 * size * pairs
    lane = iota((1, 128), 1) - 64
    masks = []
    for p in range(2):
        blocks = []
        for k in range(ref.shape[0]):
            hidden = (1e9 * LOG2E) * (ref[k, start : start + pairs, :].astype(F32) - 1.0)
            for c in range(2):
                first = (2 * c + p) * size
                mine = (lane >= first) & (lane < first + size)
                blocks.append(jnp.where(mine, hidden, 0.0).astype(BF16))
        masks.append(jnp.concatenate(blocks, axis=0))
    return masks


def keys_of(ref, masks, s, size, pairs):
    start = pl.multiple_of(s * pairs, pairs)
    even = jnp.concatenate(
        [
            ref[k, pl.ds(c * size * pairs + start, pairs), :]
            for k in range(ref.shape[0])
            for c in range(2)
        ],
        axis=0,
    )
    odd = pltpu.roll(even.astype(F32), 64, 1).astype(BF16)
    low = iota(even.shape, 1) < 64
    one = jnp.ones_like(even)
    keyed = [jnp.where(low, x, m) for x, m in zip((even, odd), masks)]
    valued = [jnp.where(low, x, one) for x in (even, odd)]
    return jnp.concatenate(keyed, axis=0), jnp.concatenate(valued, axis=0)


def partial_sums(lhs, bias_ref, piece, keyed, valued):
    width = keyed.shape[0]
    logits = mm_nt(lhs, keyed) + bias_ref[:, piece * width : (piece + 1) * width]
    return mm(jnp.exp2(logits).astype(BF16), valued)


def add_pieces(groups, size, pairs, places, lhs_ref, bias_ref, before_ref, piece_refs, out_ref):
    masks = [masks_of(ref, size, pairs) for ref in piece_refs]

    def one_line(s, carry):
        for g in range(groups):
            line = g * size + s
            keyed, valued = keys_of(piece_refs[g], masks[g], s, size, pairs)
            total = partial_sums(lhs_ref[line], bias_ref, places[g], keyed, valued)
            out_ref[line] = total if before_ref is None else before_ref[line] + total
        return carry

    lax.fori_loop(0, size, one_line, 0, unroll=2)


def add_kernel(groups, size, pairs, places, lhs_ref, bias_ref, before_ref, *refs):
    add_pieces(
        groups, size, pairs, places, lhs_ref, bias_ref, before_ref, refs[:-1], refs[-1]
    )


def finish_kernel(
    heads, groups, size, pairs, place, lhs_ref, bias_ref, sums_ref, w_ref, keep_ref, received_ref,
    *refs,
):
    piece_refs, far_refs = refs[:groups], refs[groups : 4 * groups]
    mine_ref, theirs_ref, turned_ref, range_ref, copy_ref = refs[4 * groups :]
    hidden = w_ref.shape[0]
    depth = hidden // heads
    lead = size * pairs
    blocks = 2 * heads
    row, col = iota((128, 1), 0), iota((1, 256), 1)
    picked = one_hot(iota((4 * hidden, 1), 0) == 2 * hidden + col % hidden)
    picked = jnp.where(col < 128, picked, jnp.zeros_like(picked))
    wv = mm(mm(one_hot(row == iota((1, hidden), 1)), w_ref[...]).astype(BF16), picked)
    counted = (row >= hidden) & (col >= 128)
    wv = jnp.where(counted, 1.0 / (128 - hidden), wv)
    owner = col % 128 // depth
    wv = jnp.concatenate(
        [
            jnp.where(owner == p * heads + h, wv, 0.0).astype(BF16)
            for h in range(heads)
            for p in range(2)
        ],
        axis=0,
    )
    lane = iota((1, 128), 1)
    wg = mm(
        mm(one_hot(row % hidden == iota((1, hidden), 1)), w_ref[...]).astype(BF16),
        one_hot(iota((4 * hidden, 1), 0) == 3 * hidden + lane % hidden),
    )
    wg = jnp.where(row // hidden == lane // hidden, wg, 0.0).astype(BF16)
    masks = [masks_of(ref, size, pairs) for ref in piece_refs]
    low = iota((lhs_ref.shape[1], 128), 1) < 64

    def settle(line, total):
        start = pl.multiple_of(line * pairs, pairs)
        total = total.astype(BF16)
        for n in range(2):
            for b in range(blocks):
                part = total[(n * blocks + b) * pairs : (n * blocks + b + 1) * pairs]
                turned_ref[n, pl.ds(start, pairs), b * 128 : (b + 1) * 128] = part

    range_ref[...] = jnp.ones(range_ref.shape, F32)

    def one_line(s, carry):
        for g in range(groups):
            line = g * size + s
            keyed, valued = keys_of(piece_refs[g], masks[g], s, size, pairs)
            total = sums_ref[line] + partial_sums(lhs_ref[line], bias_ref, place, keyed, valued)
            settle(line, total)
            weight = jnp.where(low, 1.0, total).reshape(-1, 8, 128)
            range_ref[0] = jnp.minimum(range_ref[0], jnp.min(weight, axis=0))
            range_ref[1] = jnp.maximum(range_ref[1], jnp.max(weight, axis=0))
        return carry

    lax.fori_loop(0, size, one_line, 0, unroll=2)
    fine = (range_ref[0] > 2.0**-80) & (range_ref[1] < 2.0**100)

    @pl.when(jnp.min(jnp.where(fine, 1.0, 0.0)) < 0.5)
    def _():
        for n, ref in enumerate(far_refs):
            pltpu.sync_copy(ref, copy_ref.at[n])
        for g in range(groups):
            ordered = [copy_ref.at[n * groups + g] for n in range(3)] + [piece_refs[g]]
            all_masks = [masks_of(ref, size, pairs) for ref in ordered]

            def exact_line(s, carry):
                line = g * size + s
                both = [keys_of(r, m, s, size, pairs) for r, m in zip(ordered, all_masks)]
                logits = []
                for n, (keyed, _) in enumerate(both):
                    width = keyed.shape[0]
                    bias = bias_ref[:, n * width : (n + 1) * width]
                    logits.append(mm_nt(lhs_ref[line], keyed) + bias)
                peak = functools.reduce(jnp.maximum, logits)
                peak = jnp.max(peak, axis=-1, keepdims=True)
                parts = [
                    mm(jnp.exp2(part - peak).astype(BF16), valued)
                    for part, (_, valued) in zip(logits, both)
                ]
                settle(line, sum(parts[1:], parts[0]))
                return carry

            lax.fori_loop(0, size, exact_line, 0)

    mixed = mm(turned_ref[...].reshape(2 * groups * lead, blocks * 128), wv)
    mixed = (mixed[:, :128] / mixed[:, 128:]).reshape(2, groups * lead, 128)
    for n, (ref, out_ref) in enumerate(((keep_ref, mine_ref), (received_ref, theirs_ref))):
        for g in range(groups):
            gate = jax.nn.sigmoid(mm(ref[g, :lead], wg))
            at = slice(g * lead, (g + 1) * lead)
            out_ref[at, :] = (gate * mixed[n, at]).astype(BF16)


def final_kernel(
    lines, heads, with_column, me_ref, line_ref, kept_ref, wo_ref, wc_ref, wout_ref,
    mine_ref, theirs_ref, out_ref, gated_ref,
):
    total = line_ref.shape[0]
    pairs = total // lines
    core = me_ref[0] % 2
    share = total // 2
    for owner, ref in ((core, mine_ref), (1 - core, theirs_ref)):
        gated_ref[pl.ds(pl.multiple_of(owner * share, share), share), :] = ref[...]
    hidden = wo_ref.shape[0]
    depth = hidden // heads
    rows_twice = one_hot(iota((128, 1), 0) % hidden == iota((1, hidden), 1))
    same_residue = iota((128, 1), 0) // hidden == iota((1, 128), 1) // hidden

    def twice(matrix, picked):
        wide = mm(mm(rows_twice, matrix).astype(BF16), picked)
        return jnp.where(same_residue, wide, 0.0).astype(BF16)

    def columns(width, chosen):
        return one_hot(iota((width, 1), 0) == chosen)

    lane = iota((1, 128), 1)
    wo = twice(wo_ref[...], columns(hidden, lane % hidden))
    row = (line_ref[...].astype(F32) + mm(gated_ref[...], wo)).astype(BF16)
    if not with_column:
        out_ref[...] = row
        return
    spread = mm(one_hot(iota((total, lines), 0) // pairs == iota((total, lines), 1)), kept_ref[...])
    own = iota((total, 2 * pairs), 1) // 2 == iota((total, 2 * pairs), 0) % pairs
    sides = one_hot(iota((2 * pairs, 128), 0) % 2 == iota((2 * pairs, 128), 1) // 64)
    kept = mm(jnp.where(own, spread, 0.0).astype(BF16), sides)

    choices = [
        lane % hidden,
        hidden + lane % hidden,
        2 * hidden + lane % depth,
        2 * hidden + depth + lane % depth,
    ]
    wc = [twice(wc_ref[...], columns(wc_ref.shape[1], chosen)) for chosen in choices]
    projected = mm(paired_norm(row, 64), jnp.concatenate(wc, axis=1))
    query, gate, key, value = [projected[:, 128 * n : 128 * (n + 1)] for n in range(4)]

    def grid(a):
        return a.reshape(lines, pairs, 128)

    count = jnp.maximum(jnp.sum(grid(kept), axis=0), 1.0)
    mean_query = jnp.sum(grid(kept * query), axis=0) / count * (depth**-0.5)
    same_head = block_matrix(128, depth, 1.0, 1.0)
    product = (mean_query[None] * grid(key)).reshape(total, 128)
    logits = grid(mm_split(product, same_head) + 1e9 * (kept - 1.0))
    exped = jnp.exp(logits - jnp.max(logits, axis=0, keepdims=True))
    mixed = jnp.sum(exped * grid(value), axis=0) / jnp.sum(exped, axis=0)
    gated = (jax.nn.sigmoid(grid(gate)) * mixed[None]).reshape(total, 128).astype(BF16)
    wout = twice(wout_ref[...], columns(hidden, lane % hidden))
    result = (row.astype(F32) + mm(gated, wout)).astype(BF16)
    shuffled = row_shuffle(result, lines, pairs)
    for t in range(pairs):
        out_ref[:, t * 128 : (t + 1) * 128] = shuffled[t * lines : (t + 1) * lines, :]


def call(kernel, out_shape, *args, **options):
    flops = options.pop("flops", 0)
    limit = pltpu.CompilerParams(vmem_limit_bytes=options.pop("mib", 8) * 1024 * 1024)
    moved = sum(a.size * a.dtype.itemsize for a in args)
    cost = pl.CostEstimate(flops=flops, bytes_accessed=moved, transcendentals=0)
    return pl.pallas_call(
        kernel, out_shape=out_shape, compiler_params=limit, cost_estimate=cost, **options
    )(*args)


def shape(*dims, dtype=BF16):
    return jax.ShapeDtypeStruct(dims, dtype)


def exchange(x, flip, devices):
    return lax.ppermute(x, "res", [(d, d ^ flip) for d in range(devices)])


def layer_normalize(values_in):
    centre = values_in - jnp.mean(values_in, axis=-1, keepdims=True)
    spread = jnp.mean(centre * centre, axis=-1, keepdims=True)
    return centre * lax.rsqrt(spread + EPS)


def column_complete(line, kept, vertical_matrix, vertical_exit_matrix, heads, depth):
    lines, columns, features = line.shape
    hidden = heads * depth
    normed = layer_normalize(line.astype(F32)).astype(BF16)
    projected = mm(normed.reshape(-1, features), vertical_matrix).reshape(lines, columns, -1)
    query, gate = projected[..., :hidden], projected[..., hidden : 2 * hidden]
    key = projected[..., 2 * hidden : 2 * hidden + depth]
    value = projected[..., 2 * hidden + depth :]
    count = jnp.maximum(jnp.sum(kept, axis=0), 1.0)[:, None]
    mean_query = jnp.sum(kept[..., None] * query, axis=0) / count * depth**-0.5
    logits = jnp.einsum("ihc,sic->sih", mean_query.reshape(columns, heads, depth), key)
    logits = logits + 1e9 * (kept - 1.0)[..., None]
    exped = jnp.exp(logits - jnp.max(logits, axis=0, keepdims=True))
    mixed = jnp.einsum("sih,sic->ihc", exped, value) / jnp.sum(exped, axis=0)[..., None]
    gate = jax.nn.sigmoid(gate).reshape(lines, columns, heads, depth)
    gated = (gate * mixed[None]).reshape(-1, hidden).astype(BF16)
    update = mm(gated, vertical_exit_matrix).reshape(lines, columns, features)
    return (line.astype(F32) + update).astype(BF16)


def on_device(
    seq_size,
    res_size,
    extra_activations,
    pair,
    present,
    amino,
    offset_matrix,
    horizontal_matrix,
    horizontal_exit_matrix,
    vertical_matrix,
    vertical_exit_matrix,
):
    lines, residues = present.shape
    pairs = residues // 2
    hidden = horizontal_exit_matrix.shape[0]
    heads = offset_matrix.shape[1]
    depth = hidden // heads
    groups = 2
    size = lines // (2 * groups)
    lead = size * pairs
    keys = res_size * residues
    rows = residues * heads
    core_bit, near, far, high = 1, 2, 4, 8
    kept = (present * amino[None, :]).astype(BF16)
    me = lax.axis_index("res").astype(jnp.int32).reshape(1)
    smem = pl.BlockSpec(memory_space=pltpu.SMEM)
    vmem = pl.BlockSpec(memory_space=pltpu.VMEM)

    rest = lead + pairs
    keep, send, line = call(
        functools.partial(prep_kernel, groups),
        [shape(groups, rest, 128)] * 2 + [shape(lines * pairs, 128)],
        me,
        extra_activations,
        kept,
        in_specs=[smem, vmem, vmem],
        scratch_shapes=[
            pltpu.VMEM((lines * pairs, 128), BF16),
            pltpu.VMEM((2 * groups, pairs, 128), BF16),
        ],
    )

    received = exchange(send, core_bit, res_size)
    chunk = jnp.concatenate(
        [keep[:, :lead], received[:, :lead], keep[:, lead:] + received[:, lead:]], axis=1
    )
    heights = [[d + high * k for k in range(res_size // high)] for d in range(high)]
    levels = lax.all_gather(chunk, "res", axis_index_groups=heights)
    own = [levels[:, g] for g in range(groups)]
    beside = [exchange(part, near, res_size) for part in own]
    across = [exchange(part, far, res_size) for part in own]

    per_step = 8
    pieces = 4
    whole = seq_size == 1
    bias_rows = [shape(rows, keys)] * 2
    bias = call(
        functools.partial(bias_kernel, whole, pieces),
        bias_rows if whole else [shape(rows, pair.shape[1])],
        pair,
        offset_matrix.T,
        chunk,
        me,
        grid=(residues // per_step,),
        in_specs=[
            pl.BlockSpec((per_step,) + pair.shape[1:], lambda n: (n, 0, 0)),
            pl.BlockSpec(offset_matrix.shape[::-1], lambda n: (0, 0)),
            pl.BlockSpec(memory_space=pl.ANY),
            smem,
        ],
        out_specs=[pl.BlockSpec((rows, pair.shape[1]), lambda n: (0, 0))] * (1 + whole),
        scratch_shapes=[
            pltpu.VMEM((rows // 128, pair.shape[1], 128), F32),
            pltpu.VMEM((2 * pair.shape[2], 2 * pair.shape[2]), BF16),
            pltpu.VMEM((2 * pair.shape[2], 2 * pair.shape[2]), BF16),
            pltpu.VMEM((pair.shape[2], rows), F32),
        ],
        flops=16 * pair.size * 128,
        mib=57,
    )
    if not whole:
        bias = call(
            functools.partial(order_kernel, residues, pieces),
            bias_rows,
            me,
            lax.all_gather(bias[0], "seq", axis=1, tiled=True),
            in_specs=[smem, vmem],
            mib=14,
        )
    bias, lhs, sums = call(
        functools.partial(query_kernel, groups, size, pairs, heads),
        [
            shape(2 * rows, keys, dtype=F32),
            shape(groups * size, 2 * rows, 128),
            shape(groups * size, 2 * rows, 128, dtype=F32),
        ],
        bias[0],
        exchange(bias[1], core_bit, res_size),
        keep,
        received,
        horizontal_matrix,
        *own,
        in_specs=[vmem] * (5 + groups),
        flops=8 * rows * keys * keys,
        mib=18,
    )

    def add(sums, places, parts):
        return call(
            functools.partial(add_kernel, groups, size, pairs, places),
            shape(*sums.shape, dtype=F32),
            lhs,
            bias,
            sums,
            *parts,
            flops=groups * size * rows * keys * 2 * 256 * 2,
            mib=20,
        )

    beside[0], across[1], sums = lax.optimization_barrier((beside[0], across[1], sums))
    corner = [
        exchange(beside[g], far, res_size) if g % 2 == 0 else exchange(across[g], near, res_size)
        for g in range(groups)
    ]
    sums = add(sums, (1, 2), (beside[0], across[1]))
    beside[1], across[0], sums = lax.optimization_barrier((beside[1], across[0], sums))
    sums = add(sums, (2, 1), (across[0], beside[1]))
    corner[0], corner[1], sums = lax.optimization_barrier((corner[0], corner[1], sums))
    anywhere = pl.BlockSpec(memory_space=pl.ANY)
    mine, theirs = call(
        functools.partial(finish_kernel, heads, groups, size, pairs, 3),
        [shape(groups * lead, 128)] * 2,
        lhs,
        bias,
        sums,
        horizontal_matrix,
        keep,
        received,
        *corner,
        *own,
        *beside,
        *across,
        in_specs=[vmem] * (6 + groups) + [anywhere] * (3 * groups),
        scratch_shapes=[
            pltpu.VMEM((2, groups * lead, 128 * 2 * heads), BF16),
            pltpu.VMEM((2, 8, 128), F32),
            pltpu.VMEM((3 * groups,) + own[0].shape, BF16),
        ],
        flops=groups * size * rows * keys * 2 * 256,
        mib=24,
    )
    returned = exchange(theirs, core_bit, res_size)

    with_column = seq_size == 1
    final_args = [
        me,
        line,
        kept,
        horizontal_exit_matrix,
        vertical_matrix,
        vertical_exit_matrix,
    ]
    final_args += [mine, returned]
    result = call(
        functools.partial(final_kernel, lines, heads, with_column),
        shape(*extra_activations.shape) if with_column else shape(lines * pairs, 128),
        *final_args,
        in_specs=[smem] + [vmem] * (len(final_args) - 1),
        scratch_shapes=[pltpu.VMEM((lines * pairs, 128), BF16)],
    )
    if with_column:
        return result
    row = result.reshape(lines, residues, hidden)
    moved = lax.all_to_all(row, "seq", split_axis=1, concat_axis=0, tiled=True)
    moved_kept = lax.all_to_all(kept, "seq", split_axis=1, concat_axis=0, tiled=True)
    updated = column_complete(
        moved, moved_kept.astype(F32), vertical_matrix, vertical_exit_matrix, heads, depth
    )
    back = lax.all_to_all(updated, "seq", split_axis=0, concat_axis=1, tiled=True)
    return back.reshape(extra_activations.shape)


def solution(mesh):
    in_specs = (
        P("seq", "res"),
        P("res", "seq", None),
        P("seq", "res"),
        P("res"),
        P(),
        P(),
        P(),
        P(),
        P(),
    )
    sizes = mesh.shape
    return jax.shard_map(
        functools.partial(on_device, sizes["seq"], sizes["res"]),
        mesh=mesh,
        in_specs=in_specs,
        out_specs=P("seq", "res"),
        check_vma=False,
    )
```

```python
import functools
import math

import jax
import jax.numpy as jnp
from jax import lax
from jax.experimental import pallas as pl
from jax.experimental.pallas import tpu as pltpu
from jax.sharding import PartitionSpec as P

F32 = jnp.float32
BF16 = jnp.bfloat16
LOG2E = math.log2(math.e)
EPS = 1e-05

NT = (((1,), (1,)), ((), ()))


def mm(a, b):
    return jnp.dot(a, b, preferred_element_type=F32)


def mm_nt(a, b):
    return lax.dot_general(a, b, NT, preferred_element_type=F32)


def iota(shape, axis):
    return lax.broadcasted_iota(jnp.int32, shape, axis)


def one_hot(condition):
    return jnp.where(condition, 1.0, 0.0).astype(BF16)


def block_matrix(size, block, on_diagonal, elsewhere):
    row, col = iota((size, 1), 0), iota((1, size), 1)
    inside = jnp.where(row == col, on_diagonal, elsewhere)
    return jnp.where(row // block == col // block, inside, 0.0).astype(BF16)


def halves(value):
    high = value.astype(BF16)
    return high, (value - high.astype(F32)).astype(BF16)


def mm_split(value, matrix):
    high, low = halves(value)
    return mm(high, matrix) + mm(low, matrix)


def paired_norm(x, width):
    lanes = x.shape[1]
    centre = mm(x, block_matrix(lanes, width, 1.0 - 1.0 / width, -1.0 / width))
    spread = mm_split(centre * centre, block_matrix(lanes, width, 1.0 / width, 1.0 / width))
    return (centre * lax.rsqrt(spread + EPS)).astype(BF16)


def row_shuffle(rows, inner, outer):
    total = rows.shape[0]
    row, col = iota((total, 1), 0), iota((1, total), 1)
    return mm(one_hot(col == (row % inner) * outer + row // inner), rows).astype(BF16)


def prep_kernel(groups, me_ref, m_ref, kept_ref, *refs):
    keep_ref, send_ref, line_ref, normed_ref, spread_ref = refs
    lines, width = m_ref.shape
    pairs = width // 128
    stacked = jnp.concatenate([m_ref[:, t * 128 : (t + 1) * 128] for t in range(pairs)], axis=0)
    normed = paired_norm(stacked, 64)
    both = row_shuffle(jnp.concatenate([normed, stacked], axis=1), pairs, lines)
    normed_ref[...] = both[:, :128]
    line_ref[...] = both[:, 128:]
    kept = kept_ref[...]
    size = lines // (2 * groups)
    residues = 2 * pairs
    row, col = iota((pairs, residues), 0), iota((pairs, residues), 1)
    evens, odds = one_hot(col == 2 * row), one_hot(col == 2 * row + 1)
    row, col = iota((128, lines), 0) - 64, iota((128, lines), 1)
    core = me_ref[0] % 2
    for n in range(2 * groups):
        start = jnp.where(n // groups == core, 0, 2 * size)
        chosen = (row >= start) & (row < start + 2 * size) & (row % size == col - n * size)
        spread = mm(one_hot(chosen), kept).astype(BF16)
        first = iota((pairs, 128), 1) < 64 + size + start
        spread_ref[n] = jnp.where(first, mm_nt(evens, spread), mm_nt(odds, spread)).astype(BF16)
    rows = size * pairs
    for ref, half in ((keep_ref, core), (send_ref, 1 - core)):
        for g in range(groups):
            index = half * groups + g
            ref[g, :rows] = normed_ref[pl.ds(pl.multiple_of(index * rows, rows), rows), :]
            ref[g, rows:] = spread_ref[index]


def bias_kernel(whole, pieces, x_ref, w_ref, after_ref, me_ref, *refs):
    outs, (acc_ref, centring_ref, wide_ref) = refs[:-3], refs[-3:]
    step = pl.program_id(0)
    heads = w_ref.shape[0]
    per_step, keys, channels = x_ref.shape
    residues = per_step * pl.num_programs(0)
    pairs = residues // 2
    tiles = acc_ref.shape[0]
    width = tiles * 128

    @pl.when(step == 0)
    def _():
        centring_ref[...] = block_matrix(
            2 * channels, channels, 1.0 - 1.0 / channels, -1.0 / channels
        )
        spread = one_hot(iota((heads, 1), 0) == iota((1, width), 1) // residues)
        wide_ref[...] = lax.dot_general(
            w_ref[...], spread, (((0,), (0,)), ((), ())), preferred_element_type=F32
        )
        acc_ref[...] = jnp.zeros(acc_ref.shape, F32)

    lane = iota((1, width), 1) % residues
    placed = []
    for n in range(per_step):
        residue = step * per_step + n
        mine = lane == (residue % 2) * pairs + residue // 2
        placed.append(jnp.where(mine, wide_ref[...], 0.0).astype(BF16))
    placed = jnp.concatenate(placed, axis=0)
    centring = centring_ref[...]
    piece = min(512, keys)
    for r in range(0, keys, piece):
        normed = []
        for n in range(0, per_step, 2):
            x = jnp.concatenate([x_ref[n, r : r + piece], x_ref[n + 1, r : r + piece]], axis=1)
            centre = mm(x, centring)
            for part in (centre[:, :channels], centre[:, channels:]):
                spread = jnp.mean(part * part, axis=-1, keepdims=True)
                normed.append((part * lax.rsqrt(spread + EPS)).astype(BF16))
        added = mm(jnp.concatenate(normed, axis=1), placed)
        for n in range(tiles):
            acc_ref[n, r : r + piece, :] += added[:, n * 128 : (n + 1) * 128]

    @pl.when(step == pl.num_programs(0) - 1)
    def _():
        if not whole:
            for n in range(tiles):
                outs[0][n * 128 : (n + 1) * 128, :] = acc_ref[n].T.astype(BF16)
            return
        levels = keys // (2 * pieces * residues)
        for flip in range(2):
            user = me_ref[0] ^ flip
            starts = [
                ((user % (2 * pieces) ^ (c + 2 * q)) + 2 * pieces * k) * residues + p
                for q in range(pieces)
                for p in range(2)
                for k in range(levels)
                for c in range(2)
            ]
            for n in range(tiles):
                for at in range(0, keys, 128):
                    rows = [
                        acc_ref[n, pl.ds(start, pairs, stride=2), :]
                        for start in starts[at // pairs : (at + 128) // pairs]
                    ]
                    turned = jnp.concatenate(rows, axis=0).T.astype(BF16)
                    outs[flip][n * 128 : (n + 1) * 128, at : at + 128] = turned


def order_kernel(residues, pieces, me_ref, bias_ref, own_ref, send_ref):
    rows, keys = bias_ref.shape
    pairs = residues // 2
    lane = iota((1, keys), 1)
    each = keys // pieces
    which, rest = lane // each, lane % each
    parity, rest = rest // (each // 2), rest % (each // 2)
    place, pair = rest // pairs, rest % pairs
    for flip, out_ref in enumerate((own_ref, send_ref)):
        device = (me_ref[0] % (2 * pieces)) ^ flip ^ ((place % 2) + 2 * which)
        device = device + 2 * pieces * (place // 2)
        target = device * residues + 2 * pair + parity
        total = jnp.zeros((rows, keys), F32)
        for start in range(0, keys, 256):
            chosen = one_hot(iota((256, keys), 0) + start == target)
            total = total + mm(bias_ref[:, start : start + 256], chosen)
        out_ref[...] = total.astype(BF16)


def query_kernel(
    groups, size, pairs, heads, own_ref, peer_ref, keep_ref, received_ref, w_ref, *refs
):
    column_refs, (bias_ref, lhs_ref, sums_ref) = refs[:groups], refs[groups:]
    rows = own_ref.shape[0]
    bias_ref[:rows, :] = own_ref[...].astype(F32) * LOG2E
    bias_ref[rows:, :] = peer_ref[...].astype(F32) * LOG2E

    hidden = w_ref.shape[0]
    depth = hidden // heads
    twice_rows = one_hot(iota((128, 1), 0) % hidden == iota((1, hidden), 1))
    wq = mm(
        mm(twice_rows, w_ref[...]).astype(BF16),
        one_hot(iota((4 * hidden, 1), 0) == iota((1, 128), 1) % hidden),
    )
    same_residue = iota((128, 1), 0) // hidden == iota((1, 128), 1) // hidden
    wq = jnp.where(same_residue, wq, 0.0).astype(BF16)
    picked = one_hot(iota((1, 4 * hidden), 1) == hidden + iota((128, 1), 0) % hidden)
    wk = mm_nt(picked, w_ref[...]).astype(BF16)
    wk = mm(wk, one_hot(iota((hidden, 1), 0) == iota((1, 128), 1))).astype(BF16)
    lead = size * pairs
    lane = iota((1, 128), 1)
    spare = lane - hidden
    for g in range(groups):
        for n, ref in enumerate((keep_ref, received_ref)):
            query = (mm(ref[g, :lead], wq) * (depth**-0.5)).astype(BF16).astype(F32)
            for s in range(size):
                q = query[s * pairs : (s + 1) * pairs]
                spread = [
                    jnp.where(lane // depth == p * heads + h, q, 0.0).astype(BF16)
                    for h in range(heads)
                    for p in range(2)
                ]
                folded = mm(jnp.concatenate(spread, axis=0), wk) * LOG2E
                picks = (spare >= 0) & (spare < 4 * size) & (spare % size == s)
                lhs_ref[g * size + s, n * rows : (n + 1) * rows, :] = jnp.where(
                    picks, 1.0, folded
                ).astype(BF16)
    add_pieces(groups, size, pairs, (0,) * groups, lhs_ref, bias_ref, None, column_refs, sums_ref)


def masks_of(ref, size, pairs):
    start = 2 * size * pairs
    lane = iota((1, 128), 1) - 64
    masks = []
    for p in range(2):
        blocks = []
        for k in range(ref.shape[0]):
            hidden = (1e9 * LOG2E) * (ref[k, start : start + pairs, :].astype(F32) - 1.0)
            for c in range(2):
                first = (2 * c + p) * size
                mine = (lane >= first) & (lane < first + size)
                blocks.append(jnp.where(mine, hidden, 0.0).astype(BF16))
        masks.append(jnp.concatenate(blocks, axis=0))
    return masks


def keys_of(ref, masks, s, size, pairs):
    start = pl.multiple_of(s * pairs, pairs)
    even = jnp.concatenate(
        [
            ref[k, pl.ds(c * size * pairs + start, pairs), :]
            for k in range(ref.shape[0])
            for c in range(2)
        ],
        axis=0,
    )
    odd = pltpu.roll(even.astype(F32), 64, 1).astype(BF16)
    low = iota(even.shape, 1) < 64
    one = jnp.ones_like(even)
    keyed = [jnp.where(low, x, m) for x, m in zip((even, odd), masks)]
    valued = [jnp.where(low, x, one) for x in (even, odd)]
    return jnp.concatenate(keyed, axis=0), jnp.concatenate(valued, axis=0)


def partial_sums(lhs, bias_ref, piece, keyed, valued):
    width = keyed.shape[0]
    logits = mm_nt(lhs, keyed) + bias_ref[:, piece * width : (piece + 1) * width]
    return mm(jnp.exp2(logits).astype(BF16), valued)


def add_pieces(groups, size, pairs, places, lhs_ref, bias_ref, before_ref, piece_refs, out_ref):
    masks = [masks_of(ref, size, pairs) for ref in piece_refs]

    def one_line(s, carry):
        for g in range(groups):
            line = g * size + s
            keyed, valued = keys_of(piece_refs[g], masks[g], s, size, pairs)
            total = partial_sums(lhs_ref[line], bias_ref, places[g], keyed, valued)
            out_ref[line] = total if before_ref is None else before_ref[line] + total
        return carry

    lax.fori_loop(0, size, one_line, 0, unroll=2)


def add_kernel(groups, size, pairs, places, lhs_ref, bias_ref, before_ref, *refs):
    add_pieces(
        groups, size, pairs, places, lhs_ref, bias_ref, before_ref, refs[:-1], refs[-1]
    )


def finish_kernel(
    heads, groups, size, pairs, place, lhs_ref, bias_ref, sums_ref, w_ref, keep_ref, received_ref,
    *refs,
):
    piece_refs, far_refs = refs[:groups], refs[groups : 4 * groups]
    mine_ref, theirs_ref, turned_ref, range_ref, copy_ref = refs[4 * groups :]
    hidden = w_ref.shape[0]
    depth = hidden // heads
    lead = size * pairs
    blocks = 2 * heads
    row, col = iota((128, 1), 0), iota((1, 256), 1)
    picked = one_hot(iota((4 * hidden, 1), 0) == 2 * hidden + col % hidden)
    picked = jnp.where(col < 128, picked, jnp.zeros_like(picked))
    wv = mm(mm(one_hot(row == iota((1, hidden), 1)), w_ref[...]).astype(BF16), picked)
    counted = (row >= hidden) & (col >= 128)
    wv = jnp.where(counted, 1.0 / (128 - hidden), wv)
    owner = col % 128 // depth
    wv = jnp.concatenate(
        [
            jnp.where(owner == p * heads + h, wv, 0.0).astype(BF16)
            for h in range(heads)
            for p in range(2)
        ],
        axis=0,
    )
    lane = iota((1, 128), 1)
    wg = mm(
        mm(one_hot(row % hidden == iota((1, hidden), 1)), w_ref[...]).astype(BF16),
        one_hot(iota((4 * hidden, 1), 0) == 3 * hidden + lane % hidden),
    )
    wg = jnp.where(row // hidden == lane // hidden, wg, 0.0).astype(BF16)
    masks = [masks_of(ref, size, pairs) for ref in piece_refs]
    low = iota((lhs_ref.shape[1], 128), 1) < 64

    def settle(line, total):
        start = pl.multiple_of(line * pairs, pairs)
        total = total.astype(BF16)
        for n in range(2):
            for b in range(blocks):
                part = total[(n * blocks + b) * pairs : (n * blocks + b + 1) * pairs]
                turned_ref[n, pl.ds(start, pairs), b * 128 : (b + 1) * 128] = part

    range_ref[...] = jnp.ones(range_ref.shape, F32)

    def one_line(s, carry):
        for g in range(groups):
            line = g * size + s
            keyed, valued = keys_of(piece_refs[g], masks[g], s, size, pairs)
            total = sums_ref[line] + partial_sums(lhs_ref[line], bias_ref, place, keyed, valued)
            settle(line, total)
            weight = jnp.where(low, 1.0, total).reshape(-1, 8, 128)
            range_ref[0] = jnp.minimum(range_ref[0], jnp.min(weight, axis=0))
            range_ref[1] = jnp.maximum(range_ref[1], jnp.max(weight, axis=0))
        return carry

    lax.fori_loop(0, size, one_line, 0, unroll=2)
    fine = (range_ref[0] > 2.0**-80) & (range_ref[1] < 2.0**100)

    @pl.when(jnp.min(jnp.where(fine, 1.0, 0.0)) < 0.5)
    def _():
        for n, ref in enumerate(far_refs):
            pltpu.sync_copy(ref, copy_ref.at[n])
        for g in range(groups):
            ordered = [copy_ref.at[n * groups + g] for n in range(3)] + [piece_refs[g]]
            all_masks = [masks_of(ref, size, pairs) for ref in ordered]

            def exact_line(s, carry):
                line = g * size + s
                both = [keys_of(r, m, s, size, pairs) for r, m in zip(ordered, all_masks)]
                logits = []
                for n, (keyed, _) in enumerate(both):
                    width = keyed.shape[0]
                    bias = bias_ref[:, n * width : (n + 1) * width]
                    logits.append(mm_nt(lhs_ref[line], keyed) + bias)
                peak = functools.reduce(jnp.maximum, logits)
                peak = jnp.max(peak, axis=-1, keepdims=True)
                parts = [
                    mm(jnp.exp2(part - peak).astype(BF16), valued)
                    for part, (_, valued) in zip(logits, both)
                ]
                settle(line, sum(parts[1:], parts[0]))
                return carry

            lax.fori_loop(0, size, exact_line, 0)

    mixed = mm(turned_ref[...].reshape(2 * groups * lead, blocks * 128), wv)
    mixed = (mixed[:, :128] / mixed[:, 128:]).reshape(2, groups * lead, 128)
    for n, (ref, out_ref) in enumerate(((keep_ref, mine_ref), (received_ref, theirs_ref))):
        for g in range(groups):
            gate = jax.nn.sigmoid(mm(ref[g, :lead], wg))
            at = slice(g * lead, (g + 1) * lead)
            out_ref[at, :] = (gate * mixed[n, at]).astype(BF16)


def final_kernel(
    lines, heads, with_column, me_ref, line_ref, kept_ref, wo_ref, wc_ref, wout_ref,
    mine_ref, theirs_ref, out_ref, gated_ref,
):
    total = line_ref.shape[0]
    pairs = total // lines
    core = me_ref[0] % 2
    share = total // 2
    for owner, ref in ((core, mine_ref), (1 - core, theirs_ref)):
        gated_ref[pl.ds(pl.multiple_of(owner * share, share), share), :] = ref[...]
    hidden = wo_ref.shape[0]
    depth = hidden // heads
    rows_twice = one_hot(iota((128, 1), 0) % hidden == iota((1, hidden), 1))
    same_residue = iota((128, 1), 0) // hidden == iota((1, 128), 1) // hidden

    def twice(matrix, picked):
        wide = mm(mm(rows_twice, matrix).astype(BF16), picked)
        return jnp.where(same_residue, wide, 0.0).astype(BF16)

    def columns(width, chosen):
        return one_hot(iota((width, 1), 0) == chosen)

    lane = iota((1, 128), 1)
    wo = twice(wo_ref[...], columns(hidden, lane % hidden))
    row = (line_ref[...].astype(F32) + mm(gated_ref[...], wo)).astype(BF16)
    if not with_column:
        out_ref[...] = row
        return
    spread = mm(one_hot(iota((total, lines), 0) // pairs == iota((total, lines), 1)), kept_ref[...])
    own = iota((total, 2 * pairs), 1) // 2 == iota((total, 2 * pairs), 0) % pairs
    sides = one_hot(iota((2 * pairs, 128), 0) % 2 == iota((2 * pairs, 128), 1) // 64)
    kept = mm(jnp.where(own, spread, 0.0).astype(BF16), sides)

    choices = [
        lane % hidden,
        hidden + lane % hidden,
        2 * hidden + lane % depth,
        2 * hidden + depth + lane % depth,
    ]
    wc = [twice(wc_ref[...], columns(wc_ref.shape[1], chosen)) for chosen in choices]
    projected = mm(paired_norm(row, 64), jnp.concatenate(wc, axis=1))
    query, gate, key, value = [projected[:, 128 * n : 128 * (n + 1)] for n in range(4)]

    def grid(a):
        return a.reshape(lines, pairs, 128)

    count = jnp.maximum(jnp.sum(grid(kept), axis=0), 1.0)
    mean_query = jnp.sum(grid(kept * query), axis=0) / count * (depth**-0.5)
    same_head = block_matrix(128, depth, 1.0, 1.0)
    product = (mean_query[None] * grid(key)).reshape(total, 128)
    logits = grid(mm_split(product, same_head) + 1e9 * (kept - 1.0))
    exped = jnp.exp(logits - jnp.max(logits, axis=0, keepdims=True))
    mixed = jnp.sum(exped * grid(value), axis=0) / jnp.sum(exped, axis=0)
    gated = (jax.nn.sigmoid(grid(gate)) * mixed[None]).reshape(total, 128).astype(BF16)
    wout = twice(wout_ref[...], columns(hidden, lane % hidden))
    result = (row.astype(F32) + mm(gated, wout)).astype(BF16)
    shuffled = row_shuffle(result, lines, pairs)
    for t in range(pairs):
        out_ref[:, t * 128 : (t + 1) * 128] = shuffled[t * lines : (t + 1) * lines, :]


def call(kernel, out_shape, *args, **options):
    flops = options.pop("flops", 0)
    limit = pltpu.CompilerParams(vmem_limit_bytes=options.pop("mib", 8) * 1024 * 1024)
    moved = sum(a.size * a.dtype.itemsize for a in args)
    cost = pl.CostEstimate(flops=flops, bytes_accessed=moved, transcendentals=0)
    return pl.pallas_call(
        kernel, out_shape=out_shape, compiler_params=limit, cost_estimate=cost, **options
    )(*args)


def shape(*dims, dtype=BF16):
    return jax.ShapeDtypeStruct(dims, dtype)


def exchange(x, flip, devices):
    return lax.ppermute(x, "res", [(d, d ^ flip) for d in range(devices)])


def layer_normalize(values_in):
    centre = values_in - jnp.mean(values_in, axis=-1, keepdims=True)
    spread = jnp.mean(centre * centre, axis=-1, keepdims=True)
    return centre * lax.rsqrt(spread + EPS)


def column_complete(line, kept, vertical_matrix, vertical_exit_matrix, heads, depth):
    lines, columns, features = line.shape
    hidden = heads * depth
    normed = layer_normalize(line.astype(F32)).astype(BF16)
    projected = mm(normed.reshape(-1, features), vertical_matrix).reshape(lines, columns, -1)
    query, gate = projected[..., :hidden], projected[..., hidden : 2 * hidden]
    key = projected[..., 2 * hidden : 2 * hidden + depth]
    value = projected[..., 2 * hidden + depth :]
    count = jnp.maximum(jnp.sum(kept, axis=0), 1.0)[:, None]
    mean_query = jnp.sum(kept[..., None] * query, axis=0) / count * depth**-0.5
    logits = jnp.einsum("ihc,sic->sih", mean_query.reshape(columns, heads, depth), key)
    logits = logits + 1e9 * (kept - 1.0)[..., None]
    exped = jnp.exp(logits - jnp.max(logits, axis=0, keepdims=True))
    mixed = jnp.einsum("sih,sic->ihc", exped, value) / jnp.sum(exped, axis=0)[..., None]
    gate = jax.nn.sigmoid(gate).reshape(lines, columns, heads, depth)
    gated = (gate * mixed[None]).reshape(-1, hidden).astype(BF16)
    update = mm(gated, vertical_exit_matrix).reshape(lines, columns, features)
    return (line.astype(F32) + update).astype(BF16)


def on_device(
    seq_size,
    res_size,
    extra_activations,
    pair,
    present,
    amino,
    offset_matrix,
    horizontal_matrix,
    horizontal_exit_matrix,
    vertical_matrix,
    vertical_exit_matrix,
):
    lines, residues = present.shape
    pairs = residues // 2
    hidden = horizontal_exit_matrix.shape[0]
    heads = offset_matrix.shape[1]
    depth = hidden // heads
    groups = 2
    size = lines // (2 * groups)
    lead = size * pairs
    keys = res_size * residues
    rows = residues * heads
    core_bit, near, far, high = 1, 2, 4, 8
    kept = (present * amino[None, :]).astype(BF16)
    me = lax.axis_index("res").astype(jnp.int32).reshape(1)
    smem = pl.BlockSpec(memory_space=pltpu.SMEM)
    vmem = pl.BlockSpec(memory_space=pltpu.VMEM)

    rest = lead + pairs
    keep, send, line = call(
        functools.partial(prep_kernel, groups),
        [shape(groups, rest, 128)] * 2 + [shape(lines * pairs, 128)],
        me,
        extra_activations,
        kept,
        in_specs=[smem, vmem, vmem],
        scratch_shapes=[
            pltpu.VMEM((lines * pairs, 128), BF16),
            pltpu.VMEM((2 * groups, pairs, 128), BF16),
        ],
    )

    received = exchange(send, core_bit, res_size)
    chunk = jnp.concatenate(
        [keep[:, :lead], received[:, :lead], keep[:, lead:] + received[:, lead:]], axis=1
    )
    heights = [[d + high * k for k in range(res_size // high)] for d in range(high)]
    own = [
        lax.all_to_all(
            jnp.broadcast_to(chunk[g], (len(heights[0]),) + chunk[g].shape),
            "res",
            split_axis=0,
            concat_axis=0,
            axis_index_groups=heights,
        )
        for g in range(groups)
    ]
    beside = [exchange(part, near, res_size) for part in own]
    across = [exchange(part, far, res_size) for part in own]

    per_step = 8
    pieces = 4
    whole = seq_size == 1
    bias_rows = [shape(rows, keys)] * 2
    bias = call(
        functools.partial(bias_kernel, whole, pieces),
        bias_rows if whole else [shape(rows, pair.shape[1])],
        pair,
        offset_matrix.T,
        chunk,
        me,
        grid=(residues // per_step,),
        in_specs=[
            pl.BlockSpec((per_step,) + pair.shape[1:], lambda n: (n, 0, 0)),
            pl.BlockSpec(offset_matrix.shape[::-1], lambda n: (0, 0)),
            pl.BlockSpec(memory_space=pl.ANY),
            smem,
        ],
        out_specs=[pl.BlockSpec((rows, pair.shape[1]), lambda n: (0, 0))] * (1 + whole),
        scratch_shapes=[
            pltpu.VMEM((rows // 128, pair.shape[1], 128), F32),
            pltpu.VMEM((2 * pair.shape[2], 2 * pair.shape[2]), BF16),
            pltpu.VMEM((pair.shape[2], rows), F32),
        ],
        flops=16 * pair.size * 128,
        mib=57,
    )
    if not whole:
        bias = call(
            functools.partial(order_kernel, residues, pieces),
            bias_rows,
            me,
            lax.all_gather(bias[0], "seq", axis=1, tiled=True),
            in_specs=[smem, vmem],
            mib=14,
        )
    bias, lhs, sums = call(
        functools.partial(query_kernel, groups, size, pairs, heads),
        [
            shape(2 * rows, keys, dtype=F32),
            shape(groups * size, 2 * rows, 128),
            shape(groups * size, 2 * rows, 128, dtype=F32),
        ],
        bias[0],
        exchange(bias[1], core_bit, res_size),
        keep,
        received,
        horizontal_matrix,
        *own,
        in_specs=[vmem] * (5 + groups),
        flops=8 * rows * keys * keys,
        mib=18,
    )

    def add(sums, places, parts):
        return call(
            functools.partial(add_kernel, groups, size, pairs, places),
            shape(*sums.shape, dtype=F32),
            lhs,
            bias,
            sums,
            *parts,
            flops=groups * size * rows * keys * 2 * 256 * 2,
            mib=20,
        )

    beside[0], across[1], sums = lax.optimization_barrier((beside[0], across[1], sums))
    corner = [
        exchange(beside[g], far, res_size) if g % 2 == 0 else exchange(across[g], near, res_size)
        for g in range(groups)
    ]
    sums = add(sums, (1, 2), (beside[0], across[1]))
    beside[1], across[0], sums = lax.optimization_barrier((beside[1], across[0], sums))
    sums = add(sums, (2, 1), (across[0], beside[1]))
    corner[0], corner[1], sums = lax.optimization_barrier((corner[0], corner[1], sums))
    anywhere = pl.BlockSpec(memory_space=pl.ANY)
    mine, theirs = call(
        functools.partial(finish_kernel, heads, groups, size, pairs, 3),
        [shape(groups * lead, 128)] * 2,
        lhs,
        bias,
        sums,
        horizontal_matrix,
        keep,
        received,
        *corner,
        *own,
        *beside,
        *across,
        in_specs=[vmem] * (6 + groups) + [anywhere] * (3 * groups),
        scratch_shapes=[
            pltpu.VMEM((2, groups * lead, 128 * 2 * heads), BF16),
            pltpu.VMEM((2, 8, 128), F32),
            pltpu.VMEM((3 * groups,) + own[0].shape, BF16),
        ],
        flops=groups * size * rows * keys * 2 * 256,
        mib=24,
    )
    returned = exchange(theirs, core_bit, res_size)

    with_column = seq_size == 1
    final_args = [
        me,
        line,
        kept,
        horizontal_exit_matrix,
        vertical_matrix,
        vertical_exit_matrix,
    ]
    final_args += [mine, returned]
    result = call(
        functools.partial(final_kernel, lines, heads, with_column),
        shape(*extra_activations.shape) if with_column else shape(lines * pairs, 128),
        *final_args,
        in_specs=[smem] + [vmem] * (len(final_args) - 1),
        scratch_shapes=[pltpu.VMEM((lines * pairs, 128), BF16)],
    )
    if with_column:
        return result
    row = result.reshape(lines, residues, hidden)
    moved = lax.all_to_all(row, "seq", split_axis=1, concat_axis=0, tiled=True)
    moved_kept = lax.all_to_all(kept, "seq", split_axis=1, concat_axis=0, tiled=True)
    updated = column_complete(
        moved, moved_kept.astype(F32), vertical_matrix, vertical_exit_matrix, heads, depth
    )
    back = lax.all_to_all(updated, "seq", split_axis=0, concat_axis=1, tiled=True)
    return back.reshape(extra_activations.shape)


def solution(mesh):
    in_specs = (
        P("seq", "res"),
        P("res", "seq", None),
        P("seq", "res"),
        P("res"),
        P(),
        P(),
        P(),
        P(),
        P(),
    )
    sizes = mesh.shape
    return jax.shard_map(
        functools.partial(on_device, sizes["seq"], sizes["res"]),
        mesh=mesh,
        in_specs=in_specs,
        out_specs=P("seq", "res"),
        check_vma=False,
    )
```

```python
import functools
import math

import jax
import jax.numpy as jnp
from jax import lax
from jax.experimental import pallas as pl
from jax.experimental.pallas import tpu as pltpu
from jax.sharding import PartitionSpec as P

F32 = jnp.float32
BF16 = jnp.bfloat16
LOG2E = math.log2(math.e)
EPS = 1e-05

NT = (((1,), (1,)), ((), ()))


def mm(a, b):
    return jnp.dot(a, b, preferred_element_type=F32)


def mm_nt(a, b):
    return lax.dot_general(a, b, NT, preferred_element_type=F32)


def iota(shape, axis):
    return lax.broadcasted_iota(jnp.int32, shape, axis)


def one_hot(condition):
    return jnp.where(condition, 1.0, 0.0).astype(BF16)


def block_matrix(size, block, on_diagonal, elsewhere):
    row, col = iota((size, 1), 0), iota((1, size), 1)
    inside = jnp.where(row == col, on_diagonal, elsewhere)
    return jnp.where(row // block == col // block, inside, 0.0).astype(BF16)


def halves(value):
    high = value.astype(BF16)
    return high, (value - high.astype(F32)).astype(BF16)


def mm_split(value, matrix):
    high, low = halves(value)
    return mm(high, matrix) + mm(low, matrix)


def paired_norm(x, width):
    lanes = x.shape[1]
    centre = mm(x, block_matrix(lanes, width, 1.0 - 1.0 / width, -1.0 / width))
    spread = mm_split(centre * centre, block_matrix(lanes, width, 1.0 / width, 1.0 / width))
    return (centre * lax.rsqrt(spread + EPS)).astype(BF16)


def row_shuffle(rows, inner, outer):
    total = rows.shape[0]
    row, col = iota((total, 1), 0), iota((1, total), 1)
    return mm(one_hot(col == (row % inner) * outer + row // inner), rows).astype(BF16)


def prep_kernel(groups, me_ref, m_ref, kept_ref, *refs):
    keep_ref, send_ref, line_ref, normed_ref, spread_ref = refs
    lines, width = m_ref.shape
    pairs = width // 128
    stacked = jnp.concatenate([m_ref[:, t * 128 : (t + 1) * 128] for t in range(pairs)], axis=0)
    normed = paired_norm(stacked, 64)
    both = row_shuffle(jnp.concatenate([normed, stacked], axis=1), pairs, lines)
    normed_ref[...] = both[:, :128]
    line_ref[...] = both[:, 128:]
    kept = kept_ref[...]
    size = lines // (2 * groups)
    residues = 2 * pairs
    row, col = iota((pairs, residues), 0), iota((pairs, residues), 1)
    evens, odds = one_hot(col == 2 * row), one_hot(col == 2 * row + 1)
    row, col = iota((128, lines), 0) - 64, iota((128, lines), 1)
    core = me_ref[0] % 2
    for n in range(2 * groups):
        start = jnp.where(n // groups == core, 0, 2 * size)
        chosen = (row >= start) & (row < start + 2 * size) & (row % size == col - n * size)
        spread = mm(one_hot(chosen), kept).astype(BF16)
        first = iota((pairs, 128), 1) < 64 + size + start
        spread_ref[n] = jnp.where(first, mm_nt(evens, spread), mm_nt(odds, spread)).astype(BF16)
    rows = size * pairs
    for ref, half in ((keep_ref, core), (send_ref, 1 - core)):
        for g in range(groups):
            index = half * groups + g
            ref[g, :rows] = normed_ref[pl.ds(pl.multiple_of(index * rows, rows), rows), :]
            ref[g, rows:] = spread_ref[index]


def bias_kernel(whole, pieces, x_ref, w_ref, after_ref, me_ref, *refs):
    outs, (acc_ref, wide_ref) = refs[:-2], refs[-2:]
    step = pl.program_id(0)
    heads = w_ref.shape[0]
    per_step, keys, channels = x_ref.shape
    residues = per_step * pl.num_programs(0)
    pairs = residues // 2
    tiles = acc_ref.shape[0]
    width = tiles * 128

    @pl.when(step == 0)
    def _():
        spread = one_hot(iota((heads, 1), 0) == iota((1, width), 1) // residues)
        wide_ref[...] = lax.dot_general(
            w_ref[...], spread, (((0,), (0,)), ((), ())), preferred_element_type=F32
        )
        acc_ref[...] = jnp.zeros(acc_ref.shape, F32)

    lane = iota((1, width), 1) % residues
    placed = []
    for n in range(per_step):
        residue = step * per_step + n
        mine = lane == (residue % 2) * pairs + residue // 2
        placed.append(jnp.where(mine, wide_ref[...], 0.0).astype(BF16))
    placed = jnp.concatenate(placed, axis=0)
    piece = min(512, keys)
    for r in range(0, keys, piece):
        normed = []
        for n in range(per_step):
            x = x_ref[n, r : r + piece].astype(F32)
            centre = x - jnp.mean(x, axis=-1, keepdims=True)
            spread = jnp.mean(centre * centre, axis=-1, keepdims=True)
            normed.append((centre * lax.rsqrt(spread + EPS)).astype(BF16))
        added = mm(jnp.concatenate(normed, axis=1), placed)
        for n in range(tiles):
            acc_ref[n, r : r + piece, :] += added[:, n * 128 : (n + 1) * 128]

    @pl.when(step == pl.num_programs(0) - 1)
    def _():
        if not whole:
            for n in range(tiles):
                outs[0][n * 128 : (n + 1) * 128, :] = acc_ref[n].T.astype(BF16)
            return
        levels = keys // (2 * pieces * residues)
        for flip in range(2):
            user = me_ref[0] ^ flip
            starts = [
                (user ^ (c + 2 * q + 2 * pieces * k)) * residues + p
                for q in range(pieces)
                for p in range(2)
                for k in range(levels)
                for c in range(2)
            ]
            for n in range(tiles):
                for at in range(0, keys, 128):
                    rows = [
                        acc_ref[n, pl.ds(start, pairs, stride=2), :]
                        for start in starts[at // pairs : (at + 128) // pairs]
                    ]
                    turned = jnp.concatenate(rows, axis=0).T.astype(BF16)
                    outs[flip][n * 128 : (n + 1) * 128, at : at + 128] = turned


def order_kernel(residues, pieces, me_ref, bias_ref, own_ref, send_ref):
    rows, keys = bias_ref.shape
    pairs = residues // 2
    lane = iota((1, keys), 1)
    each = keys // pieces
    which, rest = lane // each, lane % each
    parity, rest = rest // (each // 2), rest % (each // 2)
    place, pair = rest // pairs, rest % pairs
    for flip, out_ref in enumerate((own_ref, send_ref)):
        device = me_ref[0] ^ flip ^ ((place % 2) + 2 * which + 2 * pieces * (place // 2))
        target = device * residues + 2 * pair + parity
        total = jnp.zeros((rows, keys), F32)
        for start in range(0, keys, 256):
            chosen = one_hot(iota((256, keys), 0) + start == target)
            total = total + mm(bias_ref[:, start : start + 256], chosen)
        out_ref[...] = total.astype(BF16)


def pair_matrix(matrix, chosen):
    rows, columns = matrix.shape
    lane = iota((1, 128), 1)
    twice_rows = one_hot(iota((128, 1), 0) % rows == iota((1, rows), 1))
    picked = one_hot(iota((columns, 1), 0) == chosen)
    wide = mm(mm(twice_rows, matrix).astype(BF16), picked)
    same = iota((128, 1), 0) // rows == lane // (128 // 2)
    return jnp.where(same, wide, 0.0).astype(BF16)


def value_matrix(matrix, hidden, heads):
    depth = hidden // heads
    row, col = iota((128, 1), 0), iota((1, 256), 1)
    picked = one_hot(iota((4 * hidden, 1), 0) == 2 * hidden + col % hidden)
    picked = jnp.where(col < 128, picked, jnp.zeros_like(picked))
    wv = mm(mm(one_hot(row == iota((1, hidden), 1)), matrix).astype(BF16), picked)
    counted = (row >= hidden) & (col >= 128)
    wv = jnp.where(counted, 1.0 / (128 - hidden), wv)
    owner = col % 128 // depth
    return [
        jnp.where(owner == p * heads + h, wv, 0.0).astype(BF16)
        for h in range(heads)
        for p in range(2)
    ]


def query_kernel(
    groups, size, pairs, heads, own_ref, peer_ref, keep_ref, received_ref, w_ref, exit_ref,
    column_ref, column_exit_ref, kept_ref, *refs
):
    column_refs = refs[:groups]
    bias_ref, lhs_ref, sums_ref, wv_ref, gate_ref, final_ref, kept_wide_ref = refs[groups:]
    rows = own_ref.shape[0]
    bias_ref[:rows, :] = own_ref[...].astype(F32) * LOG2E
    bias_ref[rows:, :] = peer_ref[...].astype(F32) * LOG2E

    hidden = w_ref.shape[0]
    depth = hidden // heads
    lane = iota((1, 128), 1)
    wq = pair_matrix(w_ref[...], lane % hidden)
    wg = pair_matrix(w_ref[...], 3 * hidden + lane % hidden)
    for n, part in enumerate(value_matrix(w_ref[...], hidden, heads)):
        wv_ref[n * 128 : (n + 1) * 128, :] = part
    final = [
        (exit_ref, lane % hidden),
        (column_exit_ref, lane % hidden),
        (column_ref, lane % hidden),
        (column_ref, hidden + lane % hidden),
        (column_ref, 2 * hidden + lane % depth),
        (column_ref, 2 * hidden + depth + lane % depth),
    ]
    for n, (ref, chosen) in enumerate(final):
        final_ref[:, n * 128 : (n + 1) * 128] = pair_matrix(ref[...], chosen)
    total, lines = kept_wide_ref.shape[0], kept_ref.shape[0]
    spread = mm(one_hot(iota((total, 1), 0) // pairs == iota((1, lines), 1)), kept_ref[...])
    mine = iota((1, 2 * pairs), 1) // 2 == iota((total, 1), 0) % pairs
    sides = one_hot(iota((2 * pairs, 1), 0) % 2 == lane // 64)
    kept_wide_ref[...] = mm(jnp.where(mine, spread, 0.0).astype(BF16), sides)
    picked = one_hot(iota((1, 4 * hidden), 1) == hidden + iota((128, 1), 0) % hidden)
    wk = mm_nt(picked, w_ref[...]).astype(BF16)
    wk = mm(wk, one_hot(iota((hidden, 1), 0) == iota((1, 128), 1))).astype(BF16)
    lead = size * pairs
    spare = lane - hidden
    for g in range(groups):
        for n, ref in enumerate((keep_ref, received_ref)):
            gate_ref[n, g * lead : (g + 1) * lead] = jax.nn.sigmoid(mm(ref[g, :lead], wg))
            query = (mm(ref[g, :lead], wq) * (depth**-0.5)).astype(BF16).astype(F32)
            for s in range(size):
                q = query[s * pairs : (s + 1) * pairs]
                spread = [
                    jnp.where(lane // depth == p * heads + h, q, 0.0).astype(BF16)
                    for h in range(heads)
                    for p in range(2)
                ]
                folded = mm(jnp.concatenate(spread, axis=0), wk) * LOG2E
                picks = (spare >= 0) & (spare < 4 * size) & (spare % size == s)
                lhs_ref[g * size + s, n * rows : (n + 1) * rows, :] = jnp.where(
                    picks, 1.0, folded
                ).astype(BF16)
    add_pieces(groups, size, pairs, (0,) * groups, lhs_ref, bias_ref, None, column_refs, sums_ref)


def masks_of(ref, size, pairs):
    start = 2 * size * pairs
    lane = iota((1, 128), 1) - 64
    masks = []
    for p in range(2):
        blocks = []
        for k in range(ref.shape[0]):
            hidden = (1e9 * LOG2E) * (ref[k, start : start + pairs, :].astype(F32) - 1.0)
            for c in range(2):
                first = (2 * c + p) * size
                mine = (lane >= first) & (lane < first + size)
                blocks.append(jnp.where(mine, hidden, 0.0).astype(BF16))
        masks.append(jnp.concatenate(blocks, axis=0))
    return masks


def keys_of(ref, masks, s, size, pairs):
    start = pl.multiple_of(s * pairs, pairs)
    even = jnp.concatenate(
        [
            ref[k, pl.ds(c * size * pairs + start, pairs), :]
            for k in range(ref.shape[0])
            for c in range(2)
        ],
        axis=0,
    )
    odd = pltpu.roll(even.astype(F32), 64, 1).astype(BF16)
    low = iota(even.shape, 1) < 64
    one = jnp.ones_like(even)
    keyed = [jnp.where(low, x, m) for x, m in zip((even, odd), masks)]
    valued = [jnp.where(low, x, one) for x in (even, odd)]
    return jnp.concatenate(keyed, axis=0), jnp.concatenate(valued, axis=0)


def partial_sums(lhs, bias_ref, rows, piece, keyed, valued):
    width = keyed.shape[0]
    logits = mm_nt(lhs, keyed) + bias_ref[rows, piece * width : (piece + 1) * width]
    return mm(jnp.exp2(logits).astype(BF16), valued)


def add_pieces(groups, size, pairs, places, lhs_ref, bias_ref, before_ref, piece_refs, out_ref):
    masks = [masks_of(ref, size, pairs) for ref in piece_refs]

    def one_line(s, carry):
        for g in range(groups):
            line = g * size + s
            keyed, valued = keys_of(piece_refs[g], masks[g], s, size, pairs)
            total = partial_sums(lhs_ref[line], bias_ref, slice(None), places[g], keyed, valued)
            out_ref[line] = total if before_ref is None else before_ref[line] + total
        return carry

    lax.fori_loop(0, size, one_line, 0, unroll=2)


def add_kernel(groups, size, pairs, places, lhs_ref, bias_ref, before_ref, *refs):
    add_pieces(
        groups, size, pairs, places, lhs_ref, bias_ref, before_ref, refs[:-1], refs[-1]
    )


def finish_kernel(
    heads, groups, size, pairs, place, side, lhs_ref, bias_ref, sums_ref, wv_ref, gate_ref, *refs
):
    piece_refs, far_refs = refs[:groups], refs[groups : 4 * groups]
    out_ref, turned_ref, range_ref, copy_ref = refs[4 * groups :]
    blocks = 2 * heads
    rows = blocks * pairs
    mine = slice(side * rows, (side + 1) * rows)
    masks = [masks_of(ref, size, pairs) for ref in piece_refs]
    low = iota((rows, 128), 1) < 64

    def settle(line, total):
        start = pl.multiple_of(line * pairs, pairs)
        total = total.astype(BF16)
        for b in range(blocks):
            part = total[b * pairs : (b + 1) * pairs]
            turned_ref[pl.ds(start, pairs), b * 128 : (b + 1) * 128] = part

    range_ref[...] = jnp.ones(range_ref.shape, F32)

    def one_line(s, carry):
        for g in range(groups):
            line = g * size + s
            keyed, valued = keys_of(piece_refs[g], masks[g], s, size, pairs)
            total = sums_ref[line, mine] + partial_sums(
                lhs_ref[line, mine], bias_ref, mine, place, keyed, valued
            )
            settle(line, total)
            weight = jnp.where(low, 1.0, total).reshape(-1, 8, 128)
            range_ref[0] = jnp.minimum(range_ref[0], jnp.min(weight, axis=0))
            range_ref[1] = jnp.maximum(range_ref[1], jnp.max(weight, axis=0))
        return carry

    lax.fori_loop(0, size, one_line, 0, unroll=2)
    fine = (range_ref[0] > 2.0**-80) & (range_ref[1] < 2.0**100)

    @pl.when(jnp.min(jnp.where(fine, 1.0, 0.0)) < 0.5)
    def _():
        for n, ref in enumerate(far_refs):
            pltpu.sync_copy(ref, copy_ref.at[n])
        for g in range(groups):
            ordered = [copy_ref.at[n * groups + g] for n in range(3)] + [piece_refs[g]]
            all_masks = [masks_of(ref, size, pairs) for ref in ordered]

            def exact_line(s, carry):
                line = g * size + s
                both = [keys_of(r, m, s, size, pairs) for r, m in zip(ordered, all_masks)]
                logits = []
                for n, (keyed, _) in enumerate(both):
                    width = keyed.shape[0]
                    bias = bias_ref[mine, n * width : (n + 1) * width]
                    logits.append(mm_nt(lhs_ref[line, mine], keyed) + bias)
                peak = functools.reduce(jnp.maximum, logits)
                peak = jnp.max(peak, axis=-1, keepdims=True)
                parts = [
                    mm(jnp.exp2(part - peak).astype(BF16), valued)
                    for part, (_, valued) in zip(logits, both)
                ]
                settle(line, sum(parts[1:], parts[0]))
                return carry

            lax.fori_loop(0, size, exact_line, 0)

    mixed = mm(turned_ref[...], wv_ref[...])
    mixed = mixed[:, :128] / mixed[:, 128:]
    out_ref[...] = (gate_ref[side] * mixed).astype(BF16)


def final_kernel(
    lines, depth, with_column, me_ref, line_ref, kept_ref, w_ref, mine_ref, theirs_ref, out_ref,
    gated_ref,
):
    total = line_ref.shape[0]
    pairs = total // lines
    core = me_ref[0] % 2
    share = total // 2
    for owner, ref in ((core, mine_ref), (1 - core, theirs_ref)):
        gated_ref[pl.ds(pl.multiple_of(owner * share, share), share), :] = ref[...]
    row = (line_ref[...].astype(F32) + mm(gated_ref[...], w_ref[:, :128])).astype(BF16)
    if not with_column:
        out_ref[...] = row
        return
    kept = kept_ref[...]
    projected = mm(paired_norm(row, 64), w_ref[:, 256:])
    query, gate, key, value = [projected[:, 128 * n : 128 * (n + 1)] for n in range(4)]

    def grid(a):
        return a.reshape(lines, pairs, 128)

    count = jnp.maximum(jnp.sum(grid(kept), axis=0), 1.0)
    mean_query = jnp.sum(grid(kept * query), axis=0) / count * (depth**-0.5)
    same_head = block_matrix(128, depth, 1.0, 1.0)
    product = (mean_query[None] * grid(key)).reshape(total, 128)
    logits = grid(mm_split(product, same_head) + 1e9 * (kept - 1.0))
    exped = jnp.exp(logits - jnp.max(logits, axis=0, keepdims=True))
    mixed = jnp.sum(exped * grid(value), axis=0) / jnp.sum(exped, axis=0)
    gated = (jax.nn.sigmoid(grid(gate)) * mixed[None]).reshape(total, 128).astype(BF16)
    result = (row.astype(F32) + mm(gated, w_ref[:, 128:256])).astype(BF16)
    shuffled = row_shuffle(result, lines, pairs)
    for t in range(pairs):
        out_ref[:, t * 128 : (t + 1) * 128] = shuffled[t * lines : (t + 1) * lines, :]


def call(kernel, out_shape, *args, **options):
    flops = options.pop("flops", 0)
    limit = pltpu.CompilerParams(vmem_limit_bytes=options.pop("mib", 8) * 1024 * 1024)
    moved = sum(a.size * a.dtype.itemsize for a in args)
    cost = pl.CostEstimate(flops=flops, bytes_accessed=moved, transcendentals=0)
    return pl.pallas_call(
        kernel, out_shape=out_shape, compiler_params=limit, cost_estimate=cost, **options
    )(*args)


def shape(*dims, dtype=BF16):
    return jax.ShapeDtypeStruct(dims, dtype)


def exchange(x, flip, devices):
    return lax.ppermute(x, "res", [(d, d ^ flip) for d in range(devices)])


def layer_normalize(values_in):
    centre = values_in - jnp.mean(values_in, axis=-1, keepdims=True)
    spread = jnp.mean(centre * centre, axis=-1, keepdims=True)
    return centre * lax.rsqrt(spread + EPS)


def column_complete(line, kept, vertical_matrix, vertical_exit_matrix, heads, depth):
    lines, columns, features = line.shape
    hidden = heads * depth
    normed = layer_normalize(line.astype(F32)).astype(BF16)
    projected = mm(normed.reshape(-1, features), vertical_matrix).reshape(lines, columns, -1)
    query, gate = projected[..., :hidden], projected[..., hidden : 2 * hidden]
    key = projected[..., 2 * hidden : 2 * hidden + depth]
    value = projected[..., 2 * hidden + depth :]
    count = jnp.maximum(jnp.sum(kept, axis=0), 1.0)[:, None]
    mean_query = jnp.sum(kept[..., None] * query, axis=0) / count * depth**-0.5
    logits = jnp.einsum("ihc,sic->sih", mean_query.reshape(columns, heads, depth), key)
    logits = logits + 1e9 * (kept - 1.0)[..., None]
    exped = jnp.exp(logits - jnp.max(logits, axis=0, keepdims=True))
    mixed = jnp.einsum("sih,sic->ihc", exped, value) / jnp.sum(exped, axis=0)[..., None]
    gate = jax.nn.sigmoid(gate).reshape(lines, columns, heads, depth)
    gated = (gate * mixed[None]).reshape(-1, hidden).astype(BF16)
    update = mm(gated, vertical_exit_matrix).reshape(lines, columns, features)
    return (line.astype(F32) + update).astype(BF16)


def on_device(
    seq_size,
    res_size,
    extra_activations,
    pair,
    present,
    amino,
    offset_matrix,
    horizontal_matrix,
    horizontal_exit_matrix,
    vertical_matrix,
    vertical_exit_matrix,
):
    lines, residues = present.shape
    pairs = residues // 2
    hidden = horizontal_exit_matrix.shape[0]
    heads = offset_matrix.shape[1]
    depth = hidden // heads
    groups = 2
    size = lines // (2 * groups)
    lead = size * pairs
    keys = res_size * residues
    rows = residues * heads
    core_bit, near, far, high = 1, 2, 4, 8
    kept = (present * amino[None, :]).astype(BF16)
    me = lax.axis_index("res").astype(jnp.int32).reshape(1)
    smem = pl.BlockSpec(memory_space=pltpu.SMEM)
    vmem = pl.BlockSpec(memory_space=pltpu.VMEM)

    rest = lead + pairs
    keep, send, line = call(
        functools.partial(prep_kernel, groups),
        [shape(groups, rest, 128)] * 2 + [shape(lines * pairs, 128)],
        me,
        extra_activations,
        kept,
        in_specs=[smem, vmem, vmem],
        scratch_shapes=[
            pltpu.VMEM((lines * pairs, 128), BF16),
            pltpu.VMEM((2 * groups, pairs, 128), BF16),
        ],
    )

    received = exchange(send, core_bit, res_size)
    chunk = jnp.concatenate(
        [keep[:, :lead], received[:, :lead], keep[:, lead:] + received[:, lead:]], axis=1
    )
    levels = [chunk] + [exchange(chunk, high * k, res_size) for k in range(1, res_size // high)]
    own = [jnp.stack([level[g] for level in levels]) for g in range(groups)]
    beside = [exchange(part, near, res_size) for part in own]
    across = [exchange(part, far, res_size) for part in own]

    per_step = 8
    pieces = 4
    whole = seq_size == 1
    bias_rows = [shape(rows, keys)] * 2
    bias = call(
        functools.partial(bias_kernel, whole, pieces),
        bias_rows if whole else [shape(rows, pair.shape[1])],
        pair,
        offset_matrix.T,
        chunk,
        me,
        grid=(residues // per_step,),
        in_specs=[
            pl.BlockSpec((per_step,) + pair.shape[1:], lambda n: (n, 0, 0)),
            pl.BlockSpec(offset_matrix.shape[::-1], lambda n: (0, 0)),
            pl.BlockSpec(memory_space=pl.ANY),
            smem,
        ],
        out_specs=[pl.BlockSpec((rows, pair.shape[1]), lambda n: (0, 0))] * (1 + whole),
        scratch_shapes=[
            pltpu.VMEM((rows // 128, pair.shape[1], 128), F32),
            pltpu.VMEM((pair.shape[2], rows), F32),
        ],
        flops=16 * pair.size * 128,
        mib=57,
    )
    if not whole:
        bias = call(
            functools.partial(order_kernel, residues, pieces),
            bias_rows,
            me,
            lax.all_gather(bias[0], "seq", axis=1, tiled=True),
            in_specs=[smem, vmem],
            mib=14,
        )
    bias, lhs, sums, wv, gate, w_final, kept_wide = call(
        functools.partial(query_kernel, groups, size, pairs, heads),
        [
            shape(2 * rows, keys, dtype=F32),
            shape(groups * size, 2 * rows, 128),
            shape(groups * size, 2 * rows, 128, dtype=F32),
            shape(2 * heads * 128, 256),
            shape(2, groups * lead, 128, dtype=F32),
            shape(128, 6 * 128),
            shape(lines * pairs, 128, dtype=F32),
        ],
        bias[0],
        exchange(bias[1], core_bit, res_size),
        keep,
        received,
        horizontal_matrix,
        horizontal_exit_matrix,
        vertical_matrix,
        vertical_exit_matrix,
        kept,
        *own,
        in_specs=[vmem] * (9 + groups),
        flops=8 * rows * keys * keys,
        mib=20,
    )

    def add(sums, places, parts):
        return call(
            functools.partial(add_kernel, groups, size, pairs, places),
            shape(*sums.shape, dtype=F32),
            lhs,
            bias,
            sums,
            *parts,
            flops=groups * size * rows * keys * 2 * 256 * 2,
            mib=20,
        )

    beside[0], across[1], sums = lax.optimization_barrier((beside[0], across[1], sums))
    corner = [
        exchange(beside[g], far, res_size) if g % 2 == 0 else exchange(across[g], near, res_size)
        for g in range(groups)
    ]
    sums = add(sums, (1, 2), (beside[0], across[1]))
    beside[1], across[0], sums = lax.optimization_barrier((beside[1], across[0], sums))
    sums = add(sums, (2, 1), (across[0], beside[1]))
    corner[0], corner[1], sums = lax.optimization_barrier((corner[0], corner[1], sums))
    anywhere = pl.BlockSpec(memory_space=pl.ANY)

    def finish(side, sums):
        return call(
            functools.partial(finish_kernel, heads, groups, size, pairs, 3, side),
            shape(groups * lead, 128),
            lhs,
            bias,
            sums,
            wv,
            gate,
            *corner,
            *own,
            *beside,
            *across,
            in_specs=[vmem] * (5 + groups) + [anywhere] * (3 * groups),
            scratch_shapes=[
                pltpu.VMEM((groups * lead, 128 * 2 * heads), BF16),
                pltpu.VMEM((2, 8, 128), F32),
                pltpu.VMEM((3 * groups,) + own[0].shape, BF16),
            ],
            flops=groups * size * rows * keys * 2 * 256,
            mib=22,
        )

    theirs = finish(1, sums)
    theirs, sums = lax.optimization_barrier((theirs, sums))
    returned = exchange(theirs, core_bit, res_size)
    mine = finish(0, sums)
    with_column = seq_size == 1
    final_args = [
        me,
        line,
        kept_wide,
        w_final,
    ]
    final_args += [mine, returned]
    result = call(
        functools.partial(final_kernel, lines, depth, with_column),
        shape(*extra_activations.shape) if with_column else shape(lines * pairs, 128),
        *final_args,
        in_specs=[smem] + [vmem] * (len(final_args) - 1),
        scratch_shapes=[pltpu.VMEM((lines * pairs, 128), BF16)],
    )
    if with_column:
        return result
    row = result.reshape(lines, residues, hidden)
    moved = lax.all_to_all(row, "seq", split_axis=1, concat_axis=0, tiled=True)
    moved_kept = lax.all_to_all(kept, "seq", split_axis=1, concat_axis=0, tiled=True)
    updated = column_complete(
        moved, moved_kept.astype(F32), vertical_matrix, vertical_exit_matrix, heads, depth
    )
    back = lax.all_to_all(updated, "seq", split_axis=0, concat_axis=1, tiled=True)
    return back.reshape(extra_activations.shape)


def solution(mesh):
    in_specs = (
        P("seq", "res"),
        P("res", "seq", None),
        P("seq", "res"),
        P("res"),
        P(),
        P(),
        P(),
        P(),
        P(),
    )
    sizes = mesh.shape
    return jax.shard_map(
        functools.partial(on_device, sizes["seq"], sizes["res"]),
        mesh=mesh,
        in_specs=in_specs,
        out_specs=P("seq", "res"),
        check_vma=False,
    )
```

```python
import functools
import math

import jax
import jax.numpy as jnp
from jax import lax
from jax.experimental import pallas as pl
from jax.experimental.pallas import tpu as pltpu
from jax.sharding import PartitionSpec as P

F32 = jnp.float32
BF16 = jnp.bfloat16
LOG2E = math.log2(math.e)
EPS = 1e-05

NT = (((1,), (1,)), ((), ()))


def mm(a, b):
    return jnp.dot(a, b, preferred_element_type=F32)


def mm_nt(a, b):
    return lax.dot_general(a, b, NT, preferred_element_type=F32)


def iota(shape, axis):
    return lax.broadcasted_iota(jnp.int32, shape, axis)


def one_hot(condition):
    return jnp.where(condition, 1.0, 0.0).astype(BF16)


def block_matrix(size, block, on_diagonal, elsewhere):
    row, col = iota((size, 1), 0), iota((1, size), 1)
    inside = jnp.where(row == col, on_diagonal, elsewhere)
    return jnp.where(row // block == col // block, inside, 0.0).astype(BF16)


def halves(value):
    high = value.astype(BF16)
    return high, (value - high.astype(F32)).astype(BF16)


def mm_split(value, matrix):
    high, low = halves(value)
    return mm(high, matrix) + mm(low, matrix)


def paired_norm(x, width):
    lanes = x.shape[1]
    centre = mm(x, block_matrix(lanes, width, 1.0 - 1.0 / width, -1.0 / width))
    spread = mm_split(centre * centre, block_matrix(lanes, width, 1.0 / width, 1.0 / width))
    return (centre * lax.rsqrt(spread + EPS)).astype(BF16)


def row_shuffle(rows, inner, outer):
    total = rows.shape[0]
    row, col = iota((total, 1), 0), iota((1, total), 1)
    return mm(one_hot(col == (row % inner) * outer + row // inner), rows).astype(BF16)


def prep_kernel(groups, me_ref, m_ref, kept_ref, *refs):
    keep_ref, send_ref, line_ref, normed_ref, spread_ref = refs
    lines, width = m_ref.shape
    pairs = width // 128
    stacked = jnp.concatenate([m_ref[:, t * 128 : (t + 1) * 128] for t in range(pairs)], axis=0)
    normed = paired_norm(stacked, 64)
    both = row_shuffle(jnp.concatenate([normed, stacked], axis=1), pairs, lines)
    normed_ref[...] = both[:, :128]
    line_ref[...] = both[:, 128:]
    kept = kept_ref[...]
    size = lines // (2 * groups)
    residues = 2 * pairs
    row, col = iota((pairs, residues), 0), iota((pairs, residues), 1)
    evens, odds = one_hot(col == 2 * row), one_hot(col == 2 * row + 1)
    row, col = iota((128, lines), 0) - 64, iota((128, lines), 1)
    core = me_ref[0] % 2
    for n in range(2 * groups):
        start = jnp.where(n // groups == core, 0, 2 * size)
        chosen = (row >= start) & (row < start + 2 * size) & (row % size == col - n * size)
        spread = mm(one_hot(chosen), kept).astype(BF16)
        first = iota((pairs, 128), 1) < 64 + size + start
        spread_ref[n] = jnp.where(first, mm_nt(evens, spread), mm_nt(odds, spread)).astype(BF16)
    rows = size * pairs
    for ref, half in ((keep_ref, core), (send_ref, 1 - core)):
        for g in range(groups):
            index = half * groups + g
            ref[g, :rows] = normed_ref[pl.ds(pl.multiple_of(index * rows, rows), rows), :]
            ref[g, rows:] = spread_ref[index]


def bias_kernel(whole, pieces, x_ref, w_ref, after_ref, me_ref, *refs):
    outs, (acc_ref, centring_ref, wide_ref) = refs[:-3], refs[-3:]
    step = pl.program_id(0)
    heads = w_ref.shape[0]
    per_step, keys, channels = x_ref.shape
    residues = per_step * pl.num_programs(0)
    pairs = residues // 2
    tiles = acc_ref.shape[0]
    width = tiles * 128

    @pl.when(step == 0)
    def _():
        centring_ref[...] = block_matrix(
            2 * channels, channels, 1.0 - 1.0 / channels, -1.0 / channels
        )
        spread = one_hot(iota((heads, 1), 0) == iota((1, width), 1) // residues)
        wide_ref[...] = lax.dot_general(
            w_ref[...], spread, (((0,), (0,)), ((), ())), preferred_element_type=F32
        )
        acc_ref[...] = jnp.zeros(acc_ref.shape, F32)

    lane = iota((1, width), 1) % residues
    placed = []
    for n in range(per_step):
        residue = step * per_step + n
        mine = lane == (residue % 2) * pairs + residue // 2
        placed.append(jnp.where(mine, wide_ref[...], 0.0).astype(BF16))
    placed = jnp.concatenate(placed, axis=0)
    centring = centring_ref[...]
    piece = min(512, keys)
    for r in range(0, keys, piece):
        normed = []
        for n in range(0, per_step, 2):
            x = jnp.concatenate([x_ref[n, r : r + piece], x_ref[n + 1, r : r + piece]], axis=1)
            centre = mm(x, centring)
            for part in (centre[:, :channels], centre[:, channels:]):
                spread = jnp.mean(part * part, axis=-1, keepdims=True)
                normed.append((part * lax.rsqrt(spread + EPS)).astype(BF16))
        added = mm(jnp.concatenate(normed, axis=1), placed)
        for n in range(tiles):
            acc_ref[n, r : r + piece, :] += added[:, n * 128 : (n + 1) * 128]

    @pl.when(step == pl.num_programs(0) - 1)
    def _():
        if not whole:
            for n in range(tiles):
                outs[0][n * 128 : (n + 1) * 128, :] = acc_ref[n].T.astype(BF16)
            return
        levels = keys // (2 * pieces * residues)
        for flip in range(2):
            user = me_ref[0] ^ flip
            starts = [
                (user ^ (c + 2 * q + 2 * pieces * k)) * residues + p
                for q in range(pieces)
                for p in range(2)
                for k in range(levels)
                for c in range(2)
            ]
            for n in range(tiles):
                for at in range(0, keys, 128):
                    rows = [
                        acc_ref[n, pl.ds(start, pairs, stride=2), :]
                        for start in starts[at // pairs : (at + 128) // pairs]
                    ]
                    turned = jnp.concatenate(rows, axis=0).T.astype(BF16)
                    outs[flip][n * 128 : (n + 1) * 128, at : at + 128] = turned


def order_kernel(residues, pieces, me_ref, bias_ref, own_ref, send_ref):
    rows, keys = bias_ref.shape
    pairs = residues // 2
    lane = iota((1, keys), 1)
    each = keys // pieces
    which, rest = lane // each, lane % each
    parity, rest = rest // (each // 2), rest % (each // 2)
    place, pair = rest // pairs, rest % pairs
    for flip, out_ref in enumerate((own_ref, send_ref)):
        device = me_ref[0] ^ flip ^ ((place % 2) + 2 * which + 2 * pieces * (place // 2))
        target = device * residues + 2 * pair + parity
        total = jnp.zeros((rows, keys), F32)
        for start in range(0, keys, 256):
            chosen = one_hot(iota((256, keys), 0) + start == target)
            total = total + mm(bias_ref[:, start : start + 256], chosen)
        out_ref[...] = total.astype(BF16)


def pair_matrix(matrix, chosen):
    rows, columns = matrix.shape
    lane = iota((1, 128), 1)
    twice_rows = one_hot(iota((128, 1), 0) % rows == iota((1, rows), 1))
    picked = one_hot(iota((columns, 1), 0) == chosen)
    wide = mm(mm(twice_rows, matrix).astype(BF16), picked)
    same = iota((128, 1), 0) // rows == lane // (128 // 2)
    return jnp.where(same, wide, 0.0).astype(BF16)


def value_matrix(matrix, hidden, heads):
    depth = hidden // heads
    row, col = iota((128, 1), 0), iota((1, 256), 1)
    picked = one_hot(iota((4 * hidden, 1), 0) == 2 * hidden + col % hidden)
    picked = jnp.where(col < 128, picked, jnp.zeros_like(picked))
    wv = mm(mm(one_hot(row == iota((1, hidden), 1)), matrix).astype(BF16), picked)
    counted = (row >= hidden) & (col >= 128)
    wv = jnp.where(counted, 1.0 / (128 - hidden), wv)
    owner = col % 128 // depth
    return [
        jnp.where(owner == p * heads + h, wv, 0.0).astype(BF16)
        for h in range(heads)
        for p in range(2)
    ]


def query_kernel(
    groups, size, pairs, heads, own_ref, peer_ref, keep_ref, received_ref, w_ref, exit_ref,
    column_ref, column_exit_ref, kept_ref, *refs
):
    column_refs = refs[:groups]
    bias_ref, lhs_ref, sums_ref, wv_ref, gate_ref, final_ref, kept_wide_ref = refs[groups:]
    rows = own_ref.shape[0]
    bias_ref[:rows, :] = own_ref[...].astype(F32) * LOG2E
    bias_ref[rows:, :] = peer_ref[...].astype(F32) * LOG2E

    hidden = w_ref.shape[0]
    depth = hidden // heads
    lane = iota((1, 128), 1)
    wq = pair_matrix(w_ref[...], lane % hidden)
    wg = pair_matrix(w_ref[...], 3 * hidden + lane % hidden)
    for n, part in enumerate(value_matrix(w_ref[...], hidden, heads)):
        wv_ref[n * 128 : (n + 1) * 128, :] = part
    final = [
        (exit_ref, lane % hidden),
        (column_exit_ref, lane % hidden),
        (column_ref, lane % hidden),
        (column_ref, hidden + lane % hidden),
        (column_ref, 2 * hidden + lane % depth),
        (column_ref, 2 * hidden + depth + lane % depth),
    ]
    for n, (ref, chosen) in enumerate(final):
        final_ref[:, n * 128 : (n + 1) * 128] = pair_matrix(ref[...], chosen)
    total, lines = kept_wide_ref.shape[0], kept_ref.shape[0]
    spread = mm(one_hot(iota((total, 1), 0) // pairs == iota((1, lines), 1)), kept_ref[...])
    mine = iota((1, 2 * pairs), 1) // 2 == iota((total, 1), 0) % pairs
    sides = one_hot(iota((2 * pairs, 1), 0) % 2 == lane // 64)
    kept_wide_ref[...] = mm(jnp.where(mine, spread, 0.0).astype(BF16), sides)
    picked = one_hot(iota((1, 4 * hidden), 1) == hidden + iota((128, 1), 0) % hidden)
    wk = mm_nt(picked, w_ref[...]).astype(BF16)
    wk = mm(wk, one_hot(iota((hidden, 1), 0) == iota((1, 128), 1))).astype(BF16)
    lead = size * pairs
    spare = lane - hidden
    for g in range(groups):
        for n, ref in enumerate((keep_ref, received_ref)):
            gate_ref[n, g * lead : (g + 1) * lead] = jax.nn.sigmoid(mm(ref[g, :lead], wg))
            query = (mm(ref[g, :lead], wq) * (depth**-0.5)).astype(BF16).astype(F32)
            for s in range(size):
                q = query[s * pairs : (s + 1) * pairs]
                spread = [
                    jnp.where(lane // depth == p * heads + h, q, 0.0).astype(BF16)
                    for h in range(heads)
                    for p in range(2)
                ]
                folded = mm(jnp.concatenate(spread, axis=0), wk) * LOG2E
                picks = (spare >= 0) & (spare < 4 * size) & (spare % size == s)
                lhs_ref[g * size + s, n * rows : (n + 1) * rows, :] = jnp.where(
                    picks, 1.0, folded
                ).astype(BF16)
    add_pieces(groups, size, pairs, (0,) * groups, lhs_ref, bias_ref, None, column_refs, sums_ref)


def masks_of(ref, size, pairs):
    start = 2 * size * pairs
    lane = iota((1, 128), 1) - 64
    masks = []
    for p in range(2):
        blocks = []
        for k in range(ref.shape[0]):
            hidden = (1e9 * LOG2E) * (ref[k, start : start + pairs, :].astype(F32) - 1.0)
            for c in range(2):
                first = (2 * c + p) * size
                mine = (lane >= first) & (lane < first + size)
                blocks.append(jnp.where(mine, hidden, 0.0).astype(BF16))
        masks.append(jnp.concatenate(blocks, axis=0))
    return masks


def keys_of(ref, masks, s, size, pairs):
    start = s * pairs
    if not isinstance(s, int):
        start = pl.multiple_of(start, pairs)
    even = jnp.concatenate(
        [
            ref[k, pl.ds(c * size * pairs + start, pairs), :]
            for k in range(ref.shape[0])
            for c in range(2)
        ],
        axis=0,
    )
    odd = pltpu.roll(even.astype(F32), 64, 1).astype(BF16)
    low = iota(even.shape, 1) < 64
    one = jnp.ones_like(even)
    keyed = [jnp.where(low, x, m) for x, m in zip((even, odd), masks)]
    valued = [jnp.where(low, x, one) for x in (even, odd)]
    return jnp.concatenate(keyed, axis=0), jnp.concatenate(valued, axis=0)


def weigh(lhs, bias_ref, piece, keyed):
    width = keyed.shape[0]
    logits = mm_nt(lhs, keyed) + bias_ref[:, piece * width : (piece + 1) * width]
    return jnp.exp2(logits).astype(BF16)


def each_line(groups, size, pairs, places, lhs_ref, bias_ref, piece_refs, use):
    masks = [masks_of(ref, size, pairs) for ref in piece_refs]

    def weights_of(s, g):
        keyed, valued = keys_of(piece_refs[g], masks[g], s, size, pairs)
        return weigh(lhs_ref[g * size + s], bias_ref, places[g], keyed), valued

    order = [(s, g) for s in range(size) for g in range(groups)]
    ahead = weights_of(*order[0])
    for n, (s, g) in enumerate(order):
        now, ahead = ahead, weights_of(*order[n + 1]) if n + 1 < len(order) else None
        use(g * size + s, mm(*now))


def add_pieces(groups, size, pairs, places, lhs_ref, bias_ref, before_ref, piece_refs, out_ref):
    def use(line, total):
        out_ref[line] = total if before_ref is None else before_ref[line] + total

    each_line(groups, size, pairs, places, lhs_ref, bias_ref, piece_refs, use)


def add_kernel(groups, size, pairs, places, lhs_ref, bias_ref, before_ref, *refs):
    add_pieces(
        groups, size, pairs, places, lhs_ref, bias_ref, before_ref, refs[:-1], refs[-1]
    )


def finish_kernel(
    heads, groups, size, pairs, place, lhs_ref, bias_ref, sums_ref, wv_ref, gate_ref, *refs
):
    piece_refs, far_refs = refs[:groups], refs[groups : 4 * groups]
    mine_ref, theirs_ref, turned_ref, range_ref, copy_ref = refs[4 * groups :]
    blocks = 2 * heads
    low = iota((lhs_ref.shape[1], 128), 1) < 64

    def settle(line, total):
        start = line * pairs
        if not isinstance(line, int):
            start = pl.multiple_of(start, pairs)
        total = total.astype(BF16)
        for n in range(2):
            for b in range(blocks):
                part = total[(n * blocks + b) * pairs : (n * blocks + b + 1) * pairs]
                turned_ref[n, pl.ds(start, pairs), b * 128 : (b + 1) * 128] = part

    lowest, highest = [], []

    def use(line, total):
        total = sums_ref[line] + total
        settle(line, total)
        weight = jnp.where(low, 1.0, total).reshape(-1, 8, 128)
        lowest.append(jnp.min(weight, axis=0))
        highest.append(jnp.max(weight, axis=0))

    each_line(groups, size, pairs, (place,) * groups, lhs_ref, bias_ref, piece_refs, use)
    range_ref[0] = functools.reduce(jnp.minimum, lowest)
    range_ref[1] = functools.reduce(jnp.maximum, highest)
    fine = (range_ref[0] > 2.0**-80) & (range_ref[1] < 2.0**100)

    @pl.when(jnp.min(jnp.where(fine, 1.0, 0.0)) < 0.5)
    def _():
        for n, ref in enumerate(far_refs):
            pltpu.sync_copy(ref, copy_ref.at[n])
        for g in range(groups):
            ordered = [copy_ref.at[n * groups + g] for n in range(3)] + [piece_refs[g]]
            all_masks = [masks_of(ref, size, pairs) for ref in ordered]

            def exact_line(s, carry):
                line = g * size + s
                both = [keys_of(r, m, s, size, pairs) for r, m in zip(ordered, all_masks)]
                logits = []
                for n, (keyed, _) in enumerate(both):
                    width = keyed.shape[0]
                    bias = bias_ref[:, n * width : (n + 1) * width]
                    logits.append(mm_nt(lhs_ref[line], keyed) + bias)
                peak = functools.reduce(jnp.maximum, logits)
                peak = jnp.max(peak, axis=-1, keepdims=True)
                parts = [
                    mm(jnp.exp2(part - peak).astype(BF16), valued)
                    for part, (_, valued) in zip(logits, both)
                ]
                settle(line, sum(parts[1:], parts[0]))
                return carry

            lax.fori_loop(0, size, exact_line, 0)

    lead = groups * size * pairs
    mixed = mm(turned_ref[...].reshape(2 * lead, blocks * 128), wv_ref[...])
    mixed = (mixed[:, :128] / mixed[:, 128:]).reshape(2, lead, 128)
    for n, out_ref in enumerate((mine_ref, theirs_ref)):
        out_ref[...] = (gate_ref[n] * mixed[n]).astype(BF16)


def final_kernel(
    lines, depth, with_column, me_ref, line_ref, kept_ref, w_ref, mine_ref, theirs_ref, out_ref,
    gated_ref,
):
    total = line_ref.shape[0]
    pairs = total // lines
    core = me_ref[0] % 2
    share = total // 2
    for owner, ref in ((core, mine_ref), (1 - core, theirs_ref)):
        gated_ref[pl.ds(pl.multiple_of(owner * share, share), share), :] = ref[...]
    row = (line_ref[...].astype(F32) + mm(gated_ref[...], w_ref[:, :128])).astype(BF16)
    if not with_column:
        out_ref[...] = row
        return
    kept = kept_ref[...]
    projected = mm(paired_norm(row, 64), w_ref[:, 256:])
    query, gate, key, value = [projected[:, 128 * n : 128 * (n + 1)] for n in range(4)]

    def grid(a):
        return a.reshape(lines, pairs, 128)

    count = jnp.maximum(jnp.sum(grid(kept), axis=0), 1.0)
    mean_query = jnp.sum(grid(kept * query), axis=0) / count * (depth**-0.5)
    same_head = block_matrix(128, depth, 1.0, 1.0)
    product = (mean_query[None] * grid(key)).reshape(total, 128)
    logits = grid(mm_split(product, same_head) + 1e9 * (kept - 1.0))
    exped = jnp.exp(logits - jnp.max(logits, axis=0, keepdims=True))
    mixed = jnp.sum(exped * grid(value), axis=0) / jnp.sum(exped, axis=0)
    gated = (jax.nn.sigmoid(grid(gate)) * mixed[None]).reshape(total, 128).astype(BF16)
    result = (row.astype(F32) + mm(gated, w_ref[:, 128:256])).astype(BF16)
    shuffled = row_shuffle(result, lines, pairs)
    for t in range(pairs):
        out_ref[:, t * 128 : (t + 1) * 128] = shuffled[t * lines : (t + 1) * lines, :]


def call(kernel, out_shape, *args, **options):
    flops = options.pop("flops", 0)
    limit = pltpu.CompilerParams(vmem_limit_bytes=options.pop("mib", 8) * 1024 * 1024)
    moved = sum(a.size * a.dtype.itemsize for a in args)
    cost = pl.CostEstimate(flops=flops, bytes_accessed=moved, transcendentals=0)
    return pl.pallas_call(
        kernel, out_shape=out_shape, compiler_params=limit, cost_estimate=cost, **options
    )(*args)


def shape(*dims, dtype=BF16):
    return jax.ShapeDtypeStruct(dims, dtype)


def exchange(x, flip, devices):
    return lax.ppermute(x, "res", [(d, d ^ flip) for d in range(devices)])


def layer_normalize(values_in):
    centre = values_in - jnp.mean(values_in, axis=-1, keepdims=True)
    spread = jnp.mean(centre * centre, axis=-1, keepdims=True)
    return centre * lax.rsqrt(spread + EPS)


def column_complete(line, kept, vertical_matrix, vertical_exit_matrix, heads, depth):
    lines, columns, features = line.shape
    hidden = heads * depth
    normed = layer_normalize(line.astype(F32)).astype(BF16)
    projected = mm(normed.reshape(-1, features), vertical_matrix).reshape(lines, columns, -1)
    query, gate = projected[..., :hidden], projected[..., hidden : 2 * hidden]
    key = projected[..., 2 * hidden : 2 * hidden + depth]
    value = projected[..., 2 * hidden + depth :]
    count = jnp.maximum(jnp.sum(kept, axis=0), 1.0)[:, None]
    mean_query = jnp.sum(kept[..., None] * query, axis=0) / count * depth**-0.5
    logits = jnp.einsum("ihc,sic->sih", mean_query.reshape(columns, heads, depth), key)
    logits = logits + 1e9 * (kept - 1.0)[..., None]
    exped = jnp.exp(logits - jnp.max(logits, axis=0, keepdims=True))
    mixed = jnp.einsum("sih,sic->ihc", exped, value) / jnp.sum(exped, axis=0)[..., None]
    gate = jax.nn.sigmoid(gate).reshape(lines, columns, heads, depth)
    gated = (gate * mixed[None]).reshape(-1, hidden).astype(BF16)
    update = mm(gated, vertical_exit_matrix).reshape(lines, columns, features)
    return (line.astype(F32) + update).astype(BF16)


def on_device(
    seq_size,
    res_size,
    extra_activations,
    pair,
    present,
    amino,
    offset_matrix,
    horizontal_matrix,
    horizontal_exit_matrix,
    vertical_matrix,
    vertical_exit_matrix,
):
    lines, residues = present.shape
    pairs = residues // 2
    hidden = horizontal_exit_matrix.shape[0]
    heads = offset_matrix.shape[1]
    depth = hidden // heads
    groups = 2
    size = lines // (2 * groups)
    lead = size * pairs
    keys = res_size * residues
    rows = residues * heads
    core_bit, near, far, high = 1, 2, 4, 8
    kept = (present * amino[None, :]).astype(BF16)
    me = lax.axis_index("res").astype(jnp.int32).reshape(1)
    smem = pl.BlockSpec(memory_space=pltpu.SMEM)
    vmem = pl.BlockSpec(memory_space=pltpu.VMEM)

    rest = lead + pairs
    keep, send, line = call(
        functools.partial(prep_kernel, groups),
        [shape(groups, rest, 128)] * 2 + [shape(lines * pairs, 128)],
        me,
        extra_activations,
        kept,
        in_specs=[smem, vmem, vmem],
        scratch_shapes=[
            pltpu.VMEM((lines * pairs, 128), BF16),
            pltpu.VMEM((2 * groups, pairs, 128), BF16),
        ],
    )

    received = exchange(send, core_bit, res_size)
    chunk = jnp.concatenate(
        [keep[:, :lead], received[:, :lead], keep[:, lead:] + received[:, lead:]], axis=1
    )
    levels = [chunk] + [exchange(chunk, high * k, res_size) for k in range(1, res_size // high)]
    own = [jnp.stack([level[g] for level in levels]) for g in range(groups)]
    beside = [exchange(part, near, res_size) for part in own]
    across = [exchange(part, far, res_size) for part in own]

    per_step = 8
    pieces = 4
    whole = seq_size == 1
    bias_rows = [shape(rows, keys)] * 2
    bias = call(
        functools.partial(bias_kernel, whole, pieces),
        bias_rows if whole else [shape(rows, pair.shape[1])],
        pair,
        offset_matrix.T,
        chunk,
        me,
        grid=(residues // per_step,),
        in_specs=[
            pl.BlockSpec((per_step,) + pair.shape[1:], lambda n: (n, 0, 0)),
            pl.BlockSpec(offset_matrix.shape[::-1], lambda n: (0, 0)),
            pl.BlockSpec(memory_space=pl.ANY),
            smem,
        ],
        out_specs=[pl.BlockSpec((rows, pair.shape[1]), lambda n: (0, 0))] * (1 + whole),
        scratch_shapes=[
            pltpu.VMEM((rows // 128, pair.shape[1], 128), F32),
            pltpu.VMEM((2 * pair.shape[2], 2 * pair.shape[2]), BF16),
            pltpu.VMEM((pair.shape[2], rows), F32),
        ],
        flops=16 * pair.size * 128,
        mib=57,
    )
    if not whole:
        bias = call(
            functools.partial(order_kernel, residues, pieces),
            bias_rows,
            me,
            lax.all_gather(bias[0], "seq", axis=1, tiled=True),
            in_specs=[smem, vmem],
            mib=14,
        )
    bias, lhs, sums, wv, gate, w_final, kept_wide = call(
        functools.partial(query_kernel, groups, size, pairs, heads),
        [
            shape(2 * rows, keys, dtype=F32),
            shape(groups * size, 2 * rows, 128),
            shape(groups * size, 2 * rows, 128, dtype=F32),
            shape(2 * heads * 128, 256),
            shape(2, groups * lead, 128, dtype=F32),
            shape(128, 6 * 128),
            shape(lines * pairs, 128, dtype=F32),
        ],
        bias[0],
        exchange(bias[1], core_bit, res_size),
        keep,
        received,
        horizontal_matrix,
        horizontal_exit_matrix,
        vertical_matrix,
        vertical_exit_matrix,
        kept,
        *own,
        in_specs=[vmem] * (9 + groups),
        flops=8 * rows * keys * keys,
        mib=20,
    )

    def add(sums, places, parts):
        return call(
            functools.partial(add_kernel, groups, size, pairs, places),
            shape(*sums.shape, dtype=F32),
            lhs,
            bias,
            sums,
            *parts,
            flops=groups * size * rows * keys * 2 * 256 * 2,
            mib=20,
        )

    beside[0], across[1], sums = lax.optimization_barrier((beside[0], across[1], sums))
    corner = [
        exchange(beside[g], far, res_size) if g % 2 == 0 else exchange(across[g], near, res_size)
        for g in range(groups)
    ]
    sums = add(sums, (1, 2), (beside[0], across[1]))
    beside[1], across[0], sums = lax.optimization_barrier((beside[1], across[0], sums))
    sums = add(sums, (2, 1), (across[0], beside[1]))
    corner[0], corner[1], sums = lax.optimization_barrier((corner[0], corner[1], sums))
    anywhere = pl.BlockSpec(memory_space=pl.ANY)
    mine, theirs = call(
        functools.partial(finish_kernel, heads, groups, size, pairs, 3),
        [shape(groups * lead, 128)] * 2,
        lhs,
        bias,
        sums,
        wv,
        gate,
        *corner,
        *own,
        *beside,
        *across,
        in_specs=[vmem] * (5 + groups) + [anywhere] * (3 * groups),
        scratch_shapes=[
            pltpu.VMEM((2, groups * lead, 128 * 2 * heads), BF16),
            pltpu.VMEM((2, 8, 128), F32),
            pltpu.VMEM((3 * groups,) + own[0].shape, BF16),
        ],
        flops=groups * size * rows * keys * 2 * 256,
        mib=24,
    )
    returned = exchange(theirs, core_bit, res_size)
    with_column = seq_size == 1
    final_args = [
        me,
        line,
        kept_wide,
        w_final,
    ]
    final_args += [mine, returned]
    result = call(
        functools.partial(final_kernel, lines, depth, with_column),
        shape(*extra_activations.shape) if with_column else shape(lines * pairs, 128),
        *final_args,
        in_specs=[smem] + [vmem] * (len(final_args) - 1),
        scratch_shapes=[pltpu.VMEM((lines * pairs, 128), BF16)],
    )
    if with_column:
        return result
    row = result.reshape(lines, residues, hidden)
    moved = lax.all_to_all(row, "seq", split_axis=1, concat_axis=0, tiled=True)
    moved_kept = lax.all_to_all(kept, "seq", split_axis=1, concat_axis=0, tiled=True)
    updated = column_complete(
        moved, moved_kept.astype(F32), vertical_matrix, vertical_exit_matrix, heads, depth
    )
    back = lax.all_to_all(updated, "seq", split_axis=0, concat_axis=1, tiled=True)
    return back.reshape(extra_activations.shape)


def solution(mesh):
    in_specs = (
        P("seq", "res"),
        P("res", "seq", None),
        P("seq", "res"),
        P("res"),
        P(),
        P(),
        P(),
        P(),
        P(),
    )
    sizes = mesh.shape
    return jax.shard_map(
        functools.partial(on_device, sizes["seq"], sizes["res"]),
        mesh=mesh,
        in_specs=in_specs,
        out_specs=P("seq", "res"),
        check_vma=False,
    )
```

```python
import functools
import math

import jax
import jax.numpy as jnp
from jax import lax
from jax.experimental import pallas as pl
from jax.experimental.pallas import tpu as pltpu
from jax.sharding import PartitionSpec as P

F32 = jnp.float32
BF16 = jnp.bfloat16
LOG2E = math.log2(math.e)
EPS = 1e-05

NT = (((1,), (1,)), ((), ()))


def mm(a, b):
    return jnp.dot(a, b, preferred_element_type=F32)


def mm_nt(a, b):
    return lax.dot_general(a, b, NT, preferred_element_type=F32)


def iota(shape, axis):
    return lax.broadcasted_iota(jnp.int32, shape, axis)


def one_hot(condition):
    return jnp.where(condition, 1.0, 0.0).astype(BF16)


def block_matrix(size, block, on_diagonal, elsewhere):
    row, col = iota((size, 1), 0), iota((1, size), 1)
    inside = jnp.where(row == col, on_diagonal, elsewhere)
    return jnp.where(row // block == col // block, inside, 0.0).astype(BF16)


def halves(value):
    high = value.astype(BF16)
    return high, (value - high.astype(F32)).astype(BF16)


def mm_split(value, matrix):
    high, low = halves(value)
    return mm(high, matrix) + mm(low, matrix)


def paired_norm(x, width):
    lanes = x.shape[1]
    centre = mm(x, block_matrix(lanes, width, 1.0 - 1.0 / width, -1.0 / width))
    spread = mm_split(centre * centre, block_matrix(lanes, width, 1.0 / width, 1.0 / width))
    return (centre * lax.rsqrt(spread + EPS)).astype(BF16)


def row_shuffle(rows, inner, outer):
    total = rows.shape[0]
    row, col = iota((total, 1), 0), iota((1, total), 1)
    return mm(one_hot(col == (row % inner) * outer + row // inner), rows).astype(BF16)


def prep_kernel(groups, me_ref, m_ref, kept_ref, *refs):
    keep_ref, send_ref, line_ref, normed_ref, spread_ref = refs
    lines, width = m_ref.shape
    pairs = width // 128
    stacked = jnp.concatenate([m_ref[:, t * 128 : (t + 1) * 128] for t in range(pairs)], axis=0)
    normed = paired_norm(stacked, 64)
    both = row_shuffle(jnp.concatenate([normed, stacked], axis=1), pairs, lines)
    normed_ref[...] = both[:, :128]
    line_ref[...] = both[:, 128:]
    kept = kept_ref[...]
    size = lines // (2 * groups)
    residues = 2 * pairs
    row, col = iota((pairs, residues), 0), iota((pairs, residues), 1)
    evens, odds = one_hot(col == 2 * row), one_hot(col == 2 * row + 1)
    row, col = iota((128, lines), 0) - 64, iota((128, lines), 1)
    core = me_ref[0] % 2
    for n in range(2 * groups):
        start = jnp.where(n // groups == core, 0, 2 * size)
        chosen = (row >= start) & (row < start + 2 * size) & (row % size == col - n * size)
        spread = mm(one_hot(chosen), kept).astype(BF16)
        first = iota((pairs, 128), 1) < 64 + size + start
        spread_ref[n] = jnp.where(first, mm_nt(evens, spread), mm_nt(odds, spread)).astype(BF16)
    rows = size * pairs
    for ref, half in ((keep_ref, core), (send_ref, 1 - core)):
        for g in range(groups):
            index = half * groups + g
            ref[g, :rows] = normed_ref[pl.ds(pl.multiple_of(index * rows, rows), rows), :]
            ref[g, rows:] = spread_ref[index]


def bias_kernel(whole, pieces, residues, x_ref, w_ref, after_ref, me_ref, *refs):
    outs, (acc_ref, centring_ref, wide_ref) = refs[:-3], refs[-3:]
    step = pl.program_id(0)
    heads = w_ref.shape[0]
    per_step, _, keys, channels = x_ref.shape
    pairs = residues // 2
    tiles = acc_ref.shape[0]
    width = tiles * 128

    @pl.when(step == 0)
    def _():
        centring_ref[...] = block_matrix(
            2 * channels, channels, 1.0 - 1.0 / channels, -1.0 / channels
        )
        spread = one_hot(iota((heads, 1), 0) == iota((1, width), 1) // pairs)
        wide_ref[...] = lax.dot_general(
            w_ref[...], spread, (((0,), (0,)), ((), ())), preferred_element_type=F32
        )
        acc_ref[...] = jnp.zeros(acc_ref.shape, F32)

    lane = iota((1, width), 1) % pairs
    placed = []
    for n in range(per_step):
        mine = lane == step * per_step + n
        placed.append(jnp.where(mine, wide_ref[...], 0.0).astype(BF16))
    placed = jnp.concatenate(placed, axis=0)
    centring = centring_ref[...]
    piece = min(512, keys)
    for r in range(0, keys, piece):
        normed = []
        for n in range(0, per_step, 2):
            x = jnp.concatenate(
                [x_ref[n, 0, r : r + piece], x_ref[n + 1, 0, r : r + piece]], axis=1
            )
            centre = mm(x, centring)
            for part in (centre[:, :channels], centre[:, channels:]):
                spread = jnp.mean(part * part, axis=-1, keepdims=True)
                normed.append((part * lax.rsqrt(spread + EPS)).astype(BF16))
        added = mm(jnp.concatenate(normed, axis=1), placed)
        for n in range(tiles):
            acc_ref[n, r : r + piece, :] += added[:, n * 128 : (n + 1) * 128]

    @pl.when(step == pl.num_programs(0) - 1)
    def _():
        if not whole:
            for n in range(tiles):
                outs[0][n * 128 : (n + 1) * 128, :] = acc_ref[n].T.astype(BF16)
            return
        levels = keys // (2 * pieces * residues)
        for flip in range(2):
            user = me_ref[0] ^ flip
            starts = [
                (user ^ (c + 2 * q + 2 * pieces * k)) * residues + p
                for q in range(pieces)
                for p in range(2)
                for k in range(levels)
                for c in range(2)
            ]
            for n in range(tiles):
                for at in range(0, keys, 128):
                    rows = [
                        acc_ref[n, pl.ds(start, pairs, stride=2), :]
                        for start in starts[at // pairs : (at + 128) // pairs]
                    ]
                    turned = jnp.concatenate(rows, axis=0).T.astype(BF16)
                    outs[flip][n * 128 : (n + 1) * 128, at : at + 128] = turned


def order_kernel(residues, pieces, me_ref, bias_ref, own_ref, send_ref):
    rows, keys = bias_ref.shape
    pairs = residues // 2
    lane = iota((1, keys), 1)
    each = keys // pieces
    which, rest = lane // each, lane % each
    parity, rest = rest // (each // 2), rest % (each // 2)
    place, pair = rest // pairs, rest % pairs
    for flip, out_ref in enumerate((own_ref, send_ref)):
        device = me_ref[0] ^ flip ^ ((place % 2) + 2 * which + 2 * pieces * (place // 2))
        target = device * residues + 2 * pair + parity
        total = jnp.zeros((rows, keys), F32)
        for start in range(0, keys, 256):
            chosen = one_hot(iota((256, keys), 0) + start == target)
            total = total + mm(bias_ref[:, start : start + 256], chosen)
        out_ref[...] = total.astype(BF16)


def pair_matrix(matrix, chosen):
    rows, columns = matrix.shape
    lane = iota((1, 128), 1)
    twice_rows = one_hot(iota((128, 1), 0) % rows == iota((1, rows), 1))
    picked = one_hot(iota((columns, 1), 0) == chosen)
    wide = mm(mm(twice_rows, matrix).astype(BF16), picked)
    same = iota((128, 1), 0) // rows == lane // (128 // 2)
    return jnp.where(same, wide, 0.0).astype(BF16)


def value_matrix(matrix, hidden, heads):
    depth = hidden // heads
    row, col = iota((128, 1), 0), iota((1, 256), 1)
    picked = one_hot(iota((4 * hidden, 1), 0) == 2 * hidden + col % hidden)
    picked = jnp.where(col < 128, picked, jnp.zeros_like(picked))
    wv = mm(mm(one_hot(row == iota((1, hidden), 1)), matrix).astype(BF16), picked)
    counted = (row >= hidden) & (col >= 128)
    wv = jnp.where(counted, 1.0 / (128 - hidden), wv)
    owner = col % 128 // depth
    return [
        jnp.where(owner == p * heads + h, wv, 0.0).astype(BF16)
        for p in range(2)
        for h in range(heads)
    ]


def query_kernel(
    groups, size, pairs, heads, even_ref, odd_ref, peer_even_ref, peer_odd_ref, keep_ref,
    received_ref, w_ref, exit_ref, column_ref, column_exit_ref, kept_ref, *refs
):
    column_refs = refs[:groups]
    bias_ref, lhs_ref, sums_ref, wv_ref, gate_ref, final_ref, kept_wide_ref = refs[groups:]
    rows = 2 * even_ref.shape[0]
    for n, ref in enumerate((even_ref, odd_ref, peer_even_ref, peer_odd_ref)):
        at = slice(n * rows // 2, (n + 1) * rows // 2)
        bias_ref[at, :] = ref[...].astype(F32) * LOG2E

    hidden = w_ref.shape[0]
    depth = hidden // heads
    lane = iota((1, 128), 1)
    wq = pair_matrix(w_ref[...], lane % hidden)
    wg = pair_matrix(w_ref[...], 3 * hidden + lane % hidden)
    for n, part in enumerate(value_matrix(w_ref[...], hidden, heads)):
        wv_ref[n * 128 : (n + 1) * 128, :] = part
    final = [
        (exit_ref, lane % hidden),
        (column_exit_ref, lane % hidden),
        (column_ref, lane % hidden),
        (column_ref, hidden + lane % hidden),
        (column_ref, 2 * hidden + lane % depth),
        (column_ref, 2 * hidden + depth + lane % depth),
    ]
    for n, (ref, chosen) in enumerate(final):
        final_ref[:, n * 128 : (n + 1) * 128] = pair_matrix(ref[...], chosen)
    total, lines = kept_wide_ref.shape[0], kept_ref.shape[0]
    spread = mm(one_hot(iota((total, 1), 0) // pairs == iota((1, lines), 1)), kept_ref[...])
    mine = iota((1, 2 * pairs), 1) // 2 == iota((total, 1), 0) % pairs
    sides = one_hot(iota((2 * pairs, 1), 0) % 2 == lane // 64)
    kept_wide_ref[...] = mm(jnp.where(mine, spread, 0.0).astype(BF16), sides)
    picked = one_hot(iota((1, 4 * hidden), 1) == hidden + iota((128, 1), 0) % hidden)
    wk = mm_nt(picked, w_ref[...]).astype(BF16)
    wk = mm(wk, one_hot(iota((hidden, 1), 0) == iota((1, 128), 1))).astype(BF16)
    lead = size * pairs
    spare = lane - hidden
    for g in range(groups):
        for n, ref in enumerate((keep_ref, received_ref)):
            gate_ref[n, g * lead : (g + 1) * lead] = jax.nn.sigmoid(mm(ref[g, :lead], wg))
            query = (mm(ref[g, :lead], wq) * (depth**-0.5)).astype(BF16).astype(F32)
            for s in range(size):
                q = query[s * pairs : (s + 1) * pairs]
                spread = [
                    jnp.where(lane // depth == p * heads + h, q, 0.0).astype(BF16)
                    for p in range(2)
                    for h in range(heads)
                ]
                folded = mm(jnp.concatenate(spread, axis=0), wk) * LOG2E
                picks = (spare >= 0) & (spare < 4 * size) & (spare % size == s)
                lhs_ref[g * size + s, n * rows : (n + 1) * rows, :] = jnp.where(
                    picks, 1.0, folded
                ).astype(BF16)
    add_pieces(groups, size, pairs, (0,) * groups, lhs_ref, bias_ref, None, column_refs, sums_ref)


def masks_of(ref, size, pairs):
    start = 2 * size * pairs
    lane = iota((1, 128), 1) - 64
    masks = []
    for p in range(2):
        blocks = []
        for k in range(ref.shape[0]):
            hidden = (1e9 * LOG2E) * (ref[k, start : start + pairs, :].astype(F32) - 1.0)
            for c in range(2):
                first = (2 * c + p) * size
                mine = (lane >= first) & (lane < first + size)
                blocks.append(jnp.where(mine, hidden, 0.0).astype(BF16))
        masks.append(jnp.concatenate(blocks, axis=0))
    return masks


def keys_of(ref, masks, s, size, pairs):
    start = s * pairs
    if not isinstance(s, int):
        start = pl.multiple_of(start, pairs)
    even = jnp.concatenate(
        [
            ref[k, pl.ds(c * size * pairs + start, pairs), :]
            for k in range(ref.shape[0])
            for c in range(2)
        ],
        axis=0,
    )
    odd = pltpu.roll(even.astype(F32), 64, 1).astype(BF16)
    low = iota(even.shape, 1) < 64
    one = jnp.ones_like(even)
    keyed = [jnp.where(low, x, m) for x, m in zip((even, odd), masks)]
    valued = [jnp.where(low, x, one) for x in (even, odd)]
    return jnp.concatenate(keyed, axis=0), jnp.concatenate(valued, axis=0)


def weigh(lhs, bias_ref, piece, keyed):
    width = keyed.shape[0]
    logits = mm_nt(lhs, keyed) + bias_ref[:, piece * width : (piece + 1) * width]
    return jnp.exp2(logits).astype(BF16)


def each_line(groups, size, pairs, places, lhs_ref, bias_ref, piece_refs, use):
    masks = [masks_of(ref, size, pairs) for ref in piece_refs]

    def weights_of(s, g):
        keyed, valued = keys_of(piece_refs[g], masks[g], s, size, pairs)
        return weigh(lhs_ref[g * size + s], bias_ref, places[g], keyed), valued

    order = [(s, g) for s in range(size) for g in range(groups)]
    ahead = weights_of(*order[0])
    for n, (s, g) in enumerate(order):
        now, ahead = ahead, weights_of(*order[n + 1]) if n + 1 < len(order) else None
        use(g * size + s, mm(*now))


def add_pieces(groups, size, pairs, places, lhs_ref, bias_ref, before_ref, piece_refs, out_ref):
    def use(line, total):
        out_ref[line] = total if before_ref is None else before_ref[line] + total

    each_line(groups, size, pairs, places, lhs_ref, bias_ref, piece_refs, use)


def add_kernel(groups, size, pairs, places, lhs_ref, bias_ref, before_ref, *refs):
    add_pieces(
        groups, size, pairs, places, lhs_ref, bias_ref, before_ref, refs[:-1], refs[-1]
    )


def finish_kernel(
    heads, groups, size, pairs, place, lhs_ref, bias_ref, sums_ref, wv_ref, gate_ref, *refs
):
    piece_refs, far_refs = refs[:groups], refs[groups : 4 * groups]
    mine_ref, theirs_ref, turned_ref, range_ref, copy_ref = refs[4 * groups :]
    blocks = 2 * heads
    low = iota((lhs_ref.shape[1], 128), 1) < 64

    def settle(line, total):
        start = line * pairs
        if not isinstance(line, int):
            start = pl.multiple_of(start, pairs)
        total = total.astype(BF16)
        for n in range(2):
            for b in range(blocks):
                part = total[(n * blocks + b) * pairs : (n * blocks + b + 1) * pairs]
                turned_ref[n, pl.ds(start, pairs), b * 128 : (b + 1) * 128] = part

    lowest, highest = [], []

    def use(line, total):
        total = sums_ref[line] + total
        settle(line, total)
        weight = jnp.where(low, 1.0, total).reshape(-1, 8, 128)
        lowest.append(jnp.min(weight, axis=0))
        highest.append(jnp.max(weight, axis=0))

    each_line(groups, size, pairs, (place,) * groups, lhs_ref, bias_ref, piece_refs, use)
    range_ref[0] = functools.reduce(jnp.minimum, lowest)
    range_ref[1] = functools.reduce(jnp.maximum, highest)
    fine = (range_ref[0] > 2.0**-80) & (range_ref[1] < 2.0**100)

    @pl.when(jnp.min(jnp.where(fine, 1.0, 0.0)) < 0.5)
    def _():
        for n, ref in enumerate(far_refs):
            pltpu.sync_copy(ref, copy_ref.at[n])
        for g in range(groups):
            ordered = [copy_ref.at[n * groups + g] for n in range(3)] + [piece_refs[g]]
            all_masks = [masks_of(ref, size, pairs) for ref in ordered]

            def exact_line(s, carry):
                line = g * size + s
                both = [keys_of(r, m, s, size, pairs) for r, m in zip(ordered, all_masks)]
                logits = []
                for n, (keyed, _) in enumerate(both):
                    width = keyed.shape[0]
                    bias = bias_ref[:, n * width : (n + 1) * width]
                    logits.append(mm_nt(lhs_ref[line], keyed) + bias)
                peak = functools.reduce(jnp.maximum, logits)
                peak = jnp.max(peak, axis=-1, keepdims=True)
                parts = [
                    mm(jnp.exp2(part - peak).astype(BF16), valued)
                    for part, (_, valued) in zip(logits, both)
                ]
                settle(line, sum(parts[1:], parts[0]))
                return carry

            lax.fori_loop(0, size, exact_line, 0)

    lead = groups * size * pairs
    mixed = mm(turned_ref[...].reshape(2 * lead, blocks * 128), wv_ref[...])
    mixed = (mixed[:, :128] / mixed[:, 128:]).reshape(2, lead, 128)
    for n, out_ref in enumerate((mine_ref, theirs_ref)):
        out_ref[...] = (gate_ref[n] * mixed[n]).astype(BF16)


def final_kernel(
    lines, depth, with_column, me_ref, line_ref, kept_ref, w_ref, mine_ref, theirs_ref, out_ref,
    gated_ref,
):
    total = line_ref.shape[0]
    pairs = total // lines
    core = me_ref[0] % 2
    share = total // 2
    for owner, ref in ((core, mine_ref), (1 - core, theirs_ref)):
        gated_ref[pl.ds(pl.multiple_of(owner * share, share), share), :] = ref[...]
    row = (line_ref[...].astype(F32) + mm(gated_ref[...], w_ref[:, :128])).astype(BF16)
    if not with_column:
        out_ref[...] = row
        return
    kept = kept_ref[...]
    projected = mm(paired_norm(row, 64), w_ref[:, 256:])
    query, gate, key, value = [projected[:, 128 * n : 128 * (n + 1)] for n in range(4)]

    def grid(a):
        return a.reshape(lines, pairs, 128)

    count = jnp.maximum(jnp.sum(grid(kept), axis=0), 1.0)
    mean_query = jnp.sum(grid(kept * query), axis=0) / count * (depth**-0.5)
    same_head = block_matrix(128, depth, 1.0, 1.0)
    product = (mean_query[None] * grid(key)).reshape(total, 128)
    logits = grid(mm_split(product, same_head) + 1e9 * (kept - 1.0))
    exped = jnp.exp(logits - jnp.max(logits, axis=0, keepdims=True))
    mixed = jnp.sum(exped * grid(value), axis=0) / jnp.sum(exped, axis=0)
    gated = (jax.nn.sigmoid(grid(gate)) * mixed[None]).reshape(total, 128).astype(BF16)
    result = (row.astype(F32) + mm(gated, w_ref[:, 128:256])).astype(BF16)
    shuffled = row_shuffle(result, lines, pairs)
    for t in range(pairs):
        out_ref[:, t * 128 : (t + 1) * 128] = shuffled[t * lines : (t + 1) * lines, :]


def call(kernel, out_shape, *args, **options):
    flops = options.pop("flops", 0)
    limit = pltpu.CompilerParams(vmem_limit_bytes=options.pop("mib", 8) * 1024 * 1024)
    moved = options.pop("moved", sum(a.size * a.dtype.itemsize for a in args))
    cost = pl.CostEstimate(flops=flops, bytes_accessed=moved, transcendentals=0)
    return pl.pallas_call(
        kernel, out_shape=out_shape, compiler_params=limit, cost_estimate=cost, **options
    )(*args)


def shape(*dims, dtype=BF16):
    return jax.ShapeDtypeStruct(dims, dtype)


def exchange(x, flip, devices):
    return lax.ppermute(x, "res", [(d, d ^ flip) for d in range(devices)])


def layer_normalize(values_in):
    centre = values_in - jnp.mean(values_in, axis=-1, keepdims=True)
    spread = jnp.mean(centre * centre, axis=-1, keepdims=True)
    return centre * lax.rsqrt(spread + EPS)


def column_complete(line, kept, vertical_matrix, vertical_exit_matrix, heads, depth):
    lines, columns, features = line.shape
    hidden = heads * depth
    normed = layer_normalize(line.astype(F32)).astype(BF16)
    projected = mm(normed.reshape(-1, features), vertical_matrix).reshape(lines, columns, -1)
    query, gate = projected[..., :hidden], projected[..., hidden : 2 * hidden]
    key = projected[..., 2 * hidden : 2 * hidden + depth]
    value = projected[..., 2 * hidden + depth :]
    count = jnp.maximum(jnp.sum(kept, axis=0), 1.0)[:, None]
    mean_query = jnp.sum(kept[..., None] * query, axis=0) / count * depth**-0.5
    logits = jnp.einsum("ihc,sic->sih", mean_query.reshape(columns, heads, depth), key)
    logits = logits + 1e9 * (kept - 1.0)[..., None]
    exped = jnp.exp(logits - jnp.max(logits, axis=0, keepdims=True))
    mixed = jnp.einsum("sih,sic->ihc", exped, value) / jnp.sum(exped, axis=0)[..., None]
    gate = jax.nn.sigmoid(gate).reshape(lines, columns, heads, depth)
    gated = (gate * mixed[None]).reshape(-1, hidden).astype(BF16)
    update = mm(gated, vertical_exit_matrix).reshape(lines, columns, features)
    return (line.astype(F32) + update).astype(BF16)


def on_device(
    seq_size,
    res_size,
    extra_activations,
    pair,
    present,
    amino,
    offset_matrix,
    horizontal_matrix,
    horizontal_exit_matrix,
    vertical_matrix,
    vertical_exit_matrix,
):
    lines, residues = present.shape
    pairs = residues // 2
    hidden = horizontal_exit_matrix.shape[0]
    heads = offset_matrix.shape[1]
    depth = hidden // heads
    groups = 2
    size = lines // (2 * groups)
    lead = size * pairs
    keys = res_size * residues
    rows = residues * heads
    core_bit, near, far, high = 1, 2, 4, 8
    kept = (present * amino[None, :]).astype(BF16)
    me = lax.axis_index("res").astype(jnp.int32).reshape(1)
    smem = pl.BlockSpec(memory_space=pltpu.SMEM)
    vmem = pl.BlockSpec(memory_space=pltpu.VMEM)

    rest = lead + pairs
    keep, send, line = call(
        functools.partial(prep_kernel, groups),
        [shape(groups, rest, 128)] * 2 + [shape(lines * pairs, 128)],
        me,
        extra_activations,
        kept,
        in_specs=[smem, vmem, vmem],
        scratch_shapes=[
            pltpu.VMEM((lines * pairs, 128), BF16),
            pltpu.VMEM((2 * groups, pairs, 128), BF16),
        ],
    )

    received = exchange(send, core_bit, res_size)
    chunks = [
        jnp.concatenate([keep[g, :lead], received[g, :lead], keep[g, lead:] + received[g, lead:]])
        for g in range(groups)
    ]

    per_step = 8
    pieces = 4
    whole = seq_size == 1
    by_parity = pair.reshape((residues // 2, 2) + pair.shape[1:])

    def bias_of(parity, after):
        return call(
            functools.partial(bias_kernel, whole, pieces, residues),
            [shape(rows // 2, pair.shape[1])] * (1 + whole),
            by_parity,
            offset_matrix.T,
            after,
            me,
            grid=(residues // 2 // per_step,),
            in_specs=[
                pl.BlockSpec((per_step, 1) + pair.shape[1:], lambda n: (n, parity, 0, 0)),
                pl.BlockSpec(offset_matrix.shape[::-1], lambda n: (0, 0)),
                pl.BlockSpec(memory_space=pl.ANY),
                smem,
            ],
            out_specs=[pl.BlockSpec((rows // 2, pair.shape[1]), lambda n: (0, 0))] * (1 + whole),
            scratch_shapes=[
                pltpu.VMEM((rows // 256, pair.shape[1], 128), F32),
                pltpu.VMEM((2 * pair.shape[2], 2 * pair.shape[2]), BF16),
                pltpu.VMEM((pair.shape[2], rows // 2), F32),
            ],
            flops=8 * pair.size * 128,
            mib=48,
        )

    def levels_of(chunk):
        return [chunk] + [exchange(chunk, high * k, res_size) for k in range(1, res_size // high)]

    levels = levels_of(chunks[0])
    bias = [bias_of(0, chunks[0])]
    levels, bias[0] = lax.optimization_barrier((levels, bias[0]))
    own = [jnp.stack(levels)]
    own[0], later = lax.optimization_barrier((own[0], chunks[1]))
    beside, across = [exchange(own[0], near, res_size)], [exchange(own[0], far, res_size)]
    levels = levels_of(later)
    bias.append(bias_of(1, own[0]))
    levels, bias[1] = lax.optimization_barrier((levels, bias[1]))
    own.append(jnp.stack(levels))
    across.append(exchange(own[1], far, res_size))
    beside.append(exchange(own[1], near, res_size))
    if not whole:
        bias = [
            call(
                functools.partial(order_kernel, residues, pieces),
                [shape(rows // 2, keys)] * 2,
                me,
                lax.all_gather(part[0], "seq", axis=1, tiled=True),
                in_specs=[smem, vmem],
                mib=14,
            )
            for part in bias
        ]
    bias, lhs, sums, wv, gate, w_final, kept_wide = call(
        functools.partial(query_kernel, groups, size, pairs, heads),
        [
            shape(2 * rows, keys, dtype=F32),
            shape(groups * size, 2 * rows, 128),
            shape(groups * size, 2 * rows, 128, dtype=F32),
            shape(2 * heads * 128, 256),
            shape(2, groups * lead, 128, dtype=F32),
            shape(128, 6 * 128),
            shape(lines * pairs, 128, dtype=F32),
        ],
        *[part[0] for part in bias],
        *[exchange(part[1], core_bit, res_size) for part in bias],
        keep,
        received,
        horizontal_matrix,
        horizontal_exit_matrix,
        vertical_matrix,
        vertical_exit_matrix,
        kept,
        *own,
        in_specs=[vmem] * (11 + groups),
        moved=0,
        mib=20,
    )

    def add(sums, places, parts):
        return call(
            functools.partial(add_kernel, groups, size, pairs, places),
            shape(*sums.shape, dtype=F32),
            lhs,
            bias,
            sums,
            *parts,
            flops=groups * size * rows * keys * 2 * 256 * 2,
            mib=20,
        )

    beside[0], across[0], across[1], sums = lax.optimization_barrier(
        (beside[0], across[0], across[1], sums)
    )
    corner = [
        exchange(beside[g], far, res_size) if g % 2 == 0 else exchange(across[g], near, res_size)
        for g in range(groups)
    ]
    sums = add(sums, (1, 2), (beside[0], across[1]))
    sums = add(sums, (2, 1), (across[0], beside[1]))
    corner[0], corner[1], sums = lax.optimization_barrier((corner[0], corner[1], sums))
    anywhere = pl.BlockSpec(memory_space=pl.ANY)
    mine, theirs = call(
        functools.partial(finish_kernel, heads, groups, size, pairs, 3),
        [shape(groups * lead, 128)] * 2,
        lhs,
        bias,
        sums,
        wv,
        gate,
        *corner,
        *own,
        *beside,
        *across,
        in_specs=[vmem] * (5 + groups) + [anywhere] * (3 * groups),
        scratch_shapes=[
            pltpu.VMEM((2, groups * lead, 128 * 2 * heads), BF16),
            pltpu.VMEM((2, 8, 128), F32),
            pltpu.VMEM((3 * groups,) + own[0].shape, BF16),
        ],
        flops=groups * size * rows * keys * 2 * 256,
        mib=24,
    )
    returned = exchange(theirs, core_bit, res_size)
    with_column = seq_size == 1
    final_args = [
        me,
        line,
        kept_wide,
        w_final,
    ]
    final_args += [mine, returned]
    result = call(
        functools.partial(final_kernel, lines, depth, with_column),
        shape(*extra_activations.shape) if with_column else shape(lines * pairs, 128),
        *final_args,
        in_specs=[smem] + [vmem] * (len(final_args) - 1),
        scratch_shapes=[pltpu.VMEM((lines * pairs, 128), BF16)],
    )
    if with_column:
        return result
    row = result.reshape(lines, residues, hidden)
    moved = lax.all_to_all(row, "seq", split_axis=1, concat_axis=0, tiled=True)
    moved_kept = lax.all_to_all(kept, "seq", split_axis=1, concat_axis=0, tiled=True)
    updated = column_complete(
        moved, moved_kept.astype(F32), vertical_matrix, vertical_exit_matrix, heads, depth
    )
    back = lax.all_to_all(updated, "seq", split_axis=0, concat_axis=1, tiled=True)
    return back.reshape(extra_activations.shape)


def solution(mesh):
    in_specs = (
        P("seq", "res"),
        P("res", "seq", None),
        P("seq", "res"),
        P("res"),
        P(),
        P(),
        P(),
        P(),
        P(),
    )
    sizes = mesh.shape
    return jax.shard_map(
        functools.partial(on_device, sizes["seq"], sizes["res"]),
        mesh=mesh,
        in_specs=in_specs,
        out_specs=P("seq", "res"),
        check_vma=False,
    )
```

```python
import functools
import math

import jax
import jax.numpy as jnp
from jax import lax
from jax.experimental import pallas as pl
from jax.experimental.pallas import tpu as pltpu
from jax.sharding import PartitionSpec as P

F32 = jnp.float32
BF16 = jnp.bfloat16
LOG2E = math.log2(math.e)
EPS = 1e-05

NT = (((1,), (1,)), ((), ()))


def mm(a, b):
    return jnp.dot(a, b, preferred_element_type=F32)


def mm_nt(a, b):
    return lax.dot_general(a, b, NT, preferred_element_type=F32)


def iota(shape, axis):
    return lax.broadcasted_iota(jnp.int32, shape, axis)


def one_hot(condition):
    return jnp.where(condition, 1.0, 0.0).astype(BF16)


def block_matrix(size, block, on_diagonal, elsewhere):
    row, col = iota((size, 1), 0), iota((1, size), 1)
    inside = jnp.where(row == col, on_diagonal, elsewhere)
    return jnp.where(row // block == col // block, inside, 0.0).astype(BF16)


def halves(value):
    high = value.astype(BF16)
    return high, (value - high.astype(F32)).astype(BF16)


def mm_split(value, matrix):
    high, low = halves(value)
    return mm(high, matrix) + mm(low, matrix)


def paired_norm(x, width):
    lanes = x.shape[1]
    centre = mm(x, block_matrix(lanes, width, 1.0 - 1.0 / width, -1.0 / width))
    spread = mm_split(centre * centre, block_matrix(lanes, width, 1.0 / width, 1.0 / width))
    return (centre * lax.rsqrt(spread + EPS)).astype(BF16)


def row_shuffle(rows, inner, outer):
    total = rows.shape[0]
    row, col = iota((total, 1), 0), iota((1, total), 1)
    return mm(one_hot(col == (row % inner) * outer + row // inner), rows).astype(BF16)


def prep_kernel(groups, me_ref, m_ref, kept_ref, *refs):
    keep_ref, send_ref, line_ref, normed_ref, spread_ref = refs
    lines, width = m_ref.shape
    pairs = width // 128
    stacked = jnp.concatenate([m_ref[:, t * 128 : (t + 1) * 128] for t in range(pairs)], axis=0)
    normed = paired_norm(stacked, 64)
    both = row_shuffle(jnp.concatenate([normed, stacked], axis=1), pairs, lines)
    normed_ref[...] = both[:, :128]
    line_ref[...] = both[:, 128:]
    kept = kept_ref[...]
    size = lines // (2 * groups)
    residues = 2 * pairs
    row, col = iota((pairs, residues), 0), iota((pairs, residues), 1)
    evens, odds = one_hot(col == 2 * row), one_hot(col == 2 * row + 1)
    row, col = iota((128, lines), 0) - 64, iota((128, lines), 1)
    core = me_ref[0] % 2
    for n in range(2 * groups):
        start = jnp.where(n // groups == core, 0, 2 * size)
        chosen = (row >= start) & (row < start + 2 * size) & (row % size == col - n * size)
        spread = mm(one_hot(chosen), kept).astype(BF16)
        first = iota((pairs, 128), 1) < 64 + size + start
        spread_ref[n] = jnp.where(first, mm_nt(evens, spread), mm_nt(odds, spread)).astype(BF16)
    rows = size * pairs
    for ref, half in ((keep_ref, core), (send_ref, 1 - core)):
        for g in range(groups):
            index = half * groups + g
            ref[g, :rows] = normed_ref[pl.ds(pl.multiple_of(index * rows, rows), rows), :]
            ref[g, rows:] = spread_ref[index]


def bias_kernel(whole, pieces, residues, x_ref, w_ref, after_ref, me_ref, *refs):
    outs, (acc_ref, centring_ref, wide_ref) = refs[:-3], refs[-3:]
    step = pl.program_id(0)
    heads = w_ref.shape[0]
    per_step, keys, channels = 2 * x_ref.shape[0], x_ref.shape[2], x_ref.shape[3]
    pairs = residues // 2
    tiles = acc_ref.shape[0]
    width = tiles * 128

    @pl.when(step == 0)
    def _():
        centring_ref[...] = block_matrix(
            2 * channels, channels, 1.0 - 1.0 / channels, -1.0 / channels
        )
        spread = one_hot(iota((heads, 1), 0) == iota((1, width), 1) // residues)
        wide_ref[...] = lax.dot_general(
            w_ref[...], spread, (((0,), (0,)), ((), ())), preferred_element_type=F32
        )
        acc_ref[...] = jnp.zeros(acc_ref.shape, F32)

    lane = iota((1, width), 1) % residues
    placed = []
    for n in range(per_step):
        residue = step * per_step + n
        mine = lane == (residue % 2) * pairs + residue // 2
        placed.append(jnp.where(mine, wide_ref[...], 0.0).astype(BF16))
    placed = jnp.concatenate(placed, axis=0)
    centring = centring_ref[...]
    piece = min(512, keys)
    for r in range(0, keys, piece):
        normed = []
        for n in range(0, per_step, 2):
            x = [x_ref[n // 2, p, r : r + piece] for p in range(2)]
            x = jnp.concatenate(x, axis=1)
            centre = mm(x, centring)
            for part in (centre[:, :channels], centre[:, channels:]):
                spread = jnp.mean(part * part, axis=-1, keepdims=True)
                normed.append((part * lax.rsqrt(spread + EPS)).astype(BF16))
        added = mm(jnp.concatenate(normed, axis=1), placed)
        for n in range(tiles):
            acc_ref[n, r : r + piece, :] += added[:, n * 128 : (n + 1) * 128]

    @pl.when(step == pl.num_programs(0) - 1)
    def _():
        if not whole:
            for n in range(tiles):
                outs[0][n * 128 : (n + 1) * 128, :] = acc_ref[n].T.astype(BF16)
            return
        levels = keys // (2 * pieces * residues)
        for flip in range(2):
            user = me_ref[0] ^ flip
            starts = [
                (user ^ (c + 2 * q + 2 * pieces * k)) * residues + p
                for q in range(pieces)
                for p in range(2)
                for k in range(levels)
                for c in range(2)
            ]
            for n in range(tiles):
                for at in range(0, keys, 128):
                    rows = [
                        acc_ref[n, pl.ds(start, pairs, stride=2), :]
                        for start in starts[at // pairs : (at + 128) // pairs]
                    ]
                    turned = jnp.concatenate(rows, axis=0).T.astype(BF16)
                    outs[flip][n * 128 : (n + 1) * 128, at : at + 128] = turned


def order_kernel(residues, pieces, me_ref, bias_ref, own_ref, send_ref):
    rows, keys = bias_ref.shape
    pairs = residues // 2
    lane = iota((1, keys), 1)
    each = keys // pieces
    which, rest = lane // each, lane % each
    parity, rest = rest // (each // 2), rest % (each // 2)
    place, pair = rest // pairs, rest % pairs
    for flip, out_ref in enumerate((own_ref, send_ref)):
        device = me_ref[0] ^ flip ^ ((place % 2) + 2 * which + 2 * pieces * (place // 2))
        target = device * residues + 2 * pair + parity
        total = jnp.zeros((rows, keys), F32)
        for start in range(0, keys, 256):
            chosen = one_hot(iota((256, keys), 0) + start == target)
            total = total + mm(bias_ref[:, start : start + 256], chosen)
        out_ref[...] = total.astype(BF16)


def pair_matrix(matrix, chosen):
    rows, columns = matrix.shape
    lane = iota((1, 128), 1)
    twice_rows = one_hot(iota((128, 1), 0) % rows == iota((1, rows), 1))
    picked = one_hot(iota((columns, 1), 0) == chosen)
    wide = mm(mm(twice_rows, matrix).astype(BF16), picked)
    same = iota((128, 1), 0) // rows == lane // (128 // 2)
    return jnp.where(same, wide, 0.0).astype(BF16)


def value_matrix(matrix, hidden, heads):
    depth = hidden // heads
    row, col = iota((128, 1), 0), iota((1, 256), 1)
    picked = one_hot(iota((4 * hidden, 1), 0) == 2 * hidden + col % hidden)
    picked = jnp.where(col < 128, picked, jnp.zeros_like(picked))
    wv = mm(mm(one_hot(row == iota((1, hidden), 1)), matrix).astype(BF16), picked)
    counted = (row >= hidden) & (col >= 128)
    wv = jnp.where(counted, 1.0 / (128 - hidden), wv)
    owner = col % 128 // depth
    return [
        jnp.where(owner == p * heads + h, wv, 0.0).astype(BF16)
        for h in range(heads)
        for p in range(2)
    ]


def query_kernel(
    groups, size, pairs, heads, own_ref, peer_ref, keep_ref, received_ref, w_ref, exit_ref,
    column_ref, column_exit_ref, kept_ref, *refs
):
    pieces = [levels_of(refs[0], g, refs[1 + g]) for g in range(groups)]
    bias_ref, lhs_ref, sums_ref, wv_ref, gate_ref, final_ref, kept_wide_ref = refs[1 + groups :]
    rows = own_ref.shape[0]
    bias_ref[:rows, :] = own_ref[...].astype(F32) * LOG2E
    bias_ref[rows:, :] = peer_ref[...].astype(F32) * LOG2E

    hidden = w_ref.shape[0]
    depth = hidden // heads
    lane = iota((1, 128), 1)
    wq = pair_matrix(w_ref[...], lane % hidden)
    wg = pair_matrix(w_ref[...], 3 * hidden + lane % hidden)
    for n, part in enumerate(value_matrix(w_ref[...], hidden, heads)):
        wv_ref[n * 128 : (n + 1) * 128, :] = part
    final = [
        (exit_ref, lane % hidden),
        (column_exit_ref, lane % hidden),
        (column_ref, lane % hidden),
        (column_ref, hidden + lane % hidden),
        (column_ref, 2 * hidden + lane % depth),
        (column_ref, 2 * hidden + depth + lane % depth),
    ]
    for n, (ref, chosen) in enumerate(final):
        final_ref[:, n * 128 : (n + 1) * 128] = pair_matrix(ref[...], chosen)
    total, lines = kept_wide_ref.shape[0], kept_ref.shape[0]
    spread = mm(one_hot(iota((total, 1), 0) // pairs == iota((1, lines), 1)), kept_ref[...])
    mine = iota((1, 2 * pairs), 1) // 2 == iota((total, 1), 0) % pairs
    sides = one_hot(iota((2 * pairs, 1), 0) % 2 == lane // 64)
    kept_wide_ref[...] = mm(jnp.where(mine, spread, 0.0).astype(BF16), sides)
    picked = one_hot(iota((1, 4 * hidden), 1) == hidden + iota((128, 1), 0) % hidden)
    wk = mm_nt(picked, w_ref[...]).astype(BF16)
    wk = mm(wk, one_hot(iota((hidden, 1), 0) == iota((1, 128), 1))).astype(BF16)
    lead = size * pairs
    spare = lane - hidden
    for g in range(groups):
        for n, ref in enumerate((keep_ref, received_ref)):
            gate_ref[n, g * lead : (g + 1) * lead] = jax.nn.sigmoid(mm(ref[g, :lead], wg))
            query = (mm(ref[g, :lead], wq) * (depth**-0.5)).astype(BF16).astype(F32)
            for s in range(size):
                q = query[s * pairs : (s + 1) * pairs]
                spread = [
                    jnp.where(lane // depth == p * heads + h, q, 0.0).astype(BF16)
                    for h in range(heads)
                    for p in range(2)
                ]
                folded = mm(jnp.concatenate(spread, axis=0), wk) * LOG2E
                picks = (spare >= 0) & (spare < 4 * size) & (spare % size == s)
                lhs_ref[g * size + s, n * rows : (n + 1) * rows, :] = jnp.where(
                    picks, 1.0, folded
                ).astype(BF16)
    add_pieces(groups, size, pairs, (0,) * groups, lhs_ref, bias_ref, None, pieces, sums_ref)


def levels_of(first, g, rest):
    return [first.at[g]] + [rest.at[k] for k in range(rest.shape[0])]


def masks_of(levels, size, pairs):
    start = 2 * size * pairs
    lane = iota((1, 128), 1) - 64
    masks = []
    for p in range(2):
        blocks = []
        for level in levels:
            hidden = (1e9 * LOG2E) * (level[start : start + pairs, :].astype(F32) - 1.0)
            for c in range(2):
                first = (2 * c + p) * size
                mine = (lane >= first) & (lane < first + size)
                blocks.append(jnp.where(mine, hidden, 0.0).astype(BF16))
        masks.append(jnp.concatenate(blocks, axis=0))
    return masks


def keys_of(levels, masks, s, size, pairs):
    start = s * pairs
    if not isinstance(s, int):
        start = pl.multiple_of(start, pairs)
    even = jnp.concatenate(
        [level[pl.ds(c * size * pairs + start, pairs), :] for level in levels for c in range(2)],
        axis=0,
    )
    odd = pltpu.roll(even.astype(F32), 64, 1).astype(BF16)
    low = iota(even.shape, 1) < 64
    one = jnp.ones_like(even)
    keyed = [jnp.where(low, x, m) for x, m in zip((even, odd), masks)]
    valued = [jnp.where(low, x, one) for x in (even, odd)]
    return jnp.concatenate(keyed, axis=0), jnp.concatenate(valued, axis=0)


def weigh(lhs, bias_ref, piece, keyed):
    width = keyed.shape[0]
    logits = mm_nt(lhs, keyed) + bias_ref[:, piece * width : (piece + 1) * width]
    return jnp.exp2(logits).astype(BF16)


def each_line(groups, size, pairs, places, lhs_ref, bias_ref, pieces, use):
    masks = [masks_of(levels, size, pairs) for levels in pieces]

    def weights_of(s, g):
        keyed, valued = keys_of(pieces[g], masks[g], s, size, pairs)
        return weigh(lhs_ref[g * size + s], bias_ref, places[g], keyed), valued

    order = [(s, g) for s in range(size) for g in range(groups)]
    ahead = weights_of(*order[0])
    for n, (s, g) in enumerate(order):
        now, ahead = ahead, weights_of(*order[n + 1]) if n + 1 < len(order) else None
        use(g * size + s, mm(*now))


def add_pieces(groups, size, pairs, places, lhs_ref, bias_ref, before_ref, pieces, out_ref):
    def use(line, total):
        out_ref[line] = total if before_ref is None else before_ref[line] + total

    each_line(groups, size, pairs, places, lhs_ref, bias_ref, pieces, use)


def add_kernel(groups, size, pairs, places, lhs_ref, bias_ref, before_ref, *refs):
    pieces = [levels_of(refs[g], g, refs[groups + g]) for g in range(groups)]
    add_pieces(groups, size, pairs, places, lhs_ref, bias_ref, before_ref, pieces, refs[-1])


def finish_kernel(
    heads, groups, size, pairs, place, lhs_ref, bias_ref, sums_ref, wv_ref, gate_ref, *refs
):
    first_refs, rest_refs, far_refs = refs[:4], refs[4 : 4 + groups], refs[4 + groups : 4 + 4 * groups]
    mine_ref, theirs_ref, turned_ref, range_ref, copy_ref = refs[4 + 4 * groups :]
    last = [levels_of(first_refs[3], g, rest_refs[g]) for g in range(groups)]
    blocks = 2 * heads
    low = iota((lhs_ref.shape[1], 128), 1) < 64

    def settle(line, total):
        start = line * pairs
        if not isinstance(line, int):
            start = pl.multiple_of(start, pairs)
        total = total.astype(BF16)
        for n in range(2):
            for b in range(blocks):
                part = total[(n * blocks + b) * pairs : (n * blocks + b + 1) * pairs]
                turned_ref[n, pl.ds(start, pairs), b * 128 : (b + 1) * 128] = part

    lowest, highest = [], []

    def use(line, total):
        total = sums_ref[line] + total
        settle(line, total)
        weight = jnp.where(low, 1.0, total).reshape(-1, 8, 128)
        lowest.append(jnp.min(weight, axis=0))
        highest.append(jnp.max(weight, axis=0))

    each_line(groups, size, pairs, (place,) * groups, lhs_ref, bias_ref, last, use)
    range_ref[0] = functools.reduce(jnp.minimum, lowest)
    range_ref[1] = functools.reduce(jnp.maximum, highest)
    fine = (range_ref[0] > 2.0**-80) & (range_ref[1] < 2.0**100)

    @pl.when(jnp.min(jnp.where(fine, 1.0, 0.0)) < 0.5)
    def _():
        for n, ref in enumerate(far_refs):
            pltpu.sync_copy(ref, copy_ref.at[n])
        for g in range(groups):
            ordered = [
                levels_of(first_refs[n], g, copy_ref.at[n * groups + g]) for n in range(3)
            ] + [last[g]]
            all_masks = [masks_of(ref, size, pairs) for ref in ordered]

            def exact_line(s, carry):
                line = g * size + s
                both = [keys_of(r, m, s, size, pairs) for r, m in zip(ordered, all_masks)]
                logits = []
                for n, (keyed, _) in enumerate(both):
                    width = keyed.shape[0]
                    bias = bias_ref[:, n * width : (n + 1) * width]
                    logits.append(mm_nt(lhs_ref[line], keyed) + bias)
                peak = functools.reduce(jnp.maximum, logits)
                peak = jnp.max(peak, axis=-1, keepdims=True)
                parts = [
                    mm(jnp.exp2(part - peak).astype(BF16), valued)
                    for part, (_, valued) in zip(logits, both)
                ]
                settle(line, sum(parts[1:], parts[0]))
                return carry

            lax.fori_loop(0, size, exact_line, 0)

    lead = groups * size * pairs
    mixed = mm(turned_ref[...].reshape(2 * lead, blocks * 128), wv_ref[...])
    mixed = (mixed[:, :128] / mixed[:, 128:]).reshape(2, lead, 128)
    for n, out_ref in enumerate((mine_ref, theirs_ref)):
        out_ref[...] = (gate_ref[n] * mixed[n]).astype(BF16)


def final_kernel(
    lines, depth, with_column, me_ref, line_ref, kept_ref, w_ref, mine_ref, theirs_ref, out_ref,
    gated_ref,
):
    total = line_ref.shape[0]
    pairs = total // lines
    core = me_ref[0] % 2
    share = total // 2
    for owner, ref in ((core, mine_ref), (1 - core, theirs_ref)):
        gated_ref[pl.ds(pl.multiple_of(owner * share, share), share), :] = ref[...]
    row = (line_ref[...].astype(F32) + mm(gated_ref[...], w_ref[:, :128])).astype(BF16)
    if not with_column:
        out_ref[...] = row
        return
    kept = kept_ref[...]
    projected = mm(paired_norm(row, 64), w_ref[:, 256:])
    query, gate, key, value = [projected[:, 128 * n : 128 * (n + 1)] for n in range(4)]

    def grid(a):
        return a.reshape(lines, pairs, 128)

    count = jnp.maximum(jnp.sum(grid(kept), axis=0), 1.0)
    mean_query = jnp.sum(grid(kept * query), axis=0) / count * (depth**-0.5)
    same_head = block_matrix(128, depth, 1.0, 1.0)
    product = (mean_query[None] * grid(key)).reshape(total, 128)
    logits = grid(mm_split(product, same_head) + 1e9 * (kept - 1.0))
    exped = jnp.exp(logits - jnp.max(logits, axis=0, keepdims=True))
    mixed = jnp.sum(exped * grid(value), axis=0) / jnp.sum(exped, axis=0)
    gated = (jax.nn.sigmoid(grid(gate)) * mixed[None]).reshape(total, 128).astype(BF16)
    result = (row.astype(F32) + mm(gated, w_ref[:, 128:256])).astype(BF16)
    shuffled = row_shuffle(result, lines, pairs)
    for t in range(pairs):
        out_ref[:, t * 128 : (t + 1) * 128] = shuffled[t * lines : (t + 1) * lines, :]


def call(kernel, out_shape, *args, **options):
    flops = options.pop("flops", 0)
    limit = pltpu.CompilerParams(vmem_limit_bytes=options.pop("mib", 8) * 1024 * 1024)
    moved = options.pop("moved", sum(a.size * a.dtype.itemsize for a in args))
    cost = pl.CostEstimate(flops=flops, bytes_accessed=moved, transcendentals=0)
    return pl.pallas_call(
        kernel, out_shape=out_shape, compiler_params=limit, cost_estimate=cost, **options
    )(*args)


def shape(*dims, dtype=BF16):
    return jax.ShapeDtypeStruct(dims, dtype)


def exchange(x, flip, devices):
    return lax.ppermute(x, "res", [(d, d ^ flip) for d in range(devices)])


def layer_normalize(values_in):
    centre = values_in - jnp.mean(values_in, axis=-1, keepdims=True)
    spread = jnp.mean(centre * centre, axis=-1, keepdims=True)
    return centre * lax.rsqrt(spread + EPS)


def column_complete(line, kept, vertical_matrix, vertical_exit_matrix, heads, depth):
    lines, columns, features = line.shape
    hidden = heads * depth
    normed = layer_normalize(line.astype(F32)).astype(BF16)
    projected = mm(normed.reshape(-1, features), vertical_matrix).reshape(lines, columns, -1)
    query, gate = projected[..., :hidden], projected[..., hidden : 2 * hidden]
    key = projected[..., 2 * hidden : 2 * hidden + depth]
    value = projected[..., 2 * hidden + depth :]
    count = jnp.maximum(jnp.sum(kept, axis=0), 1.0)[:, None]
    mean_query = jnp.sum(kept[..., None] * query, axis=0) / count * depth**-0.5
    logits = jnp.einsum("ihc,sic->sih", mean_query.reshape(columns, heads, depth), key)
    logits = logits + 1e9 * (kept - 1.0)[..., None]
    exped = jnp.exp(logits - jnp.max(logits, axis=0, keepdims=True))
    mixed = jnp.einsum("sih,sic->ihc", exped, value) / jnp.sum(exped, axis=0)[..., None]
    gate = jax.nn.sigmoid(gate).reshape(lines, columns, heads, depth)
    gated = (gate * mixed[None]).reshape(-1, hidden).astype(BF16)
    update = mm(gated, vertical_exit_matrix).reshape(lines, columns, features)
    return (line.astype(F32) + update).astype(BF16)


def on_device(
    seq_size,
    res_size,
    extra_activations,
    pair,
    present,
    amino,
    offset_matrix,
    horizontal_matrix,
    horizontal_exit_matrix,
    vertical_matrix,
    vertical_exit_matrix,
):
    lines, residues = present.shape
    pairs = residues // 2
    hidden = horizontal_exit_matrix.shape[0]
    heads = offset_matrix.shape[1]
    depth = hidden // heads
    groups = 2
    size = lines // (2 * groups)
    lead = size * pairs
    keys = res_size * residues
    rows = residues * heads
    core_bit, near, far, high = 1, 2, 4, 8
    kept = (present * amino[None, :]).astype(BF16)
    me = lax.axis_index("res").astype(jnp.int32).reshape(1)
    smem = pl.BlockSpec(memory_space=pltpu.SMEM)
    vmem = pl.BlockSpec(memory_space=pltpu.VMEM)

    rest = lead + pairs
    keep, send, line = call(
        functools.partial(prep_kernel, groups),
        [shape(groups, rest, 128)] * 2 + [shape(lines * pairs, 128)],
        me,
        extra_activations,
        kept,
        in_specs=[smem, vmem, vmem],
        scratch_shapes=[
            pltpu.VMEM((lines * pairs, 128), BF16),
            pltpu.VMEM((2 * groups, pairs, 128), BF16),
        ],
    )

    received = exchange(send, core_bit, res_size)
    chunk = jnp.concatenate(
        [keep[:, :lead], received[:, :lead], keep[:, lead:] + received[:, lead:]], axis=1
    )
    early = [chunk] + [exchange(chunk, flip, res_size) for flip in (near, far)]
    levels = [exchange(chunk, high * k, res_size) for k in range(1, res_size // high)]

    per_step = 8
    pieces = 4
    whole = seq_size == 1
    bias_rows = [shape(rows, keys)] * 2
    bias = call(
        functools.partial(bias_kernel, whole, pieces, residues),
        bias_rows if whole else [shape(rows, pair.shape[1])],
        pair.reshape((residues // 2, 2) + pair.shape[1:]),
        offset_matrix.T,
        chunk,
        me,
        grid=(residues // per_step,),
        in_specs=[
            pl.BlockSpec((per_step // 2, 2) + pair.shape[1:], lambda n: (n, 0, 0, 0)),
            pl.BlockSpec(offset_matrix.shape[::-1], lambda n: (0, 0)),
            pl.BlockSpec(memory_space=pl.ANY),
            smem,
        ],
        out_specs=[pl.BlockSpec((rows, pair.shape[1]), lambda n: (0, 0))] * (1 + whole),
        scratch_shapes=[
            pltpu.VMEM((rows // 128, pair.shape[1], 128), F32),
            pltpu.VMEM((2 * pair.shape[2], 2 * pair.shape[2]), BF16),
            pltpu.VMEM((pair.shape[2], rows), F32),
        ],
        flops=16 * pair.size * 128,
        mib=48,
    )
    if not whole:
        bias = call(
            functools.partial(order_kernel, residues, pieces),
            bias_rows,
            me,
            lax.all_gather(bias[0], "seq", axis=1, tiled=True),
            in_specs=[smem, vmem],
            mib=14,
        )
    levels, bias = lax.optimization_barrier((levels, bias))
    own = [jnp.stack([level[g] for level in levels]) for g in range(groups)]
    own, early = lax.optimization_barrier((own, early))
    beside = [exchange(part, near, res_size) for part in own]
    across = [exchange(part, far, res_size) for part in own]
    early.append(exchange(early[1], far, res_size))
    bias, lhs, sums, wv, gate, w_final, kept_wide = call(
        functools.partial(query_kernel, groups, size, pairs, heads),
        [
            shape(2 * rows, keys, dtype=F32),
            shape(groups * size, 2 * rows, 128),
            shape(groups * size, 2 * rows, 128, dtype=F32),
            shape(2 * heads * 128, 256),
            shape(2, groups * lead, 128, dtype=F32),
            shape(128, 6 * 128),
            shape(lines * pairs, 128, dtype=F32),
        ],
        bias[0],
        exchange(bias[1], core_bit, res_size),
        keep,
        received,
        horizontal_matrix,
        horizontal_exit_matrix,
        vertical_matrix,
        vertical_exit_matrix,
        kept,
        chunk,
        *own,
        in_specs=[vmem] * (10 + groups),
        moved=0,
        mib=20,
    )

    def add(sums, places, parts):
        return call(
            functools.partial(add_kernel, groups, size, pairs, places),
            shape(*sums.shape, dtype=F32),
            lhs,
            bias,
            sums,
            *parts,
            flops=groups * size * rows * keys * 2 * 256 * 2,
            mib=20,
        )

    beside[0], across[1], early[3], sums = lax.optimization_barrier(
        (beside[0], across[1], early[3], sums)
    )
    corner = [
        exchange(beside[g], far, res_size) if g % 2 == 0 else exchange(across[g], near, res_size)
        for g in range(groups)
    ]
    sums = add(sums, (1, 2), (early[1], early[2], beside[0], across[1]))
    beside[1], across[0], sums = lax.optimization_barrier((beside[1], across[0], sums))
    sums = add(sums, (2, 1), (early[2], early[1], across[0], beside[1]))
    corner[0], corner[1], sums = lax.optimization_barrier((corner[0], corner[1], sums))
    anywhere = pl.BlockSpec(memory_space=pl.ANY)
    mine, theirs = call(
        functools.partial(finish_kernel, heads, groups, size, pairs, 3),
        [shape(groups * lead, 128)] * 2,
        lhs,
        bias,
        sums,
        wv,
        gate,
        *early,
        *corner,
        *own,
        *beside,
        *across,
        in_specs=[vmem] * (9 + groups) + [anywhere] * (3 * groups),
        scratch_shapes=[
            pltpu.VMEM((2, groups * lead, 128 * 2 * heads), BF16),
            pltpu.VMEM((2, 8, 128), F32),
            pltpu.VMEM((3 * groups,) + own[0].shape, BF16),
        ],
        flops=groups * size * rows * keys * 2 * 256,
        mib=24,
    )
    returned = exchange(theirs, core_bit, res_size)
    with_column = seq_size == 1
    final_args = [
        me,
        line,
        kept_wide,
        w_final,
    ]
    final_args += [mine, returned]
    result = call(
        functools.partial(final_kernel, lines, depth, with_column),
        shape(*extra_activations.shape) if with_column else shape(lines * pairs, 128),
        *final_args,
        in_specs=[smem] + [vmem] * (len(final_args) - 1),
        scratch_shapes=[pltpu.VMEM((lines * pairs, 128), BF16)],
    )
    if with_column:
        return result
    row = result.reshape(lines, residues, hidden)
    moved = lax.all_to_all(row, "seq", split_axis=1, concat_axis=0, tiled=True)
    moved_kept = lax.all_to_all(kept, "seq", split_axis=1, concat_axis=0, tiled=True)
    updated = column_complete(
        moved, moved_kept.astype(F32), vertical_matrix, vertical_exit_matrix, heads, depth
    )
    back = lax.all_to_all(updated, "seq", split_axis=0, concat_axis=1, tiled=True)
    return back.reshape(extra_activations.shape)


def solution(mesh):
    in_specs = (
        P("seq", "res"),
        P("res", "seq", None),
        P("seq", "res"),
        P("res"),
        P(),
        P(),
        P(),
        P(),
        P(),
    )
    sizes = mesh.shape
    return jax.shard_map(
        functools.partial(on_device, sizes["seq"], sizes["res"]),
        mesh=mesh,
        in_specs=in_specs,
        out_specs=P("seq", "res"),
        check_vma=False,
    )
```

```python
import functools
import math

import jax
import jax.numpy as jnp
from jax import lax
from jax.experimental import pallas as pl
from jax.experimental.pallas import tpu as pltpu
from jax.sharding import PartitionSpec as P

F32 = jnp.float32
BF16 = jnp.bfloat16
LOG2E = math.log2(math.e)
EPS = 1e-05

NT = (((1,), (1,)), ((), ()))


def mm(a, b):
    return jnp.dot(a, b, preferred_element_type=F32)


def mm_nt(a, b):
    return lax.dot_general(a, b, NT, preferred_element_type=F32)


def iota(shape, axis):
    return lax.broadcasted_iota(jnp.int32, shape, axis)


def one_hot(condition):
    return jnp.where(condition, 1.0, 0.0).astype(BF16)


def block_matrix(size, block, on_diagonal, elsewhere):
    row, col = iota((size, 1), 0), iota((1, size), 1)
    inside = jnp.where(row == col, on_diagonal, elsewhere)
    return jnp.where(row // block == col // block, inside, 0.0).astype(BF16)


def halves(value):
    high = value.astype(BF16)
    return high, (value - high.astype(F32)).astype(BF16)


def mm_split(value, matrix):
    high, low = halves(value)
    return mm(high, matrix) + mm(low, matrix)


def paired_norm(x, width):
    lanes = x.shape[1]
    centre = mm(x, block_matrix(lanes, width, 1.0 - 1.0 / width, -1.0 / width))
    spread = mm_split(centre * centre, block_matrix(lanes, width, 1.0 / width, 1.0 / width))
    return (centre * lax.rsqrt(spread + EPS)).astype(BF16)


def row_shuffle(rows, inner, outer):
    total = rows.shape[0]
    row, col = iota((total, 1), 0), iota((1, total), 1)
    return mm(one_hot(col == (row % inner) * outer + row // inner), rows).astype(BF16)


def prep_kernel(groups, me_ref, m_ref, kept_ref, *refs):
    keep_ref, send_ref, line_ref, normed_ref, spread_ref = refs
    lines, width = m_ref.shape
    pairs = width // 128
    stacked = jnp.concatenate([m_ref[:, t * 128 : (t + 1) * 128] for t in range(pairs)], axis=0)
    normed = paired_norm(stacked, 64)
    both = row_shuffle(jnp.concatenate([normed, stacked], axis=1), pairs, lines)
    normed_ref[...] = both[:, :128]
    line_ref[...] = both[:, 128:]
    kept = kept_ref[...]
    size = lines // (2 * groups)
    residues = 2 * pairs
    row, col = iota((pairs, residues), 0), iota((pairs, residues), 1)
    evens, odds = one_hot(col == 2 * row), one_hot(col == 2 * row + 1)
    row, col = iota((128, lines), 0) - 64, iota((128, lines), 1)
    core = me_ref[0] % 2
    for n in range(2 * groups):
        start = jnp.where(n // groups == core, 0, 2 * size)
        chosen = (row >= start) & (row < start + 2 * size) & (row % size == col - n * size)
        spread = mm(one_hot(chosen), kept).astype(BF16)
        first = iota((pairs, 128), 1) < 64 + size + start
        spread_ref[n] = jnp.where(first, mm_nt(evens, spread), mm_nt(odds, spread)).astype(BF16)
    rows = size * pairs
    for ref, half in ((keep_ref, core), (send_ref, 1 - core)):
        for g in range(groups):
            index = half * groups + g
            ref[g, :rows] = normed_ref[pl.ds(pl.multiple_of(index * rows, rows), rows), :]
            ref[g, rows:] = spread_ref[index]


def bias_kernel(whole, pieces, residues, x_ref, w_ref, after_ref, me_ref, *refs):
    outs, (acc_ref, centring_ref, wide_ref) = refs[:-3], refs[-3:]
    step = pl.program_id(0)
    heads = w_ref.shape[0]
    per_step, keys, channels = 2 * x_ref.shape[0], x_ref.shape[2], x_ref.shape[3]
    pairs = residues // 2
    tiles = acc_ref.shape[0]
    width = tiles * 128

    @pl.when(step == 0)
    def _():
        centring_ref[...] = block_matrix(
            2 * channels, channels, 1.0 - 1.0 / channels, -1.0 / channels
        )
        spread = one_hot(iota((heads, 1), 0) == iota((1, width), 1) // residues)
        wide_ref[...] = lax.dot_general(
            w_ref[...], spread, (((0,), (0,)), ((), ())), preferred_element_type=F32
        )
        acc_ref[...] = jnp.zeros(acc_ref.shape, F32)

    lane = iota((1, width), 1) % residues
    placed = []
    for n in range(per_step):
        residue = step * per_step + n
        mine = lane == (residue % 2) * pairs + residue // 2
        placed.append(jnp.where(mine, wide_ref[...], 0.0).astype(BF16))
    placed = jnp.concatenate(placed, axis=0)
    centring = centring_ref[...]
    piece = min(512, keys)
    for r in range(0, keys, piece):
        normed = []
        for n in range(0, per_step, 2):
            x = [x_ref[n // 2, p, r : r + piece] for p in range(2)]
            x = jnp.concatenate(x, axis=1)
            centre = mm(x, centring)
            for part in (centre[:, :channels], centre[:, channels:]):
                spread = jnp.mean(part * part, axis=-1, keepdims=True)
                normed.append((part * lax.rsqrt(spread + EPS)).astype(BF16))
        added = mm(jnp.concatenate(normed, axis=1), placed)
        for n in range(tiles):
            acc_ref[n, r : r + piece, :] += added[:, n * 128 : (n + 1) * 128]

    @pl.when(step == pl.num_programs(0) - 1)
    def _():
        if not whole:
            for n in range(tiles):
                outs[0][n * 128 : (n + 1) * 128, :] = acc_ref[n].T.astype(BF16)
            return
        levels = keys // (2 * pieces * residues)
        for flip in range(2):
            user = me_ref[0] ^ flip
            starts = [
                (user ^ (c + 2 * q + 2 * pieces * k)) * residues + p
                for q in range(pieces)
                for p in range(2)
                for k in range(levels)
                for c in range(2)
            ]
            for n in range(tiles):
                for at in range(0, keys, 128):
                    rows = [
                        acc_ref[n, pl.ds(start, pairs, stride=2), :]
                        for start in starts[at // pairs : (at + 128) // pairs]
                    ]
                    turned = jnp.concatenate(rows, axis=0).T.astype(BF16)
                    outs[flip][n * 128 : (n + 1) * 128, at : at + 128] = turned


def order_kernel(residues, pieces, me_ref, bias_ref, own_ref, send_ref):
    rows, keys = bias_ref.shape
    pairs = residues // 2
    lane = iota((1, keys), 1)
    each = keys // pieces
    which, rest = lane // each, lane % each
    parity, rest = rest // (each // 2), rest % (each // 2)
    place, pair = rest // pairs, rest % pairs
    for flip, out_ref in enumerate((own_ref, send_ref)):
        device = me_ref[0] ^ flip ^ ((place % 2) + 2 * which + 2 * pieces * (place // 2))
        target = device * residues + 2 * pair + parity
        total = jnp.zeros((rows, keys), F32)
        for start in range(0, keys, 256):
            chosen = one_hot(iota((256, keys), 0) + start == target)
            total = total + mm(bias_ref[:, start : start + 256], chosen)
        out_ref[...] = total.astype(BF16)


def pair_matrix(matrix, chosen):
    rows, columns = matrix.shape
    lane = iota((1, 128), 1)
    twice_rows = one_hot(iota((128, 1), 0) % rows == iota((1, rows), 1))
    picked = one_hot(iota((columns, 1), 0) == chosen)
    wide = mm(mm(twice_rows, matrix).astype(BF16), picked)
    same = iota((128, 1), 0) // rows == lane // (128 // 2)
    return jnp.where(same, wide, 0.0).astype(BF16)


def value_matrix(matrix, hidden, heads):
    depth = hidden // heads
    row, col = iota((128, 1), 0), iota((1, 256), 1)
    picked = one_hot(iota((4 * hidden, 1), 0) == 2 * hidden + col % hidden)
    picked = jnp.where(col < 128, picked, jnp.zeros_like(picked))
    wv = mm(mm(one_hot(row == iota((1, hidden), 1)), matrix).astype(BF16), picked)
    counted = (row >= hidden) & (col >= 128)
    wv = jnp.where(counted, 1.0 / (128 - hidden), wv)
    owner = col % 128 // depth
    return [
        jnp.where(owner == p * heads + h, wv, 0.0).astype(BF16)
        for h in range(heads)
        for p in range(2)
    ]


def setup_kernel(
    groups, size, pairs, heads, keep_ref, received_ref, w_ref, exit_ref, column_ref,
    column_exit_ref, kept_ref, lhs_ref, wv_ref, gate_ref, final_ref, kept_wide_ref
):
    rows = lhs_ref.shape[1] // 2
    hidden = w_ref.shape[0]
    depth = hidden // heads
    lane = iota((1, 128), 1)
    wq = pair_matrix(w_ref[...], lane % hidden)
    wg = pair_matrix(w_ref[...], 3 * hidden + lane % hidden)
    for n, part in enumerate(value_matrix(w_ref[...], hidden, heads)):
        wv_ref[n * 128 : (n + 1) * 128, :] = part
    final = [
        (exit_ref, lane % hidden),
        (column_exit_ref, lane % hidden),
        (column_ref, lane % hidden),
        (column_ref, hidden + lane % hidden),
        (column_ref, 2 * hidden + lane % depth),
        (column_ref, 2 * hidden + depth + lane % depth),
    ]
    for n, (ref, chosen) in enumerate(final):
        final_ref[:, n * 128 : (n + 1) * 128] = pair_matrix(ref[...], chosen)
    total, lines = kept_wide_ref.shape[0], kept_ref.shape[0]
    spread = mm(one_hot(iota((total, 1), 0) // pairs == iota((1, lines), 1)), kept_ref[...])
    mine = iota((1, 2 * pairs), 1) // 2 == iota((total, 1), 0) % pairs
    sides = one_hot(iota((2 * pairs, 1), 0) % 2 == lane // 64)
    kept_wide_ref[...] = mm(jnp.where(mine, spread, 0.0).astype(BF16), sides)
    picked = one_hot(iota((1, 4 * hidden), 1) == hidden + iota((128, 1), 0) % hidden)
    wk = mm_nt(picked, w_ref[...]).astype(BF16)
    wk = mm(wk, one_hot(iota((hidden, 1), 0) == iota((1, 128), 1))).astype(BF16)
    lead = size * pairs
    spare = lane - hidden
    for g in range(groups):
        for n, ref in enumerate((keep_ref, received_ref)):
            gate_ref[n, g * lead : (g + 1) * lead] = jax.nn.sigmoid(mm(ref[g, :lead], wg))
            query = (mm(ref[g, :lead], wq) * (depth**-0.5)).astype(BF16).astype(F32)
            for s in range(size):
                q = query[s * pairs : (s + 1) * pairs]
                spread = [
                    jnp.where(lane // depth == p * heads + h, q, 0.0).astype(BF16)
                    for h in range(heads)
                    for p in range(2)
                ]
                folded = mm(jnp.concatenate(spread, axis=0), wk) * LOG2E
                picks = (spare >= 0) & (spare < 4 * size) & (spare % size == s)
                lhs_ref[g * size + s, n * rows : (n + 1) * rows, :] = jnp.where(
                    picks, 1.0, folded
                ).astype(BF16)


def column_kernel(
    groups, size, pairs, lhs_ref, own_ref, peer_ref, first_ref, *refs
):
    rest_refs, (bias_ref, sums_ref) = refs[:groups], refs[groups:]
    rows = own_ref.shape[0]
    bias_ref[:rows, :] = own_ref[...].astype(F32) * LOG2E
    bias_ref[rows:, :] = peer_ref[...].astype(F32) * LOG2E
    pieces = [levels_of(first_ref, g, rest_refs[g]) for g in range(groups)]
    add_pieces(groups, size, pairs, (0,) * groups, lhs_ref, bias_ref, None, pieces, sums_ref)


def levels_of(first, g, rest):
    return [first.at[g]] + [rest.at[k] for k in range(rest.shape[0])]


def masks_of(levels, size, pairs):
    start = 2 * size * pairs
    lane = iota((1, 128), 1) - 64
    masks = []
    for p in range(2):
        blocks = []
        for level in levels:
            hidden = (1e9 * LOG2E) * (level[start : start + pairs, :].astype(F32) - 1.0)
            for c in range(2):
                first = (2 * c + p) * size
                mine = (lane >= first) & (lane < first + size)
                blocks.append(jnp.where(mine, hidden, 0.0).astype(BF16))
        masks.append(jnp.concatenate(blocks, axis=0))
    return masks


def keys_of(levels, masks, s, size, pairs):
    start = s * pairs
    if not isinstance(s, int):
        start = pl.multiple_of(start, pairs)
    even = jnp.concatenate(
        [level[pl.ds(c * size * pairs + start, pairs), :] for level in levels for c in range(2)],
        axis=0,
    )
    odd = pltpu.roll(even.astype(F32), 64, 1).astype(BF16)
    low = iota(even.shape, 1) < 64
    one = jnp.ones_like(even)
    keyed = [jnp.where(low, x, m) for x, m in zip((even, odd), masks)]
    valued = [jnp.where(low, x, one) for x in (even, odd)]
    return jnp.concatenate(keyed, axis=0), jnp.concatenate(valued, axis=0)


def weigh(lhs, bias_ref, piece, keyed):
    width = keyed.shape[0]
    logits = mm_nt(lhs, keyed) + bias_ref[:, piece * width : (piece + 1) * width]
    return jnp.exp2(logits).astype(BF16)


def each_line(groups, size, pairs, places, lhs_ref, bias_ref, pieces, use):
    masks = [masks_of(levels, size, pairs) for levels in pieces]

    def weights_of(s, g):
        keyed, valued = keys_of(pieces[g], masks[g], s, size, pairs)
        return weigh(lhs_ref[g * size + s], bias_ref, places[g], keyed), valued

    order = [(s, g) for s in range(size) for g in range(groups)]
    ahead = weights_of(*order[0])
    for n, (s, g) in enumerate(order):
        now, ahead = ahead, weights_of(*order[n + 1]) if n + 1 < len(order) else None
        use(g * size + s, mm(*now))


def add_pieces(groups, size, pairs, places, lhs_ref, bias_ref, before_ref, pieces, out_ref):
    def use(line, total):
        out_ref[line] = total if before_ref is None else before_ref[line] + total

    each_line(groups, size, pairs, places, lhs_ref, bias_ref, pieces, use)


def add_kernel(groups, size, pairs, places, lhs_ref, bias_ref, before_ref, *refs):
    pieces = [levels_of(refs[g], g, refs[groups + g]) for g in range(groups)]
    add_pieces(groups, size, pairs, places, lhs_ref, bias_ref, before_ref, pieces, refs[-1])


def finish_kernel(
    heads, groups, size, pairs, place, lhs_ref, bias_ref, sums_ref, wv_ref, gate_ref, *refs
):
    first_refs, rest_refs, far_refs = refs[:4], refs[4 : 4 + groups], refs[4 + groups : 4 + 4 * groups]
    mine_ref, theirs_ref, turned_ref, range_ref, copy_ref = refs[4 + 4 * groups :]
    last = [levels_of(first_refs[3], g, rest_refs[g]) for g in range(groups)]
    blocks = 2 * heads
    low = iota((lhs_ref.shape[1], 128), 1) < 64

    def settle(line, total):
        start = line * pairs
        if not isinstance(line, int):
            start = pl.multiple_of(start, pairs)
        total = total.astype(BF16)
        for n in range(2):
            for b in range(blocks):
                part = total[(n * blocks + b) * pairs : (n * blocks + b + 1) * pairs]
                turned_ref[n, pl.ds(start, pairs), b * 128 : (b + 1) * 128] = part

    lowest, highest = [], []

    def use(line, total):
        total = sums_ref[line] + total
        settle(line, total)
        weight = jnp.where(low, 1.0, total).reshape(-1, 8, 128)
        lowest.append(jnp.min(weight, axis=0))
        highest.append(jnp.max(weight, axis=0))

    each_line(groups, size, pairs, (place,) * groups, lhs_ref, bias_ref, last, use)
    range_ref[0] = functools.reduce(jnp.minimum, lowest)
    range_ref[1] = functools.reduce(jnp.maximum, highest)
    fine = (range_ref[0] > 2.0**-80) & (range_ref[1] < 2.0**100)

    @pl.when(jnp.min(jnp.where(fine, 1.0, 0.0)) < 0.5)
    def _():
        for n, ref in enumerate(far_refs):
            pltpu.sync_copy(ref, copy_ref.at[n])
        for g in range(groups):
            ordered = [
                levels_of(first_refs[n], g, copy_ref.at[n * groups + g]) for n in range(3)
            ] + [last[g]]
            all_masks = [masks_of(ref, size, pairs) for ref in ordered]

            def exact_line(s, carry):
                line = g * size + s
                both = [keys_of(r, m, s, size, pairs) for r, m in zip(ordered, all_masks)]
                logits = []
                for n, (keyed, _) in enumerate(both):
                    width = keyed.shape[0]
                    bias = bias_ref[:, n * width : (n + 1) * width]
                    logits.append(mm_nt(lhs_ref[line], keyed) + bias)
                peak = functools.reduce(jnp.maximum, logits)
                peak = jnp.max(peak, axis=-1, keepdims=True)
                parts = [
                    mm(jnp.exp2(part - peak).astype(BF16), valued)
                    for part, (_, valued) in zip(logits, both)
                ]
                settle(line, sum(parts[1:], parts[0]))
                return carry

            lax.fori_loop(0, size, exact_line, 0)

    lead = groups * size * pairs
    mixed = mm(turned_ref[...].reshape(2 * lead, blocks * 128), wv_ref[...])
    mixed = (mixed[:, :128] / mixed[:, 128:]).reshape(2, lead, 128)
    for n, out_ref in enumerate((mine_ref, theirs_ref)):
        out_ref[...] = (gate_ref[n] * mixed[n]).astype(BF16)


def final_kernel(
    lines, depth, with_column, me_ref, line_ref, kept_ref, w_ref, mine_ref, theirs_ref, out_ref,
    gated_ref,
):
    total = line_ref.shape[0]
    pairs = total // lines
    core = me_ref[0] % 2
    share = total // 2
    for owner, ref in ((core, mine_ref), (1 - core, theirs_ref)):
        gated_ref[pl.ds(pl.multiple_of(owner * share, share), share), :] = ref[...]
    row = (line_ref[...].astype(F32) + mm(gated_ref[...], w_ref[:, :128])).astype(BF16)
    if not with_column:
        out_ref[...] = row
        return
    kept = kept_ref[...]
    projected = mm(paired_norm(row, 64), w_ref[:, 256:])
    query, gate, key, value = [projected[:, 128 * n : 128 * (n + 1)] for n in range(4)]

    def grid(a):
        return a.reshape(lines, pairs, 128)

    count = jnp.maximum(jnp.sum(grid(kept), axis=0), 1.0)
    mean_query = jnp.sum(grid(kept * query), axis=0) / count * (depth**-0.5)
    same_head = block_matrix(128, depth, 1.0, 1.0)
    product = (mean_query[None] * grid(key)).reshape(total, 128)
    logits = grid(mm_split(product, same_head) + 1e9 * (kept - 1.0))
    exped = jnp.exp(logits - jnp.max(logits, axis=0, keepdims=True))
    mixed = jnp.sum(exped * grid(value), axis=0) / jnp.sum(exped, axis=0)
    gated = (jax.nn.sigmoid(grid(gate)) * mixed[None]).reshape(total, 128).astype(BF16)
    result = (row.astype(F32) + mm(gated, w_ref[:, 128:256])).astype(BF16)
    shuffled = row_shuffle(result, lines, pairs)
    for t in range(pairs):
        out_ref[:, t * 128 : (t + 1) * 128] = shuffled[t * lines : (t + 1) * lines, :]


def call(kernel, out_shape, *args, **options):
    flops = options.pop("flops", 0)
    limit = pltpu.CompilerParams(vmem_limit_bytes=options.pop("mib", 8) * 1024 * 1024)
    moved = options.pop("moved", sum(a.size * a.dtype.itemsize for a in args))
    cost = pl.CostEstimate(flops=flops, bytes_accessed=moved, transcendentals=0)
    return pl.pallas_call(
        kernel, out_shape=out_shape, compiler_params=limit, cost_estimate=cost, **options
    )(*args)


def shape(*dims, dtype=BF16):
    return jax.ShapeDtypeStruct(dims, dtype)


def exchange(x, flip, devices):
    return lax.ppermute(x, "res", [(d, d ^ flip) for d in range(devices)])


def layer_normalize(values_in):
    centre = values_in - jnp.mean(values_in, axis=-1, keepdims=True)
    spread = jnp.mean(centre * centre, axis=-1, keepdims=True)
    return centre * lax.rsqrt(spread + EPS)


def column_complete(line, kept, vertical_matrix, vertical_exit_matrix, heads, depth):
    lines, columns, features = line.shape
    hidden = heads * depth
    normed = layer_normalize(line.astype(F32)).astype(BF16)
    projected = mm(normed.reshape(-1, features), vertical_matrix).reshape(lines, columns, -1)
    query, gate = projected[..., :hidden], projected[..., hidden : 2 * hidden]
    key = projected[..., 2 * hidden : 2 * hidden + depth]
    value = projected[..., 2 * hidden + depth :]
    count = jnp.maximum(jnp.sum(kept, axis=0), 1.0)[:, None]
    mean_query = jnp.sum(kept[..., None] * query, axis=0) / count * depth**-0.5
    logits = jnp.einsum("ihc,sic->sih", mean_query.reshape(columns, heads, depth), key)
    logits = logits + 1e9 * (kept - 1.0)[..., None]
    exped = jnp.exp(logits - jnp.max(logits, axis=0, keepdims=True))
    mixed = jnp.einsum("sih,sic->ihc", exped, value) / jnp.sum(exped, axis=0)[..., None]
    gate = jax.nn.sigmoid(gate).reshape(lines, columns, heads, depth)
    gated = (gate * mixed[None]).reshape(-1, hidden).astype(BF16)
    update = mm(gated, vertical_exit_matrix).reshape(lines, columns, features)
    return (line.astype(F32) + update).astype(BF16)


def on_device(
    seq_size,
    res_size,
    extra_activations,
    pair,
    present,
    amino,
    offset_matrix,
    horizontal_matrix,
    horizontal_exit_matrix,
    vertical_matrix,
    vertical_exit_matrix,
):
    lines, residues = present.shape
    pairs = residues // 2
    hidden = horizontal_exit_matrix.shape[0]
    heads = offset_matrix.shape[1]
    depth = hidden // heads
    groups = 2
    size = lines // (2 * groups)
    lead = size * pairs
    keys = res_size * residues
    rows = residues * heads
    core_bit, near, far, high = 1, 2, 4, 8
    kept = (present * amino[None, :]).astype(BF16)
    me = lax.axis_index("res").astype(jnp.int32).reshape(1)
    smem = pl.BlockSpec(memory_space=pltpu.SMEM)
    vmem = pl.BlockSpec(memory_space=pltpu.VMEM)

    rest = lead + pairs
    keep, send, line = call(
        functools.partial(prep_kernel, groups),
        [shape(groups, rest, 128)] * 2 + [shape(lines * pairs, 128)],
        me,
        extra_activations,
        kept,
        in_specs=[smem, vmem, vmem],
        scratch_shapes=[
            pltpu.VMEM((lines * pairs, 128), BF16),
            pltpu.VMEM((2 * groups, pairs, 128), BF16),
        ],
    )

    received = exchange(send, core_bit, res_size)
    chunk = jnp.concatenate(
        [keep[:, :lead], received[:, :lead], keep[:, lead:] + received[:, lead:]], axis=1
    )
    levels = [exchange(chunk, high * k, res_size) for k in range(1, res_size // high)]
    lhs, wv, gate, w_final, kept_wide = call(
        functools.partial(setup_kernel, groups, size, pairs, heads),
        [
            shape(groups * size, 2 * rows, 128),
            shape(2 * heads * 128, 256),
            shape(2, groups * lead, 128, dtype=F32),
            shape(128, 6 * 128),
            shape(lines * pairs, 128, dtype=F32),
        ],
        keep,
        received,
        horizontal_matrix,
        horizontal_exit_matrix,
        vertical_matrix,
        vertical_exit_matrix,
        kept,
        moved=0,
        mib=14,
    )
    after, lhs = lax.optimization_barrier((chunk, lhs))
    early = [chunk] + [exchange(after, flip, res_size) for flip in (near, far)]

    per_step = 8
    pieces = 4
    whole = seq_size == 1
    bias_rows = [shape(rows, keys)] * 2
    bias = call(
        functools.partial(bias_kernel, whole, pieces, residues),
        bias_rows if whole else [shape(rows, pair.shape[1])],
        pair.reshape((residues // 2, 2) + pair.shape[1:]),
        offset_matrix.T,
        after,
        me,
        grid=(residues // per_step,),
        in_specs=[
            pl.BlockSpec((per_step // 2, 2) + pair.shape[1:], lambda n: (n, 0, 0, 0)),
            pl.BlockSpec(offset_matrix.shape[::-1], lambda n: (0, 0)),
            pl.BlockSpec(memory_space=pl.ANY),
            smem,
        ],
        out_specs=[pl.BlockSpec((rows, pair.shape[1]), lambda n: (0, 0))] * (1 + whole),
        scratch_shapes=[
            pltpu.VMEM((rows // 128, pair.shape[1], 128), F32),
            pltpu.VMEM((2 * pair.shape[2], 2 * pair.shape[2]), BF16),
            pltpu.VMEM((pair.shape[2], rows), F32),
        ],
        flops=16 * pair.size * 128,
        mib=48,
    )
    if not whole:
        bias = call(
            functools.partial(order_kernel, residues, pieces),
            bias_rows,
            me,
            lax.all_gather(bias[0], "seq", axis=1, tiled=True),
            in_specs=[smem, vmem],
            mib=14,
        )
    levels, bias = lax.optimization_barrier((levels, bias))
    own = [jnp.stack([level[g] for level in levels]) for g in range(groups)]
    own, early = lax.optimization_barrier((own, early))
    beside = [exchange(part, near, res_size) for part in own]
    across = [exchange(part, far, res_size) for part in own]
    early.append(exchange(early[1], far, res_size))
    bias, sums = call(
        functools.partial(column_kernel, groups, size, pairs),
        [
            shape(2 * rows, keys, dtype=F32),
            shape(groups * size, 2 * rows, 128, dtype=F32),
        ],
        lhs,
        bias[0],
        exchange(bias[1], core_bit, res_size),
        chunk,
        *own,
        moved=0,
        mib=20,
    )

    def add(sums, places, parts):
        return call(
            functools.partial(add_kernel, groups, size, pairs, places),
            shape(*sums.shape, dtype=F32),
            lhs,
            bias,
            sums,
            *parts,
            flops=groups * size * rows * keys * 2 * 256 * 2,
            mib=20,
        )

    beside[0], across[1], sums = lax.optimization_barrier((beside[0], across[1], sums))
    corner = [
        exchange(beside[g], far, res_size) if g % 2 == 0 else exchange(across[g], near, res_size)
        for g in range(groups)
    ]
    sums = add(sums, (1, 2), (early[1], early[2], beside[0], across[1]))
    beside[1], across[0], early[3], sums = lax.optimization_barrier(
        (beside[1], across[0], early[3], sums)
    )
    sums = add(sums, (2, 1), (early[2], early[1], across[0], beside[1]))
    corner[0], corner[1], sums = lax.optimization_barrier((corner[0], corner[1], sums))
    anywhere = pl.BlockSpec(memory_space=pl.ANY)
    mine, theirs = call(
        functools.partial(finish_kernel, heads, groups, size, pairs, 3),
        [shape(groups * lead, 128)] * 2,
        lhs,
        bias,
        sums,
        wv,
        gate,
        *early,
        *corner,
        *own,
        *beside,
        *across,
        in_specs=[vmem] * (9 + groups) + [anywhere] * (3 * groups),
        scratch_shapes=[
            pltpu.VMEM((2, groups * lead, 128 * 2 * heads), BF16),
            pltpu.VMEM((2, 8, 128), F32),
            pltpu.VMEM((3 * groups,) + own[0].shape, BF16),
        ],
        flops=groups * size * rows * keys * 2 * 256,
        mib=24,
    )
    returned = exchange(theirs, core_bit, res_size)
    with_column = seq_size == 1
    final_args = [
        me,
        line,
        kept_wide,
        w_final,
    ]
    final_args += [mine, returned]
    result = call(
        functools.partial(final_kernel, lines, depth, with_column),
        shape(*extra_activations.shape) if with_column else shape(lines * pairs, 128),
        *final_args,
        in_specs=[smem] + [vmem] * (len(final_args) - 1),
        scratch_shapes=[pltpu.VMEM((lines * pairs, 128), BF16)],
    )
    if with_column:
        return result
    row = result.reshape(lines, residues, hidden)
    moved = lax.all_to_all(row, "seq", split_axis=1, concat_axis=0, tiled=True)
    moved_kept = lax.all_to_all(kept, "seq", split_axis=1, concat_axis=0, tiled=True)
    updated = column_complete(
        moved, moved_kept.astype(F32), vertical_matrix, vertical_exit_matrix, heads, depth
    )
    back = lax.all_to_all(updated, "seq", split_axis=0, concat_axis=1, tiled=True)
    return back.reshape(extra_activations.shape)


def solution(mesh):
    in_specs = (
        P("seq", "res"),
        P("res", "seq", None),
        P("seq", "res"),
        P("res"),
        P(),
        P(),
        P(),
        P(),
        P(),
    )
    sizes = mesh.shape
    return jax.shard_map(
        functools.partial(on_device, sizes["seq"], sizes["res"]),
        mesh=mesh,
        in_specs=in_specs,
        out_specs=P("seq", "res"),
        check_vma=False,
    )
```

```python
import functools
import math

import jax
import jax.numpy as jnp
from jax import lax
from jax.experimental import pallas as pl
from jax.experimental.pallas import tpu as pltpu
from jax.sharding import PartitionSpec as P

F32 = jnp.float32
BF16 = jnp.bfloat16
LOG2E = math.log2(math.e)
EPS = 1e-05

NT = (((1,), (1,)), ((), ()))


def mm(a, b):
    return jnp.dot(a, b, preferred_element_type=F32)


def mm_nt(a, b):
    return lax.dot_general(a, b, NT, preferred_element_type=F32)


def iota(shape, axis):
    return lax.broadcasted_iota(jnp.int32, shape, axis)


def one_hot(condition):
    return jnp.where(condition, 1.0, 0.0).astype(BF16)


def block_matrix(size, block, on_diagonal, elsewhere):
    row, col = iota((size, 1), 0), iota((1, size), 1)
    inside = jnp.where(row == col, on_diagonal, elsewhere)
    return jnp.where(row // block == col // block, inside, 0.0).astype(BF16)


def halves(value):
    high = value.astype(BF16)
    return high, (value - high.astype(F32)).astype(BF16)


def mm_split(value, matrix):
    high, low = halves(value)
    return mm(high, matrix) + mm(low, matrix)


def paired_norm(x, width):
    lanes = x.shape[1]
    centre = mm(x, block_matrix(lanes, width, 1.0 - 1.0 / width, -1.0 / width))
    spread = mm_split(centre * centre, block_matrix(lanes, width, 1.0 / width, 1.0 / width))
    return (centre * lax.rsqrt(spread + EPS)).astype(BF16)


def row_shuffle(rows, inner, outer):
    total = rows.shape[0]
    row, col = iota((total, 1), 0), iota((1, total), 1)
    return mm(one_hot(col == (row % inner) * outer + row // inner), rows).astype(BF16)


def prep_kernel(groups, me_ref, m_ref, kept_ref, *refs):
    keep_ref, send_ref, line_ref, normed_ref, spread_ref = refs
    lines, width = m_ref.shape
    pairs = width // 128
    stacked = jnp.concatenate([m_ref[:, t * 128 : (t + 1) * 128] for t in range(pairs)], axis=0)
    normed = paired_norm(stacked, 64)
    both = row_shuffle(jnp.concatenate([normed, stacked], axis=1), pairs, lines)
    normed_ref[...] = both[:, :128]
    line_ref[...] = both[:, 128:]
    kept = kept_ref[:lines, :]
    size = lines // (2 * groups)
    row, col = iota((pairs, 128), 0), iota((pairs, 128), 1)
    evens, odds = one_hot(col == 2 * row), one_hot(col == 2 * row + 1)
    row, col = iota((128, lines), 0) - 64, iota((128, lines), 1)
    core = me_ref[0] % 2
    for n in range(2 * groups):
        start = jnp.where(n // groups == core, 0, 2 * size)
        chosen = (row >= start) & (row < start + 2 * size) & (row % size == col - n * size)
        spread = mm(one_hot(chosen), kept).astype(BF16)
        first = iota((pairs, 128), 1) < 64 + size + start
        spread_ref[n] = jnp.where(first, mm_nt(evens, spread), mm_nt(odds, spread)).astype(BF16)
    rows = size * pairs
    for ref, half in ((keep_ref, core), (send_ref, 1 - core)):
        for g in range(groups):
            index = half * groups + g
            ref[g, :rows] = normed_ref[pl.ds(pl.multiple_of(index * rows, rows), rows), :]
            ref[g, rows:] = spread_ref[index]


def bias_kernel(whole, pieces, residues, heads, x_ref, w_ref, after_ref, me_ref, *refs):
    outs, (acc_ref, centring_ref, wide_ref) = refs[:-3], refs[-3:]
    step = pl.program_id(0)
    per_step, keys, channels = 2 * x_ref.shape[0], x_ref.shape[2], x_ref.shape[3]
    pairs = residues // 2
    tiles = acc_ref.shape[0]
    width = tiles * 128

    @pl.when(step == 0)
    def _():
        centring_ref[...] = block_matrix(
            2 * channels, channels, 1.0 - 1.0 / channels, -1.0 / channels
        )
        w = w_ref[w_ref.shape[0] - 16 :, :]
        spread = one_hot(iota((16, 1), 0) == iota((1, width), 1) // residues)
        wide_ref[...] = lax.dot_general(
            w, spread, (((0,), (0,)), ((), ())), preferred_element_type=F32
        )
        acc_ref[...] = jnp.zeros(acc_ref.shape, F32)

    lane = iota((1, width), 1) % residues
    placed = []
    for n in range(per_step):
        residue = step * per_step + n
        mine = lane == (residue % 2) * pairs + residue // 2
        placed.append(jnp.where(mine, wide_ref[...], 0.0).astype(BF16))
    placed = jnp.concatenate(placed, axis=0)
    centring = centring_ref[...]
    piece = min(512, keys)
    for r in range(0, keys, piece):
        normed = []
        for n in range(0, per_step, 2):
            x = [x_ref[n // 2, p, r : r + piece] for p in range(2)]
            x = jnp.concatenate(x, axis=1)
            centre = mm(x, centring)
            for part in (centre[:, :channels], centre[:, channels:]):
                spread = jnp.mean(part * part, axis=-1, keepdims=True)
                normed.append((part * lax.rsqrt(spread + EPS)).astype(BF16))
        added = mm(jnp.concatenate(normed, axis=1), placed)
        for n in range(tiles):
            acc_ref[n, r : r + piece, :] += added[:, n * 128 : (n + 1) * 128]

    @pl.when(step == pl.num_programs(0) - 1)
    def _():
        if not whole:
            for n in range(tiles):
                outs[0][n * 128 : (n + 1) * 128, :] = acc_ref[n].T.astype(BF16)
            return
        levels = keys // (2 * pieces * residues)
        for flip in range(2):
            user = me_ref[0] ^ flip
            starts = [
                (user ^ (c + 2 * q + 2 * pieces * k)) * residues + p
                for q in range(pieces)
                for p in range(2)
                for k in range(levels)
                for c in range(2)
            ]
            for n in range(tiles):
                for at in range(0, keys, 128):
                    rows = [
                        acc_ref[n, pl.ds(start, pairs, stride=2), :]
                        for start in starts[at // pairs : (at + 128) // pairs]
                    ]
                    turned = jnp.concatenate(rows, axis=0).T.astype(BF16)
                    outs[flip][n * 128 : (n + 1) * 128, at : at + 128] = turned


def order_kernel(residues, pieces, me_ref, bias_ref, own_ref, send_ref):
    rows, keys = bias_ref.shape
    pairs = residues // 2
    lane = iota((1, keys), 1)
    each = keys // pieces
    which, rest = lane // each, lane % each
    parity, rest = rest // (each // 2), rest % (each // 2)
    place, pair = rest // pairs, rest % pairs
    for flip, out_ref in enumerate((own_ref, send_ref)):
        device = me_ref[0] ^ flip ^ ((place % 2) + 2 * which + 2 * pieces * (place // 2))
        target = device * residues + 2 * pair + parity
        total = jnp.zeros((rows, keys), F32)
        for start in range(0, keys, 256):
            chosen = one_hot(iota((256, keys), 0) + start == target)
            total = total + mm(bias_ref[:, start : start + 256], chosen)
        out_ref[...] = total.astype(BF16)


def pair_matrix(matrix, chosen):
    rows, columns = matrix.shape
    lane = iota((1, 128), 1)
    twice_rows = one_hot(iota((128, 1), 0) % rows == iota((1, rows), 1))
    picked = one_hot(iota((columns, 1), 0) == chosen)
    wide = mm(mm(twice_rows, matrix).astype(BF16), picked)
    same = iota((128, 1), 0) // rows == lane // (128 // 2)
    return jnp.where(same, wide, 0.0).astype(BF16)


def value_matrix(matrix, hidden, heads):
    depth = hidden // heads
    row, col = iota((128, 1), 0), iota((1, 256), 1)
    picked = one_hot(iota((4 * hidden, 1), 0) == 2 * hidden + col % hidden)
    picked = jnp.where(col < 128, picked, jnp.zeros_like(picked))
    wv = mm(mm(one_hot(row == iota((1, hidden), 1)), matrix).astype(BF16), picked)
    counted = (row >= hidden) & (col >= 128)
    wv = jnp.where(counted, 1.0 / (128 - hidden), wv)
    owner = col % 128 // depth
    return [
        jnp.where(owner == p * heads + h, wv, 0.0).astype(BF16)
        for h in range(heads)
        for p in range(2)
    ]


def presence_kernel(pairs, kept_ref, after_ref, wide_ref):
    total = wide_ref.shape[0]
    lines = total // pairs
    kept = kept_ref[:lines, :]
    spread = mm(one_hot(iota((total, 1), 0) // pairs == iota((1, lines), 1)), kept)
    mine = iota((1, 128), 1) // 2 == iota((total, 1), 0) % pairs
    sides = one_hot(iota((128, 1), 0) % 2 == iota((1, 128), 1) // 64)
    wide_ref[...] = mm(jnp.where(mine, spread, 0.0).astype(BF16), sides)


def query_kernel(
    groups, size, pairs, heads, own_ref, peer_ref, keep_ref, received_ref, w_ref, exit_ref,
    column_ref, column_exit_ref, *refs
):
    pieces = [levels_of(refs[0], g, refs[1 + g]) for g in range(groups)]
    bias_ref, lhs_ref, sums_ref, wv_ref, gate_ref, final_ref = refs[1 + groups :]
    rows = own_ref.shape[0]
    bias_ref[:rows, :] = own_ref[...].astype(F32) * LOG2E
    bias_ref[rows:, :] = peer_ref[...].astype(F32) * LOG2E

    hidden = w_ref.shape[0]
    depth = hidden // heads
    lane = iota((1, 128), 1)
    wq = pair_matrix(w_ref[...], lane % hidden)
    wg = pair_matrix(w_ref[...], 3 * hidden + lane % hidden)
    for n, part in enumerate(value_matrix(w_ref[...], hidden, heads)):
        wv_ref[n * 128 : (n + 1) * 128, :] = part
    final = [
        (exit_ref, lane % hidden),
        (column_exit_ref, lane % hidden),
        (column_ref, lane % hidden),
        (column_ref, hidden + lane % hidden),
        (column_ref, 2 * hidden + lane % depth),
        (column_ref, 2 * hidden + depth + lane % depth),
    ]
    for n, (ref, chosen) in enumerate(final):
        final_ref[:, n * 128 : (n + 1) * 128] = pair_matrix(ref[...], chosen)
    picked = one_hot(iota((1, 4 * hidden), 1) == hidden + iota((128, 1), 0) % hidden)
    wk = mm_nt(picked, w_ref[...]).astype(BF16)
    wk = mm(wk, one_hot(iota((hidden, 1), 0) == iota((1, 128), 1))).astype(BF16)
    lead = size * pairs
    spare = lane - hidden
    for g in range(groups):
        for n, ref in enumerate((keep_ref, received_ref)):
            gate_ref[n, g * lead : (g + 1) * lead] = jax.nn.sigmoid(mm(ref[g, :lead], wg))
            query = (mm(ref[g, :lead], wq) * (depth**-0.5)).astype(BF16).astype(F32)
            for s in range(size):
                q = query[s * pairs : (s + 1) * pairs]
                spread = [
                    jnp.where(lane // depth == p * heads + h, q, 0.0).astype(BF16)
                    for h in range(heads)
                    for p in range(2)
                ]
                folded = mm(jnp.concatenate(spread, axis=0), wk) * LOG2E
                picks = (spare >= 0) & (spare < 4 * size) & (spare % size == s)
                lhs_ref[g * size + s, n * rows : (n + 1) * rows, :] = jnp.where(
                    picks, 1.0, folded
                ).astype(BF16)
    add_pieces(groups, size, pairs, (0,) * groups, lhs_ref, bias_ref, None, pieces, sums_ref)


def levels_of(first, g, rest):
    return [first.at[g]] + [rest.at[k] for k in range(rest.shape[0])]


def masks_of(levels, size, pairs):
    start = 2 * size * pairs
    lane = iota((1, 128), 1) - 64
    masks = []
    for p in range(2):
        blocks = []
        for level in levels:
            hidden = (1e9 * LOG2E) * (level[start : start + pairs, :].astype(F32) - 1.0)
            for c in range(2):
                first = (2 * c + p) * size
                mine = (lane >= first) & (lane < first + size)
                blocks.append(jnp.where(mine, hidden, 0.0).astype(BF16))
        masks.append(jnp.concatenate(blocks, axis=0))
    return masks


def keys_of(levels, masks, s, size, pairs):
    start = s * pairs
    if not isinstance(s, int):
        start = pl.multiple_of(start, pairs)
    even = jnp.concatenate(
        [level[pl.ds(c * size * pairs + start, pairs), :] for level in levels for c in range(2)],
        axis=0,
    )
    odd = pltpu.roll(even.astype(F32), 64, 1).astype(BF16)
    low = iota(even.shape, 1) < 64
    one = jnp.ones_like(even)
    keyed = [jnp.where(low, x, m) for x, m in zip((even, odd), masks)]
    valued = [jnp.where(low, x, one) for x in (even, odd)]
    return jnp.concatenate(keyed, axis=0), jnp.concatenate(valued, axis=0)


def weigh(lhs, bias_ref, piece, keyed):
    width = keyed.shape[0]
    logits = mm_nt(lhs, keyed) + bias_ref[:, piece * width : (piece + 1) * width]
    return jnp.exp2(logits).astype(BF16)


def each_line(groups, size, pairs, places, lhs_ref, bias_ref, pieces, use):
    masks = [masks_of(levels, size, pairs) for levels in pieces]

    def weights_of(s, g):
        keyed, valued = keys_of(pieces[g], masks[g], s, size, pairs)
        return weigh(lhs_ref[g * size + s], bias_ref, places[g], keyed), valued

    order = [(s, g) for s in range(size) for g in range(groups)]
    ahead = weights_of(*order[0])
    for n, (s, g) in enumerate(order):
        now, ahead = ahead, weights_of(*order[n + 1]) if n + 1 < len(order) else None
        use(g * size + s, mm(*now))


def add_pieces(groups, size, pairs, places, lhs_ref, bias_ref, before_ref, pieces, out_ref):
    def use(line, total):
        out_ref[line] = total if before_ref is None else before_ref[line] + total

    each_line(groups, size, pairs, places, lhs_ref, bias_ref, pieces, use)


def add_kernel(groups, size, pairs, places, lhs_ref, bias_ref, before_ref, *refs):
    pieces = [levels_of(refs[g], g, refs[groups + g]) for g in range(groups)]
    add_pieces(groups, size, pairs, places, lhs_ref, bias_ref, before_ref, pieces, refs[-1])


def finish_kernel(
    heads, groups, size, pairs, place, lhs_ref, bias_ref, sums_ref, wv_ref, gate_ref, *refs
):
    first_refs, last_refs, far_refs = refs[:3], refs[3 : 3 + groups], refs[3 + groups : 3 + 4 * groups]
    mine_ref, theirs_ref, turned_ref, mixed_ref, range_ref, copy_ref = refs[3 + 4 * groups :]
    last = [[ref.at[k] for k in range(ref.shape[0])] for ref in last_refs]
    blocks = 2 * heads
    low = iota((lhs_ref.shape[1], 128), 1) < 64

    def settle(line, total):
        start = line * pairs
        if not isinstance(line, int):
            start = pl.multiple_of(start, pairs)
        total = total.astype(BF16)
        for n in range(2):
            for b in range(blocks):
                part = total[(n * blocks + b) * pairs : (n * blocks + b + 1) * pairs]
                turned_ref[n, pl.ds(start, pairs), b * 128 : (b + 1) * 128] = part

    def mix(first, last):
        rows = [
            (n, slice((g * size + first) * pairs, (g * size + last) * pairs))
            for n in range(2)
            for g in range(groups)
        ]
        mixed = mm(jnp.concatenate([turned_ref[n, at, :] for n, at in rows], axis=0), wv_ref[...])
        mixed = mixed[:, :128] / mixed[:, 128:]
        height = (last - first) * pairs
        for k, (n, at) in enumerate(rows):
            mixed_ref[n, at, :] = mixed[k * height : (k + 1) * height]

    lowest, highest = [], []

    def use(line, total):
        total = sums_ref[line] + total
        settle(line, total)
        weight = jnp.where(low, 1.0, total).reshape(-1, 8, 128)
        lowest.append(jnp.min(weight, axis=0))
        highest.append(jnp.max(weight, axis=0))
        if len(lowest) == groups * (size // 2):
            mix(0, size // 2)

    each_line(groups, size, pairs, (place,) * groups, lhs_ref, bias_ref, last, use)
    mix(size // 2, size)
    range_ref[0] = functools.reduce(jnp.minimum, lowest)
    range_ref[1] = functools.reduce(jnp.maximum, highest)
    fine = (range_ref[0] > 2.0**-80) & (range_ref[1] < 2.0**100)

    @pl.when(jnp.min(jnp.where(fine, 1.0, 0.0)) < 0.5)
    def _():
        for n, ref in enumerate(far_refs):
            pltpu.sync_copy(ref, copy_ref.at[n])
        for g in range(groups):
            ordered = [
                levels_of(first_refs[n], g, copy_ref.at[n * groups + g]) for n in range(3)
            ] + [last[g]]
            all_masks = [masks_of(ref, size, pairs) for ref in ordered]

            def exact_line(s, carry):
                line = g * size + s
                both = [keys_of(r, m, s, size, pairs) for r, m in zip(ordered, all_masks)]
                logits = []
                for n, (keyed, _) in enumerate(both):
                    width = keyed.shape[0]
                    bias = bias_ref[:, n * width : (n + 1) * width]
                    logits.append(mm_nt(lhs_ref[line], keyed) + bias)
                peak = functools.reduce(jnp.maximum, logits)
                peak = jnp.max(peak, axis=-1, keepdims=True)
                parts = [
                    mm(jnp.exp2(part - peak).astype(BF16), valued)
                    for part, (_, valued) in zip(logits, both)
                ]
                settle(line, sum(parts[1:], parts[0]))
                return carry

            lax.fori_loop(0, size, exact_line, 0)
        mix(0, size)

    for n, out_ref in enumerate((mine_ref, theirs_ref)):
        out_ref[...] = (gate_ref[n] * mixed_ref[n]).astype(BF16)


def final_kernel(
    lines, depth, with_column, me_ref, line_ref, kept_ref, w_ref, mine_ref, theirs_ref, out_ref,
    gated_ref,
):
    total = line_ref.shape[0]
    pairs = total // lines
    core = me_ref[0] % 2
    share = total // 2
    for owner, ref in ((core, mine_ref), (1 - core, theirs_ref)):
        gated_ref[pl.ds(pl.multiple_of(owner * share, share), share), :] = ref[...]
    row = (line_ref[...].astype(F32) + mm(gated_ref[...], w_ref[:, :128])).astype(BF16)
    if not with_column:
        out_ref[...] = row
        return
    kept = kept_ref[...]
    projected = mm(paired_norm(row, 64), w_ref[:, 256:])
    query, gate, key, value = [projected[:, 128 * n : 128 * (n + 1)] for n in range(4)]

    def grid(a):
        return a.reshape(lines, pairs, 128)

    count = jnp.maximum(jnp.sum(grid(kept), axis=0), 1.0)
    mean_query = jnp.sum(grid(kept * query), axis=0) / count * (depth**-0.5)
    same_head = block_matrix(128, depth, 1.0, 1.0)
    product = (mean_query[None] * grid(key)).reshape(total, 128)
    logits = grid(mm_split(product, same_head) + 1e9 * (kept - 1.0))
    exped = jnp.exp(logits - jnp.max(logits, axis=0, keepdims=True))
    mixed = jnp.sum(exped * grid(value), axis=0) / jnp.sum(exped, axis=0)
    gated = (jax.nn.sigmoid(grid(gate)) * mixed[None]).reshape(total, 128).astype(BF16)
    result = (row.astype(F32) + mm(gated, w_ref[:, 128:256])).astype(BF16)
    shuffled = row_shuffle(result, lines, pairs)
    for t in range(pairs):
        out_ref[:, t * 128 : (t + 1) * 128] = shuffled[t * lines : (t + 1) * lines, :]


def call(kernel, out_shape, *args, **options):
    flops = options.pop("flops", 0)
    limit = pltpu.CompilerParams(vmem_limit_bytes=options.pop("mib", 8) * 1024 * 1024)
    moved = options.pop("moved", sum(a.size * a.dtype.itemsize for a in args))
    cost = pl.CostEstimate(flops=flops, bytes_accessed=moved, transcendentals=0)
    return pl.pallas_call(
        kernel, out_shape=out_shape, compiler_params=limit, cost_estimate=cost, **options
    )(*args)


def shape(*dims, dtype=BF16):
    return jax.ShapeDtypeStruct(dims, dtype)


def exchange(x, flip, devices):
    return lax.ppermute(x, "res", [(d, d ^ flip) for d in range(devices)])


def layer_normalize(values_in):
    centre = values_in - jnp.mean(values_in, axis=-1, keepdims=True)
    spread = jnp.mean(centre * centre, axis=-1, keepdims=True)
    return centre * lax.rsqrt(spread + EPS)


def column_complete(line, kept, vertical_matrix, vertical_exit_matrix, heads, depth):
    lines, columns, features = line.shape
    hidden = heads * depth
    normed = layer_normalize(line.astype(F32)).astype(BF16)
    projected = mm(normed.reshape(-1, features), vertical_matrix).reshape(lines, columns, -1)
    query, gate = projected[..., :hidden], projected[..., hidden : 2 * hidden]
    key = projected[..., 2 * hidden : 2 * hidden + depth]
    value = projected[..., 2 * hidden + depth :]
    count = jnp.maximum(jnp.sum(kept, axis=0), 1.0)[:, None]
    mean_query = jnp.sum(kept[..., None] * query, axis=0) / count * depth**-0.5
    logits = jnp.einsum("ihc,sic->sih", mean_query.reshape(columns, heads, depth), key)
    logits = logits + 1e9 * (kept - 1.0)[..., None]
    exped = jnp.exp(logits - jnp.max(logits, axis=0, keepdims=True))
    mixed = jnp.einsum("sih,sic->ihc", exped, value) / jnp.sum(exped, axis=0)[..., None]
    gate = jax.nn.sigmoid(gate).reshape(lines, columns, heads, depth)
    gated = (gate * mixed[None]).reshape(-1, hidden).astype(BF16)
    update = mm(gated, vertical_exit_matrix).reshape(lines, columns, features)
    return (line.astype(F32) + update).astype(BF16)


def on_device(
    seq_size,
    res_size,
    extra_activations,
    pair,
    present,
    amino,
    offset_matrix,
    horizontal_matrix,
    horizontal_exit_matrix,
    vertical_matrix,
    vertical_exit_matrix,
):
    lines, residues = present.shape
    pairs = residues // 2
    hidden = horizontal_exit_matrix.shape[0]
    heads = offset_matrix.shape[1]
    depth = hidden // heads
    groups = 2
    size = lines // (2 * groups)
    lead = size * pairs
    keys = res_size * residues
    rows = residues * heads
    core_bit, near, far, high = 1, 2, 4, 8
    kept = (present * amino[None, :]).astype(BF16)
    wide = jnp.pad(present, ((0, 16), (0, 128 - residues)))
    wide = (wide * jnp.pad(amino, (0, 128 - residues))[None, :]).astype(BF16)
    small = wide + jnp.pad(offset_matrix.T, ((lines, 16 - heads), (0, 0)))
    me = lax.axis_index("res").astype(jnp.int32).reshape(1)
    smem = pl.BlockSpec(memory_space=pltpu.SMEM)
    vmem = pl.BlockSpec(memory_space=pltpu.VMEM)

    rest = lead + pairs
    keep, send, line = call(
        functools.partial(prep_kernel, groups),
        [shape(groups, rest, 128)] * 2 + [shape(lines * pairs, 128)],
        me,
        extra_activations,
        small,
        in_specs=[smem, vmem, vmem],
        scratch_shapes=[
            pltpu.VMEM((lines * pairs, 128), BF16),
            pltpu.VMEM((2 * groups, pairs, 128), BF16),
        ],
    )

    received = exchange(send, core_bit, res_size)
    chunk = jnp.concatenate(
        [keep[:, :lead], received[:, :lead], keep[:, lead:] + received[:, lead:]], axis=1
    )
    levels = [exchange(chunk, high * k, res_size) for k in range(1, res_size // high)]
    kept_wide = call(
        functools.partial(presence_kernel, pairs),
        shape(lines * pairs, 128, dtype=F32),
        small,
        chunk,
        in_specs=[vmem, pl.BlockSpec(memory_space=pl.ANY)],
    )
    after = lax.optimization_barrier(chunk)
    early = [chunk] + [exchange(after, flip, res_size) for flip in (near, far)]

    per_step = 8
    pieces = 4
    whole = seq_size == 1
    bias_rows = [shape(rows, keys)] * 2
    bias = call(
        functools.partial(bias_kernel, whole, pieces, residues, heads),
        bias_rows if whole else [shape(rows, pair.shape[1])],
        pair.reshape((residues // 2, 2) + pair.shape[1:]),
        small,
        after,
        me,
        grid=(residues // per_step,),
        in_specs=[
            pl.BlockSpec((per_step // 2, 2) + pair.shape[1:], lambda n: (n, 0, 0, 0)),
            pl.BlockSpec(small.shape, lambda n: (0, 0)),
            pl.BlockSpec(memory_space=pl.ANY),
            smem,
        ],
        out_specs=[pl.BlockSpec((rows, pair.shape[1]), lambda n: (0, 0))] * (1 + whole),
        scratch_shapes=[
            pltpu.VMEM((rows // 128, pair.shape[1], 128), F32),
            pltpu.VMEM((2 * pair.shape[2], 2 * pair.shape[2]), BF16),
            pltpu.VMEM((pair.shape[2], rows), F32),
        ],
        flops=16 * pair.size * 128,
        mib=48,
    )
    if not whole:
        bias = call(
            functools.partial(order_kernel, residues, pieces),
            bias_rows,
            me,
            lax.all_gather(bias[0], "seq", axis=1, tiled=True),
            in_specs=[smem, vmem],
            mib=14,
        )
    levels, bias = lax.optimization_barrier((levels, bias))
    own = [jnp.stack([level[g] for level in levels]) for g in range(groups)]
    own, early = lax.optimization_barrier((own, early))
    beside = [exchange(part, near, res_size) for part in own]
    across = [exchange(part, far, res_size) for part in own]
    bias, lhs, sums, wv, gate, w_final = call(
        functools.partial(query_kernel, groups, size, pairs, heads),
        [
            shape(2 * rows, keys, dtype=F32),
            shape(groups * size, 2 * rows, 128),
            shape(groups * size, 2 * rows, 128, dtype=F32),
            shape(2 * heads * 128, 256),
            shape(2, groups * lead, 128, dtype=F32),
            shape(128, 6 * 128),
        ],
        bias[0],
        exchange(bias[1], core_bit, res_size),
        keep,
        received,
        horizontal_matrix,
        horizontal_exit_matrix,
        vertical_matrix,
        vertical_exit_matrix,
        chunk,
        *own,
        in_specs=[vmem] * (9 + groups),
        moved=0,
        mib=20,
    )

    def add(sums, places, parts):
        return call(
            functools.partial(add_kernel, groups, size, pairs, places),
            shape(*sums.shape, dtype=F32),
            lhs,
            bias,
            sums,
            *parts,
            flops=groups * size * rows * keys * 2 * 256 * 2 // 2,
            moved=0,
            mib=20,
        )

    beside[0], across[1], sums = lax.optimization_barrier((beside[0], across[1], sums))
    corner = [
        exchange(jnp.concatenate([early[1][:1], beside[0]]), far, res_size),
        exchange(jnp.concatenate([early[2][1:], across[1]]), near, res_size),
    ]
    sums = add(sums, (1, 2), (early[1], early[2], beside[0], across[1]))
    beside[1], across[0], sums = lax.optimization_barrier((beside[1], across[0], sums))
    sums = add(sums, (2, 1), (early[2], early[1], across[0], beside[1]))
    corner[0], corner[1], sums = lax.optimization_barrier((corner[0], corner[1], sums))
    anywhere = pl.BlockSpec(memory_space=pl.ANY)
    mine, theirs = call(
        functools.partial(finish_kernel, heads, groups, size, pairs, 3),
        [shape(groups * lead, 128)] * 2,
        lhs,
        bias,
        sums,
        wv,
        gate,
        *early,
        *corner,
        *own,
        *beside,
        *across,
        in_specs=[vmem] * (8 + groups) + [anywhere] * (3 * groups),
        scratch_shapes=[
            pltpu.VMEM((2, groups * lead, 128 * 2 * heads), BF16),
            pltpu.VMEM((2, groups * lead, 128), F32),
            pltpu.VMEM((2, 8, 128), F32),
            pltpu.VMEM((3 * groups,) + own[0].shape, BF16),
        ],
        flops=groups * size * rows * keys * 2 * 256,
        mib=24,
    )
    returned = exchange(theirs, core_bit, res_size)
    with_column = seq_size == 1
    final_args = [
        me,
        line,
        kept_wide,
        w_final,
    ]
    final_args += [mine, returned]
    result = call(
        functools.partial(final_kernel, lines, depth, with_column),
        shape(*extra_activations.shape) if with_column else shape(lines * pairs, 128),
        *final_args,
        in_specs=[smem] + [vmem] * (len(final_args) - 1),
        scratch_shapes=[pltpu.VMEM((lines * pairs, 128), BF16)],
    )
    if with_column:
        return result
    row = result.reshape(lines, residues, hidden)
    moved = lax.all_to_all(row, "seq", split_axis=1, concat_axis=0, tiled=True)
    moved_kept = lax.all_to_all(kept, "seq", split_axis=1, concat_axis=0, tiled=True)
    updated = column_complete(
        moved, moved_kept.astype(F32), vertical_matrix, vertical_exit_matrix, heads, depth
    )
    back = lax.all_to_all(updated, "seq", split_axis=0, concat_axis=1, tiled=True)
    return back.reshape(extra_activations.shape)


def solution(mesh):
    in_specs = (
        P("seq", "res"),
        P("res", "seq", None),
        P("seq", "res"),
        P("res"),
        P(),
        P(),
        P(),
        P(),
        P(),
    )
    sizes = mesh.shape
    return jax.shard_map(
        functools.partial(on_device, sizes["seq"], sizes["res"]),
        mesh=mesh,
        in_specs=in_specs,
        out_specs=P("seq", "res"),
        check_vma=False,
    )
```

```python
import functools
import math

import jax
import jax.numpy as jnp
from jax import lax
from jax.experimental import pallas as pl
from jax.experimental.pallas import tpu as pltpu
from jax.sharding import PartitionSpec as P

F32 = jnp.float32
BF16 = jnp.bfloat16
LOG2E = math.log2(math.e)
EPS = 1e-05

NT = (((1,), (1,)), ((), ()))


def mm(a, b):
    return jnp.dot(a, b, preferred_element_type=F32)


def mm_nt(a, b):
    return lax.dot_general(a, b, NT, preferred_element_type=F32)


def iota(shape, axis):
    return lax.broadcasted_iota(jnp.int32, shape, axis)


def one_hot(condition):
    return jnp.where(condition, 1.0, 0.0).astype(BF16)


def block_matrix(size, block, on_diagonal, elsewhere):
    row, col = iota((size, 1), 0), iota((1, size), 1)
    inside = jnp.where(row == col, on_diagonal, elsewhere)
    return jnp.where(row // block == col // block, inside, 0.0).astype(BF16)


def halves(value):
    high = value.astype(BF16)
    return high, (value - high.astype(F32)).astype(BF16)


def mm_split(value, matrix):
    high, low = halves(value)
    return mm(high, matrix) + mm(low, matrix)


def paired_norm(x, width):
    lanes = x.shape[1]
    centre = mm(x, block_matrix(lanes, width, 1.0 - 1.0 / width, -1.0 / width))
    spread = mm_split(centre * centre, block_matrix(lanes, width, 1.0 / width, 1.0 / width))
    return (centre * lax.rsqrt(spread + EPS)).astype(BF16)


def row_shuffle(rows, inner, outer):
    total = rows.shape[0]
    row, col = iota((total, 1), 0), iota((1, total), 1)
    return mm(one_hot(col == (row % inner) * outer + row // inner), rows).astype(BF16)


def prep_kernel(groups, me_ref, m_ref, kept_ref, *refs):
    keep_ref, send_ref, line_ref, normed_ref, spread_ref = refs
    lines, width = m_ref.shape
    pairs = width // 128
    stacked = jnp.concatenate([m_ref[:, t * 128 : (t + 1) * 128] for t in range(pairs)], axis=0)
    normed = paired_norm(stacked, 64)
    both = row_shuffle(jnp.concatenate([normed, stacked], axis=1), pairs, lines)
    normed_ref[...] = both[:, :128]
    line_ref[...] = both[:, 128:]
    kept = kept_ref[...]
    size = lines // (2 * groups)
    residues = 2 * pairs
    row, col = iota((pairs, residues), 0), iota((pairs, residues), 1)
    evens, odds = one_hot(col == 2 * row), one_hot(col == 2 * row + 1)
    row, col = iota((128, lines), 0) - 64, iota((128, lines), 1)
    core = me_ref[0] % 2
    for n in range(2 * groups):
        start = jnp.where(n // groups == core, 0, 2 * size)
        chosen = (row >= start) & (row < start + 2 * size) & (row % size == col - n * size)
        spread = mm(one_hot(chosen), kept).astype(BF16)
        first = iota((pairs, 128), 1) < 64 + size + start
        spread_ref[n] = jnp.where(first, mm_nt(evens, spread), mm_nt(odds, spread)).astype(BF16)
    rows = size * pairs
    for ref, half in ((keep_ref, core), (send_ref, 1 - core)):
        for g in range(groups):
            index = half * groups + g
            ref[g, :rows] = normed_ref[pl.ds(pl.multiple_of(index * rows, rows), rows), :]
            ref[g, rows:] = spread_ref[index]


def bias_kernel(whole, pieces, residues, x_ref, w_ref, after_ref, me_ref, *refs):
    outs, (acc_ref, centring_ref, wide_ref) = refs[:-3], refs[-3:]
    step = pl.program_id(0)
    heads = w_ref.shape[0]
    per_step, keys, channels = 2 * x_ref.shape[0], x_ref.shape[2], x_ref.shape[3]
    pairs = residues // 2
    tiles = acc_ref.shape[0]
    width = tiles * 128

    @pl.when(step == 0)
    def _():
        centring_ref[...] = block_matrix(
            2 * channels, channels, 1.0 - 1.0 / channels, -1.0 / channels
        )
        spread = one_hot(iota((heads, 1), 0) == iota((1, width), 1) // residues)
        wide_ref[...] = lax.dot_general(
            w_ref[...], spread, (((0,), (0,)), ((), ())), preferred_element_type=F32
        )
        acc_ref[...] = jnp.zeros(acc_ref.shape, F32)

    lane = iota((1, width), 1) % residues
    placed = []
    for n in range(per_step):
        residue = step * per_step + n
        mine = lane == (residue % 2) * pairs + residue // 2
        placed.append(jnp.where(mine, wide_ref[...], 0.0).astype(BF16))
    placed = jnp.concatenate(placed, axis=0)
    centring = centring_ref[...]
    piece = min(512, keys)
    for r in range(0, keys, piece):
        normed = []
        for n in range(0, per_step, 2):
            x = [x_ref[n // 2, p, r : r + piece] for p in range(2)]
            x = jnp.concatenate(x, axis=1)
            centre = mm(x, centring)
            for part in (centre[:, :channels], centre[:, channels:]):
                spread = jnp.mean(part * part, axis=-1, keepdims=True)
                normed.append((part * lax.rsqrt(spread + EPS)).astype(BF16))
        added = mm(jnp.concatenate(normed, axis=1), placed)
        for n in range(tiles):
            acc_ref[n, r : r + piece, :] += added[:, n * 128 : (n + 1) * 128]

    @pl.when(step == pl.num_programs(0) - 1)
    def _():
        if not whole:
            for n in range(tiles):
                outs[0][n * 128 : (n + 1) * 128, :] = acc_ref[n].T.astype(BF16)
            return
        levels = keys // (2 * pieces * residues)
        for flip in range(2):
            user = me_ref[0] ^ flip
            starts = [
                (user ^ (c + 2 * q + 2 * pieces * k)) * residues + p
                for q in range(pieces)
                for p in range(2)
                for k in range(levels)
                for c in range(2)
            ]
            for n in range(tiles):
                for at in range(0, keys, 128):
                    rows = [
                        acc_ref[n, pl.ds(start, pairs, stride=2), :]
                        for start in starts[at // pairs : (at + 128) // pairs]
                    ]
                    turned = jnp.concatenate(rows, axis=0).T.astype(BF16)
                    outs[flip][n * 128 : (n + 1) * 128, at : at + 128] = turned


def order_kernel(residues, pieces, me_ref, bias_ref, own_ref, send_ref):
    rows, keys = bias_ref.shape
    pairs = residues // 2
    lane = iota((1, keys), 1)
    each = keys // pieces
    which, rest = lane // each, lane % each
    parity, rest = rest // (each // 2), rest % (each // 2)
    place, pair = rest // pairs, rest % pairs
    for flip, out_ref in enumerate((own_ref, send_ref)):
        device = me_ref[0] ^ flip ^ ((place % 2) + 2 * which + 2 * pieces * (place // 2))
        target = device * residues + 2 * pair + parity
        total = jnp.zeros((rows, keys), F32)
        for start in range(0, keys, 256):
            chosen = one_hot(iota((256, keys), 0) + start == target)
            total = total + mm(bias_ref[:, start : start + 256], chosen)
        out_ref[...] = total.astype(BF16)


def pair_matrix(matrix, chosen):
    rows, columns = matrix.shape
    lane = iota((1, 128), 1)
    twice_rows = one_hot(iota((128, 1), 0) % rows == iota((1, rows), 1))
    picked = one_hot(iota((columns, 1), 0) == chosen)
    wide = mm(mm(twice_rows, matrix).astype(BF16), picked)
    same = iota((128, 1), 0) // rows == lane // (128 // 2)
    return jnp.where(same, wide, 0.0).astype(BF16)


def value_matrix(matrix, hidden, heads):
    depth = hidden // heads
    row, col = iota((128, 1), 0), iota((1, 256), 1)
    picked = one_hot(iota((4 * hidden, 1), 0) == 2 * hidden + col % hidden)
    picked = jnp.where(col < 128, picked, jnp.zeros_like(picked))
    wv = mm(mm(one_hot(row == iota((1, hidden), 1)), matrix).astype(BF16), picked)
    counted = (row >= hidden) & (col >= 128)
    wv = jnp.where(counted, 1.0 / (128 - hidden), wv)
    owner = col % 128 // depth
    return [
        jnp.where(owner == p * heads + h, wv, 0.0).astype(BF16)
        for h in range(heads)
        for p in range(2)
    ]


def presence_kernel(pairs, kept_ref, after_ref, wide_ref):
    total, lines = wide_ref.shape[0], kept_ref.shape[0]
    spread = mm(one_hot(iota((total, 1), 0) // pairs == iota((1, lines), 1)), kept_ref[...])
    mine = iota((1, 2 * pairs), 1) // 2 == iota((total, 1), 0) % pairs
    sides = one_hot(iota((2 * pairs, 1), 0) % 2 == iota((1, 128), 1) // 64)
    wide_ref[...] = mm(jnp.where(mine, spread, 0.0).astype(BF16), sides)


def query_kernel(
    groups, size, pairs, heads, own_ref, peer_ref, keep_ref, received_ref, w_ref, exit_ref,
    column_ref, column_exit_ref, *refs
):
    pieces = [levels_of(refs[0], g, refs[1 + g]) for g in range(groups)]
    bias_ref, lhs_ref, sums_ref, wv_ref, gate_ref, final_ref = refs[1 + groups :]
    rows = own_ref.shape[0]
    bias_ref[:rows, :] = own_ref[...].astype(F32) * LOG2E
    bias_ref[rows:, :] = peer_ref[...].astype(F32) * LOG2E

    hidden = w_ref.shape[0]
    depth = hidden // heads
    lane = iota((1, 128), 1)
    wq = pair_matrix(w_ref[...], lane % hidden)
    wg = pair_matrix(w_ref[...], 3 * hidden + lane % hidden)
    for n, part in enumerate(value_matrix(w_ref[...], hidden, heads)):
        wv_ref[n * 128 : (n + 1) * 128, :] = part
    final = [
        (exit_ref, lane % hidden),
        (column_exit_ref, lane % hidden),
        (column_ref, lane % hidden),
        (column_ref, hidden + lane % hidden),
        (column_ref, 2 * hidden + lane % depth),
        (column_ref, 2 * hidden + depth + lane % depth),
    ]
    for n, (ref, chosen) in enumerate(final):
        final_ref[:, n * 128 : (n + 1) * 128] = pair_matrix(ref[...], chosen)
    picked = one_hot(iota((1, 4 * hidden), 1) == hidden + iota((128, 1), 0) % hidden)
    wk = mm_nt(picked, w_ref[...]).astype(BF16)
    wk = mm(wk, one_hot(iota((hidden, 1), 0) == iota((1, 128), 1))).astype(BF16)
    lead = size * pairs
    spare = lane - hidden
    for g in range(groups):
        for n, ref in enumerate((keep_ref, received_ref)):
            gate_ref[n, g * lead : (g + 1) * lead] = jax.nn.sigmoid(mm(ref[g, :lead], wg))
            query = (mm(ref[g, :lead], wq) * (depth**-0.5)).astype(BF16).astype(F32)
            for s in range(size):
                q = query[s * pairs : (s + 1) * pairs]
                spread = [
                    jnp.where(lane // depth == p * heads + h, q, 0.0).astype(BF16)
                    for h in range(heads)
                    for p in range(2)
                ]
                folded = mm(jnp.concatenate(spread, axis=0), wk) * LOG2E
                picks = (spare >= 0) & (spare < 4 * size) & (spare % size == s)
                lhs_ref[g * size + s, n * rows : (n + 1) * rows, :] = jnp.where(
                    picks, 1.0, folded
                ).astype(BF16)
    add_pieces(groups, size, pairs, (0,) * groups, lhs_ref, bias_ref, None, pieces, sums_ref)


def levels_of(first, g, rest):
    return [first.at[g]] + [rest.at[k] for k in range(rest.shape[0])]


def masks_of(levels, size, pairs):
    start = 2 * size * pairs
    lane = iota((1, 128), 1) - 64
    masks = []
    for p in range(2):
        blocks = []
        for level in levels:
            hidden = (1e9 * LOG2E) * (level[start : start + pairs, :].astype(F32) - 1.0)
            for c in range(2):
                first = (2 * c + p) * size
                mine = (lane >= first) & (lane < first + size)
                blocks.append(jnp.where(mine, hidden, 0.0).astype(BF16))
        masks.append(jnp.concatenate(blocks, axis=0))
    return masks


def keys_of(levels, masks, s, size, pairs):
    start = s * pairs
    if not isinstance(s, int):
        start = pl.multiple_of(start, pairs)
    even = jnp.concatenate(
        [level[pl.ds(c * size * pairs + start, pairs), :] for level in levels for c in range(2)],
        axis=0,
    )
    odd = pltpu.roll(even.astype(F32), 64, 1).astype(BF16)
    low = iota(even.shape, 1) < 64
    one = jnp.ones_like(even)
    keyed = [jnp.where(low, x, m) for x, m in zip((even, odd), masks)]
    valued = [jnp.where(low, x, one) for x in (even, odd)]
    return jnp.concatenate(keyed, axis=0), jnp.concatenate(valued, axis=0)


def weigh(lhs, bias_ref, piece, keyed):
    width = keyed.shape[0]
    logits = mm_nt(lhs, keyed) + bias_ref[:, piece * width : (piece + 1) * width]
    return jnp.exp2(logits).astype(BF16)


def each_line(groups, size, pairs, places, lhs_ref, bias_ref, pieces, use):
    masks = [masks_of(levels, size, pairs) for levels in pieces]

    def weights_of(s, g):
        keyed, valued = keys_of(pieces[g], masks[g], s, size, pairs)
        return weigh(lhs_ref[g * size + s], bias_ref, places[g], keyed), valued

    order = [(s, g) for s in range(size) for g in range(groups)]
    ahead = weights_of(*order[0])
    for n, (s, g) in enumerate(order):
        now, ahead = ahead, weights_of(*order[n + 1]) if n + 1 < len(order) else None
        use(g * size + s, mm(*now))


def add_pieces(groups, size, pairs, places, lhs_ref, bias_ref, before_ref, pieces, out_ref):
    def use(line, total):
        out_ref[line] = total if before_ref is None else before_ref[line] + total

    each_line(groups, size, pairs, places, lhs_ref, bias_ref, pieces, use)


def add_kernel(groups, size, pairs, places, lhs_ref, bias_ref, before_ref, *refs):
    pieces = [levels_of(refs[g], g, refs[groups + g]) for g in range(groups)]
    add_pieces(groups, size, pairs, places, lhs_ref, bias_ref, before_ref, pieces, refs[-1])


def finish_kernel(
    heads, groups, size, pairs, place, lhs_ref, bias_ref, sums_ref, wv_ref, gate_ref, *refs
):
    first_refs, last_refs, far_refs = refs[:3], refs[3 : 3 + groups], refs[3 + groups : 3 + 4 * groups]
    mine_ref, theirs_ref, turned_ref, copy_ref = refs[3 + 4 * groups :]
    last = [[ref.at[k] for k in range(ref.shape[0])] for ref in last_refs]
    blocks = 2 * heads

    def settle(line, total):
        start = line * pairs
        if not isinstance(line, int):
            start = pl.multiple_of(start, pairs)
        total = total.astype(BF16)
        for n in range(2):
            for b in range(blocks):
                part = total[(n * blocks + b) * pairs : (n * blocks + b + 1) * pairs]
                turned_ref[n, pl.ds(start, pairs), b * 128 : (b + 1) * 128] = part

    def mix():
        lead = groups * size * pairs
        mixed = mm(turned_ref[...].reshape(2 * lead, blocks * 128), wv_ref[...])
        weights = mixed[:, 128:]
        mixed = (mixed[:, :128] / weights).reshape(2, lead, 128)
        for n, out_ref in enumerate((mine_ref, theirs_ref)):
            out_ref[...] = (gate_ref[n] * mixed[n]).astype(BF16)
        return weights


    def use(line, total):
        total = sums_ref[line] + total
        settle(line, total)

    each_line(groups, size, pairs, (place,) * groups, lhs_ref, bias_ref, last, use)
    weights = mix()
    fine = (weights > 2.0**-80) & (weights < 2.0**100)

    @pl.when(jnp.min(jnp.where(fine, 1.0, 0.0)) < 0.5)
    def _():
        for n, ref in enumerate(far_refs):
            pltpu.sync_copy(ref, copy_ref.at[n])
        for g in range(groups):
            ordered = [
                levels_of(first_refs[n], g, copy_ref.at[n * groups + g]) for n in range(3)
            ] + [last[g]]
            all_masks = [masks_of(ref, size, pairs) for ref in ordered]

            def exact_line(s, carry):
                line = g * size + s
                both = [keys_of(r, m, s, size, pairs) for r, m in zip(ordered, all_masks)]
                logits = []
                for n, (keyed, _) in enumerate(both):
                    width = keyed.shape[0]
                    bias = bias_ref[:, n * width : (n + 1) * width]
                    logits.append(mm_nt(lhs_ref[line], keyed) + bias)
                peak = functools.reduce(jnp.maximum, logits)
                peak = jnp.max(peak, axis=-1, keepdims=True)
                parts = [
                    mm(jnp.exp2(part - peak).astype(BF16), valued)
                    for part, (_, valued) in zip(logits, both)
                ]
                settle(line, sum(parts[1:], parts[0]))
                return carry

            lax.fori_loop(0, size, exact_line, 0)
        mix()


def final_kernel(
    lines, depth, with_column, me_ref, line_ref, kept_ref, w_ref, mine_ref, theirs_ref, out_ref,
    gated_ref,
):
    total = line_ref.shape[0]
    pairs = total // lines
    core = me_ref[0] % 2
    share = total // 2
    for owner, ref in ((core, mine_ref), (1 - core, theirs_ref)):
        gated_ref[pl.ds(pl.multiple_of(owner * share, share), share), :] = ref[...]
    row = (line_ref[...].astype(F32) + mm(gated_ref[...], w_ref[:, :128])).astype(BF16)
    if not with_column:
        out_ref[...] = row
        return
    kept = kept_ref[...]
    projected = mm(paired_norm(row, 64), w_ref[:, 256:])
    query, gate, key, value = [projected[:, 128 * n : 128 * (n + 1)] for n in range(4)]

    def grid(a):
        return a.reshape(lines, pairs, 128)

    count = jnp.maximum(jnp.sum(grid(kept), axis=0), 1.0)
    mean_query = jnp.sum(grid(kept * query), axis=0) / count * (depth**-0.5)
    same_head = block_matrix(128, depth, 1.0, 1.0)
    product = (mean_query[None] * grid(key)).reshape(total, 128)
    logits = grid(mm_split(product, same_head) + 1e9 * (kept - 1.0))
    exped = jnp.exp(logits - jnp.max(logits, axis=0, keepdims=True))
    mixed = jnp.sum(exped * grid(value), axis=0) / jnp.sum(exped, axis=0)
    gated = (jax.nn.sigmoid(grid(gate)) * mixed[None]).reshape(total, 128).astype(BF16)
    result = (row.astype(F32) + mm(gated, w_ref[:, 128:256])).astype(BF16)
    shuffled = row_shuffle(result, lines, pairs)
    for t in range(pairs):
        out_ref[:, t * 128 : (t + 1) * 128] = shuffled[t * lines : (t + 1) * lines, :]


def call(kernel, out_shape, *args, **options):
    flops = options.pop("flops", 0)
    limit = pltpu.CompilerParams(vmem_limit_bytes=options.pop("mib", 8) * 1024 * 1024)
    moved = options.pop("moved", sum(a.size * a.dtype.itemsize for a in args))
    cost = pl.CostEstimate(flops=flops, bytes_accessed=moved, transcendentals=0)
    return pl.pallas_call(
        kernel, out_shape=out_shape, compiler_params=limit, cost_estimate=cost, **options
    )(*args)


def shape(*dims, dtype=BF16):
    return jax.ShapeDtypeStruct(dims, dtype)


def exchange(x, flip, devices):
    return lax.ppermute(x, "res", [(d, d ^ flip) for d in range(devices)])


def layer_normalize(values_in):
    centre = values_in - jnp.mean(values_in, axis=-1, keepdims=True)
    spread = jnp.mean(centre * centre, axis=-1, keepdims=True)
    return centre * lax.rsqrt(spread + EPS)


def column_complete(line, kept, vertical_matrix, vertical_exit_matrix, heads, depth):
    lines, columns, features = line.shape
    hidden = heads * depth
    normed = layer_normalize(line.astype(F32)).astype(BF16)
    projected = mm(normed.reshape(-1, features), vertical_matrix).reshape(lines, columns, -1)
    query, gate = projected[..., :hidden], projected[..., hidden : 2 * hidden]
    key = projected[..., 2 * hidden : 2 * hidden + depth]
    value = projected[..., 2 * hidden + depth :]
    count = jnp.maximum(jnp.sum(kept, axis=0), 1.0)[:, None]
    mean_query = jnp.sum(kept[..., None] * query, axis=0) / count * depth**-0.5
    logits = jnp.einsum("ihc,sic->sih", mean_query.reshape(columns, heads, depth), key)
    logits = logits + 1e9 * (kept - 1.0)[..., None]
    exped = jnp.exp(logits - jnp.max(logits, axis=0, keepdims=True))
    mixed = jnp.einsum("sih,sic->ihc", exped, value) / jnp.sum(exped, axis=0)[..., None]
    gate = jax.nn.sigmoid(gate).reshape(lines, columns, heads, depth)
    gated = (gate * mixed[None]).reshape(-1, hidden).astype(BF16)
    update = mm(gated, vertical_exit_matrix).reshape(lines, columns, features)
    return (line.astype(F32) + update).astype(BF16)


def on_device(
    seq_size,
    res_size,
    extra_activations,
    pair,
    present,
    amino,
    offset_matrix,
    horizontal_matrix,
    horizontal_exit_matrix,
    vertical_matrix,
    vertical_exit_matrix,
):
    lines, residues = present.shape
    pairs = residues // 2
    hidden = horizontal_exit_matrix.shape[0]
    heads = offset_matrix.shape[1]
    depth = hidden // heads
    groups = 2
    size = lines // (2 * groups)
    lead = size * pairs
    keys = res_size * residues
    rows = residues * heads
    core_bit, near, far, high = 1, 2, 4, 8
    kept = (present * amino[None, :]).astype(BF16)
    me = lax.axis_index("res").astype(jnp.int32).reshape(1)
    smem = pl.BlockSpec(memory_space=pltpu.SMEM)
    vmem = pl.BlockSpec(memory_space=pltpu.VMEM)

    rest = lead + pairs
    keep, send, line = call(
        functools.partial(prep_kernel, groups),
        [shape(groups, rest, 128)] * 2 + [shape(lines * pairs, 128)],
        me,
        extra_activations,
        kept,
        in_specs=[smem, vmem, vmem],
        scratch_shapes=[
            pltpu.VMEM((lines * pairs, 128), BF16),
            pltpu.VMEM((2 * groups, pairs, 128), BF16),
        ],
    )

    received = exchange(send, core_bit, res_size)
    chunk = jnp.concatenate(
        [keep[:, :lead], received[:, :lead], keep[:, lead:] + received[:, lead:]], axis=1
    )
    levels = [exchange(chunk, high * k, res_size) for k in range(1, res_size // high)]
    kept_wide = call(
        functools.partial(presence_kernel, pairs),
        shape(lines * pairs, 128, dtype=F32),
        kept,
        chunk,
        in_specs=[vmem, pl.BlockSpec(memory_space=pl.ANY)],
    )
    after = lax.optimization_barrier(chunk)
    early = [chunk] + [exchange(after, flip, res_size) for flip in (near, far)]

    per_step = 8
    pieces = 4
    whole = seq_size == 1
    bias_rows = [shape(rows, keys)] * 2
    bias = call(
        functools.partial(bias_kernel, whole, pieces, residues),
        bias_rows if whole else [shape(rows, pair.shape[1])],
        pair.reshape((residues // 2, 2) + pair.shape[1:]),
        offset_matrix.T,
        after,
        me,
        grid=(residues // per_step,),
        in_specs=[
            pl.BlockSpec((per_step // 2, 2) + pair.shape[1:], lambda n: (n, 0, 0, 0)),
            pl.BlockSpec(offset_matrix.shape[::-1], lambda n: (0, 0)),
            pl.BlockSpec(memory_space=pl.ANY),
            smem,
        ],
        out_specs=[pl.BlockSpec((rows, pair.shape[1]), lambda n: (0, 0))] * (1 + whole),
        scratch_shapes=[
            pltpu.VMEM((rows // 128, pair.shape[1], 128), F32),
            pltpu.VMEM((2 * pair.shape[2], 2 * pair.shape[2]), BF16),
            pltpu.VMEM((pair.shape[2], rows), F32),
        ],
        flops=16 * pair.size * 128,
        mib=48,
    )
    if not whole:
        bias = call(
            functools.partial(order_kernel, residues, pieces),
            bias_rows,
            me,
            lax.all_gather(bias[0], "seq", axis=1, tiled=True),
            in_specs=[smem, vmem],
            mib=14,
        )
    levels, bias = lax.optimization_barrier((levels, bias))
    own = [jnp.stack([level[g] for level in levels]) for g in range(groups)]
    own, early = lax.optimization_barrier((own, early))
    beside = [exchange(part, near, res_size) for part in own]
    across = [exchange(part, far, res_size) for part in own]
    bias, lhs, sums, wv, gate, w_final = call(
        functools.partial(query_kernel, groups, size, pairs, heads),
        [
            shape(2 * rows, keys, dtype=F32),
            shape(groups * size, 2 * rows, 128),
            shape(groups * size, 2 * rows, 128, dtype=F32),
            shape(2 * heads * 128, 256),
            shape(2, groups * lead, 128, dtype=F32),
            shape(128, 6 * 128),
        ],
        bias[0],
        exchange(bias[1], core_bit, res_size),
        keep,
        received,
        horizontal_matrix,
        horizontal_exit_matrix,
        vertical_matrix,
        vertical_exit_matrix,
        chunk,
        *own,
        in_specs=[vmem] * (9 + groups),
        moved=0,
        mib=20,
    )

    def add(sums, places, parts):
        return call(
            functools.partial(add_kernel, groups, size, pairs, places),
            shape(*sums.shape, dtype=F32),
            lhs,
            bias,
            sums,
            *parts,
            flops=groups * size * rows * keys * 2 * 256 * 2 // 2,
            moved=0,
            mib=20,
        )

    beside[0], across[1], sums = lax.optimization_barrier((beside[0], across[1], sums))
    corner = [
        exchange(jnp.concatenate([early[1][:1], beside[0]]), far, res_size),
        exchange(jnp.concatenate([early[2][1:], across[1]]), near, res_size),
    ]
    sums = add(sums, (1, 2), (early[1], early[2], beside[0], across[1]))
    beside[1], across[0], sums = lax.optimization_barrier((beside[1], across[0], sums))
    sums = add(sums, (2, 1), (early[2], early[1], across[0], beside[1]))
    corner[0], corner[1], sums = lax.optimization_barrier((corner[0], corner[1], sums))
    anywhere = pl.BlockSpec(memory_space=pl.ANY)
    mine, theirs = call(
        functools.partial(finish_kernel, heads, groups, size, pairs, 3),
        [shape(groups * lead, 128)] * 2,
        lhs,
        bias,
        sums,
        wv,
        gate,
        *early,
        *corner,
        *own,
        *beside,
        *across,
        in_specs=[vmem] * (8 + groups) + [anywhere] * (3 * groups),
        scratch_shapes=[
            pltpu.VMEM((2, groups * lead, 128 * 2 * heads), BF16),
            pltpu.VMEM((3 * groups,) + own[0].shape, BF16),
        ],
        flops=groups * size * rows * keys * 2 * 256,
        mib=24,
    )
    returned = exchange(theirs, core_bit, res_size)
    with_column = seq_size == 1
    final_args = [
        me,
        line,
        kept_wide,
        w_final,
    ]
    final_args += [mine, returned]
    result = call(
        functools.partial(final_kernel, lines, depth, with_column),
        shape(*extra_activations.shape) if with_column else shape(lines * pairs, 128),
        *final_args,
        in_specs=[smem] + [vmem] * (len(final_args) - 1),
        scratch_shapes=[pltpu.VMEM((lines * pairs, 128), BF16)],
    )
    if with_column:
        return result
    row = result.reshape(lines, residues, hidden)
    moved = lax.all_to_all(row, "seq", split_axis=1, concat_axis=0, tiled=True)
    moved_kept = lax.all_to_all(kept, "seq", split_axis=1, concat_axis=0, tiled=True)
    updated = column_complete(
        moved, moved_kept.astype(F32), vertical_matrix, vertical_exit_matrix, heads, depth
    )
    back = lax.all_to_all(updated, "seq", split_axis=0, concat_axis=1, tiled=True)
    return back.reshape(extra_activations.shape)


def solution(mesh):
    in_specs = (
        P("seq", "res"),
        P("res", "seq", None),
        P("seq", "res"),
        P("res"),
        P(),
        P(),
        P(),
        P(),
        P(),
    )
    sizes = mesh.shape
    return jax.shard_map(
        functools.partial(on_device, sizes["seq"], sizes["res"]),
        mesh=mesh,
        in_specs=in_specs,
        out_specs=P("seq", "res"),
        check_vma=False,
    )
```
